32 devices in a mesh: dp: 8 (over y, x, core), rows: 4 (over z).
Axes of the slice: x: 2, y: 2, z: 4, core: 2. Of those that a mesh axis runs over, the one named last changes fastest.
Arguments:
- images: bfloat16 [8, 12, 48, 1280], P('dp', 'rows'), may hold values from -6 to 6
- cotangent: bfloat16 [8, 12, 48, 1280], P('dp', 'rows'), may hold values from -6 to 6
- first_weight: bfloat16 [8, 4, 9, 51200], P('dp', 'rows'), may hold values from -0.0546875 to 0.0546875
- second_weight: bfloat16 [8, 4, 9, 51200], P('dp', 'rows'), may hold values from -0.0546875 to 0.0546875
- first_basis: float32 [64, 1280], replicated, may hold values from -0.15625 to 0.15625
- second_basis: float32 [64, 1280], replicated, may hold values from -0.15625 to 0.15625
Outputs:
- block_output: bfloat16 [8, 12, 48, 1280], P('dp', 'rows')
- first_grad: float32 [8, 4, 9, 51200], P('dp', 'rows')
- second_grad: float32 [8, 4, 9, 51200], P('dp', 'rows')
The draws below stay inside these ranges and needn't reach their ends.
All inputs are finite; a program needn't handle non-finite values.
Results may differ from the reference program's by a relative error of at most 0.014.
Values may be sent and summed in bfloat16 or wider, within the bound.
No kernel may reach another device: no remote copies, remote signals or barrier semaphores. Data moves between devices by JAX's collectives and lax.ppermute only.
A program may use at most 192 MiB of HBM per device.

```python
import math
import jax
import jax.numpy as jnp
from jax import lax

CHANNELS = 1280
GROUPS = 32
RANK = 64
LAT_W = 48
IMAGES = 8
LAT_H = 12
N_DP = 8
N_ROWS = 4


def strengthened(drawn, stream_key, source, target, blocks, factor):
    def block_of(axis_at):
        return (jnp.arange(drawn.shape[axis_at]) // (drawn.shape[axis_at] // blocks)).reshape((-1,) + (1,) * (drawn.ndim - 1 - axis_at))

    near = jax.random.permutation(stream_key, blocks)[block_of(target)]
    second = (block_of(target) + blocks // 2) % blocks
    return jnp.where((block_of(source) == near) | (block_of(source) == second), factor * drawn, drawn)


def steps_of(own_key, shape, pieces, smallest, top_value):
    level, own = 1.0, jax.random.fold_in(own_key, 6)
    for axis_at, parts in pieces:
        heights = jnp.exp(jax.random.uniform(jax.random.fold_in(own, axis_at), (parts,), jnp.float32, smallest / len(pieces), top_value / len(pieces)))
        level = level * jnp.repeat(heights, shape[axis_at] // parts).reshape([-1 if axis == axis_at else 1 for axis in range(len(shape))])
    return level


def normal_values(stream_key, dims, scale, bound, shards=(), kind=jnp.bfloat16):
    factor_of = steps_of(stream_key, dims, shards, -0.22, 0.18) if shards else 1.0
    values = jax.random.normal(stream_key, dims, jnp.float32) * scale * factor_of
    return jnp.minimum(jnp.maximum(values, -bound), bound).astype(kind)


def heavy_noise(own_key, extent, scale, most, pieces, heavy, held_as=jnp.bfloat16):
    entries = scale * jax.random.normal(own_key, extent, jnp.float32)
    if pieces:
        entries = entries * steps_of(own_key, extent, pieces, -0.22, 0.18)
    return jnp.clip(strengthened(entries, jax.random.fold_in(own_key, 3), *heavy), -most, most).astype(held_as)


def setup_inputs(seed: int = 0) -> dict:
    key_of = jax.random.split(jax.random.key(seed), 7)
    return {
        "images": normal_values(key_of[0], (IMAGES, LAT_H, LAT_W, CHANNELS), 1.0, 6.0, ((0, 8), (1, 4))),
        "cotangent": heavy_noise(key_of[1], (IMAGES, LAT_H, LAT_W, CHANNELS), 1.0, 6.0, ((0, 8), (1, 4)), (0, 3, 8, 2.0)),
        "first_weight": normal_values(key_of[2], (N_DP, N_ROWS, 9, (CHANNELS // N_DP) * (CHANNELS // N_ROWS)), (9 * CHANNELS) ** -0.5, 0.0546875, ((0, 8), (1, 4))),
        "second_weight": normal_values(key_of[3], (N_DP, N_ROWS, 9, (CHANNELS // N_DP) * (CHANNELS // N_ROWS)), (9 * CHANNELS) ** -0.5, 0.0546875, ((0, 8), (1, 4))),
        "first_basis": normal_values(key_of[4], (RANK, CHANNELS), CHANNELS ** -0.5, 0.15625, (), jnp.float32),
        "second_basis": normal_values(key_of[5], (RANK, CHANNELS), CHANNELS ** -0.5, 0.15625, (), jnp.float32),
    }


def normalize(values):
    full_shape = values.shape
    size_group = CHANNELS // GROUPS
    grouped = values.reshape(full_shape[:-1] + (full_shape[-1] // size_group, size_group))
    center = lax.optimization_barrier(jnp.mean(grouped, axis=(1, 2, 4), keepdims=True))
    spread = lax.optimization_barrier(jnp.mean(jnp.square(grouped - center), axis=(1, 2, 4), keepdims=True))
    return ((grouped - center) / jnp.sqrt(spread + 1e-05)).reshape(full_shape)

def activate(values):
    return jax.nn.silu(normalize(values))

def convolve(inputs, kernel):
    padded = jnp.pad(inputs.astype(jnp.float32), ((0, 0), (1, 1), (1, 1), (0, 0)))
    kernel_wide = kernel.astype(jnp.float32)
    height = inputs.shape[1]
    width = inputs.shape[2]
    summed = jnp.zeros(inputs.shape[:3] + (kernel.shape[3],), jnp.float32)
    for row_tap in range(3):
        for col_tap in range(3):
            window = padded[:, row_tap:row_tap + height, col_tap:col_tap + width]
            summed = summed + jnp.einsum('nhwc,cd->nhwd', window, kernel_wide[row_tap, col_tap])
    return summed

def weight_grad(inputs, grads):
    padded = jnp.pad(inputs.astype(jnp.float32), ((0, 0), (1, 1), (1, 1), (0, 0)))
    grads_wide = grads.astype(jnp.float32)
    height = inputs.shape[1]
    width = inputs.shape[2]
    taps = []
    for row_tap in range(3):
        row_list = []
        for col_tap in range(3):
            window = padded[:, row_tap:row_tap + height, col_tap:col_tap + width]
            row_list.append(jnp.einsum('nhwc,nhwd->cd', window, grads_wide))
        taps.append(jnp.stack(row_list))
    return jnp.stack(taps)

def project(raw_grad, basis):
    coefficient = jnp.einsum('abcd,rc->abrd', raw_grad, basis, precision=lax.Precision.HIGHEST)
    return raw_grad - jnp.einsum('rc,abrd->abcd', basis, coefficient, precision=lax.Precision.HIGHEST)

def first_kernel(flat):
    dp_width = CHANNELS // N_DP
    rows_width = CHANNELS // N_ROWS
    blocks = flat.reshape(N_DP, N_ROWS, 3, 3, dp_width, rows_width)
    return jnp.transpose(blocks, (2, 3, 0, 4, 1, 5)).reshape(3, 3, CHANNELS, CHANNELS)

def second_kernel(flat):
    dp_width = CHANNELS // N_DP
    rows_width = CHANNELS // N_ROWS
    blocks = flat.reshape(N_DP, N_ROWS, 3, 3, dp_width, rows_width)
    return jnp.transpose(blocks, (2, 3, 1, 5, 0, 4)).reshape(3, 3, CHANNELS, CHANNELS)

def first_flat(grad):
    dp_width = CHANNELS // N_DP
    rows_width = CHANNELS // N_ROWS
    blocks = grad.reshape(3, 3, N_DP, dp_width, N_ROWS, rows_width)
    return jnp.transpose(blocks, (2, 4, 0, 1, 3, 5)).reshape(N_DP, N_ROWS, 9, dp_width * rows_width)

def second_flat(grad):
    dp_width = CHANNELS // N_DP
    rows_width = CHANNELS // N_ROWS
    blocks = grad.reshape(3, 3, N_ROWS, rows_width, N_DP, dp_width)
    return jnp.transpose(blocks, (4, 2, 0, 1, 5, 3)).reshape(N_DP, N_ROWS, 9, dp_width * rows_width)

def reference(images, cotangent, first_weight, second_weight, first_basis, second_basis):
    grad_scale = 1.0 / math.sqrt(IMAGES * LAT_H * LAT_W)
    kernel_one = first_kernel(first_weight)
    kernel_two = second_kernel(second_weight)
    activated = activate(images.astype(jnp.float32)).astype(jnp.bfloat16)
    first_out = convolve(activated, kernel_one)
    hidden = activate(first_out).astype(jnp.bfloat16)
    second_out = convolve(hidden, kernel_two)
    block_output = (images.astype(jnp.float32) + second_out).astype(jnp.bfloat16)
    flipped = jnp.transpose(kernel_two[::-1, ::-1], (0, 1, 3, 2))
    hidden_grad = convolve(cotangent, flipped)
    unused, pullback = jax.vjp(activate, first_out)
    pre_grad = pullback(hidden_grad)[0].astype(jnp.bfloat16)
    raw_first = weight_grad(activated, pre_grad)
    raw_second = weight_grad(hidden, cotangent)
    first_grad = first_flat(project(raw_first, first_basis) * grad_scale)
    second_grad = second_flat(project(raw_second, second_basis) * grad_scale)
    return (block_output, first_grad, second_grad)
```

```python
import functools
import math

import jax
import jax.numpy as jnp
import numpy as np
from jax import lax
from jax.experimental import pallas as pl
from jax.experimental.pallas import tpu as pltpu
from jax.sharding import PartitionSpec as P

GROUPS = 32
EPS = 1e-5
VMEM_LIMIT = 48 * 1024 * 1024
F32 = jnp.float32
BF16 = jnp.bfloat16


def vmem():
    return pl.BlockSpec(memory_space=pltpu.VMEM)


def smem():
    return pl.BlockSpec(memory_space=pltpu.SMEM)


def params():
    return pltpu.CompilerParams(vmem_limit_bytes=VMEM_LIMIT)


def cost(flops, moved):
    return pl.CostEstimate(flops=int(flops), bytes_accessed=int(moved), transcendentals=0)


def group_sums(row, same_group):
    high = row.astype(BF16).astype(F32)
    rest = row - high
    middle = rest.astype(BF16).astype(F32)
    low = rest - middle
    at = lax.broadcasted_iota(jnp.int32, (16, row.shape[1]), 0)
    stacked = jnp.where(at == 0, high, jnp.where(at == 1, middle, jnp.where(at == 2, low, 0.0)))
    sums = jnp.dot(stacked.astype(BF16), same_group, preferred_element_type=F32)
    return jnp.sum(sums, axis=0, keepdims=True)


def normalized(values, same_group, count):
    center = group_sums(jnp.sum(values, axis=0, keepdims=True), same_group) / count
    moved = values - center
    spread = group_sums(jnp.sum(moved * moved, axis=0, keepdims=True), same_group) / count
    scale = 1.0 / jnp.sqrt(spread + EPS)
    return moved * scale, scale


def columns(values, flip):
    width = values.shape[1]
    at = lax.broadcasted_iota(jnp.int32, values.shape, 1)
    before = jnp.where(at == 0, 0.0, pltpu.roll(values, 1, axis=1))
    after = jnp.where(at == width - 1, 0.0, pltpu.roll(values, width - 1, axis=1))
    parts = [after, values, before] if flip else [before, values, after]
    return jnp.concatenate(parts, axis=2).astype(BF16)


def conv_rows(taps, weight_ref, rows, flip):
    _, width, depth = taps.shape
    total = None
    for tap in range(3):
        window = taps[tap : tap + rows].reshape(rows * width, depth)
        term = jnp.dot(window, weight_ref[2 - tap if flip else tap], preferred_element_type=F32)
        total = term if total is None else total + term
    return total


def clear_edges(taps):
    rows = taps.shape[0]
    taps[0:1] = jnp.zeros((1,) + taps.shape[1:], taps.dtype)
    taps[rows - 1 : rows] = jnp.zeros((1,) + taps.shape[1:], taps.dtype)


def split_kernel(blocks, at_ref, x_ref, *outs):
    width = x_ref.shape[-1] // blocks
    for away in range(blocks):
        for block in range(blocks):

            @pl.when(jnp.bitwise_xor(at_ref[0], away) == block)
            def _(away=away, block=block):
                outs[away][...] = x_ref[:, :, block * width : (block + 1) * width]


def split_blocks(x, blocks, chip):
    shape = jax.ShapeDtypeStruct(x.shape[:2] + (x.shape[2] // blocks,), x.dtype)
    return pl.pallas_call(
        functools.partial(split_kernel, blocks),
        out_shape=[shape] * blocks,
        in_specs=[smem(), vmem()],
        out_specs=[vmem()] * blocks,
        compiler_params=params(),
        cost_estimate=cost(0, 4 * x.size),
        name="split_blocks",
    )(chip, x)


def first_kernel(bands, count, at_ref, *refs):
    parts = refs[:bands]
    weight_ref, group_ref, basis_ref, act_ref, sums_ref, whole, taps = refs[bands:]
    band = parts[0].shape[1]
    width = act_ref.shape[-1]
    rows = act_ref.shape[1]
    cells = rows * act_ref.shape[2]
    rank = basis_ref.shape[1] // 2
    for away in range(bands):
        start = jnp.bitwise_xor(at_ref[0], away) * band
        whole[pl.ds(start, band)] = parts[away][0]
    clear_edges(taps)
    for half in range(2):
        values = whole[:, :, half * width : (half + 1) * width].astype(F32)
        unit, _ = normalized(values.reshape(cells, width), group_ref[...], count)
        active = (unit / (1.0 + jnp.exp(-unit))).astype(BF16)
        act_ref[half] = active.reshape(act_ref.shape[1:])
        taps[1 : rows + 1] = columns(active.astype(F32).reshape(act_ref.shape[1:]), False)
        total = conv_rows(taps, weight_ref, rows, False)
        along = jnp.dot(active, basis_ref[...], preferred_element_type=F32)
        along = along[:, :rank] + along[:, rank:]
        sums_ref[half] = jnp.concatenate([total, along], axis=1).astype(BF16)


def first_conv(parts, weight, same_group, basis, row, rows, count):
    bands = len(parts)
    pairs, band, width, double = parts[0].shape
    depth = double // 2
    rank = basis.shape[1] // 2
    wide = weight.shape[2]
    cells = rows * width
    return pl.pallas_call(
        functools.partial(first_kernel, bands, count),
        grid=(pairs,),
        out_shape=[
            jax.ShapeDtypeStruct((2 * pairs, rows, width, depth), BF16),
            jax.ShapeDtypeStruct((2 * pairs, cells, wide + rank), BF16),
        ],
        in_specs=[smem()]
        + [pl.BlockSpec((1, band, width, double), lambda s: (s, 0, 0, 0))] * bands
        + [vmem(), vmem(), vmem()],
        out_specs=[
            pl.BlockSpec((2, rows, width, depth), lambda s: (s, 0, 0, 0)),
            pl.BlockSpec((2, cells, wide + rank), lambda s: (s, 0, 0)),
        ],
        scratch_shapes=[
            pltpu.VMEM((rows, width, double), BF16),
            pltpu.VMEM((rows + 2, width, 3 * depth), BF16),
        ],
        compiler_params=params(),
        cost_estimate=cost(36 * pairs * cells * depth * wide, 8 * pairs * cells * depth),
        name="first_conv",
    )(row, *parts, weight, same_group, basis)


def back_kernel(bands, at_ref, *refs):
    parts = refs[:bands]
    weight_ref, whole_ref, sums_ref, whole, taps = refs[bands:]
    band = parts[0].shape[1]
    width = whole_ref.shape[-1]
    rows = whole_ref.shape[1]
    for away in range(bands):
        start = jnp.bitwise_xor(at_ref[0], away) * band
        whole[pl.ds(start, band)] = parts[away][0]
    clear_edges(taps)
    for half in range(2):
        values = whole[:, :, half * width : (half + 1) * width]
        whole_ref[half] = values
        taps[1 : rows + 1] = columns(values.astype(F32), True)
        sums_ref[half] = conv_rows(taps, weight_ref, rows, True).astype(BF16)


def back_conv(parts, weight, row, rows):
    bands = len(parts)
    pairs, band, width, double = parts[0].shape
    depth = double // 2
    wide = weight.shape[2]
    cells = rows * width
    return pl.pallas_call(
        functools.partial(back_kernel, bands),
        grid=(pairs,),
        out_shape=[
            jax.ShapeDtypeStruct((2 * pairs, rows, width, depth), BF16),
            jax.ShapeDtypeStruct((2 * pairs, cells, wide), BF16),
        ],
        in_specs=[smem()]
        + [pl.BlockSpec((1, band, width, double), lambda s: (s, 0, 0, 0))] * bands
        + [vmem()],
        out_specs=[
            pl.BlockSpec((2, rows, width, depth), lambda s: (s, 0, 0, 0)),
            pl.BlockSpec((2, cells, wide), lambda s: (s, 0, 0)),
        ],
        scratch_shapes=[
            pltpu.VMEM((rows, width, double), BF16),
            pltpu.VMEM((rows + 2, width, 3 * depth), BF16),
        ],
        compiler_params=params(),
        cost_estimate=cost(36 * pairs * cells * depth * wide, 8 * pairs * cells * depth),
        name="back_conv",
    )(row, *parts, weight)


def hidden_kernel(terms, count, *refs):
    group_ref, basis_ref, pay_ref, unit_ref, scale_ref, along_ref = refs[terms:]
    wide = unit_ref.shape[1]
    rank = basis_ref.shape[1] // 2
    total = refs[0][...].astype(F32)
    for term in refs[1:terms]:
        total = total + term[...].astype(F32)
    unit, scale = normalized(total[:, :wide], group_ref[...], count)
    unit_ref[...] = unit
    scale_ref[...] = scale
    hidden = (unit / (1.0 + jnp.exp(-unit))).astype(BF16)
    pay_ref[...] = jnp.concatenate([hidden.astype(F32), total[:, wide:]], axis=1).astype(BF16)
    along = jnp.dot(hidden, basis_ref[...], preferred_element_type=F32)
    along = along[:, :rank] + along[:, rank:]
    half = along.shape[0] // 2
    along_ref[...] = jnp.concatenate([along[:half], along[half:]], axis=1).astype(BF16)


def hidden_step(terms, same_group, basis, count):
    cells, both = terms[0].shape
    rank = basis.shape[1] // 2
    wide = both - rank
    return pl.pallas_call(
        functools.partial(hidden_kernel, len(terms), count),
        out_shape=[
            jax.ShapeDtypeStruct((cells, both), BF16),
            jax.ShapeDtypeStruct((cells, wide), F32),
            jax.ShapeDtypeStruct((1, wide), F32),
            jax.ShapeDtypeStruct((cells // 2, 2 * rank), BF16),
        ],
        in_specs=[vmem()] * (len(terms) + 2),
        out_specs=[vmem()] * 4,
        compiler_params=params(),
        cost_estimate=cost(40 * cells * wide, 16 * cells * wide),
        name="hidden_step",
    )(*terms, same_group, basis)


def second_kernel(slots, bands, at_ref, *refs):
    pays = refs[:slots]
    weight_ref = refs[slots]
    outs = refs[slots + 1 : slots + 1 + bands]
    whole, taps = refs[slots + 1 + bands :]
    band, width, double = outs[0].shape[1:]
    rows = whole.shape[0]
    depth = taps.shape[2] // 3
    wide = double // 2
    clear_edges(taps)
    for slot in range(slots):
        hidden = pays[slot][:, :depth].astype(F32).reshape(rows, width, depth)
        taps[1 : rows + 1] = columns(hidden, False)
        whole[...] = conv_rows(taps, weight_ref, rows, False).reshape(rows, width, wide)
        half = slot % 2
        for away in range(bands):
            start = jnp.bitwise_xor(at_ref[0], away) * band
            outs[away][slot // 2, :, :, half * wide : (half + 1) * wide] = whole[
                pl.ds(start, band)
            ].astype(BF16)


def second_conv(pays, weight, row, rows, bands):
    slots = len(pays)
    cells, _ = pays[0].shape
    width = cells // rows
    depth = weight.shape[1] // 3
    wide = weight.shape[2]
    out = jax.ShapeDtypeStruct((slots // 2, rows // bands, width, 2 * wide), BF16)
    return pl.pallas_call(
        functools.partial(second_kernel, slots, bands),
        out_shape=[out] * bands,
        in_specs=[smem()] + [vmem()] * (slots + 1),
        out_specs=[vmem()] * bands,
        scratch_shapes=[
            pltpu.VMEM((rows, width, wide), F32),
            pltpu.VMEM((rows + 2, width, 3 * depth), BF16),
        ],
        compiler_params=params(),
        cost_estimate=cost(18 * slots * cells * depth * wide, 4 * slots * cells * depth),
        name="second_conv",
    )(row, *pays, weight)


def band_kernel(terms, *refs):
    outs = refs[terms:]
    wide = outs[0].shape[-1]
    total = refs[0][...].astype(F32)
    for term in refs[1:terms]:
        total = total + term[...].astype(F32)
    for slot, out in enumerate(outs):
        half = slot % 2
        out[...] = total[slot // 2, :, :, half * wide : (half + 1) * wide].astype(BF16)


def band_step(terms):
    pairs, band, width, double = terms[0].shape
    out = jax.ShapeDtypeStruct((band, width, double // 2), BF16)
    return pl.pallas_call(
        functools.partial(band_kernel, len(terms)),
        out_shape=[out] * (2 * pairs),
        in_specs=[vmem()] * len(terms),
        out_specs=[vmem()] * (2 * pairs),
        compiler_params=params(),
        cost_estimate=cost(0, 2 * terms[0].size * len(terms)),
        name="band_step",
    )(*terms)


def join_kernel(blocks, at_ref, x_ref, *refs):
    out = refs[blocks]
    width = x_ref.shape[-1] // blocks
    for away in range(blocks):
        for block in range(blocks):

            @pl.when(jnp.bitwise_xor(at_ref[0], away) == block)
            def _(away=away, block=block):
                lanes = slice(block * width, (block + 1) * width)
                added = x_ref[:, :, lanes].astype(F32) + refs[away][...].astype(F32)
                out[:, :, lanes] = added.astype(BF16)


def join_blocks(x, parts, chip):
    return pl.pallas_call(
        functools.partial(join_kernel, len(parts)),
        out_shape=jax.ShapeDtypeStruct(x.shape, BF16),
        in_specs=[smem(), vmem()] + [vmem()] * len(parts),
        out_specs=vmem(),
        compiler_params=params(),
        cost_estimate=cost(0, 6 * x.size),
        name="join_blocks",
    )(chip, x, *parts)


def pre_kernel(terms, count, *refs):
    unit_ref, scale_ref, group_ref, out_ref = refs[terms:]
    total = refs[0][...].astype(F32)
    for term in refs[1:terms]:
        total = total + term[...].astype(F32)
    unit = unit_ref[...]
    gate = 1.0 / (1.0 + jnp.exp(-unit))
    grad = total * (gate * (1.0 + unit * (1.0 - gate)))
    mean = group_sums(jnp.sum(grad, axis=0, keepdims=True), group_ref[...]) / count
    along = group_sums(jnp.sum(grad * unit, axis=0, keepdims=True), group_ref[...]) / count
    out_ref[...] = (scale_ref[...] * (grad - mean - unit * along)).astype(BF16)


def pre_step(terms, unit, scale, same_group, count):
    cells, wide = unit.shape
    return pl.pallas_call(
        functools.partial(pre_kernel, len(terms), count),
        out_shape=jax.ShapeDtypeStruct((cells, wide), BF16),
        in_specs=[vmem()] * (len(terms) + 3),
        out_specs=vmem(),
        compiler_params=params(),
        cost_estimate=cost(40 * cells * wide, 16 * cells * wide),
        name="pre_step",
    )(*terms, unit, scale, same_group)


def project(values, along, basis):
    both = jnp.concatenate([along, along], axis=1)
    return values - jnp.dot(both, basis, preferred_element_type=F32)


def grad_body(core_ref, left, left_t, taps, keep_ref, send_ref, width, flip):
    half = left.shape[1] // 2
    span = left.shape[0]
    wide = taps.shape[1] // 3
    turned = left[...].T

    @pl.when(core_ref[0] == 0)
    def _():
        left_t[...] = turned

    @pl.when(core_ref[0] != 0)
    def _():
        left_t[:half] = turned[half:]
        left_t[half:] = turned[:half]

    for tap in range(3):
        window = taps[tap * width : tap * width + span]
        result = jnp.dot(left_t[...], window, preferred_element_type=F32)
        first = 3 * (2 - tap if flip else tap)
        for q in range(3):
            lanes = slice(q * wide, (q + 1) * wide)
            keep_ref[first + q] = result[:half, lanes]
            send_ref[first + q] = result[half:, lanes].astype(BF16)


def fill_taps(taps, slot, rows, width, value):
    start = (slot * (rows + 1) + 1) * width
    taps[start : start + rows * width] = value.reshape(rows * width, value.shape[2])


def clear_gaps(left, taps, slots, rows, width):
    gap = rows + 1
    for slot in range(slots + 1):
        begin = slot * gap * width
        end = taps.shape[0] if slot == slots else begin + width
        taps[begin:end] = jnp.zeros((end - begin, taps.shape[1]), taps.dtype)
    for slot in range(slots):
        begin = (slot * gap + rows) * width
        end = left.shape[0] if slot == slots - 1 else begin + width
        left[begin:end] = jnp.zeros((end - begin, left.shape[1]), left.dtype)


def first_grad_kernel(slots, core_ref, act_ref, *refs):
    pays = refs[:slots]
    grads = refs[slots : 2 * slots]
    basis_ref, keep_ref, send_ref, left, left_t, taps = refs[2 * slots :]
    rows, width, depth = act_ref.shape[1:]
    cells = rows * width
    rank = basis_ref.shape[0] // 2
    wide = taps.shape[1] // 3
    clear_gaps(left, taps, slots, rows, width)
    for slot in range(slots):
        values = act_ref[slot].reshape(cells, depth).astype(F32)
        along = pays[slot][:, wide : wide + rank]
        begin = slot * (rows + 1) * width
        left[begin : begin + cells] = project(values, along, basis_ref[...]).astype(BF16)
        right = grads[slot][...].astype(F32).reshape(rows, width, wide)
        fill_taps(taps, slot, rows, width, columns(right, True))
    grad_body(core_ref, left, left_t, taps, keep_ref, send_ref, width, True)


def second_grad_kernel(slots, core_ref, cot_ref, *refs):
    pays = refs[:slots]
    alongs = refs[slots : 2 * slots]
    basis_ref, keep_ref, send_ref, left, left_t, taps = refs[2 * slots :]
    rows, width, depth = cot_ref.shape[1:]
    cells = rows * width
    rank = basis_ref.shape[0] // 2
    wide = taps.shape[1] // 3
    clear_gaps(left, taps, slots, rows, width)
    for slot in range(slots):
        begin = slot * (rows + 1) * width
        left[begin : begin + cells] = cot_ref[slot].reshape(cells, depth)
        packed = alongs[slot][...]
        along = jnp.concatenate([packed[:, :rank], packed[:, rank:]], axis=0)
        values = pays[slot][:, :wide].astype(F32)
        right = project(values, along, basis_ref[...]).astype(BF16).astype(F32)
        fill_taps(taps, slot, rows, width, columns(right.reshape(rows, width, wide), False))
    grad_body(core_ref, left, left_t, taps, keep_ref, send_ref, width, False)


def weight_grad(kernel, name, core, left, firsts, seconds, basis, wide):
    slots, rows, width, depth = left.shape
    used = slots * (rows + 1) * width
    span = -(-used // 128) * 128
    half = depth // 2
    tap_rows = 2 * width + span
    return pl.pallas_call(
        functools.partial(kernel, slots),
        out_shape=[
            jax.ShapeDtypeStruct((9, half, wide), F32),
            jax.ShapeDtypeStruct((9, half, wide), BF16),
        ],
        in_specs=[smem()] + [vmem()] * (2 + 2 * slots),
        out_specs=[vmem()] * 2,
        scratch_shapes=[
            pltpu.VMEM((span, depth), BF16),
            pltpu.VMEM((depth, span), BF16),
            pltpu.VMEM((tap_rows, 3 * wide), BF16),
        ],
        compiler_params=params(),
        cost_estimate=cost(18 * slots * rows * width * depth * wide, 20 * depth * wide * 9),
        name=name,
    )(core, left, *firsts, *seconds, basis)


def two_parts(basis):
    high = lax.reduce_precision(basis, 8, 7)
    return high.astype(BF16), (basis - high).astype(BF16)


def same_groups(width, size):
    at = np.arange(width) // size
    return jnp.asarray((at[:, None] == at[None, :]).astype(np.float32), BF16)


def body(images, cotangent, first_weight, second_weight, first_basis, second_basis):
    n_dp = lax.axis_size("dp")
    n_rows = lax.axis_size("rows")
    chips = n_dp // 2
    _, band, width, channels = images.shape
    rows = band * n_rows
    dp_width = channels // n_dp
    chip_width = channels // chips
    row_width = channels // n_rows
    group = channels // GROUPS
    count = float(rows * width * group)
    grad_scale = 1.0 / math.sqrt(n_dp * images.shape[0] * rows * width)

    at_dp = lax.axis_index("dp")
    at_row = lax.axis_index("rows")
    chip = (at_dp // 2).astype(jnp.int32)
    core = (at_dp % 2).astype(jnp.int32)
    chip_at, core_at, row_at = chip[None], core[None], at_row.astype(jnp.int32)[None]

    def to_core(x):
        return lax.ppermute(x, "dp", [(i, i ^ 1) for i in range(n_dp)])

    def to_chip(x, away):
        return lax.ppermute(x, "dp", [(i, i ^ (2 * away)) for i in range(n_dp)])

    def to_row(x, away):
        return lax.ppermute(x, "rows", [(i, i ^ away) for i in range(n_rows)])

    def chips_gather(x):
        return [x] + [to_chip(x, away) for away in range(1, chips)]

    def rows_gather(x):
        return [x] + [to_row(x, away) for away in range(1, n_rows)]

    def chips_swap(parts):
        return [parts[0]] + [to_chip(parts[away], away) for away in range(1, chips)]

    def rows_swap(parts):
        return [parts[0]] + [to_row(parts[away], away) for away in range(1, n_rows)]

    def spread(x):
        slots = chips_swap(split_blocks(x[0], chips, chip_at))
        pairs = [
            jnp.concatenate([slots[s], slots[s + 1]], axis=-1) for s in range(0, chips, 2)
        ]
        return rows_gather(jnp.stack(pairs))

    image_parts = spread(images)
    cot_parts = spread(cotangent)

    own_first = first_weight.reshape(9, dp_width, row_width)
    own_second = second_weight.reshape(9, dp_width, row_width)
    other_first = to_core(own_first)
    other_second = to_core(own_second)

    def both_halves(own, other):
        low = jnp.where(core == 0, own, other)
        high = jnp.where(core == 0, other, own)
        return jnp.concatenate([low, high], axis=1)

    first_full = both_halves(own_first, other_first)
    second_full = both_halves(own_second, other_second)
    weight_one = first_full.reshape(3, 3 * chip_width, row_width)
    weight_back = second_full.reshape(3, 3 * chip_width, row_width)
    weight_two = jnp.swapaxes(second_full, 1, 2).reshape(3, 3 * row_width, chip_width)

    chip_groups = same_groups(chip_width, group)
    row_groups = same_groups(row_width, group)
    basis_one = lax.dynamic_slice_in_dim(first_basis, chip * chip_width, chip_width, 1)
    basis_two = lax.dynamic_slice_in_dim(second_basis, at_row * row_width, row_width, 1)
    one_high, one_low = two_parts(basis_one)
    two_high, two_low = two_parts(basis_two)
    one_rows = jnp.concatenate([one_high, one_low], axis=0)
    two_rows = jnp.concatenate([two_high, two_low], axis=0)

    active, first_sums = first_conv(
        image_parts, weight_one, chip_groups, one_rows.T, row_at, rows, count
    )
    first_terms = chips_swap([first_sums[slot] for slot in range(chips)])
    pay, unit, scale, along_part = hidden_step(first_terms, row_groups, two_rows.T, count)
    pays = chips_gather(pay)

    whole_cot, back_sums = back_conv(cot_parts, weight_back, row_at, rows)
    back_terms = chips_swap([back_sums[slot] for slot in range(chips)])
    pre_grad = pre_step(back_terms, unit, scale, row_groups, count)
    pre_grads = chips_gather(pre_grad)

    band_sums = rows_swap(second_conv(pays, weight_two, row_at, rows, n_rows))
    block_output = join_blocks(images[0], chips_swap(band_step(band_sums)), chip_at)[None]

    along_terms = rows_gather(along_part)
    along_sum = along_terms[0].astype(F32)
    for term in along_terms[1:]:
        along_sum = along_sum + term.astype(F32)
    alongs = chips_gather(along_sum.astype(BF16))

    def finish(keep, send):
        total = (keep + to_core(send).astype(F32)) * grad_scale
        return total.reshape(1, 1, 9, dp_width * row_width)

    second_grad = finish(
        *weight_grad(
            second_grad_kernel, "second_grad", core_at, whole_cot, pays, alongs, two_rows,
            row_width,
        )
    )
    first_grad = finish(
        *weight_grad(
            first_grad_kernel, "first_grad", core_at, active, pays, pre_grads, one_rows,
            row_width,
        )
    )
    return (block_output, first_grad, second_grad)


def solution(mesh):
    split = P("dp", "rows", None, None)
    return jax.shard_map(
        body,
        mesh=mesh,
        in_specs=(split, split, split, split, P(), P()),
        out_specs=(split, split, split),
        check_vma=False,
    )
```

```python
import functools
import math

import jax
import jax.numpy as jnp
import numpy as np
from jax import lax
from jax.experimental import pallas as pl
from jax.experimental.pallas import tpu as pltpu
from jax.sharding import PartitionSpec as P

GROUPS = 32
EPS = 1e-5
VMEM_LIMIT = 48 * 1024 * 1024
F32 = jnp.float32
BF16 = jnp.bfloat16


def vmem():
    return pl.BlockSpec(memory_space=pltpu.VMEM)


def smem():
    return pl.BlockSpec(memory_space=pltpu.SMEM)


def unread(after):
    return [pl.BlockSpec(memory_space=pl.ANY)] * len(after)


def params():
    return pltpu.CompilerParams(vmem_limit_bytes=VMEM_LIMIT)


def cost(flops, moved):
    return pl.CostEstimate(flops=int(flops), bytes_accessed=int(moved), transcendentals=0)


def group_sums(row, same_group):
    high = row.astype(BF16).astype(F32)
    rest = row - high
    middle = rest.astype(BF16).astype(F32)
    low = rest - middle
    at = lax.broadcasted_iota(jnp.int32, (16, row.shape[1]), 0)
    stacked = jnp.where(at == 0, high, jnp.where(at == 1, middle, jnp.where(at == 2, low, 0.0)))
    sums = jnp.dot(stacked.astype(BF16), same_group, preferred_element_type=F32)
    return jnp.sum(sums, axis=0, keepdims=True)


def normalized(values, same_group, count):
    center = group_sums(jnp.sum(values, axis=0, keepdims=True), same_group) / count
    moved = values - center
    spread = group_sums(jnp.sum(moved * moved, axis=0, keepdims=True), same_group) / count
    scale = 1.0 / jnp.sqrt(spread + EPS)
    return moved * scale, scale


def columns(values, flip):
    width = values.shape[1]
    at = lax.broadcasted_iota(jnp.int32, values.shape, 1)
    before = jnp.where(at == 0, 0.0, pltpu.roll(values, 1, axis=1))
    after = jnp.where(at == width - 1, 0.0, pltpu.roll(values, width - 1, axis=1))
    parts = [after, values, before] if flip else [before, values, after]
    return jnp.concatenate([part.astype(BF16) for part in parts], axis=2)


def conv_rows(taps, weight_ref, rows, flip):
    _, width, depth = taps.shape
    total = None
    for tap in range(3):
        window = taps[tap : tap + rows].reshape(rows * width, depth)
        term = jnp.dot(window, weight_ref[2 - tap if flip else tap], preferred_element_type=F32)
        total = term if total is None else total + term
    return total


def side_by_side(values):
    half = values.shape[0] // 2
    return jnp.concatenate([values[:half], values[half:]], axis=1)


def stacked_again(values):
    half = values.shape[1] // 2
    return jnp.concatenate([values[:, :half], values[:, half:]], axis=0)


def clear_edges(taps):
    rows = taps.shape[0]
    taps[0:1] = jnp.zeros((1,) + taps.shape[1:], taps.dtype)
    taps[rows - 1 : rows] = jnp.zeros((1,) + taps.shape[1:], taps.dtype)


def split_kernel(blocks, at_ref, x_ref, *refs):
    outs = refs[-blocks:]
    width = x_ref.shape[-1] // blocks
    for away in range(blocks):
        for block in range(blocks):

            @pl.when(jnp.bitwise_xor(at_ref[0], away) == block)
            def _(away=away, block=block):
                outs[away][...] = x_ref[:, :, block * width : (block + 1) * width]


def split_blocks(x, blocks, chip, after=()):
    shape = jax.ShapeDtypeStruct(x.shape[:2] + (x.shape[2] // blocks,), x.dtype)
    return pl.pallas_call(
        functools.partial(split_kernel, blocks),
        out_shape=[shape] * blocks,
        in_specs=[smem(), vmem()] + unread(after),
        out_specs=[vmem()] * blocks,
        compiler_params=params(),
        cost_estimate=cost(0, 4 * x.size),
        name="split_blocks",
    )(chip, x, *after)


def pack_kernel(slots, *refs):
    out = refs[-1]
    width = refs[0].shape[-1]
    for slot in range(slots):
        half = slot % 2
        out[slot // 2, :, :, half * width : (half + 1) * width] = refs[slot][...]


def pack_slots(slots, after=()):
    band, width, depth = slots[0].shape
    return pl.pallas_call(
        functools.partial(pack_kernel, len(slots)),
        out_shape=jax.ShapeDtypeStruct((len(slots) // 2, band, width, 2 * depth), BF16),
        in_specs=[vmem()] * len(slots) + unread(after),
        out_specs=vmem(),
        compiler_params=params(),
        cost_estimate=cost(0, 4 * len(slots) * slots[0].size),
        name="pack_slots",
    )(*slots, *after)


def first_kernel(places, count, at_ref, *refs):
    parts = refs[: len(places)]
    weight_ref, group_ref, basis_ref = refs[len(places) : len(places) + 3]
    act_ref, even_ref, odd_ref, whole, taps = refs[-5:]
    band = parts[0].shape[1]
    width = act_ref.shape[-1]
    rows = act_ref.shape[1]
    cells = rows * act_ref.shape[2]
    rank = basis_ref.shape[1] // 2
    for part, (away, who) in zip(parts, places):

        @pl.when(jnp.logical_or(who < 0, at_ref[1] == who))
        def _(part=part, away=away):
            start = jnp.bitwise_xor(at_ref[0], away) * band
            whole[pl.ds(start, band)] = part[0]

    clear_edges(taps)
    for half in range(2):
        values = whole[:, :, half * width : (half + 1) * width].astype(F32)
        unit, _ = normalized(values.reshape(cells, width), group_ref[...], count)
        active = (unit / (1.0 + jnp.exp(-unit))).astype(BF16)
        act_ref[half] = active.reshape(act_ref.shape[1:])
        taps[1 : rows + 1] = columns(active.astype(F32).reshape(act_ref.shape[1:]), False)
        total = conv_rows(taps, weight_ref, rows, False)
        along = jnp.dot(active, basis_ref[...], preferred_element_type=F32)
        along = along[:, :rank] + along[:, rank:]
        sums_ref = odd_ref if half else even_ref
        sums_ref[...] = jnp.concatenate([total, along], axis=1).astype(BF16)


def first_conv(parts, places, pair, weight, same_group, basis, row, rows, count, after=()):
    _, band, width, double = parts[0].shape
    depth = double // 2
    rank = basis.shape[1] // 2
    wide = weight.shape[2]
    cells = rows * width
    sums = jax.ShapeDtypeStruct((cells, wide + rank), BF16)
    return pl.pallas_call(
        functools.partial(first_kernel, places, count),
        grid=(1,),
        out_shape=[jax.ShapeDtypeStruct((2, rows, width, depth), BF16), sums, sums],
        in_specs=[smem()]
        + [pl.BlockSpec((1, band, width, double), lambda s: (pair, 0, 0, 0))] * len(parts)
        + [vmem(), vmem(), vmem()]
        + unread(after),
        out_specs=[vmem()] * 3,
        scratch_shapes=[
            pltpu.VMEM((rows, width, double), BF16),
            pltpu.VMEM((rows + 2, width, 3 * depth), BF16),
        ],
        compiler_params=params(),
        cost_estimate=cost(36 * cells * depth * wide, 8 * cells * depth),
        name="first_conv",
    )(row, *parts, weight, same_group, basis, *after)


def back_kernel(parts_ref, weight_ref, *refs):
    whole_ref, even_ref, odd_ref, whole, taps = refs[-5:]
    bands, _, band = parts_ref.shape[:3]
    width = whole_ref.shape[-1]
    rows = whole_ref.shape[1]
    for at in range(bands):
        whole[at * band : (at + 1) * band] = parts_ref[at, 0]
    clear_edges(taps)
    for half in range(2):
        values = whole[:, :, half * width : (half + 1) * width]
        whole_ref[half] = values
        taps[1 : rows + 1] = columns(values.astype(F32), True)
        total = conv_rows(taps, weight_ref, rows, True)
        sums_ref = odd_ref if half else even_ref
        sums_ref[...] = side_by_side(total).astype(BF16)


def back_conv(parts, pair, weight, after=()):
    bands, _, band, width, double = parts.shape
    rows = bands * band
    depth = double // 2
    wide = weight.shape[2]
    cells = rows * width
    sums = jax.ShapeDtypeStruct((cells // 2, 2 * wide), BF16)
    return pl.pallas_call(
        back_kernel,
        grid=(1,),
        out_shape=[jax.ShapeDtypeStruct((2, rows, width, depth), BF16), sums, sums],
        in_specs=[
            pl.BlockSpec((bands, 1, band, width, double), lambda s: (0, pair, 0, 0, 0)),
            vmem(),
        ]
        + unread(after),
        out_specs=[vmem()] * 3,
        scratch_shapes=[
            pltpu.VMEM((rows, width, double), BF16),
            pltpu.VMEM((rows + 2, width, 3 * depth), BF16),
        ],
        compiler_params=params(),
        cost_estimate=cost(36 * cells * depth * wide, 8 * cells * depth),
        name="back_conv",
    )(parts, weight, *after)


def hidden_kernel(terms, count, *refs):
    group_ref, pay_ref, unit_ref, scale_ref = refs[terms:]
    wide = unit_ref.shape[1]
    total = refs[0][...].astype(F32)
    for term in refs[1:terms]:
        total = total + term[...].astype(F32)
    unit, scale = normalized(total[:, :wide], group_ref[...], count)
    unit_ref[...] = unit
    scale_ref[...] = scale
    hidden = (unit / (1.0 + jnp.exp(-unit))).astype(BF16)
    pay_ref[...] = jnp.concatenate([hidden.astype(F32), total[:, wide:]], axis=1).astype(BF16)


def hidden_step(terms, same_group, count):
    cells, both = terms[0].shape
    wide = same_group.shape[0]
    return pl.pallas_call(
        functools.partial(hidden_kernel, len(terms), count),
        out_shape=[
            jax.ShapeDtypeStruct((cells, both), BF16),
            jax.ShapeDtypeStruct((cells, wide), F32),
            jax.ShapeDtypeStruct((1, wide), F32),
        ],
        in_specs=[vmem()] * (len(terms) + 1),
        out_specs=[vmem()] * 3,
        compiler_params=params(),
        cost_estimate=cost(40 * cells * wide, 16 * cells * wide),
        name="hidden_step",
    )(*terms, same_group)


def second_kernel(bands, at_ref, *refs):
    pays = refs[:2]
    weight_ref, basis_ref = refs[2:4]
    along_ref, whole, taps = refs[-3:]
    outs = refs[-3 - bands : -3]
    rank = basis_ref.shape[1] // 2
    along = jnp.dot(pays[0][:, : taps.shape[2] // 3], basis_ref[...], preferred_element_type=F32)
    along_ref[...] = side_by_side(along[:, :rank] + along[:, rank:]).astype(BF16)
    band, width, double = outs[0].shape
    rows = whole.shape[0]
    depth = taps.shape[2] // 3
    wide = double // 2
    clear_edges(taps)
    for half in range(2):
        hidden = pays[half][:, :depth].astype(F32).reshape(rows, width, depth)
        taps[1 : rows + 1] = columns(hidden, False)
        whole[...] = conv_rows(taps, weight_ref, rows, False).reshape(rows, width, wide)
        for away in range(bands):
            start = jnp.bitwise_xor(at_ref[0], away) * band
            outs[away][:, :, half * wide : (half + 1) * wide] = whole[pl.ds(start, band)].astype(
                BF16
            )


def second_conv(pays, weight, basis, row, rows, bands, after=()):
    cells, _ = pays[0].shape
    width = cells // rows
    depth = weight.shape[1] // 3
    wide = weight.shape[2]
    out = jax.ShapeDtypeStruct((rows // bands, width, 2 * wide), BF16)
    return pl.pallas_call(
        functools.partial(second_kernel, bands),
        out_shape=[out] * bands + [jax.ShapeDtypeStruct((cells // 2, basis.shape[1]), BF16)],
        in_specs=[smem()] + [vmem()] * 4 + unread(after),
        out_specs=[vmem()] * (bands + 1),
        scratch_shapes=[
            pltpu.VMEM((rows, width, wide), F32),
            pltpu.VMEM((rows + 2, width, 3 * depth), BF16),
        ],
        compiler_params=params(),
        cost_estimate=cost(36 * cells * depth * wide, 8 * cells * depth),
        name="second_conv",
    )(row, *pays, weight, basis, *after)


def band_kernel(terms, *refs):
    outs = refs[-2:]
    wide = outs[0].shape[-1]
    total = refs[0][...].astype(F32)
    for term in refs[1:terms]:
        total = total + term[...].astype(F32)
    for half in range(2):
        outs[half][...] = total[:, :, half * wide : (half + 1) * wide].astype(BF16)


def band_step(terms, after=()):
    band, width, double = terms[0].shape
    out = jax.ShapeDtypeStruct((band, width, double // 2), BF16)
    return pl.pallas_call(
        functools.partial(band_kernel, len(terms)),
        out_shape=[out] * 2,
        in_specs=[vmem()] * len(terms) + unread(after),
        out_specs=[vmem()] * 2,
        compiler_params=params(),
        cost_estimate=cost(0, 2 * terms[0].size * len(terms)),
        name="band_step",
    )(*terms, *after)


def join_kernel(blocks, at_ref, x_ref, *refs):
    out = refs[blocks]
    width = x_ref.shape[-1] // blocks
    for away in range(blocks):
        for block in range(blocks):

            @pl.when(jnp.bitwise_xor(at_ref[0], away) == block)
            def _(away=away, block=block):
                lanes = slice(block * width, (block + 1) * width)
                added = x_ref[:, :, lanes].astype(F32) + refs[away][...].astype(F32)
                out[:, :, lanes] = added.astype(BF16)


def join_blocks(x, parts, chip):
    return pl.pallas_call(
        functools.partial(join_kernel, len(parts)),
        out_shape=jax.ShapeDtypeStruct(x.shape, BF16),
        in_specs=[smem(), vmem()] + [vmem()] * len(parts),
        out_specs=vmem(),
        compiler_params=params(),
        cost_estimate=cost(0, 6 * x.size),
        name="join_blocks",
    )(chip, x, *parts)


def pre_kernel(terms, count, *refs):
    unit_ref, scale_ref, group_ref = refs[terms : terms + 3]
    out_ref = refs[-1]
    total = refs[0][...].astype(F32)
    for term in refs[1:terms]:
        total = total + term[...].astype(F32)
    unit = unit_ref[...]
    gate = 1.0 / (1.0 + jnp.exp(-unit))
    grad = stacked_again(total) * (gate * (1.0 + unit * (1.0 - gate)))
    mean = group_sums(jnp.sum(grad, axis=0, keepdims=True), group_ref[...]) / count
    along = group_sums(jnp.sum(grad * unit, axis=0, keepdims=True), group_ref[...]) / count
    out_ref[...] = side_by_side(scale_ref[...] * (grad - mean - unit * along)).astype(BF16)


def pre_step(terms, unit, scale, same_group, count, after=()):
    cells, wide = unit.shape
    return pl.pallas_call(
        functools.partial(pre_kernel, len(terms), count),
        out_shape=jax.ShapeDtypeStruct((cells // 2, 2 * wide), BF16),
        in_specs=[vmem()] * (len(terms) + 3) + unread(after),
        out_specs=vmem(),
        compiler_params=params(),
        cost_estimate=cost(40 * cells * wide, 16 * cells * wide),
        name="pre_step",
    )(*terms, unit, scale, same_group, *after)


def project(values, along, basis):
    both = jnp.concatenate([along, along], axis=1)
    return values - jnp.dot(both, basis, preferred_element_type=F32)


def grad_body(core_ref, left, left_t, taps, keep_ref, send_ref, width, flip):
    half = left.shape[1] // 2
    span = left.shape[0]
    wide = taps.shape[1] // 3
    turned = left[...].T

    @pl.when(core_ref[0] == 0)
    def _():
        left_t[...] = turned

    @pl.when(core_ref[0] != 0)
    def _():
        left_t[:half] = turned[half:]
        left_t[half:] = turned[:half]

    for tap in range(3):
        window = taps[tap * width : tap * width + span]
        result = jnp.dot(left_t[...], window, preferred_element_type=F32)
        first = 3 * (2 - tap if flip else tap)
        for q in range(3):
            lanes = slice(q * wide, (q + 1) * wide)
            keep_ref[first + q] = result[:half, lanes]
            send_ref[first + q] = result[half:, lanes].astype(BF16)


def fill_taps(taps, slot, rows, width, value):
    start = (slot * (rows + 1) + 1) * width
    taps[start : start + rows * width] = value.reshape(rows * width, value.shape[2])


def clear_gaps(left, taps, slots, rows, width):
    gap = rows + 1
    for slot in range(slots + 1):
        begin = slot * gap * width
        end = taps.shape[0] if slot == slots else begin + width
        taps[begin:end] = jnp.zeros((end - begin, taps.shape[1]), taps.dtype)
    for slot in range(slots):
        begin = (slot * gap + rows) * width
        end = left.shape[0] if slot == slots - 1 else begin + width
        left[begin:end] = jnp.zeros((end - begin, left.shape[1]), left.dtype)


def first_grad_kernel(slots, core_ref, *refs):
    acts = refs[: slots // 2]
    pays = refs[slots // 2 : slots // 2 + slots]
    grads_ref, basis_ref = refs[slots // 2 + slots : slots // 2 + slots + 2]
    keep_ref, send_ref, left, left_t, taps = refs[-5:]
    rows, width, depth = acts[0].shape[1:]
    cells = rows * width
    rank = basis_ref.shape[0] // 2
    wide = taps.shape[1] // 3
    clear_gaps(left, taps, slots, rows, width)
    for slot in range(slots):
        values = acts[slot // 2][slot % 2].reshape(cells, depth).astype(F32)
        along = pays[slot][:, wide : wide + rank]
        begin = slot * (rows + 1) * width
        left[begin : begin + cells] = project(values, along, basis_ref[...]).astype(BF16)
        right = grads_ref[jnp.bitwise_xor(core_ref[1], slot)].astype(F32)
        right = stacked_again(right).reshape(rows, width, wide)
        fill_taps(taps, slot, rows, width, columns(right, True))
    grad_body(core_ref, left, left_t, taps, keep_ref, send_ref, width, True)


def second_grad_kernel(slots, core_ref, *refs):
    cots = refs[: slots // 2]
    pays = refs[slots // 2 : slots // 2 + slots]
    alongs = refs[slots // 2 + slots : slots // 2 + 2 * slots]
    basis_ref = refs[slots // 2 + 2 * slots]
    keep_ref, send_ref, left, left_t, taps = refs[-5:]
    rows, width, depth = cots[0].shape[1:]
    cells = rows * width
    rank = basis_ref.shape[0] // 2
    wide = taps.shape[1] // 3
    clear_gaps(left, taps, slots, rows, width)
    for slot in range(slots):
        begin = slot * (rows + 1) * width
        left[begin : begin + cells] = cots[slot // 2][slot % 2].reshape(cells, depth)
        packed = alongs[slot][...]
        along = jnp.concatenate([packed[:, :rank], packed[:, rank:]], axis=0)
        values = pays[slot][:, :wide].astype(F32)
        right = project(values, along, basis_ref[...]).astype(BF16).astype(F32)
        fill_taps(taps, slot, rows, width, columns(right.reshape(rows, width, wide), False))
    grad_body(core_ref, left, left_t, taps, keep_ref, send_ref, width, False)


def weight_grad(kernel, name, core, lefts, firsts, seconds, basis, wide, after=()):
    slots = len(firsts)
    _, rows, width, depth = lefts[0].shape
    used = slots * (rows + 1) * width
    span = -(-used // 128) * 128
    half = depth // 2
    tap_rows = 2 * width + span
    return pl.pallas_call(
        functools.partial(kernel, slots),
        out_shape=[
            jax.ShapeDtypeStruct((9, half, wide), F32),
            jax.ShapeDtypeStruct((9, half, wide), BF16),
        ],
        in_specs=[smem()] + [vmem()] * (1 + len(lefts) + slots + len(seconds)) + unread(after),
        out_specs=[vmem()] * 2,
        scratch_shapes=[
            pltpu.VMEM((span, depth), BF16),
            pltpu.VMEM((depth, span), BF16),
            pltpu.VMEM((tap_rows, 3 * wide), BF16),
        ],
        compiler_params=params(),
        cost_estimate=cost(18 * slots * rows * width * depth * wide, 20 * depth * wide * 9),
        name=name,
    )(core, *lefts, *firsts, *seconds, basis, *after)


def two_parts(basis):
    high = lax.reduce_precision(basis, 8, 7)
    return high.astype(BF16), (basis - high).astype(BF16)


def same_groups(width, size):
    at = np.arange(width) // size
    return jnp.asarray((at[:, None] == at[None, :]).astype(np.float32), BF16)


def body(images, cotangent, first_weight, second_weight, first_basis, second_basis):
    n_dp = lax.axis_size("dp")
    n_rows = lax.axis_size("rows")
    chips = n_dp // 2
    _, band, width, channels = images.shape
    rows = band * n_rows
    dp_width = channels // n_dp
    chip_width = channels // chips
    row_width = channels // n_rows
    group = channels // GROUPS
    count = float(rows * width * group)
    grad_scale = 1.0 / math.sqrt(n_dp * images.shape[0] * rows * width)

    at_dp = lax.axis_index("dp")
    at_row = lax.axis_index("rows")
    chip = (at_dp // 2).astype(jnp.int32)
    core = (at_dp % 2).astype(jnp.int32)
    row = at_row.astype(jnp.int32)
    chip_at, core_at = chip[None], jnp.stack([core, chip])
    row_at = jnp.stack([row, (row + 1) // 2 % 2])

    def to_core(x):
        return lax.ppermute(x, "dp", [(i, i ^ 1) for i in range(n_dp)])

    def to_chip(x, away):
        return lax.ppermute(x, "dp", [(i, i ^ (2 * away)) for i in range(n_dp)])

    def to_row(x, away):
        return lax.ppermute(x, "rows", [(i, i ^ away) for i in range(n_rows)])

    def chips_gather(x):
        return [x] + [to_chip(x, away) for away in range(1, chips)]

    def rows_gather(x):
        return [x] + [to_row(x, away) for away in range(1, n_rows)]

    def chips_swap(parts):
        return [parts[0]] + [to_chip(parts[away], away) for away in range(1, chips)]

    def rows_swap(parts):
        return [parts[0]] + [to_row(parts[away], away) for away in range(1, n_rows)]

    def line_gather(x):
        if n_rows != 4:
            return rows_gather(x), [(away, -1) for away in range(n_rows)]

        def step(value, pairs):
            return lax.ppermute(value, "rows", pairs)

        near = step(x, [(0, 1), (1, 0), (2, 3), (3, 2)])
        middle = step(x, [(1, 2), (2, 1)])
        outward = step(middle, [(1, 0), (2, 3)])
        across = step(near, [(1, 2), (2, 1)])
        over = step(near, [(1, 3), (2, 0)])
        places = [(0, -1), (1, -1), (3, 1), (2, 0), (2, 1), (3, 0)]
        return [x, near, middle, outward, across, over], places

    image_slots = chips_swap(split_blocks(images[0], chips, chip_at))
    image_pack = pack_slots(image_slots)
    image_parts, places = line_gather(image_pack)
    first_weight, second_weight, _ = lax.optimization_barrier(
        (first_weight, second_weight, image_pack)
    )
    cot_slots = chips_swap(split_blocks(cotangent[0], chips, chip_at, image_parts[1:2]))
    cot_pack = pack_slots(cot_slots, image_parts[-1:])
    cot_parts = lax.all_gather(cot_pack, "rows")

    own_first = first_weight.reshape(9, dp_width, row_width)
    own_second = second_weight.reshape(9, dp_width, row_width)
    other_first = to_core(own_first)
    other_second = to_core(own_second)

    def both_halves(own, other):
        low = jnp.where(core == 0, own, other)
        high = jnp.where(core == 0, other, own)
        return jnp.concatenate([low, high], axis=1)

    first_full = both_halves(own_first, other_first)
    second_full = both_halves(own_second, other_second)
    weight_one = first_full.reshape(3, 3 * chip_width, row_width)
    weight_back = second_full.reshape(3, 3 * chip_width, row_width)
    weight_two = jnp.swapaxes(second_full, 1, 2).reshape(3, 3 * row_width, chip_width)

    chip_groups = same_groups(chip_width, group)
    row_groups = same_groups(row_width, group)
    basis_one = lax.dynamic_slice_in_dim(first_basis, chip * chip_width, chip_width, 1)
    basis_two = lax.dynamic_slice_in_dim(second_basis, at_row * row_width, row_width, 1)
    one_high, one_low = two_parts(basis_one)
    two_high, two_low = two_parts(basis_two)
    one_rows = jnp.concatenate([one_high, one_low], axis=0)
    two_rows = jnp.concatenate([two_high, two_low], axis=0)

    pairs = chips // 2
    active, first_sums = [None] * pairs, []
    done = (cot_pack,)
    for pair in reversed(range(pairs)):
        active[pair], even, odd = first_conv(
            image_parts, places, pair, weight_one, chip_groups, one_rows.T, row_at, rows, count, done
        )
        first_sums = [even, odd] + first_sums
        done = (even,)
    first_terms = chips_swap(first_sums)
    pay, unit, scale = hidden_step(first_terms, row_groups, count)
    pays = chips_gather(pay)

    whole_cot, back_sums, band_terms = [None] * pairs, [], []
    done = tuple(pays[: chips - 1])
    for pair in range(pairs):
        *sums, part = second_conv(
            pays[2 * pair : 2 * pair + 2], weight_two, two_rows.T, row_at, rows, n_rows, done
        )
        band_terms.append(rows_swap(sums))
        done = (sums[0],)
        if pair > 0:
            continue
        along, done = part, (sums[0], pays[-1])
        for back in reversed(range(pairs)):
            whole_cot[back], even, odd = back_conv(cot_parts, back, weight_back, done)
            back_sums = [even, odd] + back_sums
            done = (even,)
    blocks = list(band_step(band_terms[0]))
    back_terms = chips_swap(back_sums)
    pre_grad = pre_step(back_terms, unit, scale, row_groups, count, done + (blocks[0],))
    same_core = [[2 * at + side for at in range(chips)] for side in range(2)]
    pre_grads = lax.all_gather(pre_grad, "dp", axis_index_groups=same_core)

    away = 1
    while away < n_rows:
        along = (along.astype(F32) + to_row(along, away).astype(F32)).astype(BF16)
        away *= 2
    alongs = [along]
    away = 1
    while away < chips:
        other = to_chip(jnp.stack(alongs), away)
        alongs = alongs + [other[at] for at in range(away)]
        away *= 2

    def finish(keep, send):
        total = (keep + to_core(send).astype(F32)) * grad_scale
        return total.reshape(1, 1, 9, dp_width * row_width)

    second_halves = weight_grad(
        second_grad_kernel, "second_grad", core_at, whole_cot, pays, alongs, two_rows,
        row_width, (pre_grad,),
    )
    for terms in band_terms[1:]:
        blocks += band_step(terms, second_halves[1:])
    block_output = join_blocks(images[0], chips_swap(blocks), chip_at)[None]
    second_grad = finish(*second_halves)
    first_halves = weight_grad(
        first_grad_kernel, "first_grad", core_at, active, pays, [pre_grads], one_rows,
        row_width, (second_halves[1], blocks[0], blocks[-1]),
    )
    first_grad = finish(*first_halves)
    return (block_output, first_grad, second_grad)


def solution(mesh):
    split = P("dp", "rows", None, None)
    return jax.shard_map(
        body,
        mesh=mesh,
        in_specs=(split, split, split, split, P(), P()),
        out_specs=(split, split, split),
        check_vma=False,
    )
```

```python
import functools
import math

import jax
import jax.numpy as jnp
import numpy as np
from jax import lax
from jax.experimental import pallas as pl
from jax.experimental.pallas import tpu as pltpu
from jax.sharding import PartitionSpec as P

GROUPS = 32
EPS = 1e-5
VMEM_LIMIT = 48 * 1024 * 1024
F32 = jnp.float32
BF16 = jnp.bfloat16


def vmem():
    return pl.BlockSpec(memory_space=pltpu.VMEM)


def smem():
    return pl.BlockSpec(memory_space=pltpu.SMEM)


def unread(after):
    return [pl.BlockSpec(memory_space=pl.ANY)] * len(after)


def params():
    return pltpu.CompilerParams(vmem_limit_bytes=VMEM_LIMIT)


def cost(flops, moved):
    return pl.CostEstimate(flops=int(flops), bytes_accessed=int(moved), transcendentals=0)


def group_sums(row, same_group):
    high = row.astype(BF16).astype(F32)
    rest = row - high
    middle = rest.astype(BF16).astype(F32)
    low = rest - middle
    at = lax.broadcasted_iota(jnp.int32, (16, row.shape[1]), 0)
    stacked = jnp.where(at == 0, high, jnp.where(at == 1, middle, jnp.where(at == 2, low, 0.0)))
    sums = jnp.dot(stacked.astype(BF16), same_group, preferred_element_type=F32)
    return jnp.sum(sums, axis=0, keepdims=True)


def normalized(values, same_group, count):
    center = group_sums(jnp.sum(values, axis=0, keepdims=True), same_group) / count
    moved = values - center
    spread = group_sums(jnp.sum(moved * moved, axis=0, keepdims=True), same_group) / count
    scale = 1.0 / jnp.sqrt(spread + EPS)
    return moved * scale, scale


def columns(values, flip):
    width = values.shape[1]
    at = lax.broadcasted_iota(jnp.int32, values.shape, 1)
    before = jnp.where(at == 0, 0.0, pltpu.roll(values, 1, axis=1))
    after = jnp.where(at == width - 1, 0.0, pltpu.roll(values, width - 1, axis=1))
    parts = [after, values, before] if flip else [before, values, after]
    return jnp.concatenate([part.astype(BF16) for part in parts], axis=2)


def conv_rows(taps, weight_ref, rows, flip):
    _, width, depth = taps.shape
    total = None
    for tap in range(3):
        window = taps[tap : tap + rows].reshape(rows * width, depth)
        term = jnp.dot(window, weight_ref[2 - tap if flip else tap], preferred_element_type=F32)
        total = term if total is None else total + term
    return total


def side_by_side(values):
    half = values.shape[0] // 2
    return jnp.concatenate([values[:half], values[half:]], axis=1)


def stacked_again(values):
    half = values.shape[1] // 2
    return jnp.concatenate([values[:, :half], values[:, half:]], axis=0)


def clear_edges(taps):
    rows = taps.shape[0]
    taps[0:1] = jnp.zeros((1,) + taps.shape[1:], taps.dtype)
    taps[rows - 1 : rows] = jnp.zeros((1,) + taps.shape[1:], taps.dtype)


def split_kernel(blocks, at_ref, x_ref, *refs):
    outs = refs[-blocks:]
    width = x_ref.shape[-1] // blocks
    for away in range(blocks):
        for block in range(blocks):

            @pl.when(jnp.bitwise_xor(at_ref[0], away) == block)
            def _(away=away, block=block):
                outs[away][...] = x_ref[:, :, block * width : (block + 1) * width]


def split_blocks(x, blocks, chip, after=()):
    shape = jax.ShapeDtypeStruct(x.shape[:2] + (x.shape[2] // blocks,), x.dtype)
    return pl.pallas_call(
        functools.partial(split_kernel, blocks),
        out_shape=[shape] * blocks,
        in_specs=[smem(), vmem()] + unread(after),
        out_specs=[vmem()] * blocks,
        compiler_params=params(),
        cost_estimate=cost(0, 4 * x.size),
        name="split_blocks",
    )(chip, x, *after)


def pack_kernel(slots, *refs):
    out = refs[-1]
    width = refs[0].shape[-1]
    for slot in range(slots):
        half = slot % 2
        out[slot // 2, :, :, half * width : (half + 1) * width] = refs[slot][...]


def pack_slots(slots, after=()):
    band, width, depth = slots[0].shape
    return pl.pallas_call(
        functools.partial(pack_kernel, len(slots)),
        out_shape=jax.ShapeDtypeStruct((len(slots) // 2, band, width, 2 * depth), BF16),
        in_specs=[vmem()] * len(slots) + unread(after),
        out_specs=vmem(),
        compiler_params=params(),
        cost_estimate=cost(0, 4 * len(slots) * slots[0].size),
        name="pack_slots",
    )(*slots, *after)


def assemble(whole, parts, pair, row):
    for away, part in enumerate(parts):
        band = part.shape[1]
        whole[pl.ds(jnp.bitwise_xor(row, away) * band, band)] = part[pair]


def first_kernel(slots, bands, count, at_ref, *refs):
    parts = refs[:bands]
    weight_ref, group_ref, basis_ref = refs[bands : bands + 3]
    whole, taps = refs[-2:]
    outs = refs[-2 - 2 * len(slots) : -2]
    rows, width, depth = outs[0].shape
    rank = basis_ref.shape[1] // 2
    cells = rows * width
    clear_edges(taps)
    held = None
    for at, slot in enumerate(slots):
        act_ref, sums_ref = outs[2 * at : 2 * at + 2]
        if slot // 2 != held:
            held = slot // 2
            assemble(whole, parts, held, at_ref[0])
        half = slot % 2
        values = whole[:, :, half * depth : (half + 1) * depth].astype(F32)
        unit, _ = normalized(values.reshape(cells, depth), group_ref[...], count)
        active = (unit / (1.0 + jnp.exp(-unit))).astype(BF16)
        act_ref[...] = active.reshape(act_ref.shape)
        taps[1 : rows + 1] = columns(active.astype(F32).reshape(act_ref.shape), False)
        total = conv_rows(taps, weight_ref, rows, False)
        along = jnp.dot(active, basis_ref[...], preferred_element_type=F32)
        along = along[:, :rank] + along[:, rank:]
        sums_ref[...] = jnp.concatenate([total, along], axis=1).astype(BF16)


def first_conv(parts, slots, weight, same_group, basis, row, rows, count, after=()):
    _, band, width, double = parts[0].shape
    depth = double // 2
    rank = basis.shape[1] // 2
    wide = weight.shape[2]
    cells = rows * width
    outs = [
        jax.ShapeDtypeStruct((rows, width, depth), BF16),
        jax.ShapeDtypeStruct((cells, wide + rank), BF16),
    ]
    made = pl.pallas_call(
        functools.partial(first_kernel, slots, len(parts), count),
        out_shape=outs * len(slots),
        in_specs=[smem()] + [vmem()] * (len(parts) + 3) + unread(after),
        out_specs=[vmem()] * (2 * len(slots)),
        scratch_shapes=[
            pltpu.VMEM((rows, width, double), BF16),
            pltpu.VMEM((rows + 2, width, 3 * depth), BF16),
        ],
        compiler_params=params(),
        cost_estimate=cost(18 * len(slots) * cells * depth * wide, 8 * cells * depth),
        name="first_conv",
    )(row, *parts, weight, same_group, basis, *after)
    return [(made[2 * at], made[2 * at + 1]) for at in range(len(slots))]


def back_kernel(slots, parts_ref, weight_ref, *refs):
    whole, taps = refs[-2:]
    outs = refs[-2 - 2 * slots : -2]
    bands, _, band = parts_ref.shape[:3]
    rows, width, depth = outs[0].shape
    clear_edges(taps)
    for slot in reversed(range(slots)):
        cot_ref, sums_ref = outs[2 * slot : 2 * slot + 2]
        if slot % 2:
            for at in range(bands):
                whole[at * band : (at + 1) * band] = parts_ref[at, slot // 2]
        half = slot % 2
        values = whole[:, :, half * depth : (half + 1) * depth]
        cot_ref[...] = values
        taps[1 : rows + 1] = columns(values.astype(F32), True)
        sums_ref[...] = side_by_side(conv_rows(taps, weight_ref, rows, True)).astype(BF16)


def back_conv(parts, weight, after=()):
    bands, pairs, band, width, double = parts.shape
    rows = bands * band
    depth = double // 2
    wide = weight.shape[2]
    cells = rows * width
    slots = 2 * pairs
    outs = [
        jax.ShapeDtypeStruct((rows, width, depth), BF16),
        jax.ShapeDtypeStruct((cells // 2, 2 * wide), BF16),
    ]
    made = pl.pallas_call(
        functools.partial(back_kernel, slots),
        out_shape=outs * slots,
        in_specs=[vmem()] * 2 + unread(after),
        out_specs=[vmem()] * (2 * slots),
        scratch_shapes=[
            pltpu.VMEM((rows, width, double), BF16),
            pltpu.VMEM((rows + 2, width, 3 * depth), BF16),
        ],
        compiler_params=params(),
        cost_estimate=cost(18 * slots * cells * depth * wide, 8 * slots * cells * depth),
        name="back_conv",
    )(parts, weight, *after)
    return [(made[2 * at], made[2 * at + 1]) for at in range(slots)]


def hidden_kernel(terms, count, *refs):
    group_ref, basis_ref = refs[terms : terms + 2]
    pay_ref, unit_ref, scale_ref, along_ref = refs[-4:]
    wide = unit_ref.shape[1]
    rank = basis_ref.shape[1] // 2
    total = refs[0][...].astype(F32)
    for term in refs[1:terms]:
        total = total + term[...].astype(F32)
    unit, scale = normalized(total[:, :wide], group_ref[...], count)
    unit_ref[...] = unit
    scale_ref[...] = scale
    hidden = (unit / (1.0 + jnp.exp(-unit))).astype(BF16)
    pay_ref[...] = jnp.concatenate([hidden.astype(F32), total[:, wide:]], axis=1).astype(BF16)
    along = jnp.dot(hidden, basis_ref[...], preferred_element_type=F32)
    along_ref[...] = side_by_side(along[:, :rank] + along[:, rank:]).astype(BF16)


def hidden_step(terms, same_group, basis, count, after=()):
    cells, both = terms[0].shape
    wide = same_group.shape[0]
    return pl.pallas_call(
        functools.partial(hidden_kernel, len(terms), count),
        out_shape=[
            jax.ShapeDtypeStruct((cells, both), BF16),
            jax.ShapeDtypeStruct((cells, wide), F32),
            jax.ShapeDtypeStruct((1, wide), F32),
            jax.ShapeDtypeStruct((cells // 2, basis.shape[1]), BF16),
        ],
        in_specs=[vmem()] * (len(terms) + 2) + unread(after),
        out_specs=[vmem()] * 4,
        compiler_params=params(),
        cost_estimate=cost(40 * cells * wide, 16 * cells * wide),
        name="hidden_step",
    )(*terms, same_group, basis, *after)


def second_kernel(slots, bands, at_ref, *refs):
    pays = refs[:slots]
    weight_ref = refs[slots]
    whole, taps = refs[-2:]
    outs = refs[-2 - bands : -2]
    band, width, double = outs[0].shape[1:]
    rows = whole.shape[0]
    depth = taps.shape[2] // 3
    wide = double // 2
    clear_edges(taps)
    for slot in range(slots):
        hidden = pays[slot][:, :depth].astype(F32).reshape(rows, width, depth)
        taps[1 : rows + 1] = columns(hidden, False)
        whole[...] = conv_rows(taps, weight_ref, rows, False).reshape(rows, width, wide)
        lanes = slice(slot % 2 * wide, (slot % 2 + 1) * wide)
        for away in range(bands):
            start = jnp.bitwise_xor(at_ref[0], away) * band
            outs[away][slot // 2, :, :, lanes] = whole[pl.ds(start, band)].astype(BF16)


def second_conv(pays, weight, row, rows, bands, after=()):
    slots = len(pays)
    cells, _ = pays[0].shape
    width = cells // rows
    depth = weight.shape[1] // 3
    wide = weight.shape[2]
    out = jax.ShapeDtypeStruct((slots // 2, rows // bands, width, 2 * wide), BF16)
    return pl.pallas_call(
        functools.partial(second_kernel, slots, bands),
        out_shape=[out] * bands,
        in_specs=[smem()] + [vmem()] * (slots + 1) + unread(after),
        out_specs=[vmem()] * bands,
        scratch_shapes=[
            pltpu.VMEM((rows, width, wide), F32),
            pltpu.VMEM((rows + 2, width, 3 * depth), BF16),
        ],
        compiler_params=params(),
        cost_estimate=cost(18 * slots * cells * depth * wide, 4 * slots * cells * depth),
        name="second_conv",
    )(row, *pays, weight, *after)


def band_kernel(terms, slots, *refs):
    outs = refs[-slots:]
    wide = outs[0].shape[-1]
    total = refs[0][...].astype(F32)
    for term in refs[1:terms]:
        total = total + term[...].astype(F32)
    for slot, out in enumerate(outs):
        lanes = slice(slot % 2 * wide, (slot % 2 + 1) * wide)
        out[...] = total[slot // 2, :, :, lanes].astype(BF16)


def band_step(terms, after=()):
    pairs, band, width, double = terms[0].shape
    out = jax.ShapeDtypeStruct((band, width, double // 2), BF16)
    return pl.pallas_call(
        functools.partial(band_kernel, len(terms), 2 * pairs),
        out_shape=[out] * (2 * pairs),
        in_specs=[vmem()] * len(terms) + unread(after),
        out_specs=[vmem()] * (2 * pairs),
        compiler_params=params(),
        cost_estimate=cost(0, 2 * terms[0].size * len(terms)),
        name="band_step",
    )(*terms, *after)


def join_kernel(blocks, at_ref, x_ref, *refs):
    out = refs[blocks]
    width = x_ref.shape[-1] // blocks
    for away in range(blocks):
        for block in range(blocks):

            @pl.when(jnp.bitwise_xor(at_ref[0], away) == block)
            def _(away=away, block=block):
                lanes = slice(block * width, (block + 1) * width)
                added = x_ref[:, :, lanes].astype(F32) + refs[away][...].astype(F32)
                out[:, :, lanes] = added.astype(BF16)


def join_blocks(x, parts, chip):
    return pl.pallas_call(
        functools.partial(join_kernel, len(parts)),
        out_shape=jax.ShapeDtypeStruct(x.shape, BF16),
        in_specs=[smem(), vmem()] + [vmem()] * len(parts),
        out_specs=vmem(),
        compiler_params=params(),
        cost_estimate=cost(0, 6 * x.size),
        name="join_blocks",
    )(chip, x, *parts)


def pre_kernel(terms, count, *refs):
    unit_ref, scale_ref, group_ref = refs[terms : terms + 3]
    out_ref = refs[-1]
    total = refs[0][...].astype(F32)
    for term in refs[1:terms]:
        total = total + term[...].astype(F32)
    unit = unit_ref[...]
    gate = 1.0 / (1.0 + jnp.exp(-unit))
    grad = stacked_again(total) * (gate * (1.0 + unit * (1.0 - gate)))
    mean = group_sums(jnp.sum(grad, axis=0, keepdims=True), group_ref[...]) / count
    along = group_sums(jnp.sum(grad * unit, axis=0, keepdims=True), group_ref[...]) / count
    out_ref[...] = side_by_side(scale_ref[...] * (grad - mean - unit * along)).astype(BF16)


def pre_step(terms, unit, scale, same_group, count, after=()):
    cells, wide = unit.shape
    return pl.pallas_call(
        functools.partial(pre_kernel, len(terms), count),
        out_shape=jax.ShapeDtypeStruct((cells // 2, 2 * wide), BF16),
        in_specs=[vmem()] * (len(terms) + 3) + unread(after),
        out_specs=vmem(),
        compiler_params=params(),
        cost_estimate=cost(40 * cells * wide, 16 * cells * wide),
        name="pre_step",
    )(*terms, unit, scale, same_group, *after)


def project(values, along, basis):
    both = jnp.concatenate([along, along], axis=1)
    return values - jnp.dot(both, basis, preferred_element_type=F32)


def grad_body(core_ref, left, left_t, taps, keep_ref, send_ref, width, flip):
    half = left.shape[1] // 2
    span = left.shape[0]
    wide = taps.shape[1] // 3
    turned = left[...].T

    @pl.when(core_ref[0] == 0)
    def _():
        left_t[...] = turned

    @pl.when(core_ref[0] != 0)
    def _():
        left_t[:half] = turned[half:]
        left_t[half:] = turned[:half]

    for tap in range(3):
        window = taps[tap * width : tap * width + span]
        result = jnp.dot(left_t[...], window, preferred_element_type=F32)
        first = 3 * (2 - tap if flip else tap)
        for q in range(3):
            lanes = slice(q * wide, (q + 1) * wide)
            keep_ref[first + q] = result[:half, lanes]
            send_ref[first + q] = result[half:, lanes].astype(BF16)


def fill_taps(taps, slot, rows, width, value):
    start = (slot * (rows + 1) + 1) * width
    taps[start : start + rows * width] = value.reshape(rows * width, value.shape[2])


def clear_gaps(left, taps, slots, rows, width):
    gap = rows + 1
    for slot in range(slots + 1):
        begin = slot * gap * width
        end = taps.shape[0] if slot == slots else begin + width
        taps[begin:end] = jnp.zeros((end - begin, taps.shape[1]), taps.dtype)
    for slot in range(slots):
        begin = (slot * gap + rows) * width
        end = left.shape[0] if slot == slots - 1 else begin + width
        left[begin:end] = jnp.zeros((end - begin, left.shape[1]), left.dtype)


def first_grad_kernel(slots, core_ref, *refs):
    acts, pays, grads = (refs[at * slots : (at + 1) * slots] for at in range(3))
    basis_ref = refs[3 * slots]
    keep_ref, send_ref, left, left_t, taps = refs[-5:]
    rows, width, depth = acts[0].shape
    cells = rows * width
    rank = basis_ref.shape[0] // 2
    wide = taps.shape[1] // 3
    clear_gaps(left, taps, slots, rows, width)
    for slot in range(slots):
        values = acts[slot][...].reshape(cells, depth).astype(F32)
        along = pays[slot][:, wide : wide + rank]
        begin = slot * (rows + 1) * width
        left[begin : begin + cells] = project(values, along, basis_ref[...]).astype(BF16)
        right = stacked_again(grads[slot][...].astype(F32)).reshape(rows, width, wide)
        fill_taps(taps, slot, rows, width, columns(right, True))
    grad_body(core_ref, left, left_t, taps, keep_ref, send_ref, width, True)


def second_grad_kernel(slots, core_ref, *refs):
    cots, pays = (refs[at * slots : (at + 1) * slots] for at in range(2))
    alongs_ref, basis_ref = refs[2 * slots : 2 * slots + 2]
    keep_ref, send_ref, left, left_t, taps = refs[-5:]
    rows, width, depth = cots[0].shape
    cells = rows * width
    rank = basis_ref.shape[0] // 2
    wide = taps.shape[1] // 3
    clear_gaps(left, taps, slots, rows, width)
    for slot in range(slots):
        begin = slot * (rows + 1) * width
        left[begin : begin + cells] = cots[slot][...].reshape(cells, depth)
        packed = alongs_ref[jnp.bitwise_xor(core_ref[1], slot)]
        along = jnp.concatenate([packed[:, :rank], packed[:, rank:]], axis=0)
        values = pays[slot][:, :wide].astype(F32)
        right = project(values, along, basis_ref[...]).astype(BF16).astype(F32)
        fill_taps(taps, slot, rows, width, columns(right.reshape(rows, width, wide), False))
    grad_body(core_ref, left, left_t, taps, keep_ref, send_ref, width, False)


def weight_grad(kernel, name, core, lefts, firsts, seconds, basis, wide, after=()):
    slots = len(firsts)
    rows, width, depth = lefts[0].shape
    used = slots * (rows + 1) * width
    span = -(-used // 128) * 128
    half = depth // 2
    tap_rows = 2 * width + span
    return pl.pallas_call(
        functools.partial(kernel, slots),
        out_shape=[
            jax.ShapeDtypeStruct((9, half, wide), F32),
            jax.ShapeDtypeStruct((9, half, wide), BF16),
        ],
        in_specs=[smem()] + [vmem()] * (1 + len(lefts) + slots + len(seconds)) + unread(after),
        out_specs=[vmem()] * 2,
        scratch_shapes=[
            pltpu.VMEM((span, depth), BF16),
            pltpu.VMEM((depth, span), BF16),
            pltpu.VMEM((tap_rows, 3 * wide), BF16),
        ],
        compiler_params=params(),
        cost_estimate=cost(18 * slots * rows * width * depth * wide, 20 * depth * wide * 9),
        name=name,
    )(core, *lefts, *firsts, *seconds, basis, *after)


def halves_kernel(turn, core_ref, own_ref, other_ref, *refs):
    outs = refs[-2:] if turn else refs[-1:]
    half = own_ref.shape[1]

    @pl.when(core_ref[0] == 0)
    def _():
        outs[0][:, :half] = own_ref[...]
        outs[0][:, half:] = other_ref[...]

    @pl.when(core_ref[0] != 0)
    def _():
        outs[0][:, :half] = other_ref[...]
        outs[0][:, half:] = own_ref[...]

    if turn:
        for tap in range(9):
            outs[1][tap] = outs[0][tap].T


def join_halves(core, own, other, turn, after=()):
    _, half, wide = own.shape
    outs = [jax.ShapeDtypeStruct((9, 2 * half, wide), BF16)]
    if turn:
        outs.append(jax.ShapeDtypeStruct((9, wide, 2 * half), BF16))
    return pl.pallas_call(
        functools.partial(halves_kernel, turn),
        out_shape=outs,
        in_specs=[smem(), vmem(), vmem()] + unread(after),
        out_specs=[vmem()] * len(outs),
        compiler_params=params(),
        cost_estimate=cost(0, 8 * own.size),
        name="join_halves",
    )(core, own, other, *after)


def basis_kernel(blocks, at_ref, basis_ref, *refs):
    rows_ref, columns_ref = refs[-2:]
    rank, channels = basis_ref.shape
    width = channels // blocks
    for block in range(blocks):

        @pl.when(at_ref[0] == block)
        def _(block=block):
            values = basis_ref[:, block * width : (block + 1) * width]
            high = values.astype(BF16).astype(F32)
            both = jnp.concatenate([high, values - high], axis=0)
            rows_ref[...] = both.astype(BF16)
            columns_ref[...] = both.T.astype(BF16)


def basis_parts(at, basis, blocks, after=()):
    rank, channels = basis.shape
    width = channels // blocks
    return pl.pallas_call(
        functools.partial(basis_kernel, blocks),
        out_shape=[
            jax.ShapeDtypeStruct((2 * rank, width), BF16),
            jax.ShapeDtypeStruct((width, 2 * rank), BF16),
        ],
        in_specs=[smem(), vmem()] + unread(after),
        out_specs=[vmem()] * 2,
        compiler_params=params(),
        cost_estimate=cost(0, 4 * basis.size),
        name="basis_parts",
    )(at, basis, *after)


def flat_kernel(scale, keep_ref, got_ref, out_ref, *held):
    taps, half, wide = keep_ref.shape
    whole = wide // 128
    step = 2 * whole + 1
    count = half // 2
    zeros = jnp.zeros((half, 64), F32)
    for tap in range(taps):
        total = (keep_ref[tap] + got_ref[tap].astype(F32)) * scale
        for at in range(whole):
            held[at][...] = total[:, 128 * at : 128 * (at + 1)]
            held[whole + 2 + at][...] = total[:, 128 * at + 64 : 128 * (at + 1) + 64]
        held[whole][...] = jnp.concatenate([total[:, 128 * whole :], zeros], axis=1)
        held[whole + 1][...] = jnp.concatenate([zeros, total[:, :64]], axis=1)
        even, odd = pl.ds(0, count, stride=2), pl.ds(1, count, stride=2)
        rows = [held[at][even, :] for at in range(whole)]
        rows.append(held[whole][even, :] + held[whole + 1][odd, :])
        rows += [held[whole + 2 + at][odd, :] for at in range(whole)]
        for at, row in enumerate(rows):
            out_ref[pl.ds(tap * count * step + at, count, stride=step), :] = row


def flat_grad(keep, got, scale):
    taps, half, wide = keep.shape
    if wide % 128 != 64 or half % 2:
        return ((keep + got.astype(F32)) * scale).reshape(1, 1, taps, half * wide)
    return pl.pallas_call(
        functools.partial(flat_kernel, scale),
        out_shape=jax.ShapeDtypeStruct((taps * half * wide // 128, 128), F32),
        in_specs=[vmem()] * 2,
        out_specs=vmem(),
        scratch_shapes=[pltpu.VMEM((half, 128), F32)] * (2 * (wide // 128) + 2),
        compiler_params=params(),
        cost_estimate=cost(0, 10 * keep.size),
        name="flat_grad",
    )(keep, got).reshape(1, 1, taps, half * wide)


def same_groups(width, size):
    at = np.arange(width) // size
    return jnp.asarray((at[:, None] == at[None, :]).astype(np.float32), BF16)


def body(images, cotangent, first_weight, second_weight, first_basis, second_basis):
    n_dp = lax.axis_size("dp")
    n_rows = lax.axis_size("rows")
    chips = n_dp // 2
    _, band, width, channels = images.shape
    rows = band * n_rows
    dp_width = channels // n_dp
    chip_width = channels // chips
    row_width = channels // n_rows
    group = channels // GROUPS
    count = float(rows * width * group)
    grad_scale = 1.0 / math.sqrt(n_dp * images.shape[0] * rows * width)

    at_dp = lax.axis_index("dp")
    at_row = lax.axis_index("rows")
    chip = (at_dp // 2).astype(jnp.int32)
    core = (at_dp % 2).astype(jnp.int32)
    row = at_row.astype(jnp.int32)
    chip_at, row_at, core_at = chip[None], row[None], jnp.stack([core, chip])
    same_core = [[2 * at + side for at in range(chips)] for side in range(2)]

    def to_core(x):
        return lax.ppermute(x, "dp", [(i, i ^ 1) for i in range(n_dp)])

    def to_chip(x, away):
        return lax.ppermute(x, "dp", [(i, i ^ (2 * away)) for i in range(n_dp)])

    def to_row(x, away):
        return lax.ppermute(x, "rows", [(i, i ^ away) for i in range(n_rows)])

    def chips_gather(x):
        return [x] + [to_chip(x, away) for away in range(1, chips)]

    def rows_gather(x):
        return [x] + [to_row(x, away) for away in range(1, n_rows)]

    def chips_swap(parts):
        return [parts[0]] + [to_chip(parts[away], away) for away in range(1, chips)]

    def rows_swap(parts):
        return [parts[0]] + [to_row(parts[away], away) for away in range(1, n_rows)]

    chip_groups = same_groups(chip_width, group)
    row_groups = same_groups(row_width, group)

    image_slots = chips_swap(split_blocks(images[0], chips, chip_at))
    first_weight, _ = lax.optimization_barrier((first_weight, image_slots[1]))
    own_first = first_weight.reshape(9, dp_width, row_width)
    image_pack = pack_slots(image_slots, (own_first,))
    image_parts = rows_gather(image_pack)
    landed = tuple(image_parts[1:-1])

    cot_slots = chips_swap(split_blocks(cotangent[0], chips, chip_at, landed))
    cot_pack = pack_slots(cot_slots)
    cot_parts = lax.all_gather(cot_pack, "rows")
    (first_full,) = join_halves(core_at, own_first, to_core(own_first), False, landed)
    weight_one = first_full.reshape(3, 3 * chip_width, row_width)
    one_rows, one_columns = basis_parts(chip_at, first_basis, chips, landed)
    two_rows, two_columns = basis_parts(row_at, second_basis, n_rows, landed)

    sent = list(range(chips - 1, 0, -1))
    made = first_conv(
        image_parts, sent, weight_one, chip_groups, one_columns, row_at, rows, count, (cot_pack,)
    )
    own_made = first_conv(
        image_parts, [0], weight_one, chip_groups, one_columns, row_at, rows, count, made[0][1:]
    )
    made = own_made + made[::-1]
    active = [pair[0] for pair in made]
    first_terms = chips_swap([pair[1] for pair in made])

    second_weight, _ = lax.optimization_barrier((second_weight, made[1][1]))
    own_second = second_weight.reshape(9, dp_width, row_width)
    second_full, second_turned = join_halves(core_at, own_second, to_core(own_second), True)
    weight_back = second_full.reshape(3, 3 * chip_width, row_width)
    weight_two = second_turned.reshape(3, 3 * row_width, chip_width)

    pay, unit, scale, along_part = hidden_step(
        first_terms, row_groups, two_columns, count, (second_full,)
    )
    pays = chips_gather(pay)
    along = lax.psum(along_part, "rows")
    alongs = lax.all_gather(along, "dp", axis_index_groups=same_core)

    back = back_conv(cot_parts, weight_back, (pay,))
    whole_cot = [pair[0] for pair in back]
    back_terms = chips_swap([pair[1] for pair in back])

    sums = second_conv(pays, weight_two, row_at, rows, n_rows, back[0][1:])
    band_terms = rows_swap(sums)

    pre_grad = pre_step(back_terms, unit, scale, row_groups, count, (sums[0], along))
    pre_grads = chips_gather(pre_grad)

    second_halves = weight_grad(
        second_grad_kernel, "second_grad", core_at, whole_cot, pays, [alongs], two_rows,
        row_width, (pre_grad,),
    )
    blocks = band_step(band_terms)
    first_halves = weight_grad(
        first_grad_kernel, "first_grad", core_at, active, pays, pre_grads, one_rows,
        row_width, (second_halves[1], blocks[0]),
    )
    block_output = join_blocks(images[0], chips_swap(blocks), chip_at)[None]
    second_grad = flat_grad(second_halves[0], to_core(second_halves[1]), grad_scale)
    first_grad = flat_grad(first_halves[0], to_core(first_halves[1]), grad_scale)
    return (block_output, first_grad, second_grad)


def solution(mesh):
    split = P("dp", "rows", None, None)
    return jax.shard_map(
        body,
        mesh=mesh,
        in_specs=(split, split, split, split, P(), P()),
        out_specs=(split, split, split),
        check_vma=False,
    )
```

```python
import functools
import math

import jax
import jax.numpy as jnp
import numpy as np
from jax import lax
from jax.experimental import pallas as pl
from jax.experimental.pallas import tpu as pltpu
from jax.sharding import PartitionSpec as P

GROUPS = 32
EPS = 1e-5
MIB = 1024 * 1024
F32 = jnp.float32
BF16 = jnp.bfloat16


def vmem():
    return pl.BlockSpec(memory_space=pltpu.VMEM)


def smem():
    return pl.BlockSpec(memory_space=pltpu.SMEM)


def unread(after):
    return [pl.BlockSpec(memory_space=pl.ANY)] * len(after)


def params(held=8):
    return pltpu.CompilerParams(vmem_limit_bytes=held * MIB)


def cost(flops, moved):
    return pl.CostEstimate(flops=int(flops), bytes_accessed=int(moved), transcendentals=0)


def group_sums(row, same_group):
    high = row.astype(BF16).astype(F32)
    rest = row - high
    middle = rest.astype(BF16).astype(F32)
    low = rest - middle
    at = lax.broadcasted_iota(jnp.int32, (16, row.shape[1]), 0)
    stacked = jnp.where(at == 0, high, jnp.where(at == 1, middle, jnp.where(at == 2, low, 0.0)))
    sums = jnp.dot(stacked.astype(BF16), same_group, preferred_element_type=F32)
    return jnp.sum(sums, axis=0, keepdims=True)


def normalized(values, same_group, count):
    center = group_sums(jnp.sum(values, axis=0, keepdims=True), same_group) / count
    moved = values - center
    spread = group_sums(jnp.sum(moved * moved, axis=0, keepdims=True), same_group) / count
    scale = 1.0 / jnp.sqrt(spread + EPS)
    return moved * scale, scale


def columns(values, flip):
    width = values.shape[1]
    at = lax.broadcasted_iota(jnp.int32, values.shape, 1)
    before = jnp.where(at == 0, 0.0, pltpu.roll(values, 1, axis=1))
    after = jnp.where(at == width - 1, 0.0, pltpu.roll(values, width - 1, axis=1))
    parts = [after, values, before] if flip else [before, values, after]
    return jnp.concatenate([part.astype(BF16) for part in parts], axis=2)


def conv_rows(taps, weight_ref, rows, flip):
    _, width, depth = taps.shape
    total = None
    for tap in range(3):
        window = taps[tap : tap + rows].reshape(rows * width, depth)
        term = jnp.dot(window, weight_ref[2 - tap if flip else tap], preferred_element_type=F32)
        total = term if total is None else total + term
    return total


def side_by_side(values):
    half = values.shape[0] // 2
    return jnp.concatenate([values[:half], values[half:]], axis=1)


def stacked_again(values):
    half = values.shape[1] // 2
    return jnp.concatenate([values[:, :half], values[:, half:]], axis=0)


def clear_edges(taps):
    rows = taps.shape[0]
    taps[0:1] = jnp.zeros((1,) + taps.shape[1:], taps.dtype)
    taps[rows - 1 : rows] = jnp.zeros((1,) + taps.shape[1:], taps.dtype)


def split_kernel(blocks, at_ref, *refs):
    outs = refs[-blocks:]
    width = outs[0].shape[-1]
    for away in range(blocks):
        for block in range(blocks):

            @pl.when(jnp.bitwise_xor(at_ref[0], away) == block)
            def _(away=away, block=block):
                for at, x_ref in enumerate(refs[:-blocks]):
                    outs[away][at] = x_ref[:, :, block * width : (block + 1) * width]


def split_blocks(arrays, blocks, chip):
    height, width, channels = arrays[0].shape
    shape = jax.ShapeDtypeStruct((len(arrays), height, width, channels // blocks), BF16)
    return pl.pallas_call(
        functools.partial(split_kernel, blocks),
        out_shape=[shape] * blocks,
        in_specs=[smem()] + [vmem()] * len(arrays),
        out_specs=[vmem()] * blocks,
        compiler_params=params(),
        cost_estimate=cost(0, 4 * len(arrays) * arrays[0].size),
        name="split_blocks",
    )(chip, *arrays)


def pack_kernel(slots, at, *refs):
    out = refs[-1]
    width = refs[0].shape[-1]
    for slot in range(slots):
        half = slot % 2
        out[slot // 2, :, :, half * width : (half + 1) * width] = refs[slot][at]


def pack_slots(slots, at, after=()):
    _, band, width, depth = slots[0].shape
    return pl.pallas_call(
        functools.partial(pack_kernel, len(slots), at),
        out_shape=jax.ShapeDtypeStruct((len(slots) // 2, band, width, 2 * depth), BF16),
        in_specs=[vmem()] * len(slots) + unread(after),
        out_specs=vmem(),
        compiler_params=params(),
        cost_estimate=cost(0, 2 * len(slots) * slots[0].size),
        name="pack_slots",
    )(*slots, *after)


def assemble(whole, parts, pair, row):
    for away, part in enumerate(parts):
        band = part.shape[1]
        whole[pl.ds(jnp.bitwise_xor(row, away) * band, band)] = part[pair]


def first_kernel(slots, bands, count, at_ref, *refs):
    parts = refs[:bands]
    weight_ref, group_ref, basis_ref = refs[bands : bands + 3]
    whole, taps = refs[-2:]
    outs = refs[-2 - 2 * len(slots) : -2]
    rows, width, depth = outs[0].shape
    rank = basis_ref.shape[1] // 2
    cells = rows * width
    clear_edges(taps)
    held = None
    for at, slot in enumerate(slots):
        act_ref, sums_ref = outs[2 * at : 2 * at + 2]
        if slot // 2 != held:
            held = slot // 2
            assemble(whole, parts, held, at_ref[0])
        half = slot % 2
        values = whole[:, :, half * depth : (half + 1) * depth].astype(F32)
        unit, _ = normalized(values.reshape(cells, depth), group_ref[...], count)
        active = (unit / (1.0 + jnp.exp(-unit))).astype(BF16)
        act_ref[...] = active.reshape(act_ref.shape)
        taps[1 : rows + 1] = columns(active.astype(F32).reshape(act_ref.shape), False)
        total = conv_rows(taps, weight_ref, rows, False)
        along = jnp.dot(active, basis_ref[...], preferred_element_type=F32)
        along = along[:, :rank] + along[:, rank:]
        sums_ref[...] = jnp.concatenate([total, along], axis=1).astype(BF16)


def first_conv(parts, slots, weight, same_group, basis, row, rows, count, after=()):
    _, band, width, double = parts[0].shape
    depth = double // 2
    rank = basis.shape[1] // 2
    wide = weight.shape[2]
    cells = rows * width
    outs = [
        jax.ShapeDtypeStruct((rows, width, depth), BF16),
        jax.ShapeDtypeStruct((cells, wide + rank), BF16),
    ]
    made = pl.pallas_call(
        functools.partial(first_kernel, slots, len(parts), count),
        out_shape=outs * len(slots),
        in_specs=[smem()] + [vmem()] * (len(parts) + 3) + unread(after),
        out_specs=[vmem()] * (2 * len(slots)),
        scratch_shapes=[
            pltpu.VMEM((rows, width, double), BF16),
            pltpu.VMEM((rows + 2, width, 3 * depth), BF16),
        ],
        compiler_params=params(14),
        cost_estimate=cost(18 * len(slots) * cells * depth * wide, 8 * cells * depth),
        name="first_conv",
    )(row, *parts, weight, same_group, basis, *after)
    return [(made[2 * at], made[2 * at + 1]) for at in range(len(slots))]


def back_kernel(slots, parts_ref, weight_ref, *refs):
    whole, taps = refs[-2:]
    outs = refs[-2 - 2 * slots : -2]
    bands, _, band = parts_ref.shape[:3]
    rows, width, depth = outs[0].shape
    clear_edges(taps)
    for slot in reversed(range(slots)):
        cot_ref, sums_ref = outs[2 * slot : 2 * slot + 2]
        if slot % 2:
            for at in range(bands):
                whole[at * band : (at + 1) * band] = parts_ref[at, slot // 2]
        half = slot % 2
        values = whole[:, :, half * depth : (half + 1) * depth]
        cot_ref[...] = values
        taps[1 : rows + 1] = columns(values.astype(F32), True)
        sums_ref[...] = side_by_side(conv_rows(taps, weight_ref, rows, True)).astype(BF16)


def back_conv(parts, weight, after=()):
    bands, pairs, band, width, double = parts.shape
    rows = bands * band
    depth = double // 2
    wide = weight.shape[2]
    cells = rows * width
    slots = 2 * pairs
    outs = [
        jax.ShapeDtypeStruct((rows, width, depth), BF16),
        jax.ShapeDtypeStruct((cells // 2, 2 * wide), BF16),
    ]
    made = pl.pallas_call(
        functools.partial(back_kernel, slots),
        out_shape=outs * slots,
        in_specs=[vmem()] * 2 + unread(after),
        out_specs=[vmem()] * (2 * slots),
        scratch_shapes=[
            pltpu.VMEM((rows, width, double), BF16),
            pltpu.VMEM((rows + 2, width, 3 * depth), BF16),
        ],
        compiler_params=params(14),
        cost_estimate=cost(18 * slots * cells * depth * wide, 8 * slots * cells * depth),
        name="back_conv",
    )(parts, weight, *after)
    return [(made[2 * at], made[2 * at + 1]) for at in range(slots)]


def hidden_kernel(terms, count, *refs):
    group_ref, basis_ref = refs[terms : terms + 2]
    pay_ref, unit_ref, scale_ref, along_ref = refs[-4:]
    wide = unit_ref.shape[1]
    rank = basis_ref.shape[1] // 2
    total = refs[0][...].astype(F32)
    for term in refs[1:terms]:
        total = total + term[...].astype(F32)
    unit, scale = normalized(total[:, :wide], group_ref[...], count)
    unit_ref[...] = unit
    scale_ref[...] = scale
    hidden = (unit / (1.0 + jnp.exp(-unit))).astype(BF16)
    pay_ref[...] = jnp.concatenate([hidden.astype(F32), total[:, wide:]], axis=1).astype(BF16)
    along = jnp.dot(hidden, basis_ref[...], preferred_element_type=F32)
    along_ref[...] = side_by_side(along[:, :rank] + along[:, rank:]).astype(BF16)


def hidden_step(terms, same_group, basis, count, after=()):
    cells, both = terms[0].shape
    wide = same_group.shape[0]
    return pl.pallas_call(
        functools.partial(hidden_kernel, len(terms), count),
        out_shape=[
            jax.ShapeDtypeStruct((cells, both), BF16),
            jax.ShapeDtypeStruct((cells, wide), F32),
            jax.ShapeDtypeStruct((1, wide), F32),
            jax.ShapeDtypeStruct((cells // 2, basis.shape[1]), BF16),
        ],
        in_specs=[vmem()] * (len(terms) + 2) + unread(after),
        out_specs=[vmem()] * 4,
        compiler_params=params(14),
        cost_estimate=cost(40 * cells * wide, 16 * cells * wide),
        name="hidden_step",
    )(*terms, same_group, basis, *after)


def second_kernel(slots, bands, at_ref, *refs):
    pays = refs[:slots]
    weight_ref = refs[slots]
    whole, taps = refs[-2:]
    outs = refs[-2 - bands : -2]
    band, width, double = outs[0].shape[1:]
    rows = whole.shape[0]
    depth = taps.shape[2] // 3
    wide = double // 2
    clear_edges(taps)
    for slot in range(slots):
        hidden = pays[slot][:, :depth].astype(F32).reshape(rows, width, depth)
        taps[1 : rows + 1] = columns(hidden, False)
        whole[...] = conv_rows(taps, weight_ref, rows, False).reshape(rows, width, wide)
        lanes = slice(slot % 2 * wide, (slot % 2 + 1) * wide)
        for away in range(bands):
            start = jnp.bitwise_xor(at_ref[0], away) * band
            outs[away][slot // 2, :, :, lanes] = whole[pl.ds(start, band)].astype(BF16)


def second_conv(pays, weight, row, rows, bands, after=()):
    slots = len(pays)
    cells, _ = pays[0].shape
    width = cells // rows
    depth = weight.shape[1] // 3
    wide = weight.shape[2]
    out = jax.ShapeDtypeStruct((slots // 2, rows // bands, width, 2 * wide), BF16)
    return pl.pallas_call(
        functools.partial(second_kernel, slots, bands),
        out_shape=[out] * bands,
        in_specs=[smem()] + [vmem()] * (slots + 1) + unread(after),
        out_specs=[vmem()] * bands,
        scratch_shapes=[
            pltpu.VMEM((rows, width, wide), F32),
            pltpu.VMEM((rows + 2, width, 3 * depth), BF16),
        ],
        compiler_params=params(14),
        cost_estimate=cost(18 * slots * cells * depth * wide, 4 * slots * cells * depth),
        name="second_conv",
    )(row, *pays, weight, *after)


def band_kernel(terms, slots, *refs):
    outs = refs[-slots:]
    wide = outs[0].shape[-1]
    total = refs[0][...].astype(F32)
    for term in refs[1:terms]:
        total = total + term[...].astype(F32)
    for slot, out in enumerate(outs):
        lanes = slice(slot % 2 * wide, (slot % 2 + 1) * wide)
        out[...] = total[slot // 2, :, :, lanes].astype(BF16)


def band_step(terms, after=()):
    pairs, band, width, double = terms[0].shape
    out = jax.ShapeDtypeStruct((band, width, double // 2), BF16)
    return pl.pallas_call(
        functools.partial(band_kernel, len(terms), 2 * pairs),
        out_shape=[out] * (2 * pairs),
        in_specs=[vmem()] * len(terms) + unread(after),
        out_specs=[vmem()] * (2 * pairs),
        compiler_params=params(),
        cost_estimate=cost(0, 2 * terms[0].size * len(terms)),
        name="band_step",
    )(*terms, *after)


def join_kernel(blocks, at_ref, x_ref, *refs):
    out = refs[blocks]
    width = x_ref.shape[-1] // blocks
    for away in range(blocks):
        for block in range(blocks):

            @pl.when(jnp.bitwise_xor(at_ref[0], away) == block)
            def _(away=away, block=block):
                lanes = slice(block * width, (block + 1) * width)
                added = x_ref[:, :, lanes].astype(F32) + refs[away][...].astype(F32)
                out[:, :, lanes] = added.astype(BF16)


def join_blocks(x, parts, chip):
    return pl.pallas_call(
        functools.partial(join_kernel, len(parts)),
        out_shape=jax.ShapeDtypeStruct(x.shape, BF16),
        in_specs=[smem(), vmem()] + [vmem()] * len(parts),
        out_specs=vmem(),
        compiler_params=params(),
        cost_estimate=cost(0, 6 * x.size),
        name="join_blocks",
    )(chip, x, *parts)


def pre_kernel(terms, count, *refs):
    unit_ref, scale_ref, group_ref = refs[terms : terms + 3]
    out_ref = refs[-1]
    total = refs[0][...].astype(F32)
    for term in refs[1:terms]:
        total = total + term[...].astype(F32)
    unit = unit_ref[...]
    gate = 1.0 / (1.0 + jnp.exp(-unit))
    grad = stacked_again(total) * (gate * (1.0 + unit * (1.0 - gate)))
    mean = group_sums(jnp.sum(grad, axis=0, keepdims=True), group_ref[...]) / count
    along = group_sums(jnp.sum(grad * unit, axis=0, keepdims=True), group_ref[...]) / count
    out_ref[...] = side_by_side(scale_ref[...] * (grad - mean - unit * along)).astype(BF16)


def pre_step(terms, unit, scale, same_group, count, after=()):
    cells, wide = unit.shape
    return pl.pallas_call(
        functools.partial(pre_kernel, len(terms), count),
        out_shape=jax.ShapeDtypeStruct((cells // 2, 2 * wide), BF16),
        in_specs=[vmem()] * (len(terms) + 3) + unread(after),
        out_specs=vmem(),
        compiler_params=params(14),
        cost_estimate=cost(40 * cells * wide, 16 * cells * wide),
        name="pre_step",
    )(*terms, unit, scale, same_group, *after)


def project(values, along, basis):
    both = jnp.concatenate([along, along], axis=1)
    return values - jnp.dot(both, basis, preferred_element_type=F32)


def grad_body(core_ref, left, left_t, taps, keep_ref, send_ref, width, flip):
    half = left.shape[1] // 2
    span = left.shape[0]
    wide = taps.shape[1] // 3
    turned = left[...].T

    @pl.when(core_ref[0] == 0)
    def _():
        left_t[...] = turned

    @pl.when(core_ref[0] != 0)
    def _():
        left_t[:half] = turned[half:]
        left_t[half:] = turned[:half]

    for tap in range(3):
        window = taps[tap * width : tap * width + span]
        result = jnp.dot(left_t[...], window, preferred_element_type=F32)
        first = 3 * (2 - tap if flip else tap)
        for q in range(3):
            lanes = slice(q * wide, (q + 1) * wide)
            keep_ref[first + q] = result[:half, lanes]
            send_ref[first + q] = result[half:, lanes].astype(BF16)


def fill_taps(taps, slot, rows, width, value):
    start = (slot * (rows + 1) + 1) * width
    taps[start : start + rows * width] = value.reshape(rows * width, value.shape[2])


def clear_gaps(left, taps, slots, rows, width):
    gap = rows + 1
    for slot in range(slots + 1):
        begin = slot * gap * width
        end = taps.shape[0] if slot == slots else begin + width
        taps[begin:end] = jnp.zeros((end - begin, taps.shape[1]), taps.dtype)
    for slot in range(slots):
        begin = (slot * gap + rows) * width
        end = left.shape[0] if slot == slots - 1 else begin + width
        left[begin:end] = jnp.zeros((end - begin, left.shape[1]), left.dtype)


def first_grad_kernel(slots, core_ref, *refs):
    acts, pays, grads = (refs[at * slots : (at + 1) * slots] for at in range(3))
    basis_ref = refs[3 * slots]
    keep_ref, send_ref, left, left_t, taps = refs[-5:]
    rows, width, depth = acts[0].shape
    cells = rows * width
    rank = basis_ref.shape[0] // 2
    wide = taps.shape[1] // 3
    clear_gaps(left, taps, slots, rows, width)
    for slot in range(slots):
        values = acts[slot][...].reshape(cells, depth).astype(F32)
        along = pays[slot][:, wide : wide + rank]
        begin = slot * (rows + 1) * width
        left[begin : begin + cells] = project(values, along, basis_ref[...]).astype(BF16)
        right = stacked_again(grads[slot][...].astype(F32)).reshape(rows, width, wide)
        fill_taps(taps, slot, rows, width, columns(right, True))
    grad_body(core_ref, left, left_t, taps, keep_ref, send_ref, width, True)


def second_grad_kernel(slots, core_ref, *refs):
    cots, pays = (refs[at * slots : (at + 1) * slots] for at in range(2))
    alongs_ref, basis_ref = refs[2 * slots : 2 * slots + 2]
    keep_ref, send_ref, left, left_t, taps = refs[-5:]
    rows, width, depth = cots[0].shape
    cells = rows * width
    rank = basis_ref.shape[0] // 2
    wide = taps.shape[1] // 3
    clear_gaps(left, taps, slots, rows, width)
    for slot in range(slots):
        begin = slot * (rows + 1) * width
        left[begin : begin + cells] = cots[slot][...].reshape(cells, depth)
        packed = alongs_ref[slot]
        along = jnp.concatenate([packed[:, :rank], packed[:, rank:]], axis=0)
        values = pays[slot][:, :wide].astype(F32)
        right = project(values, along, basis_ref[...]).astype(BF16).astype(F32)
        fill_taps(taps, slot, rows, width, columns(right.reshape(rows, width, wide), False))
    grad_body(core_ref, left, left_t, taps, keep_ref, send_ref, width, False)


def weight_grad(kernel, name, core, lefts, firsts, seconds, basis, wide, after=()):
    slots = len(firsts)
    rows, width, depth = lefts[0].shape
    used = slots * (rows + 1) * width
    span = -(-used // 128) * 128
    half = depth // 2
    tap_rows = 2 * width + span
    return pl.pallas_call(
        functools.partial(kernel, slots),
        out_shape=[
            jax.ShapeDtypeStruct((9, half, wide), F32),
            jax.ShapeDtypeStruct((9, half, wide), BF16),
        ],
        in_specs=[smem()] + [vmem()] * (1 + len(lefts) + slots + len(seconds)) + unread(after),
        out_specs=[vmem()] * 2,
        scratch_shapes=[
            pltpu.VMEM((span, depth), BF16),
            pltpu.VMEM((depth, span), BF16),
            pltpu.VMEM((tap_rows, 3 * wide), BF16),
        ],
        compiler_params=params(28),
        cost_estimate=cost(18 * slots * rows * width * depth * wide, 20 * depth * wide * 9),
        name=name,
    )(core, *lefts, *firsts, *seconds, basis, *after)


def halves_kernel(turn, core_ref, own_ref, other_ref, *refs):
    outs = refs[-2:] if turn else refs[-1:]
    half = own_ref.shape[1]

    @pl.when(core_ref[0] == 0)
    def _():
        outs[0][:, :half] = own_ref[...]
        outs[0][:, half:] = other_ref[...]

    @pl.when(core_ref[0] != 0)
    def _():
        outs[0][:, :half] = other_ref[...]
        outs[0][:, half:] = own_ref[...]

    if turn:
        for tap in range(9):
            outs[1][tap] = outs[0][tap].T


def join_halves(core, own, other, turn, after=()):
    _, half, wide = own.shape
    outs = [jax.ShapeDtypeStruct((9, 2 * half, wide), BF16)]
    if turn:
        outs.append(jax.ShapeDtypeStruct((9, wide, 2 * half), BF16))
    return pl.pallas_call(
        functools.partial(halves_kernel, turn),
        out_shape=outs,
        in_specs=[smem(), vmem(), vmem()] + unread(after),
        out_specs=[vmem()] * len(outs),
        compiler_params=params(8),
        cost_estimate=cost(0, 8 * own.size),
        name="join_halves",
    )(core, own, other, *after)


def basis_kernel(blocks, at_ref, basis_ref, *refs):
    rows_ref, columns_ref = refs[-2:]
    rank, channels = basis_ref.shape
    width = channels // blocks
    for block in range(blocks):

        @pl.when(at_ref[0] == block)
        def _(block=block):
            values = basis_ref[:, block * width : (block + 1) * width]
            high = values.astype(BF16).astype(F32)
            both = jnp.concatenate([high, values - high], axis=0)
            rows_ref[...] = both.astype(BF16)
            columns_ref[...] = both.T.astype(BF16)


def basis_parts(at, basis, blocks, after=()):
    rank, channels = basis.shape
    width = channels // blocks
    return pl.pallas_call(
        functools.partial(basis_kernel, blocks),
        out_shape=[
            jax.ShapeDtypeStruct((2 * rank, width), BF16),
            jax.ShapeDtypeStruct((width, 2 * rank), BF16),
        ],
        in_specs=[smem(), vmem()] + unread(after),
        out_specs=[vmem()] * 2,
        compiler_params=params(),
        cost_estimate=cost(0, 4 * basis.size),
        name="basis_parts",
    )(at, basis, *after)


def flat_kernel(scale, keep_ref, got_ref, out_ref, *held):
    taps, half, wide = keep_ref.shape
    whole = wide // 128
    step = 2 * whole + 1
    count = half // 2
    zeros = jnp.zeros((half, 64), F32)
    for tap in range(taps):
        total = (keep_ref[tap] + got_ref[tap].astype(F32)) * scale
        for at in range(whole):
            held[at][...] = total[:, 128 * at : 128 * (at + 1)]
            held[whole + 2 + at][...] = total[:, 128 * at + 64 : 128 * (at + 1) + 64]
        held[whole][...] = jnp.concatenate([total[:, 128 * whole :], zeros], axis=1)
        held[whole + 1][...] = jnp.concatenate([zeros, total[:, :64]], axis=1)
        even, odd = pl.ds(0, count, stride=2), pl.ds(1, count, stride=2)
        rows = [held[at][even, :] for at in range(whole)]
        rows.append(held[whole][even, :] + held[whole + 1][odd, :])
        rows += [held[whole + 2 + at][odd, :] for at in range(whole)]
        for at, row in enumerate(rows):
            out_ref[pl.ds(tap * count * step + at, count, stride=step), :] = row


def flat_grad(keep, got, scale):
    taps, half, wide = keep.shape
    if wide % 128 != 64 or half % 2:
        return ((keep + got.astype(F32)) * scale).reshape(1, 1, taps, half * wide)
    return pl.pallas_call(
        functools.partial(flat_kernel, scale),
        out_shape=jax.ShapeDtypeStruct((taps * half * wide // 128, 128), F32),
        in_specs=[vmem()] * 2,
        out_specs=vmem(),
        scratch_shapes=[pltpu.VMEM((half, 128), F32)] * (2 * (wide // 128) + 2),
        compiler_params=params(8),
        cost_estimate=cost(0, 10 * keep.size),
        name="flat_grad",
    )(keep, got).reshape(1, 1, taps, half * wide)


def same_groups(width, size):
    at = np.arange(width) // size
    return jnp.asarray((at[:, None] == at[None, :]).astype(np.float32), BF16)


def body(images, cotangent, first_weight, second_weight, first_basis, second_basis):
    n_dp = lax.axis_size("dp")
    n_rows = lax.axis_size("rows")
    chips = n_dp // 2
    _, band, width, channels = images.shape
    rows = band * n_rows
    dp_width = channels // n_dp
    chip_width = channels // chips
    row_width = channels // n_rows
    group = channels // GROUPS
    count = float(rows * width * group)
    grad_scale = 1.0 / math.sqrt(n_dp * images.shape[0] * rows * width)

    at_dp = lax.axis_index("dp")
    at_row = lax.axis_index("rows")
    chip = (at_dp // 2).astype(jnp.int32)
    core = (at_dp % 2).astype(jnp.int32)
    row = at_row.astype(jnp.int32)
    chip_at, row_at, core_at = chip[None], row[None], core[None]

    def to_core(x):
        return lax.ppermute(x, "dp", [(i, i ^ 1) for i in range(n_dp)])

    def to_chip(x, away):
        return lax.ppermute(x, "dp", [(i, i ^ (2 * away)) for i in range(n_dp)])

    def to_row(x, away):
        return lax.ppermute(x, "rows", [(i, i ^ away) for i in range(n_rows)])

    def chips_gather(x):
        return [x] + [to_chip(x, away) for away in range(1, chips)]

    def rows_gather(x):
        return [x] + [to_row(x, away) for away in range(1, n_rows)]

    def chips_swap(parts):
        return [parts[0]] + [to_chip(parts[away], away) for away in range(1, chips)]

    def rows_swap(parts):
        return [parts[0]] + [to_row(parts[away], away) for away in range(1, n_rows)]

    chip_groups = same_groups(chip_width, group)
    row_groups = same_groups(row_width, group)

    slots = chips_swap(split_blocks([images[0], cotangent[0]], chips, chip_at))
    image_parts = rows_gather(pack_slots(slots, 0))
    cot_pack = pack_slots(slots, 1, tuple(image_parts[1:]))
    cot_parts = lax.all_gather(cot_pack, "rows")

    first_weight, second_weight, _ = lax.optimization_barrier(
        (first_weight, second_weight, slots[1])
    )
    own_first = first_weight.reshape(9, dp_width, row_width)
    own_second = second_weight.reshape(9, dp_width, row_width)
    (first_full,) = join_halves(core_at, own_first, to_core(own_first), False)
    second_full, second_turned = join_halves(core_at, own_second, to_core(own_second), True)
    weight_one = first_full.reshape(3, 3 * chip_width, row_width)
    weight_back = second_full.reshape(3, 3 * chip_width, row_width)
    weight_two = second_turned.reshape(3, 3 * row_width, chip_width)
    one_rows, one_columns = basis_parts(chip_at, first_basis, chips)
    two_rows, two_columns = basis_parts(row_at, second_basis, n_rows)

    sent = list(range(chips - 1, 0, -1))
    made = first_conv(
        image_parts, sent, weight_one, chip_groups, one_columns, row_at, rows, count,
        (cot_pack, second_full, two_rows),
    )
    own_made = first_conv(
        image_parts, [0], weight_one, chip_groups, one_columns, row_at, rows, count, made[0][1:]
    )
    made = own_made + made[::-1]
    active = [pair[0] for pair in made]
    first_terms = chips_swap([pair[1] for pair in made])

    pay, unit, scale, along = hidden_step(first_terms, row_groups, two_columns, count)
    pays = chips_gather(pay)

    steps = []
    away = 1
    while away < n_rows:
        along = (along.astype(F32) + to_row(along, away).astype(F32)).astype(BF16)
        steps.append(along)
        away *= 2
    along = along[None]
    away = 1
    while away < chips:
        along = jnp.concatenate([along, to_chip(along, away)])
        steps.append(along)
        away *= 2

    back = back_conv(cot_parts, weight_back, (pay, steps[0]))
    whole_cot = [pair[0] for pair in back]
    back_terms = chips_swap([pair[1] for pair in back])

    sums = second_conv(pays, weight_two, row_at, rows, n_rows, (back[0][1], steps[1]))
    band_terms = rows_swap(sums)

    pre_grad = pre_step(back_terms, unit, scale, row_groups, count, (sums[0], steps[2]))
    pre_grads = chips_gather(pre_grad)

    second_halves = weight_grad(
        second_grad_kernel, "second_grad", core_at, whole_cot, pays, [along], two_rows,
        row_width, (pre_grad,),
    )
    blocks = band_step(band_terms)
    first_halves = weight_grad(
        first_grad_kernel, "first_grad", core_at, active, pays, pre_grads, one_rows,
        row_width, (second_halves[1], blocks[0]),
    )
    block_output = join_blocks(images[0], chips_swap(blocks), chip_at)[None]
    second_grad = flat_grad(second_halves[0], to_core(second_halves[1]), grad_scale)
    first_grad = flat_grad(first_halves[0], to_core(first_halves[1]), grad_scale)
    return (block_output, first_grad, second_grad)


def solution(mesh):
    split = P("dp", "rows", None, None)
    return jax.shard_map(
        body,
        mesh=mesh,
        in_specs=(split, split, split, split, P(), P()),
        out_specs=(split, split, split),
        check_vma=False,
    )
```

```python
import functools
import math

import jax
import jax.numpy as jnp
import numpy as np
from jax import lax
from jax.experimental import pallas as pl
from jax.experimental.pallas import tpu as pltpu
from jax.sharding import PartitionSpec as P

GROUPS = 32
EPS = 1e-5
MIB = 1024 * 1024
F32 = jnp.float32
BF16 = jnp.bfloat16


def whole_block(x):
    zeros = (0,) * len(x.shape)
    return pl.BlockSpec(x.shape, lambda _: zeros, pipeline_mode=pl.Buffered(1))


def smem():
    return pl.BlockSpec(memory_space=pltpu.SMEM)


def unread(after):
    return [pl.BlockSpec(memory_space=pl.ANY)] * len(after)


def run(kernel, name, outs, scalars, arrays, after=(), scratch=(), held=8, flops=0):
    moved = sum(x.size * x.dtype.itemsize for x in list(arrays) + list(outs))
    return pl.pallas_call(
        kernel,
        grid=(1,),
        out_shape=list(outs),
        in_specs=[smem()] * len(scalars) + [whole_block(x) for x in arrays] + unread(after),
        out_specs=[whole_block(x) for x in outs],
        scratch_shapes=list(scratch),
        compiler_params=pltpu.CompilerParams(vmem_limit_bytes=held * MIB),
        cost_estimate=cost(flops, moved),
        name=name,
    )(*scalars, *arrays, *after)


def cost(flops, moved):
    return pl.CostEstimate(flops=int(flops), bytes_accessed=int(moved), transcendentals=0)


def group_sums(row, same_group):
    high = row.astype(BF16).astype(F32)
    rest = row - high
    middle = rest.astype(BF16).astype(F32)
    low = rest - middle
    at = lax.broadcasted_iota(jnp.int32, (16, row.shape[1]), 0)
    stacked = jnp.where(at == 0, high, jnp.where(at == 1, middle, jnp.where(at == 2, low, 0.0)))
    sums = jnp.dot(stacked.astype(BF16), same_group, preferred_element_type=F32)
    return jnp.sum(sums, axis=0, keepdims=True)


def normalized(values, same_group, count):
    center = group_sums(jnp.sum(values, axis=0, keepdims=True), same_group) / count
    moved = values - center
    spread = group_sums(jnp.sum(moved * moved, axis=0, keepdims=True), same_group) / count
    scale = 1.0 / jnp.sqrt(spread + EPS)
    return moved * scale, scale


def columns(values, flip):
    width = values.shape[1]
    at = lax.broadcasted_iota(jnp.int32, values.shape, 1)
    before = jnp.where(at == 0, 0.0, pltpu.roll(values, 1, axis=1))
    after = jnp.where(at == width - 1, 0.0, pltpu.roll(values, width - 1, axis=1))
    parts = [after, values, before] if flip else [before, values, after]
    return jnp.concatenate([part.astype(BF16) for part in parts], axis=2)


def conv_rows(taps, weight_ref, rows, flip):
    _, width, depth = taps.shape
    total = None
    for tap in range(3):
        window = taps[tap : tap + rows].reshape(rows * width, depth)
        term = jnp.dot(window, weight_ref[2 - tap if flip else tap], preferred_element_type=F32)
        total = term if total is None else total + term
    return total


def side_by_side(values):
    half = values.shape[0] // 2
    return jnp.concatenate([values[:half], values[half:]], axis=1)


def stacked_again(values):
    half = values.shape[1] // 2
    return jnp.concatenate([values[:, :half], values[:, half:]], axis=0)


def clear_edges(taps):
    rows = taps.shape[0]
    taps[0:1] = jnp.zeros((1,) + taps.shape[1:], taps.dtype)
    taps[rows - 1 : rows] = jnp.zeros((1,) + taps.shape[1:], taps.dtype)


def split_kernel(blocks, at_ref, *refs):
    outs = refs[-blocks:]
    width = outs[0].shape[-1]
    for away in range(blocks):
        for block in range(blocks):

            @pl.when(jnp.bitwise_xor(at_ref[0], away) == block)
            def _(away=away, block=block):
                for at, x_ref in enumerate(refs[:-blocks]):
                    outs[away][at] = x_ref[:, :, block * width : (block + 1) * width]


def split_blocks(arrays, blocks, chip):
    height, width, channels = arrays[0].shape
    shape = jax.ShapeDtypeStruct((len(arrays), height, width, channels // blocks), BF16)
    return run(
        functools.partial(split_kernel, blocks), "split_blocks", [shape] * blocks, [chip], arrays
    )


def pack_kernel(slots, at, *refs):
    out = refs[-1]
    width = refs[0].shape[-1]
    for slot in range(slots):
        half = slot % 2
        out[slot // 2, :, :, half * width : (half + 1) * width] = refs[slot][at]


def pack_slots(slots, at, after=()):
    _, band, width, depth = slots[0].shape
    out = jax.ShapeDtypeStruct((len(slots) // 2, band, width, 2 * depth), BF16)
    return run(
        functools.partial(pack_kernel, len(slots), at), "pack_slots", [out], [], slots, after
    )[0]


def assemble(whole, parts, places, pair, at_ref):
    for part, (away, who) in zip(parts, places):

        @pl.when(jnp.logical_or(who < 0, at_ref[1] == who))
        def _(part=part, away=away):
            band = part.shape[1]
            whole[pl.ds(jnp.bitwise_xor(at_ref[0], away) * band, band)] = part[pair]


def first_kernel(slots, places, count, at_ref, *refs):
    parts = refs[: len(places)]
    weight_ref, group_ref, basis_ref = refs[len(places) : len(places) + 3]
    whole, taps = refs[-2:]
    outs = refs[-2 - 2 * len(slots) : -2]
    rows, width, depth = outs[0].shape
    rank = basis_ref.shape[1] // 2
    cells = rows * width
    clear_edges(taps)
    held = None
    for at, slot in enumerate(slots):
        act_ref, sums_ref = outs[2 * at : 2 * at + 2]
        if slot // 2 != held:
            held = slot // 2
            assemble(whole, parts, places, held, at_ref)
        half = slot % 2
        values = whole[:, :, half * depth : (half + 1) * depth].astype(F32)
        unit, _ = normalized(values.reshape(cells, depth), group_ref[...], count)
        active = (unit / (1.0 + jnp.exp(-unit))).astype(BF16)
        act_ref[...] = active.reshape(act_ref.shape)
        taps[1 : rows + 1] = columns(active.astype(F32).reshape(act_ref.shape), False)
        total = conv_rows(taps, weight_ref, rows, False)
        along = jnp.dot(active, basis_ref[...], preferred_element_type=F32)
        along = along[:, :rank] + along[:, rank:]
        sums_ref[...] = jnp.concatenate([total, along], axis=1).astype(BF16)


def first_conv(parts, places, slots, weight, same_group, basis, row, rows, count, after=()):
    _, band, width, double = parts[0].shape
    depth = double // 2
    rank = basis.shape[1] // 2
    wide = weight.shape[2]
    cells = rows * width
    outs = [
        jax.ShapeDtypeStruct((rows, width, depth), BF16),
        jax.ShapeDtypeStruct((cells, wide + rank), BF16),
    ]
    made = run(
        functools.partial(first_kernel, slots, places, count),
        "first_conv",
        outs * len(slots),
        [row],
        [*parts, weight, same_group, basis],
        after,
        [
            pltpu.VMEM((rows, width, double), BF16),
            pltpu.VMEM((rows + 2, width, 3 * depth), BF16),
        ],
        24,
        18 * len(slots) * cells * depth * wide,
    )
    return [(made[2 * at], made[2 * at + 1]) for at in range(len(slots))]


def back_kernel(slots, parts_ref, weight_ref, *refs):
    whole, taps = refs[-2:]
    outs = refs[-2 - 2 * slots : -2]
    bands, _, band = parts_ref.shape[:3]
    rows, width, depth = outs[0].shape
    clear_edges(taps)
    for slot in reversed(range(slots)):
        cot_ref, sums_ref = outs[2 * slot : 2 * slot + 2]
        if slot % 2:
            for at in range(bands):
                whole[at * band : (at + 1) * band] = parts_ref[at, slot // 2]
        half = slot % 2
        values = whole[:, :, half * depth : (half + 1) * depth]
        cot_ref[...] = values
        taps[1 : rows + 1] = columns(values.astype(F32), True)
        sums_ref[...] = side_by_side(conv_rows(taps, weight_ref, rows, True)).astype(BF16)


def back_conv(parts, weight, after=()):
    bands, pairs, band, width, double = parts.shape
    rows = bands * band
    depth = double // 2
    wide = weight.shape[2]
    cells = rows * width
    slots = 2 * pairs
    outs = [
        jax.ShapeDtypeStruct((rows, width, depth), BF16),
        jax.ShapeDtypeStruct((cells // 2, 2 * wide), BF16),
    ]
    made = run(
        functools.partial(back_kernel, slots),
        "back_conv",
        outs * slots,
        [],
        [parts, weight],
        after,
        [
            pltpu.VMEM((rows, width, double), BF16),
            pltpu.VMEM((rows + 2, width, 3 * depth), BF16),
        ],
        24,
        18 * slots * cells * depth * wide,
    )
    return [(made[2 * at], made[2 * at + 1]) for at in range(slots)]


def hidden_kernel(terms, count, *refs):
    group_ref, basis_ref = refs[terms : terms + 2]
    pay_ref, unit_ref, scale_ref, along_ref = refs[-4:]
    wide = unit_ref.shape[1]
    rank = basis_ref.shape[1] // 2
    total = refs[0][...].astype(F32)
    for term in refs[1:terms]:
        total = total + term[...].astype(F32)
    unit, scale = normalized(total[:, :wide], group_ref[...], count)
    unit_ref[...] = unit
    scale_ref[...] = scale
    hidden = (unit / (1.0 + jnp.exp(-unit))).astype(BF16)
    pay_ref[...] = jnp.concatenate([hidden.astype(F32), total[:, wide:]], axis=1).astype(BF16)
    along = jnp.dot(hidden, basis_ref[...], preferred_element_type=F32)
    along_ref[...] = side_by_side(along[:, :rank] + along[:, rank:]).astype(BF16)


def hidden_step(terms, same_group, basis, count, after=()):
    cells, both = terms[0].shape
    wide = same_group.shape[0]
    return run(
        functools.partial(hidden_kernel, len(terms), count),
        "hidden_step",
        [
            jax.ShapeDtypeStruct((cells, both), BF16),
            jax.ShapeDtypeStruct((cells, wide), F32),
            jax.ShapeDtypeStruct((1, wide), F32),
            jax.ShapeDtypeStruct((cells // 2, basis.shape[1]), BF16),
        ],
        [],
        [*terms, same_group, basis],
        after,
        held=16,
        flops=40 * cells * wide,
    )


def second_kernel(slots, bands, at_ref, *refs):
    pays = refs[:slots]
    weight_ref, along_ref, other_ref = refs[slots : slots + 3]
    later_ref, whole, taps = refs[-3:]
    outs = refs[-3 - bands : -3]
    later_ref[...] = (along_ref[...].astype(F32) + other_ref[...].astype(F32)).astype(BF16)
    band, width, double = outs[0].shape[1:]
    rows = whole.shape[0]
    depth = taps.shape[2] // 3
    wide = double // 2
    clear_edges(taps)
    for slot in range(slots):
        hidden = pays[slot][:, :depth].astype(F32).reshape(rows, width, depth)
        taps[1 : rows + 1] = columns(hidden, False)
        whole[...] = conv_rows(taps, weight_ref, rows, False).reshape(rows, width, wide)
        lanes = slice(slot % 2 * wide, (slot % 2 + 1) * wide)
        for away in range(bands):
            start = jnp.bitwise_xor(at_ref[0], away) * band
            outs[away][slot // 2, :, :, lanes] = whole[pl.ds(start, band)].astype(BF16)


def second_conv(pays, weight, alongs, row, rows, bands, after=()):
    slots = len(pays)
    cells, _ = pays[0].shape
    width = cells // rows
    depth = weight.shape[1] // 3
    wide = weight.shape[2]
    out = jax.ShapeDtypeStruct((slots // 2, rows // bands, width, 2 * wide), BF16)
    return run(
        functools.partial(second_kernel, slots, bands),
        "second_conv",
        [out] * bands + alongs[:1],
        [row],
        [*pays, weight, *alongs],
        after,
        [
            pltpu.VMEM((rows, width, wide), F32),
            pltpu.VMEM((rows + 2, width, 3 * depth), BF16),
        ],
        24,
        18 * slots * cells * depth * wide,
    )


def band_kernel(terms, slots, *refs):
    outs = refs[-slots:]
    wide = outs[0].shape[-1]
    total = refs[0][...].astype(F32)
    for term in refs[1:terms]:
        total = total + term[...].astype(F32)
    for slot, out in enumerate(outs):
        lanes = slice(slot % 2 * wide, (slot % 2 + 1) * wide)
        out[...] = total[slot // 2, :, :, lanes].astype(BF16)


def band_step(terms, after=()):
    pairs, band, width, double = terms[0].shape
    out = jax.ShapeDtypeStruct((band, width, double // 2), BF16)
    return run(
        functools.partial(band_kernel, len(terms), 2 * pairs),
        "band_step",
        [out] * (2 * pairs),
        [],
        terms,
        after,
    )


def join_kernel(blocks, at_ref, x_ref, *refs):
    out = refs[-1]
    width = x_ref.shape[-1] // blocks
    for away in range(blocks):
        for block in range(blocks):

            @pl.when(jnp.bitwise_xor(at_ref[0], away) == block)
            def _(away=away, block=block):
                lanes = slice(block * width, (block + 1) * width)
                added = x_ref[:, :, lanes].astype(F32) + refs[away][...].astype(F32)
                out[:, :, lanes] = added.astype(BF16)


def join_blocks(x, parts, chip, after=()):
    return run(
        functools.partial(join_kernel, len(parts)),
        "join_blocks",
        [x],
        [chip],
        [x, *parts],
        after,
    )[0]


def pre_kernel(terms, count, *refs):
    unit_ref, scale_ref, group_ref, along_ref, other_ref = refs[terms : terms + 5]
    out_ref, later_ref = refs[-2:]
    later_ref[...] = (along_ref[...].astype(F32) + other_ref[...].astype(F32)).astype(BF16)
    total = refs[0][...].astype(F32)
    for term in refs[1:terms]:
        total = total + term[...].astype(F32)
    unit = unit_ref[...]
    gate = 1.0 / (1.0 + jnp.exp(-unit))
    grad = stacked_again(total) * (gate * (1.0 + unit * (1.0 - gate)))
    mean = group_sums(jnp.sum(grad, axis=0, keepdims=True), group_ref[...]) / count
    along = group_sums(jnp.sum(grad * unit, axis=0, keepdims=True), group_ref[...]) / count
    out_ref[...] = side_by_side(scale_ref[...] * (grad - mean - unit * along)).astype(BF16)


def pre_step(terms, unit, scale, same_group, alongs, count, after=()):
    cells, wide = unit.shape
    return run(
        functools.partial(pre_kernel, len(terms), count),
        "pre_step",
        [jax.ShapeDtypeStruct((cells // 2, 2 * wide), BF16), alongs[0]],
        [],
        [*terms, unit, scale, same_group, *alongs],
        after,
        held=16,
        flops=40 * cells * wide,
    )


def project(values, along, basis):
    both = jnp.concatenate([along, along], axis=1)
    return values - jnp.dot(both, basis, preferred_element_type=F32)


def grad_body(core_ref, left, left_t, taps, keep_ref, send_ref, width, flip):
    half = left.shape[1] // 2
    span = left.shape[0]
    wide = taps.shape[1] // 3
    turned = left[...].T

    @pl.when(core_ref[0] == 0)
    def _():
        left_t[...] = turned

    @pl.when(core_ref[0] != 0)
    def _():
        left_t[:half] = turned[half:]
        left_t[half:] = turned[:half]

    for tap in range(3):
        window = taps[tap * width : tap * width + span]
        result = jnp.dot(left_t[...], window, preferred_element_type=F32)
        first = 3 * (2 - tap if flip else tap)
        for q in range(3):
            lanes = slice(q * wide, (q + 1) * wide)
            keep_ref[first + q] = result[:half, lanes]
            send_ref[first + q] = result[half:, lanes].astype(BF16)


def fill_taps(taps, slot, rows, width, value):
    start = (slot * (rows + 1) + 1) * width
    taps[start : start + rows * width] = value.reshape(rows * width, value.shape[2])


def clear_gaps(left, taps, slots, rows, width):
    gap = rows + 1
    for slot in range(slots + 1):
        begin = slot * gap * width
        end = taps.shape[0] if slot == slots else begin + width
        taps[begin:end] = jnp.zeros((end - begin, taps.shape[1]), taps.dtype)
    for slot in range(slots):
        begin = (slot * gap + rows) * width
        end = left.shape[0] if slot == slots - 1 else begin + width
        left[begin:end] = jnp.zeros((end - begin, left.shape[1]), left.dtype)


def first_grad_kernel(slots, core_ref, *refs):
    acts, pays, grads = (refs[at * slots : (at + 1) * slots] for at in range(3))
    basis_ref = refs[3 * slots]
    keep_ref, send_ref, left, left_t, taps = refs[-5:]
    rows, width, depth = acts[0].shape
    cells = rows * width
    rank = basis_ref.shape[0] // 2
    wide = taps.shape[1] // 3
    clear_gaps(left, taps, slots, rows, width)
    for slot in range(slots):
        values = acts[slot][...].reshape(cells, depth).astype(F32)
        along = pays[slot][:, wide : wide + rank]
        begin = slot * (rows + 1) * width
        left[begin : begin + cells] = project(values, along, basis_ref[...]).astype(BF16)
        right = stacked_again(grads[slot][...].astype(F32)).reshape(rows, width, wide)
        fill_taps(taps, slot, rows, width, columns(right, True))
    grad_body(core_ref, left, left_t, taps, keep_ref, send_ref, width, True)


def second_grad_kernel(slots, core_ref, *refs):
    cots, pays = (refs[at * slots : (at + 1) * slots] for at in range(2))
    alongs_ref, basis_ref = refs[2 * slots : 2 * slots + 2]
    keep_ref, send_ref, left, left_t, taps = refs[-5:]
    rows, width, depth = cots[0].shape
    cells = rows * width
    rank = basis_ref.shape[0] // 2
    wide = taps.shape[1] // 3
    clear_gaps(left, taps, slots, rows, width)
    for slot in range(slots):
        begin = slot * (rows + 1) * width
        left[begin : begin + cells] = cots[slot][...].reshape(cells, depth)
        packed = alongs_ref[slot]
        along = jnp.concatenate([packed[:, :rank], packed[:, rank:]], axis=0)
        values = pays[slot][:, :wide].astype(F32)
        right = project(values, along, basis_ref[...]).astype(BF16).astype(F32)
        fill_taps(taps, slot, rows, width, columns(right.reshape(rows, width, wide), False))
    grad_body(core_ref, left, left_t, taps, keep_ref, send_ref, width, False)


def weight_grad(kernel, name, core, lefts, firsts, seconds, basis, wide, after=()):
    slots = len(firsts)
    rows, width, depth = lefts[0].shape
    used = slots * (rows + 1) * width
    span = -(-used // 128) * 128
    half = depth // 2
    tap_rows = 2 * width + span
    return run(
        functools.partial(kernel, slots),
        name,
        [
            jax.ShapeDtypeStruct((9, half, wide), F32),
            jax.ShapeDtypeStruct((9, half, wide), BF16),
        ],
        [core],
        [*lefts, *firsts, *seconds, basis],
        after,
        [
            pltpu.VMEM((span, depth), BF16),
            pltpu.VMEM((depth, span), BF16),
            pltpu.VMEM((tap_rows, 3 * wide), BF16),
        ],
        36,
        18 * slots * rows * width * depth * wide,
    )


def halves_kernel(turn, core_ref, own_ref, other_ref, *refs):
    outs = refs[-2:] if turn else refs[-1:]
    half = own_ref.shape[1]

    @pl.when(core_ref[0] == 0)
    def _():
        outs[0][:, :half] = own_ref[...]
        outs[0][:, half:] = other_ref[...]

    @pl.when(core_ref[0] != 0)
    def _():
        outs[0][:, :half] = other_ref[...]
        outs[0][:, half:] = own_ref[...]

    if turn:
        for tap in range(9):
            outs[1][tap] = outs[0][tap].T


def join_halves(core, own, other, turn, after=()):
    _, half, wide = own.shape
    outs = [jax.ShapeDtypeStruct((9, 2 * half, wide), BF16)]
    if turn:
        outs.append(jax.ShapeDtypeStruct((9, wide, 2 * half), BF16))
    return run(
        functools.partial(halves_kernel, turn), "join_halves", outs, [core], [own, other], after,
        held=16,
    )


def basis_kernel(blocks, at_ref, basis_ref, *refs):
    rows_ref, columns_ref = refs[-2:]
    rank, channels = basis_ref.shape
    width = channels // blocks
    for block in range(blocks):

        @pl.when(at_ref[0] == block)
        def _(block=block):
            values = basis_ref[:, block * width : (block + 1) * width]
            high = values.astype(BF16).astype(F32)
            both = jnp.concatenate([high, values - high], axis=0)
            rows_ref[...] = both.astype(BF16)
            columns_ref[...] = both.T.astype(BF16)


def basis_parts(at, basis, blocks, after=()):
    rank, channels = basis.shape
    width = channels // blocks
    return run(
        functools.partial(basis_kernel, blocks),
        "basis_parts",
        [
            jax.ShapeDtypeStruct((2 * rank, width), BF16),
            jax.ShapeDtypeStruct((width, 2 * rank), BF16),
        ],
        [at],
        [basis],
        after,
    )


def flat_kernel(scale, keep_ref, got_ref, *refs):
    held = refs[-2 * (keep_ref.shape[2] // 128) - 2 :]
    out_ref = refs[-len(held) - 1]
    taps, half, wide = keep_ref.shape
    whole = wide // 128
    step = 2 * whole + 1
    count = half // 2
    zeros = jnp.zeros((half, 64), F32)
    for tap in range(taps):
        total = (keep_ref[tap] + got_ref[tap].astype(F32)) * scale
        for at in range(whole):
            held[at][...] = total[:, 128 * at : 128 * (at + 1)]
            held[whole + 2 + at][...] = total[:, 128 * at + 64 : 128 * (at + 1) + 64]
        held[whole][...] = jnp.concatenate([total[:, 128 * whole :], zeros], axis=1)
        held[whole + 1][...] = jnp.concatenate([zeros, total[:, :64]], axis=1)
        even, odd = pl.ds(0, count, stride=2), pl.ds(1, count, stride=2)
        rows = [held[at][even, :] for at in range(whole)]
        rows.append(held[whole][even, :] + held[whole + 1][odd, :])
        rows += [held[whole + 2 + at][odd, :] for at in range(whole)]
        for at, row in enumerate(rows):
            out_ref[pl.ds(tap * count * step + at, count, stride=step), :] = row


def flat_grad(keep, got, scale, after=()):
    taps, half, wide = keep.shape
    if wide % 128 != 64 or half % 2:
        return ((keep + got.astype(F32)) * scale).reshape(1, 1, taps, half * wide)
    return run(
        functools.partial(flat_kernel, scale),
        "flat_grad",
        [jax.ShapeDtypeStruct((taps * half * wide // 128, 128), F32)],
        [],
        [keep, got],
        after,
        scratch=[pltpu.VMEM((half, 128), F32)] * (2 * (wide // 128) + 2),
        held=16,
    )[0].reshape(1, 1, taps, half * wide)


def same_groups(width, size):
    at = np.arange(width) // size
    return jnp.asarray((at[:, None] == at[None, :]).astype(np.float32), BF16)


def body(images, cotangent, first_weight, second_weight, first_basis, second_basis):
    n_dp = lax.axis_size("dp")
    n_rows = lax.axis_size("rows")
    chips = n_dp // 2
    _, band, width, channels = images.shape
    rows = band * n_rows
    dp_width = channels // n_dp
    chip_width = channels // chips
    row_width = channels // n_rows
    group = channels // GROUPS
    count = float(rows * width * group)
    grad_scale = 1.0 / math.sqrt(n_dp * images.shape[0] * rows * width)

    at_dp = lax.axis_index("dp")
    at_row = lax.axis_index("rows")
    chip = (at_dp // 2).astype(jnp.int32)
    core = (at_dp % 2).astype(jnp.int32)
    row = at_row.astype(jnp.int32)
    chip_at, core_at = chip[None], core[None]
    row_at = jnp.stack([row, (row + 1) // 2 % 2])

    def to_core(x):
        return lax.ppermute(x, "dp", [(i, i ^ 1) for i in range(n_dp)])

    def to_chip(x, away):
        return lax.ppermute(x, "dp", [(i, i ^ (2 * away)) for i in range(n_dp)])

    def to_row(x, away):
        return lax.ppermute(x, "rows", [(i, i ^ away) for i in range(n_rows)])

    def chips_gather(x):
        return [x] + [to_chip(x, away) for away in range(1, chips)]

    def rows_gather(x):
        if n_rows != 4:
            return [x] + [to_row(x, away) for away in range(1, n_rows)], [
                (away, -1) for away in range(n_rows)
            ]
        second = to_row(x, 2)
        middle = lax.ppermute(x, "rows", [(1, 2), (2, 1)])
        first = to_row(x, 1)
        passed = lax.ppermute(second, "rows", [(2, 3), (1, 0)])
        return [x, first, second, middle, passed], [(0, -1), (1, -1), (2, -1), (3, 1), (3, 0)]

    def chips_swap(parts):
        return [parts[0]] + [to_chip(parts[away], away) for away in range(1, chips)]

    def rows_swap(parts):
        far = [to_row(parts[away], away) for away in range(n_rows - 1, 0, -1)]
        return parts[:1] + far[::-1]

    chip_groups = same_groups(chip_width, group)
    row_groups = same_groups(row_width, group)

    slots = chips_swap(split_blocks([images[0], cotangent[0]], chips, chip_at))
    image_parts, places = rows_gather(pack_slots(slots, 0))

    first_weight, second_weight, _ = lax.optimization_barrier(
        (first_weight, second_weight, slots[1])
    )
    own_first = first_weight.reshape(9, dp_width, row_width)
    own_second = second_weight.reshape(9, dp_width, row_width)
    (first_full,) = join_halves(core_at, own_first, to_core(own_first), False)
    second_full, second_turned = join_halves(core_at, own_second, to_core(own_second), True)
    weight_one = first_full.reshape(3, 3 * chip_width, row_width)
    weight_back = second_full.reshape(3, 3 * chip_width, row_width)
    weight_two = second_turned.reshape(3, 3 * row_width, chip_width)
    one_rows, one_columns = basis_parts(chip_at, first_basis, chips)
    two_rows, two_columns = basis_parts(row_at, second_basis, n_rows)

    cot_pack = pack_slots(slots, 1, (*image_parts[1:], first_full, second_full, one_rows, two_rows))
    cot_parts = lax.all_gather(cot_pack, "rows")

    sent = list(range(chips - 1, 0, -1))
    made = first_conv(
        image_parts, places, sent, weight_one, chip_groups, one_columns, row_at, rows, count,
        (cot_pack,),
    )
    own_made = first_conv(
        image_parts, places, [0], weight_one, chip_groups, one_columns, row_at, rows, count,
        made[0][1:],
    )
    made = own_made + made[::-1]
    active = [pair[0] for pair in made]
    first_terms = chips_swap([pair[1] for pair in made])

    pay, unit, scale, along = hidden_step(first_terms, row_groups, two_columns, count)
    pays = chips_gather(pay)

    back = back_conv(cot_parts, weight_back, (pay,))
    whole_cot = [pair[0] for pair in back]
    back_terms = chips_swap([pair[1] for pair in back])

    *sums, along = second_conv(
        pays, weight_two, [along, to_row(along, 1)], row_at, rows, n_rows, (back[0][1],)
    )
    band_terms = rows_swap(sums)

    pre_grad, along = pre_step(
        back_terms, unit, scale, row_groups, [along, to_row(along, 2)], count, (sums[0], band_terms[-1])
    )
    pre_grads = chips_gather(pre_grad)
    away = 4
    while away < n_rows:
        along = (along.astype(F32) + to_row(along, away).astype(F32)).astype(BF16)
        away *= 2
    along = along[None]
    away = 1
    while away < chips:
        along = jnp.concatenate([along, to_chip(along, away)])
        away *= 2

    second_halves = weight_grad(
        second_grad_kernel, "second_grad", core_at, whole_cot, pays, [along], two_rows,
        row_width, (pre_grad,),
    )
    blocks = band_step(band_terms, second_halves[1:])
    first_halves = weight_grad(
        first_grad_kernel, "first_grad", core_at, active, pays, pre_grads, one_rows,
        row_width, (second_halves[1], blocks[0]),
    )
    second_grad = flat_grad(second_halves[0], to_core(second_halves[1]), grad_scale)
    block_output = join_blocks(images[0], chips_swap(blocks), chip_at, (second_grad,))[None]
    first_grad = flat_grad(
        first_halves[0], to_core(first_halves[1]), grad_scale, (block_output,)
    )
    return (block_output, first_grad, second_grad)


def solution(mesh):
    split = P("dp", "rows", None, None)
    return jax.shard_map(
        body,
        mesh=mesh,
        in_specs=(split, split, split, split, P(), P()),
        out_specs=(split, split, split),
        check_vma=False,
    )
```

```python
import functools
import math

import jax
import jax.numpy as jnp
import numpy as np
from jax import lax
from jax.experimental import pallas as pl
from jax.experimental.pallas import tpu as pltpu
from jax.sharding import PartitionSpec as P

GROUPS = 32
EPS = 1e-5
MIB = 1024 * 1024
F32 = jnp.float32
BF16 = jnp.bfloat16


def whole_block(x):
    zeros = (0,) * len(x.shape)
    return pl.BlockSpec(x.shape, lambda _: zeros, pipeline_mode=pl.Buffered(1))


def smem():
    return pl.BlockSpec(memory_space=pltpu.SMEM)


def unread(after):
    return [pl.BlockSpec(memory_space=pl.ANY)] * len(after)


def run(kernel, name, outs, scalars, arrays, after=(), scratch=(), held=8, flops=0, fetch=False):
    moved = sum(x.size * x.dtype.itemsize for x in list(arrays) + list(outs))
    held_there = pl.BlockSpec(memory_space=pltpu.VMEM)
    return pl.pallas_call(
        kernel,
        grid=(1,) if fetch else (),
        out_shape=list(outs),
        in_specs=[smem()] * len(scalars)
        + [whole_block(x) if fetch else held_there for x in arrays]
        + unread(after),
        out_specs=[held_there] * len(outs),
        scratch_shapes=list(scratch),
        compiler_params=pltpu.CompilerParams(vmem_limit_bytes=held * MIB),
        cost_estimate=cost(flops, moved),
        name=name,
    )(*scalars, *arrays, *after)


def cost(flops, moved):
    return pl.CostEstimate(flops=int(flops), bytes_accessed=int(moved), transcendentals=0)


def group_sums(row, same_group):
    high = row.astype(BF16).astype(F32)
    rest = row - high
    middle = rest.astype(BF16).astype(F32)
    low = rest - middle
    at = lax.broadcasted_iota(jnp.int32, (16, row.shape[1]), 0)
    stacked = jnp.where(at == 0, high, jnp.where(at == 1, middle, jnp.where(at == 2, low, 0.0)))
    sums = jnp.dot(stacked.astype(BF16), same_group, preferred_element_type=F32)
    return jnp.sum(sums, axis=0, keepdims=True)


def normalized(values, same_group, count):
    center = group_sums(jnp.sum(values, axis=0, keepdims=True), same_group) / count
    moved = values - center
    spread = group_sums(jnp.sum(moved * moved, axis=0, keepdims=True), same_group) / count
    scale = 1.0 / jnp.sqrt(spread + EPS)
    return moved * scale, scale


def silu(unit):
    half = 0.5 * unit
    return half + half * jnp.tanh(half)


def add_into(out_ref, one_ref, other_ref):
    out_ref[...] = (one_ref[...].astype(F32) + other_ref[...].astype(F32)).astype(BF16)


def columns(values, flip):
    width = values.shape[1]
    at = lax.broadcasted_iota(jnp.int32, values.shape, 1)
    before = jnp.where(at == 0, 0.0, pltpu.roll(values, 1, axis=1))
    after = jnp.where(at == width - 1, 0.0, pltpu.roll(values, width - 1, axis=1))
    parts = [after, values, before] if flip else [before, values, after]
    return jnp.concatenate([part.astype(BF16) for part in parts], axis=2)


def conv_rows(taps, weight_ref, rows, flip):
    _, width, depth = taps.shape
    total = None
    for tap in range(3):
        window = taps[tap : tap + rows].reshape(rows * width, depth)
        term = jnp.dot(window, weight_ref[2 - tap if flip else tap], preferred_element_type=F32)
        total = term if total is None else total + term
    return total


def side_by_side(values):
    half = values.shape[0] // 2
    return jnp.concatenate([values[:half], values[half:]], axis=1)


def stacked_again(values):
    half = values.shape[1] // 2
    return jnp.concatenate([values[:, :half], values[:, half:]], axis=0)


def clear_edges(taps):
    rows = taps.shape[0]
    taps[0:1] = jnp.zeros((1,) + taps.shape[1:], taps.dtype)
    taps[rows - 1 : rows] = jnp.zeros((1,) + taps.shape[1:], taps.dtype)


def split_kernel(blocks, at_ref, *refs):
    outs = refs[-blocks:]
    width = outs[0].shape[-1]
    for away in range(blocks):
        for block in range(blocks):

            @pl.when(jnp.bitwise_xor(at_ref[0], away) == block)
            def _(away=away, block=block):
                for at, x_ref in enumerate(refs[:-blocks]):
                    outs[away][at] = x_ref[:, :, block * width : (block + 1) * width]


def split_blocks(arrays, blocks, chip):
    height, width, channels = arrays[0].shape
    shape = jax.ShapeDtypeStruct((len(arrays), height, width, channels // blocks), BF16)
    return run(
        functools.partial(split_kernel, blocks), "split_blocks", [shape] * blocks, [chip], arrays,
        fetch=True,
    )


def pack_kernel(slots, at, *refs):
    out = refs[-1]
    width = refs[0].shape[-1]
    for slot in range(slots):
        half = slot % 2
        out[slot // 2, :, :, half * width : (half + 1) * width] = refs[slot][at]


def pack_slots(slots, at, after=()):
    _, band, width, depth = slots[0].shape
    out = jax.ShapeDtypeStruct((len(slots) // 2, band, width, 2 * depth), BF16)
    return run(
        functools.partial(pack_kernel, len(slots), at), "pack_slots", [out], [], slots, after
    )[0]


def assemble(whole, parts, places, pair, at_ref):
    for part, (away, who) in zip(parts, places):

        @pl.when(jnp.logical_or(who < 0, at_ref[1] == who))
        def _(part=part, away=away):
            band = part.shape[1]
            whole[pl.ds(jnp.bitwise_xor(at_ref[0], away) * band, band)] = part[pair]


def first_kernel(slots, places, count, at_ref, *refs):
    parts = refs[: len(places)]
    weight_ref, group_ref, basis_ref = refs[len(places) : len(places) + 3]
    whole, taps = refs[-2:]
    outs = refs[-2 - 2 * len(slots) : -2]
    rows, width, depth = outs[0].shape
    rank = basis_ref.shape[1] // 2
    cells = rows * width
    clear_edges(taps)
    held = None
    for at, slot in enumerate(slots):
        act_ref, sums_ref = outs[2 * at : 2 * at + 2]
        if slot // 2 != held:
            held = slot // 2
            assemble(whole, parts, places, held, at_ref)
        half = slot % 2
        values = whole[:, :, half * depth : (half + 1) * depth].astype(F32)
        unit, _ = normalized(values.reshape(cells, depth), group_ref[...], count)
        active = silu(unit).astype(BF16)
        act_ref[...] = active.reshape(act_ref.shape)
        taps[1 : rows + 1] = columns(active.astype(F32).reshape(act_ref.shape), False)
        total = conv_rows(taps, weight_ref, rows, False)
        along = jnp.dot(active, basis_ref[...], preferred_element_type=F32)
        along = along[:, :rank] + along[:, rank:]
        sums_ref[...] = jnp.concatenate([total, along], axis=1).astype(BF16)


def first_conv(parts, places, slots, weight, same_group, basis, row, rows, count, after=()):
    _, band, width, double = parts[0].shape
    depth = double // 2
    rank = basis.shape[1] // 2
    wide = weight.shape[2]
    cells = rows * width
    outs = [
        jax.ShapeDtypeStruct((rows, width, depth), BF16),
        jax.ShapeDtypeStruct((cells, wide + rank), BF16),
    ]
    made = run(
        functools.partial(first_kernel, slots, places, count),
        "first_conv",
        outs * len(slots),
        [row],
        [*parts, weight, same_group, basis],
        after,
        [
            pltpu.VMEM((rows, width, double), BF16),
            pltpu.VMEM((rows + 2, width, 3 * depth), BF16),
        ],
        14,
        18 * len(slots) * cells * depth * wide,
    )
    return [(made[2 * at], made[2 * at + 1]) for at in range(len(slots))]


def back_kernel(slots, parts_ref, weight_ref, along_ref, other_ref, *refs):
    later_ref, whole, taps = refs[-3:]
    outs = refs[-3 - 2 * slots : -3]
    add_into(later_ref, along_ref, other_ref)
    bands, _, band = parts_ref.shape[:3]
    rows, width, depth = outs[0].shape
    clear_edges(taps)
    for slot in reversed(range(slots)):
        cot_ref, sums_ref = outs[2 * slot : 2 * slot + 2]
        if slot % 2:
            for at in range(bands):
                whole[at * band : (at + 1) * band] = parts_ref[at, slot // 2]
        half = slot % 2
        values = whole[:, :, half * depth : (half + 1) * depth]
        cot_ref[...] = values
        taps[1 : rows + 1] = columns(values.astype(F32), True)
        sums_ref[...] = side_by_side(conv_rows(taps, weight_ref, rows, True)).astype(BF16)


def back_conv(parts, weight, alongs, after=()):
    bands, pairs, band, width, double = parts.shape
    rows = bands * band
    depth = double // 2
    wide = weight.shape[2]
    cells = rows * width
    slots = 2 * pairs
    outs = [
        jax.ShapeDtypeStruct((rows, width, depth), BF16),
        jax.ShapeDtypeStruct((cells // 2, 2 * wide), BF16),
    ]
    made = run(
        functools.partial(back_kernel, slots),
        "back_conv",
        outs * slots + alongs[:1],
        [],
        [parts, weight, *alongs],
        after,
        [
            pltpu.VMEM((rows, width, double), BF16),
            pltpu.VMEM((rows + 2, width, 3 * depth), BF16),
        ],
        14,
        18 * slots * cells * depth * wide,
    )
    return [(made[2 * at], made[2 * at + 1]) for at in range(slots)], made[-1]


def hidden_kernel(terms, count, *refs):
    group_ref, basis_ref = refs[terms : terms + 2]
    pay_ref, unit_ref, scale_ref, along_ref = refs[-4:]
    wide = unit_ref.shape[1]
    rank = basis_ref.shape[1] // 2
    total = refs[0][...].astype(F32)
    for term in refs[1:terms]:
        total = total + term[...].astype(F32)
    unit, scale = normalized(total[:, :wide], group_ref[...], count)
    unit_ref[...] = unit
    scale_ref[...] = scale
    hidden = silu(unit).astype(BF16)
    pay_ref[...] = jnp.concatenate([hidden.astype(F32), total[:, wide:]], axis=1).astype(BF16)
    along = jnp.dot(hidden, basis_ref[...], preferred_element_type=F32)
    along_ref[...] = side_by_side(along[:, :rank] + along[:, rank:]).astype(BF16)


def hidden_step(terms, same_group, basis, count, after=()):
    cells, both = terms[0].shape
    wide = same_group.shape[0]
    return run(
        functools.partial(hidden_kernel, len(terms), count),
        "hidden_step",
        [
            jax.ShapeDtypeStruct((cells, both), BF16),
            jax.ShapeDtypeStruct((cells, wide), F32),
            jax.ShapeDtypeStruct((1, wide), F32),
            jax.ShapeDtypeStruct((cells // 2, basis.shape[1]), BF16),
        ],
        [],
        [*terms, same_group, basis],
        after,
        held=12,
        flops=40 * cells * wide,
    )


def second_kernel(slots, bands, at_ref, *refs):
    pays = refs[:slots]
    weight_ref, along_ref, other_ref = refs[slots : slots + 3]
    later_ref, whole, taps = refs[-3:]
    outs = refs[-3 - bands : -3]
    add_into(later_ref, along_ref, other_ref)
    band, width, double = outs[0].shape[1:]
    rows = whole.shape[0]
    depth = taps.shape[2] // 3
    wide = double // 2
    clear_edges(taps)
    for slot in range(slots):
        hidden = pays[slot][:, :depth].astype(F32).reshape(rows, width, depth)
        taps[1 : rows + 1] = columns(hidden, False)
        whole[...] = conv_rows(taps, weight_ref, rows, False).reshape(rows, width, wide)
        lanes = slice(slot % 2 * wide, (slot % 2 + 1) * wide)
        for away in range(bands):
            start = jnp.bitwise_xor(at_ref[0], away) * band
            outs[away][slot // 2, :, :, lanes] = whole[pl.ds(start, band)].astype(BF16)


def second_conv(pays, weight, alongs, row, rows, bands, after=()):
    slots = len(pays)
    cells, _ = pays[0].shape
    width = cells // rows
    depth = weight.shape[1] // 3
    wide = weight.shape[2]
    out = jax.ShapeDtypeStruct((slots // 2, rows // bands, width, 2 * wide), BF16)
    return run(
        functools.partial(second_kernel, slots, bands),
        "second_conv",
        [out] * bands + alongs[:1],
        [row],
        [*pays, weight, *alongs],
        after,
        [
            pltpu.VMEM((rows, width, wide), F32),
            pltpu.VMEM((rows + 2, width, 3 * depth), BF16),
        ],
        14,
        18 * slots * cells * depth * wide,
    )


def band_kernel(terms, slots, *refs):
    outs = refs[-slots:]
    wide = outs[0].shape[-1]
    total = refs[0][...].astype(F32)
    for term in refs[1:terms]:
        total = total + term[...].astype(F32)
    for slot, out in enumerate(outs):
        lanes = slice(slot % 2 * wide, (slot % 2 + 1) * wide)
        out[...] = total[slot // 2, :, :, lanes].astype(BF16)


def band_step(terms, after=()):
    pairs, band, width, double = terms[0].shape
    out = jax.ShapeDtypeStruct((band, width, double // 2), BF16)
    return run(
        functools.partial(band_kernel, len(terms), 2 * pairs),
        "band_step",
        [out] * (2 * pairs),
        [],
        terms,
        after,
    )


def join_kernel(blocks, at_ref, x_ref, *refs):
    out = refs[-1]
    width = x_ref.shape[-1] // blocks
    for away in range(blocks):
        for block in range(blocks):

            @pl.when(jnp.bitwise_xor(at_ref[0], away) == block)
            def _(away=away, block=block):
                lanes = slice(block * width, (block + 1) * width)
                added = x_ref[:, :, lanes].astype(F32) + refs[away][...].astype(F32)
                out[:, :, lanes] = added.astype(BF16)


def join_blocks(x, parts, chip, after=()):
    return run(
        functools.partial(join_kernel, len(parts)),
        "join_blocks",
        [x],
        [chip],
        [x, *parts],
        after,
    )[0]


def pre_kernel(terms, count, *refs):
    unit_ref, scale_ref, group_ref, along_ref, other_ref = refs[terms : terms + 5]
    out_ref, later_ref = refs[-2:]
    later_ref[0] = along_ref[...]
    later_ref[1] = other_ref[...]
    total = refs[0][...].astype(F32)
    for term in refs[1:terms]:
        total = total + term[...].astype(F32)
    unit = unit_ref[...]
    gate = 0.5 + 0.5 * jnp.tanh(0.5 * unit)
    grad = stacked_again(total) * (gate * (1.0 + unit * (1.0 - gate)))
    mean = group_sums(jnp.sum(grad, axis=0, keepdims=True), group_ref[...]) / count
    along = group_sums(jnp.sum(grad * unit, axis=0, keepdims=True), group_ref[...]) / count
    out_ref[...] = side_by_side(scale_ref[...] * (grad - mean - unit * along)).astype(BF16)


def pre_step(terms, unit, scale, same_group, alongs, count, after=()):
    cells, wide = unit.shape
    stacked = jax.ShapeDtypeStruct((2, *alongs[0].shape), BF16)
    return run(
        functools.partial(pre_kernel, len(terms), count),
        "pre_step",
        [jax.ShapeDtypeStruct((cells // 2, 2 * wide), BF16), stacked],
        [],
        [*terms, unit, scale, same_group, *alongs],
        after,
        held=12,
        flops=40 * cells * wide,
    )


def project(values, along, basis):
    both = jnp.concatenate([along, along], axis=1)
    return values - jnp.dot(both, basis, preferred_element_type=F32)


def grad_body(core_ref, left, left_t, taps, keep_ref, send_ref, width, flip):
    half = left.shape[1] // 2
    span = left.shape[0]
    wide = taps.shape[1] // 3
    turned = left[...].T

    @pl.when(core_ref[0] == 0)
    def _():
        left_t[...] = turned

    @pl.when(core_ref[0] != 0)
    def _():
        left_t[:half] = turned[half:]
        left_t[half:] = turned[:half]

    for tap in range(3):
        window = taps[tap * width : tap * width + span]
        result = jnp.dot(left_t[...], window, preferred_element_type=F32)
        first = 3 * (2 - tap if flip else tap)
        for q in range(3):
            lanes = slice(q * wide, (q + 1) * wide)
            keep_ref[first + q] = result[:half, lanes]
            send_ref[first + q] = result[half:, lanes].astype(BF16)


def fill_taps(taps, slot, rows, width, value):
    start = (slot * (rows + 1) + 1) * width
    taps[start : start + rows * width] = value.reshape(rows * width, value.shape[2])


def clear_gaps(left, taps, slots, rows, width):
    gap = rows + 1
    for slot in range(slots + 1):
        begin = slot * gap * width
        end = taps.shape[0] if slot == slots else begin + width
        taps[begin:end] = jnp.zeros((end - begin, taps.shape[1]), taps.dtype)
    for slot in range(slots):
        begin = (slot * gap + rows) * width
        end = left.shape[0] if slot == slots - 1 else begin + width
        left[begin:end] = jnp.zeros((end - begin, left.shape[1]), left.dtype)


def first_grad_kernel(slots, core_ref, *refs):
    acts, pays, grads = (refs[at * slots : (at + 1) * slots] for at in range(3))
    basis_ref = refs[3 * slots]
    keep_ref, send_ref, left, left_t, taps = refs[-5:]
    rows, width, depth = acts[0].shape
    cells = rows * width
    rank = basis_ref.shape[0] // 2
    wide = taps.shape[1] // 3
    clear_gaps(left, taps, slots, rows, width)
    for slot in range(slots):
        values = acts[slot][...].reshape(cells, depth).astype(F32)
        along = pays[slot][:, wide : wide + rank]
        begin = slot * (rows + 1) * width
        left[begin : begin + cells] = project(values, along, basis_ref[...]).astype(BF16)
        right = stacked_again(grads[slot][...].astype(F32)).reshape(rows, width, wide)
        fill_taps(taps, slot, rows, width, columns(right, True))
    grad_body(core_ref, left, left_t, taps, keep_ref, send_ref, width, True)


def second_grad_kernel(slots, core_ref, *refs):
    cots, pays = (refs[at * slots : (at + 1) * slots] for at in range(2))
    alongs = refs[2 * slots : 2 * slots + slots // 2]
    basis_ref = refs[2 * slots + slots // 2]
    keep_ref, send_ref, left, left_t, taps = refs[-5:]
    rows, width, depth = cots[0].shape
    cells = rows * width
    rank = basis_ref.shape[0] // 2
    wide = taps.shape[1] // 3
    clear_gaps(left, taps, slots, rows, width)
    for slot in range(slots):
        begin = slot * (rows + 1) * width
        left[begin : begin + cells] = cots[slot][...].reshape(cells, depth)
        packed = alongs[slot // 2][slot % 2]
        along = jnp.concatenate([packed[:, :rank], packed[:, rank:]], axis=0)
        values = pays[slot][:, :wide].astype(F32)
        right = project(values, along, basis_ref[...]).astype(BF16).astype(F32)
        fill_taps(taps, slot, rows, width, columns(right.reshape(rows, width, wide), False))
    grad_body(core_ref, left, left_t, taps, keep_ref, send_ref, width, False)


def weight_grad(kernel, name, core, lefts, firsts, seconds, basis, wide, after=()):
    slots = len(firsts)
    rows, width, depth = lefts[0].shape
    used = slots * (rows + 1) * width
    span = -(-used // 128) * 128
    half = depth // 2
    tap_rows = 2 * width + span
    return run(
        functools.partial(kernel, slots),
        name,
        [
            jax.ShapeDtypeStruct((9, half, wide), F32),
            jax.ShapeDtypeStruct((9, half, wide), BF16),
        ],
        [core],
        [*lefts, *firsts, *seconds, basis],
        after,
        [
            pltpu.VMEM((span, depth), BF16),
            pltpu.VMEM((depth, span), BF16),
            pltpu.VMEM((tap_rows, 3 * wide), BF16),
        ],
        28,
        18 * slots * rows * width * depth * wide,
    )


def halves_kernel(turn, core_ref, own_ref, other_ref, *refs):
    outs = refs[-2:] if turn else refs[-1:]
    half = own_ref.shape[1]

    @pl.when(core_ref[0] == 0)
    def _():
        outs[0][:, :half] = own_ref[...]
        outs[0][:, half:] = other_ref[...]

    @pl.when(core_ref[0] != 0)
    def _():
        outs[0][:, :half] = other_ref[...]
        outs[0][:, half:] = own_ref[...]

    if turn:
        for tap in range(9):
            outs[1][tap] = outs[0][tap].T


def join_halves(core, own, other, turn, after=()):
    _, half, wide = own.shape
    outs = [jax.ShapeDtypeStruct((9, 2 * half, wide), BF16)]
    if turn:
        outs.append(jax.ShapeDtypeStruct((9, wide, 2 * half), BF16))
    return run(
        functools.partial(halves_kernel, turn), "join_halves", outs, [core], [own, other], after,
        held=12,
    )


def basis_kernel(blocks, at_ref, basis_ref, *refs):
    rows_ref, columns_ref = refs[-2:]
    rank, channels = basis_ref.shape
    width = channels // blocks
    for block in range(blocks):

        @pl.when(at_ref[0] == block)
        def _(block=block):
            values = basis_ref[:, block * width : (block + 1) * width]
            high = values.astype(BF16).astype(F32)
            both = jnp.concatenate([high, values - high], axis=0)
            rows_ref[...] = both.astype(BF16)
            columns_ref[...] = both.T.astype(BF16)


def basis_parts(at, basis, blocks, after=()):
    rank, channels = basis.shape
    width = channels // blocks
    return run(
        functools.partial(basis_kernel, blocks),
        "basis_parts",
        [
            jax.ShapeDtypeStruct((2 * rank, width), BF16),
            jax.ShapeDtypeStruct((width, 2 * rank), BF16),
        ],
        [at],
        [basis],
        after,
    )


def flat_kernel(scale, keep_ref, got_ref, *refs):
    held = refs[-2 * (keep_ref.shape[2] // 128) - 2 :]
    out_ref = refs[-len(held) - 1]
    taps, half, wide = keep_ref.shape
    whole = wide // 128
    step = 2 * whole + 1
    count = half // 2
    zeros = jnp.zeros((half, 64), F32)
    for tap in range(taps):
        total = (keep_ref[tap] + got_ref[tap].astype(F32)) * scale
        for at in range(whole):
            held[at][...] = total[:, 128 * at : 128 * (at + 1)]
            held[whole + 2 + at][...] = total[:, 128 * at + 64 : 128 * (at + 1) + 64]
        held[whole][...] = jnp.concatenate([total[:, 128 * whole :], zeros], axis=1)
        held[whole + 1][...] = jnp.concatenate([zeros, total[:, :64]], axis=1)
        even, odd = pl.ds(0, count, stride=2), pl.ds(1, count, stride=2)
        rows = [held[at][even, :] for at in range(whole)]
        rows.append(held[whole][even, :] + held[whole + 1][odd, :])
        rows += [held[whole + 2 + at][odd, :] for at in range(whole)]
        for at, row in enumerate(rows):
            out_ref[pl.ds(tap * count * step + at, count, stride=step), :] = row


def flat_grad(keep, got, scale, after=()):
    taps, half, wide = keep.shape
    if wide % 128 != 64 or half % 2:
        return (keep + got.astype(F32)) * scale
    return run(
        functools.partial(flat_kernel, scale),
        "flat_grad",
        [jax.ShapeDtypeStruct((taps * half * wide // 128, 128), F32)],
        [],
        [keep, got],
        after,
        scratch=[pltpu.VMEM((half, 128), F32)] * (2 * (wide // 128) + 2),
        held=12,
    )[0]


def same_groups(width, size):
    at = np.arange(width) // size
    return jnp.asarray((at[:, None] == at[None, :]).astype(np.float32), BF16)


def body(images, cotangent, first_weight, second_weight, first_basis, second_basis):
    n_dp = lax.axis_size("dp")
    n_rows = lax.axis_size("rows")
    chips = n_dp // 2
    _, band, width, channels = images.shape
    rows = band * n_rows
    dp_width = channels // n_dp
    chip_width = channels // chips
    row_width = channels // n_rows
    group = channels // GROUPS
    count = float(rows * width * group)
    grad_scale = 1.0 / math.sqrt(n_dp * images.shape[0] * rows * width)

    at_dp = lax.axis_index("dp")
    at_row = lax.axis_index("rows")
    chip = (at_dp // 2).astype(jnp.int32)
    core = (at_dp % 2).astype(jnp.int32)
    row = at_row.astype(jnp.int32)
    chip_at, core_at = chip[None], core[None]
    row_at = jnp.stack([row, (row + 1) // 2 % 2])

    def to_core(x):
        return lax.ppermute(x, "dp", [(i, i ^ 1) for i in range(n_dp)])

    def to_chip(x, away):
        return lax.ppermute(x, "dp", [(i, i ^ (2 * away)) for i in range(n_dp)])

    def to_row(x, away):
        return lax.ppermute(x, "rows", [(i, i ^ away) for i in range(n_rows)])

    def chips_gather(x):
        return [x] + [to_chip(x, away) for away in range(1, chips)]

    def rows_gather(x):
        if n_rows != 4:
            return [x] + [to_row(x, away) for away in range(1, n_rows)], [
                (away, -1) for away in range(n_rows)
            ]
        second = to_row(x, 2)
        first = to_row(x, 1)
        passed = lax.ppermute(second, "rows", [(2, 3), (1, 0)])
        later, _ = lax.optimization_barrier((x, second))
        middle = lax.ppermute(later, "rows", [(1, 2), (2, 1)])
        return [x, first, second, middle, passed], [(0, -1), (1, -1), (2, -1), (3, 1), (3, 0)]

    def chips_swap(parts):
        return [parts[0]] + [to_chip(parts[away], away) for away in range(1, chips)]

    def rows_swap(parts):
        far = [to_row(parts[away], away) for away in range(n_rows - 1, 0, -1)]
        return parts[:1] + far[::-1]

    chip_groups = same_groups(chip_width, group)
    row_groups = same_groups(row_width, group)

    slots = chips_swap(split_blocks([images[0], cotangent[0]], chips, chip_at))
    image_parts, places = rows_gather(pack_slots(slots, 0))

    first_weight, _ = lax.optimization_barrier((first_weight, slots[1]))
    own_first = first_weight.reshape(9, dp_width, row_width)
    (first_full,) = join_halves(core_at, own_first, to_core(own_first), False)
    weight_one = first_full.reshape(3, 3 * chip_width, row_width)
    second_weight, _ = lax.optimization_barrier((second_weight, image_parts[1:3]))
    own_second = second_weight.reshape(9, dp_width, row_width)
    second_full, second_turned = join_halves(core_at, own_second, to_core(own_second), True)
    weight_back = second_full.reshape(3, 3 * chip_width, row_width)
    weight_two = second_turned.reshape(3, 3 * row_width, chip_width)
    one_rows, one_columns = basis_parts(chip_at, first_basis, chips)
    two_rows, two_columns = basis_parts(row_at, second_basis, n_rows)

    cot_pack = pack_slots(slots, 1, (*image_parts[1:], first_full, second_full, one_rows, two_rows))
    cot_parts = lax.all_gather(cot_pack, "rows")

    sent = list(range(chips - 1, 0, -1))
    made = first_conv(
        image_parts, places, sent, weight_one, chip_groups, one_columns, row_at, rows, count,
        (cot_pack,),
    )
    own_made = first_conv(
        image_parts, places, [0], weight_one, chip_groups, one_columns, row_at, rows, count,
        made[0][1:],
    )
    made = own_made + made[::-1]
    active = [pair[0] for pair in made]
    first_terms = chips_swap([pair[1] for pair in made])

    pay, unit, scale, along = hidden_step(first_terms, row_groups, two_columns, count)
    pays = chips_gather(pay)

    away = 4
    while away < n_rows:
        along = (along.astype(F32) + to_row(along, away).astype(F32)).astype(BF16)
        away *= 2
    back, along = back_conv(cot_parts, weight_back, [along, to_row(along, 1)], (pay,))
    whole_cot = [pair[0] for pair in back]
    back_terms = chips_swap([pair[1] for pair in back])

    *sums, along = second_conv(
        pays, weight_two, [along, to_row(along, 2)], row_at, rows, n_rows, (back[0][1],)
    )
    band_terms = rows_swap(sums)

    pre_grad, along = pre_step(
        back_terms, unit, scale, row_groups, [along, to_chip(along, 1)], count,
        (sums[0], band_terms[-1]),
    )
    pre_grads = chips_gather(pre_grad)
    alongs = [along]
    away = 2
    while away < chips:
        alongs += [to_chip(part, away) for part in alongs]
        away *= 2

    second_halves = weight_grad(
        second_grad_kernel, "second_grad", core_at, whole_cot, pays, alongs, two_rows,
        row_width, (pre_grad,),
    )
    blocks = band_step(band_terms, second_halves[1:])
    first_halves = weight_grad(
        first_grad_kernel, "first_grad", core_at, active, pays, pre_grads, one_rows,
        row_width, (second_halves[1], blocks[0]),
    )
    second_grad = flat_grad(second_halves[0], to_core(second_halves[1]), grad_scale)
    block_output = join_blocks(images[0], chips_swap(blocks), chip_at, (second_grad,))[None]
    first_grad = flat_grad(
        first_halves[0], to_core(first_halves[1]), grad_scale, (block_output,)
    )
    first_grad = first_grad.reshape(1, 1, 9, dp_width * row_width)
    second_grad = second_grad.reshape(1, 1, 9, dp_width * row_width)
    return (block_output, first_grad, second_grad)


def solution(mesh):
    split = P("dp", "rows", None, None)
    return jax.shard_map(
        body,
        mesh=mesh,
        in_specs=(split, split, split, split, P(), P()),
        out_specs=(split, split, split),
        check_vma=False,
    )
```

```python
import functools
import math

import jax
import jax.numpy as jnp
import numpy as np
from jax import lax
from jax.experimental import pallas as pl
from jax.experimental.pallas import tpu as pltpu
from jax.sharding import PartitionSpec as P

GROUPS = 32
EPS = 1e-5
MIB = 1024 * 1024
F32 = jnp.float32
BF16 = jnp.bfloat16


def whole_block(x):
    zeros = (0,) * len(x.shape)
    return pl.BlockSpec(x.shape, lambda _: zeros, pipeline_mode=pl.Buffered(1))


def smem():
    return pl.BlockSpec(memory_space=pltpu.SMEM)


def unread(after):
    return [pl.BlockSpec(memory_space=pl.ANY)] * len(after)


def run(kernel, name, outs, scalars, arrays, after=(), scratch=(), held=8, flops=0, fetch=False):
    outs = [*outs, jax.ShapeDtypeStruct((8, 128), F32)]
    moved = sum(x.size * x.dtype.itemsize for x in list(arrays) + outs)
    held_there = pl.BlockSpec(memory_space=pltpu.VMEM)
    used = len(scalars) + len(arrays)
    token_at = used + len(after) + len(outs) - 1

    def whole(*refs):
        refs[token_at][...] = jnp.zeros((8, 128), F32)
        kernel(*refs[:used], *refs[used + len(after) : token_at], *refs[token_at + 1 :])

    *made, token = pl.pallas_call(
        whole,
        grid=(1,) if fetch else (),
        out_shape=outs,
        in_specs=[smem()] * len(scalars)
        + [whole_block(x) if fetch else held_there for x in arrays]
        + unread(after),
        out_specs=[held_there] * len(outs),
        scratch_shapes=list(scratch),
        compiler_params=pltpu.CompilerParams(vmem_limit_bytes=held * MIB),
        cost_estimate=cost(flops, moved),
        name=name,
    )(*scalars, *arrays, *after)
    return made, token


def cost(flops, moved):
    return pl.CostEstimate(flops=int(flops), bytes_accessed=int(moved), transcendentals=0)


def group_sums(row, same_group):
    high = row.astype(BF16).astype(F32)
    rest = row - high
    middle = rest.astype(BF16).astype(F32)
    low = rest - middle
    at = lax.broadcasted_iota(jnp.int32, (16, row.shape[1]), 0)
    stacked = jnp.where(at == 0, high, jnp.where(at == 1, middle, jnp.where(at == 2, low, 0.0)))
    sums = jnp.dot(stacked.astype(BF16), same_group, preferred_element_type=F32)
    return jnp.sum(sums, axis=0, keepdims=True)


def normalized(values, same_group, count):
    center = group_sums(jnp.sum(values, axis=0, keepdims=True), same_group) / count
    moved = values - center
    spread = group_sums(jnp.sum(moved * moved, axis=0, keepdims=True), same_group) / count
    scale = 1.0 / jnp.sqrt(spread + EPS)
    return moved * scale, scale


def silu(unit):
    half = 0.5 * unit
    return half + half * jnp.tanh(half)


def add_into(out_ref, one_ref, other_ref):
    out_ref[...] = (one_ref[...].astype(F32) + other_ref[...].astype(F32)).astype(BF16)


def columns(values, flip):
    width = values.shape[1]
    at = lax.broadcasted_iota(jnp.int32, values.shape, 1)
    before = jnp.where(at == 0, 0.0, pltpu.roll(values, 1, axis=1))
    after = jnp.where(at == width - 1, 0.0, pltpu.roll(values, width - 1, axis=1))
    parts = [after, values, before] if flip else [before, values, after]
    return jnp.concatenate([part.astype(BF16) for part in parts], axis=2)


def conv_rows(taps, weight_ref, rows, flip):
    _, width, depth = taps.shape
    total = None
    for tap in range(3):
        window = taps[tap : tap + rows].reshape(rows * width, depth)
        term = jnp.dot(window, weight_ref[2 - tap if flip else tap], preferred_element_type=F32)
        total = term if total is None else total + term
    return total


def side_by_side(values):
    half = values.shape[0] // 2
    return jnp.concatenate([values[:half], values[half:]], axis=1)


def stacked_again(values):
    half = values.shape[1] // 2
    return jnp.concatenate([values[:, :half], values[:, half:]], axis=0)


def clear_edges(taps):
    rows = taps.shape[0]
    taps[0:1] = jnp.zeros((1,) + taps.shape[1:], taps.dtype)
    taps[rows - 1 : rows] = jnp.zeros((1,) + taps.shape[1:], taps.dtype)


def split_kernel(blocks, at_ref, *refs):
    arrays, outs = refs[:-blocks], refs[-blocks:]
    width = outs[0].shape[-1] // len(arrays)
    for away in range(blocks):
        for block in range(blocks):

            @pl.when(jnp.bitwise_xor(at_ref[0], away) == block)
            def _(away=away, block=block):
                for at, x_ref in enumerate(arrays):
                    lanes = slice(at * width, (at + 1) * width)
                    outs[away][:, :, lanes] = x_ref[:, :, block * width : (block + 1) * width]


def split_blocks(arrays, blocks, chip):
    height, width, channels = arrays[0].shape
    shape = jax.ShapeDtypeStruct((height, width, len(arrays) * channels // blocks), BF16)
    made, _ = run(
        functools.partial(split_kernel, blocks), "split_blocks", [shape] * blocks, [chip], arrays,
        held=50, fetch=True,
    )
    return made


def pack_kernel(at, *refs):
    slots, out = refs[:-1], refs[-1]
    width = slots[0].shape[-1] // 2
    for slot, ref in enumerate(slots):
        lanes = slice(slot % 2 * width, (slot % 2 + 1) * width)
        out[slot // 2, :, :, lanes] = ref[:, :, at * width : (at + 1) * width]


def pack_slots(slots, at, after=()):
    out = jax.ShapeDtypeStruct((len(slots) // 2, *slots[0].shape), BF16)
    (packed,), token = run(
        functools.partial(pack_kernel, at), "pack_slots", [out], [], slots, after
    )
    return packed, token


def assemble(whole, parts, places, pair, at_ref):
    for part, (away, who) in zip(parts, places):

        @pl.when(jnp.logical_or(who < 0, at_ref[1] == who))
        def _(part=part, away=away):
            band = part.shape[1]
            whole[pl.ds(jnp.bitwise_xor(at_ref[0], away) * band, band)] = part[pair]


def first_kernel(slots, places, count, at_ref, *refs):
    parts = refs[: len(places)]
    weight_ref, group_ref, basis_ref = refs[len(places) : len(places) + 3]
    whole, taps = refs[-2:]
    outs = refs[-2 - 2 * len(slots) : -2]
    rows, width, depth = outs[0].shape
    rank = basis_ref.shape[1] // 2
    cells = rows * width
    clear_edges(taps)
    held = None
    for at, slot in enumerate(slots):
        act_ref, sums_ref = outs[2 * at : 2 * at + 2]
        if slot // 2 != held:
            held = slot // 2
            assemble(whole, parts, places, held, at_ref)
        half = slot % 2
        values = whole[:, :, half * depth : (half + 1) * depth].astype(F32)
        unit, _ = normalized(values.reshape(cells, depth), group_ref[...], count)
        active = silu(unit).astype(BF16)
        act_ref[...] = active.reshape(act_ref.shape)
        taps[1 : rows + 1] = columns(active.astype(F32).reshape(act_ref.shape), False)
        total = conv_rows(taps, weight_ref, rows, False)
        along = jnp.dot(active, basis_ref[...], preferred_element_type=F32)
        along = along[:, :rank] + along[:, rank:]
        sums_ref[...] = jnp.concatenate([total, along], axis=1).astype(BF16)


def first_conv(parts, places, slots, weight, same_group, basis, row, rows, count, after=()):
    _, band, width, double = parts[0].shape
    depth = double // 2
    rank = basis.shape[1] // 2
    wide = weight.shape[2]
    cells = rows * width
    outs = [
        jax.ShapeDtypeStruct((rows, width, depth), BF16),
        jax.ShapeDtypeStruct((cells, wide + rank), BF16),
    ]
    made, token = run(
        functools.partial(first_kernel, slots, places, count),
        "first_conv",
        outs * len(slots),
        [row],
        [*parts, weight, same_group, basis],
        after,
        [
            pltpu.VMEM((rows, width, double), BF16),
            pltpu.VMEM((rows + 2, width, 3 * depth), BF16),
        ],
        14,
        18 * len(slots) * cells * depth * wide,
    )
    return [(made[2 * at], made[2 * at + 1]) for at in range(len(slots))], token


def back_kernel(slots, parts_ref, weight_ref, along_ref, other_ref, *refs):
    later_ref, whole, taps = refs[-3:]
    outs = refs[-3 - 2 * slots : -3]
    add_into(later_ref, along_ref, other_ref)
    bands, _, band = parts_ref.shape[:3]
    rows, width, depth = outs[0].shape
    clear_edges(taps)
    for slot in reversed(range(slots)):
        cot_ref, sums_ref = outs[2 * slot : 2 * slot + 2]
        if slot % 2:
            for at in range(bands):
                whole[at * band : (at + 1) * band] = parts_ref[at, slot // 2]
        half = slot % 2
        values = whole[:, :, half * depth : (half + 1) * depth]
        cot_ref[...] = values
        taps[1 : rows + 1] = columns(values.astype(F32), True)
        sums_ref[...] = side_by_side(conv_rows(taps, weight_ref, rows, True)).astype(BF16)


def back_conv(parts, weight, alongs, after=()):
    bands, pairs, band, width, double = parts.shape
    rows = bands * band
    depth = double // 2
    wide = weight.shape[2]
    cells = rows * width
    slots = 2 * pairs
    outs = [
        jax.ShapeDtypeStruct((rows, width, depth), BF16),
        jax.ShapeDtypeStruct((cells // 2, 2 * wide), BF16),
    ]
    made, token = run(
        functools.partial(back_kernel, slots),
        "back_conv",
        outs * slots + alongs[:1],
        [],
        [parts, weight, *alongs],
        after,
        [
            pltpu.VMEM((rows, width, double), BF16),
            pltpu.VMEM((rows + 2, width, 3 * depth), BF16),
        ],
        14,
        18 * slots * cells * depth * wide,
    )
    return [(made[2 * at], made[2 * at + 1]) for at in range(slots)], made[-1], token


def hidden_kernel(terms, count, *refs):
    group_ref, basis_ref = refs[terms : terms + 2]
    pay_ref, unit_ref, scale_ref, along_ref = refs[-4:]
    wide = unit_ref.shape[1]
    rank = basis_ref.shape[1] // 2
    total = refs[0][...].astype(F32)
    for term in refs[1:terms]:
        total = total + term[...].astype(F32)
    unit, scale = normalized(total[:, :wide], group_ref[...], count)
    unit_ref[...] = unit
    scale_ref[...] = scale
    hidden = silu(unit).astype(BF16)
    pay_ref[...] = jnp.concatenate([hidden.astype(F32), total[:, wide:]], axis=1).astype(BF16)
    along = jnp.dot(hidden, basis_ref[...], preferred_element_type=F32)
    along_ref[...] = side_by_side(along[:, :rank] + along[:, rank:]).astype(BF16)


def hidden_step(terms, same_group, basis, count, after=()):
    cells, both = terms[0].shape
    wide = same_group.shape[0]
    return run(
        functools.partial(hidden_kernel, len(terms), count),
        "hidden_step",
        [
            jax.ShapeDtypeStruct((cells, both), BF16),
            jax.ShapeDtypeStruct((cells, wide), F32),
            jax.ShapeDtypeStruct((1, wide), F32),
            jax.ShapeDtypeStruct((cells // 2, basis.shape[1]), BF16),
        ],
        [],
        [*terms, same_group, basis],
        after,
        held=12,
        flops=40 * cells * wide,
    )


def second_kernel(slots, bands, at_ref, *refs):
    pays = refs[:slots]
    weight_ref, along_ref, other_ref = refs[slots : slots + 3]
    later_ref, whole, taps = refs[-3:]
    outs = refs[-3 - bands : -3]
    add_into(later_ref, along_ref, other_ref)
    band, width, double = outs[0].shape[1:]
    rows = whole.shape[0]
    depth = taps.shape[2] // 3
    wide = double // 2
    clear_edges(taps)
    for slot in range(slots):
        hidden = pays[slot][:, :depth].astype(F32).reshape(rows, width, depth)
        taps[1 : rows + 1] = columns(hidden, False)
        whole[...] = conv_rows(taps, weight_ref, rows, False).reshape(rows, width, wide)
        lanes = slice(slot % 2 * wide, (slot % 2 + 1) * wide)
        for away in range(bands):
            start = jnp.bitwise_xor(at_ref[0], away) * band
            outs[away][slot // 2, :, :, lanes] = whole[pl.ds(start, band)].astype(BF16)


def second_conv(pays, weight, alongs, row, rows, bands, after=()):
    slots = len(pays)
    cells, _ = pays[0].shape
    width = cells // rows
    depth = weight.shape[1] // 3
    wide = weight.shape[2]
    out = jax.ShapeDtypeStruct((slots // 2, rows // bands, width, 2 * wide), BF16)
    return run(
        functools.partial(second_kernel, slots, bands),
        "second_conv",
        [out] * bands + alongs[:1],
        [row],
        [*pays, weight, *alongs],
        after,
        [
            pltpu.VMEM((rows, width, wide), F32),
            pltpu.VMEM((rows + 2, width, 3 * depth), BF16),
        ],
        14,
        18 * slots * cells * depth * wide,
    )


def band_kernel(terms, slots, *refs):
    outs = refs[-slots:]
    wide = outs[0].shape[-1]
    total = refs[0][...].astype(F32)
    for term in refs[1:terms]:
        total = total + term[...].astype(F32)
    for slot, out in enumerate(outs):
        lanes = slice(slot % 2 * wide, (slot % 2 + 1) * wide)
        out[...] = total[slot // 2, :, :, lanes].astype(BF16)


def band_step(terms, after=()):
    pairs, band, width, double = terms[0].shape
    out = jax.ShapeDtypeStruct((band, width, double // 2), BF16)
    return run(
        functools.partial(band_kernel, len(terms), 2 * pairs),
        "band_step",
        [out] * (2 * pairs),
        [],
        terms,
        after,
    )


def join_kernel(blocks, at_ref, x_ref, *refs):
    out = refs[-1]
    width = x_ref.shape[-1] // blocks
    for away in range(blocks):
        for block in range(blocks):

            @pl.when(jnp.bitwise_xor(at_ref[0], away) == block)
            def _(away=away, block=block):
                lanes = slice(block * width, (block + 1) * width)
                added = x_ref[:, :, lanes].astype(F32) + refs[away][...].astype(F32)
                out[:, :, lanes] = added.astype(BF16)


def join_blocks(x, parts, chip, after=()):
    return run(
        functools.partial(join_kernel, len(parts)),
        "join_blocks",
        [x],
        [chip],
        [x, *parts],
        after,
    )


def pre_kernel(terms, count, *refs):
    unit_ref, scale_ref, group_ref, along_ref, other_ref = refs[terms : terms + 5]
    out_ref, later_ref = refs[-2:]
    later_ref[0] = along_ref[...]
    later_ref[1] = other_ref[...]
    total = refs[0][...].astype(F32)
    for term in refs[1:terms]:
        total = total + term[...].astype(F32)
    unit = unit_ref[...]
    gate = 0.5 + 0.5 * jnp.tanh(0.5 * unit)
    grad = stacked_again(total) * (gate * (1.0 + unit * (1.0 - gate)))
    mean = group_sums(jnp.sum(grad, axis=0, keepdims=True), group_ref[...]) / count
    along = group_sums(jnp.sum(grad * unit, axis=0, keepdims=True), group_ref[...]) / count
    out_ref[...] = side_by_side(scale_ref[...] * (grad - mean - unit * along)).astype(BF16)


def pre_step(terms, unit, scale, same_group, alongs, count, after=()):
    cells, wide = unit.shape
    stacked = jax.ShapeDtypeStruct((2, *alongs[0].shape), BF16)
    return run(
        functools.partial(pre_kernel, len(terms), count),
        "pre_step",
        [jax.ShapeDtypeStruct((cells // 2, 2 * wide), BF16), stacked],
        [],
        [*terms, unit, scale, same_group, *alongs],
        after,
        held=12,
        flops=40 * cells * wide,
    )


def project(values, along, basis):
    both = jnp.concatenate([along, along], axis=1)
    return values - jnp.dot(both, basis, preferred_element_type=F32)


def grad_body(core_ref, left, left_t, taps, keep_ref, send_ref, width, flip):
    half = left.shape[1] // 2
    span = left.shape[0]
    wide = taps.shape[1] // 3
    turned = left[...].T

    @pl.when(core_ref[0] == 0)
    def _():
        left_t[...] = turned

    @pl.when(core_ref[0] != 0)
    def _():
        left_t[:half] = turned[half:]
        left_t[half:] = turned[:half]

    for tap in range(3):
        window = taps[tap * width : tap * width + span]
        result = jnp.dot(left_t[...], window, preferred_element_type=F32)
        first = 3 * (2 - tap if flip else tap)
        for q in range(3):
            lanes = slice(q * wide, (q + 1) * wide)
            keep_ref[first + q] = result[:half, lanes]
            send_ref[first + q] = result[half:, lanes].astype(BF16)


def fill_taps(taps, slot, rows, width, value):
    start = (slot * (rows + 1) + 1) * width
    taps[start : start + rows * width] = value.reshape(rows * width, value.shape[2])


def clear_gaps(left, taps, slots, rows, width):
    gap = rows + 1
    for slot in range(slots + 1):
        begin = slot * gap * width
        end = taps.shape[0] if slot == slots else begin + width
        taps[begin:end] = jnp.zeros((end - begin, taps.shape[1]), taps.dtype)
    for slot in range(slots):
        begin = (slot * gap + rows) * width
        end = left.shape[0] if slot == slots - 1 else begin + width
        left[begin:end] = jnp.zeros((end - begin, left.shape[1]), left.dtype)


def first_grad_kernel(slots, core_ref, *refs):
    acts, pays, grads = (refs[at * slots : (at + 1) * slots] for at in range(3))
    basis_ref = refs[3 * slots]
    keep_ref, send_ref, left, left_t, taps = refs[-5:]
    rows, width, depth = acts[0].shape
    cells = rows * width
    rank = basis_ref.shape[0] // 2
    wide = taps.shape[1] // 3
    clear_gaps(left, taps, slots, rows, width)
    for slot in range(slots):
        values = acts[slot][...].reshape(cells, depth).astype(F32)
        along = pays[slot][:, wide : wide + rank]
        begin = slot * (rows + 1) * width
        left[begin : begin + cells] = project(values, along, basis_ref[...]).astype(BF16)
        right = stacked_again(grads[slot][...].astype(F32)).reshape(rows, width, wide)
        fill_taps(taps, slot, rows, width, columns(right, True))
    grad_body(core_ref, left, left_t, taps, keep_ref, send_ref, width, True)


def second_grad_kernel(slots, core_ref, *refs):
    cots, pays = (refs[at * slots : (at + 1) * slots] for at in range(2))
    alongs = refs[2 * slots : 2 * slots + slots // 2]
    basis_ref = refs[2 * slots + slots // 2]
    keep_ref, send_ref, left, left_t, taps = refs[-5:]
    rows, width, depth = cots[0].shape
    cells = rows * width
    rank = basis_ref.shape[0] // 2
    wide = taps.shape[1] // 3
    clear_gaps(left, taps, slots, rows, width)
    for slot in range(slots):
        begin = slot * (rows + 1) * width
        left[begin : begin + cells] = cots[slot][...].reshape(cells, depth)
        packed = alongs[slot // 2][slot % 2]
        along = jnp.concatenate([packed[:, :rank], packed[:, rank:]], axis=0)
        values = pays[slot][:, :wide].astype(F32)
        right = project(values, along, basis_ref[...]).astype(BF16).astype(F32)
        fill_taps(taps, slot, rows, width, columns(right.reshape(rows, width, wide), False))
    grad_body(core_ref, left, left_t, taps, keep_ref, send_ref, width, False)


def weight_grad(kernel, name, core, lefts, firsts, seconds, basis, wide, after=()):
    slots = len(firsts)
    rows, width, depth = lefts[0].shape
    used = slots * (rows + 1) * width
    span = -(-used // 128) * 128
    half = depth // 2
    tap_rows = 2 * width + span
    return run(
        functools.partial(kernel, slots),
        name,
        [
            jax.ShapeDtypeStruct((9, half, wide), F32),
            jax.ShapeDtypeStruct((9, half, wide), BF16),
        ],
        [core],
        [*lefts, *firsts, *seconds, basis],
        after,
        [
            pltpu.VMEM((span, depth), BF16),
            pltpu.VMEM((depth, span), BF16),
            pltpu.VMEM((tap_rows, 3 * wide), BF16),
        ],
        28,
        18 * slots * rows * width * depth * wide,
    )


def halves_kernel(turn, core_ref, own_ref, other_ref, *refs):
    outs = refs[-2:] if turn else refs[-1:]
    half = own_ref.shape[1]

    @pl.when(core_ref[0] == 0)
    def _():
        outs[0][:, :half] = own_ref[...]
        outs[0][:, half:] = other_ref[...]

    @pl.when(core_ref[0] != 0)
    def _():
        outs[0][:, :half] = other_ref[...]
        outs[0][:, half:] = own_ref[...]

    if turn:
        for tap in range(9):
            outs[1][tap] = outs[0][tap].T


def join_halves(core, own, other, turn, after=()):
    _, half, wide = own.shape
    outs = [jax.ShapeDtypeStruct((9, 2 * half, wide), BF16)]
    if turn:
        outs.append(jax.ShapeDtypeStruct((9, wide, 2 * half), BF16))
    return run(
        functools.partial(halves_kernel, turn), "join_halves", outs, [core], [own, other], after,
        held=12,
    )


def basis_kernel(blocks, at_ref, basis_ref, *refs):
    rows_ref, columns_ref = refs[-2:]
    rank, channels = basis_ref.shape
    width = channels // blocks
    for block in range(blocks):

        @pl.when(at_ref[0] == block)
        def _(block=block):
            values = basis_ref[:, block * width : (block + 1) * width]
            high = values.astype(BF16).astype(F32)
            both = jnp.concatenate([high, values - high], axis=0)
            rows_ref[...] = both.astype(BF16)
            columns_ref[...] = both.T.astype(BF16)


def basis_parts(at, basis, blocks, after=()):
    rank, channels = basis.shape
    width = channels // blocks
    return run(
        functools.partial(basis_kernel, blocks),
        "basis_parts",
        [
            jax.ShapeDtypeStruct((2 * rank, width), BF16),
            jax.ShapeDtypeStruct((width, 2 * rank), BF16),
        ],
        [at],
        [basis],
        after,
    )


def flat_kernel(scale, keep_ref, got_ref, *refs):
    held = refs[-2 * (keep_ref.shape[2] // 128) - 2 :]
    out_ref = refs[-len(held) - 1]
    taps, half, wide = keep_ref.shape
    whole = wide // 128
    step = 2 * whole + 1
    count = half // 2
    zeros = jnp.zeros((half, 64), F32)
    for tap in range(taps):
        total = (keep_ref[tap] + got_ref[tap].astype(F32)) * scale
        for at in range(whole):
            held[at][...] = total[:, 128 * at : 128 * (at + 1)]
            held[whole + 2 + at][...] = total[:, 128 * at + 64 : 128 * (at + 1) + 64]
        held[whole][...] = jnp.concatenate([total[:, 128 * whole :], zeros], axis=1)
        held[whole + 1][...] = jnp.concatenate([zeros, total[:, :64]], axis=1)
        even, odd = pl.ds(0, count, stride=2), pl.ds(1, count, stride=2)
        rows = [held[at][even, :] for at in range(whole)]
        rows.append(held[whole][even, :] + held[whole + 1][odd, :])
        rows += [held[whole + 2 + at][odd, :] for at in range(whole)]
        for at, row in enumerate(rows):
            out_ref[pl.ds(tap * count * step + at, count, stride=step), :] = row


def flat_grad(keep, got, scale, after=()):
    taps, half, wide = keep.shape
    if wide % 128 != 64 or half % 2:
        made = (keep + got.astype(F32)) * scale
        return made, made
    (made,), token = run(
        functools.partial(flat_kernel, scale),
        "flat_grad",
        [jax.ShapeDtypeStruct((taps * half * wide // 128, 128), F32)],
        [],
        [keep, got],
        after,
        scratch=[pltpu.VMEM((half, 128), F32)] * (2 * (wide // 128) + 2),
        held=12,
    )
    return made, token


def same_groups(width, size):
    at = np.arange(width) // size
    return jnp.asarray((at[:, None] == at[None, :]).astype(np.float32), BF16)


def body(images, cotangent, first_weight, second_weight, first_basis, second_basis):
    n_dp = lax.axis_size("dp")
    n_rows = lax.axis_size("rows")
    chips = n_dp // 2
    _, band, width, channels = images.shape
    rows = band * n_rows
    dp_width = channels // n_dp
    chip_width = channels // chips
    row_width = channels // n_rows
    group = channels // GROUPS
    count = float(rows * width * group)
    grad_scale = 1.0 / math.sqrt(n_dp * images.shape[0] * rows * width)

    at_dp = lax.axis_index("dp")
    at_row = lax.axis_index("rows")
    chip = (at_dp // 2).astype(jnp.int32)
    core = (at_dp % 2).astype(jnp.int32)
    row = at_row.astype(jnp.int32)
    chip_at, core_at = chip[None], core[None]
    row_at = jnp.stack([row, (row + 1) // 2 % 2])

    def to_core(x):
        return lax.ppermute(x, "dp", [(i, i ^ 1) for i in range(n_dp)])

    def to_chip(x, away):
        return lax.ppermute(x, "dp", [(i, i ^ (2 * away)) for i in range(n_dp)])

    def to_row(x, away):
        return lax.ppermute(x, "rows", [(i, i ^ away) for i in range(n_rows)])

    def chips_gather(x):
        return [x] + [to_chip(x, away) for away in range(1, chips)]

    def rows_gather(x):
        if n_rows != 4:
            return [x] + [to_row(x, away) for away in range(1, n_rows)], [
                (away, -1) for away in range(n_rows)
            ]
        second = to_row(x, 2)
        first = to_row(x, 1)
        passed = lax.ppermute(second, "rows", [(2, 3), (1, 0)])
        later, _ = lax.optimization_barrier((x, second))
        middle = lax.ppermute(later, "rows", [(1, 2), (2, 1)])
        return [x, first, second, middle, passed], [(0, -1), (1, -1), (2, -1), (3, 1), (3, 0)]

    def chips_swap(parts):
        return [parts[0]] + [to_chip(parts[away], away) for away in range(1, chips)]

    def rows_swap(parts):
        far = [to_row(parts[away], away) for away in range(n_rows - 1, 0, -1)]
        return parts[:1] + far[::-1]

    chip_groups = same_groups(chip_width, group)
    row_groups = same_groups(row_width, group)

    slots = chips_swap(split_blocks([images[0], cotangent[0]], chips, chip_at))
    image_pack, _ = pack_slots(slots, 0)
    image_parts, places = rows_gather(image_pack)

    first_weight, second_weight, _ = lax.optimization_barrier(
        (first_weight, second_weight, slots[1])
    )
    own_first = first_weight.reshape(9, dp_width, row_width)
    own_second = second_weight.reshape(9, dp_width, row_width)
    early = tuple(image_parts[1:3])
    (one_rows, one_columns), one_done = basis_parts(chip_at, first_basis, chips, early)
    (two_rows, two_columns), two_done = basis_parts(row_at, second_basis, n_rows, early)
    (first_full,), first_done = join_halves(core_at, own_first, to_core(own_first), False, early)
    cot_pack, cot_done = pack_slots(
        slots, 1, (*image_parts[3:], one_done, two_done, first_done)
    )
    cot_parts = lax.all_gather(cot_pack, "rows")
    (second_full, second_turned), second_done = join_halves(
        core_at, own_second, to_core(own_second), True, (cot_done,)
    )
    weight_one = first_full.reshape(3, 3 * chip_width, row_width)
    weight_back = second_full.reshape(3, 3 * chip_width, row_width)
    weight_two = second_turned.reshape(3, 3 * row_width, chip_width)

    sent = list(range(chips - 1, 0, -1))
    made, made_done = first_conv(
        image_parts, places, sent, weight_one, chip_groups, one_columns, row_at, rows, count,
        (second_done,),
    )
    own_made, _ = first_conv(
        image_parts, places, [0], weight_one, chip_groups, one_columns, row_at, rows, count,
        (made_done,),
    )
    made = own_made + made[::-1]
    active = [pair[0] for pair in made]
    first_terms = chips_swap([pair[1] for pair in made])

    (pay, unit, scale, along), hidden_done = hidden_step(
        first_terms, row_groups, two_columns, count
    )
    pays = chips_gather(pay)

    away = 4
    while away < n_rows:
        along = (along.astype(F32) + to_row(along, away).astype(F32)).astype(BF16)
        away *= 2
    back, along, back_done = back_conv(
        cot_parts, weight_back, [along, to_row(along, 1)], (hidden_done,)
    )
    whole_cot = [pair[0] for pair in back]
    back_terms = chips_swap([pair[1] for pair in back])

    (*sums, along), sums_done = second_conv(
        pays, weight_two, [along, to_row(along, 2)], row_at, rows, n_rows, (back_done,)
    )
    band_terms = rows_swap(sums)

    (pre_grad, along), pre_done = pre_step(
        back_terms, unit, scale, row_groups, [along, to_chip(along, 1)], count,
        (sums_done, band_terms[-1]),
    )
    pre_grads = chips_gather(pre_grad)
    alongs = [along]
    away = 2
    while away < chips:
        alongs += [to_chip(part, away) for part in alongs]
        away *= 2

    second_halves, second_made = weight_grad(
        second_grad_kernel, "second_grad", core_at, whole_cot, pays, alongs, two_rows,
        row_width, (pre_done,),
    )
    blocks, blocks_done = band_step(band_terms, (second_made,))
    first_halves, _ = weight_grad(
        first_grad_kernel, "first_grad", core_at, active, pays, pre_grads, one_rows,
        row_width, (blocks_done,),
    )
    second_grad, flat_done = flat_grad(
        second_halves[0], to_core(second_halves[1]), grad_scale
    )
    (block_output,), output_done = join_blocks(
        images[0], chips_swap(blocks), chip_at, (flat_done,)
    )
    first_grad, _ = flat_grad(
        first_halves[0], to_core(first_halves[1]), grad_scale, (output_done,)
    )
    block_output = block_output[None]
    first_grad = first_grad.reshape(1, 1, 9, dp_width * row_width)
    second_grad = second_grad.reshape(1, 1, 9, dp_width * row_width)
    return (block_output, first_grad, second_grad)


def solution(mesh):
    split = P("dp", "rows", None, None)
    return jax.shard_map(
        body,
        mesh=mesh,
        in_specs=(split, split, split, split, P(), P()),
        out_specs=(split, split, split),
        check_vma=False,
    )
```

```python
import functools
import math

import jax
import jax.numpy as jnp
import numpy as np
from jax import lax
from jax.experimental import pallas as pl
from jax.experimental.pallas import tpu as pltpu
from jax.sharding import PartitionSpec as P

GROUPS = 32
EPS = 1e-5
MIB = 1024 * 1024
F32 = jnp.float32
BF16 = jnp.bfloat16


def whole_block(x):
    zeros = (0,) * len(x.shape)
    return pl.BlockSpec(x.shape, lambda _: zeros, pipeline_mode=pl.Buffered(1))


def smem():
    return pl.BlockSpec(memory_space=pltpu.SMEM)


def unread(after):
    return [pl.BlockSpec(memory_space=pltpu.VMEM)] * len(after)


def run(kernel, name, outs, scalars, arrays, after=(), scratch=(), held=8, flops=0, fetch=False):
    outs = [*outs, jax.ShapeDtypeStruct((8, 128), F32)]
    moved = sum(x.size * x.dtype.itemsize for x in list(arrays) + outs)
    held_there = pl.BlockSpec(memory_space=pltpu.VMEM)
    used = len(scalars) + len(arrays)
    token_at = used + len(after) + len(outs) - 1

    def whole(*refs):
        refs[token_at][...] = jnp.zeros((8, 128), F32)
        kernel(*refs[:used], *refs[used + len(after) : token_at], *refs[token_at + 1 :])

    *made, token = pl.pallas_call(
        whole,
        grid=(1,) if fetch else (),
        out_shape=outs,
        in_specs=[smem()] * len(scalars)
        + [whole_block(x) if fetch else held_there for x in arrays]
        + unread(after),
        out_specs=[held_there] * len(outs),
        scratch_shapes=list(scratch),
        compiler_params=pltpu.CompilerParams(vmem_limit_bytes=held * MIB),
        cost_estimate=cost(flops, moved),
        name=name,
    )(*scalars, *arrays, *after)
    return made, token


def cost(flops, moved):
    return pl.CostEstimate(flops=int(flops), bytes_accessed=int(moved), transcendentals=0)


def group_sums(row, same_group):
    high = row.astype(BF16).astype(F32)
    rest = row - high
    middle = rest.astype(BF16).astype(F32)
    low = rest - middle
    at = lax.broadcasted_iota(jnp.int32, (16, row.shape[1]), 0)
    stacked = jnp.where(at == 0, high, jnp.where(at == 1, middle, jnp.where(at == 2, low, 0.0)))
    sums = jnp.dot(stacked.astype(BF16), same_group, preferred_element_type=F32)
    return jnp.sum(sums, axis=0, keepdims=True)


def normalized(values, same_group, count):
    center = group_sums(jnp.sum(values, axis=0, keepdims=True), same_group) / count
    moved = values - center
    spread = group_sums(jnp.sum(moved * moved, axis=0, keepdims=True), same_group) / count
    scale = 1.0 / jnp.sqrt(spread + EPS)
    return moved * scale, scale


def silu(unit):
    half = 0.5 * unit
    return half + half * jnp.tanh(half)


def add_into(out_ref, one_ref, other_ref):
    out_ref[...] = (one_ref[...].astype(F32) + other_ref[...].astype(F32)).astype(BF16)


def columns(values, flip):
    width = values.shape[1]
    at = lax.broadcasted_iota(jnp.int32, values.shape, 1)
    before = jnp.where(at == 0, 0.0, pltpu.roll(values, 1, axis=1))
    after = jnp.where(at == width - 1, 0.0, pltpu.roll(values, width - 1, axis=1))
    parts = [after, values, before] if flip else [before, values, after]
    return jnp.concatenate([part.astype(BF16) for part in parts], axis=2)


def conv_rows(taps, weight_ref, rows, flip):
    _, width, depth = taps.shape
    total = None
    for tap in range(3):
        window = taps[tap : tap + rows].reshape(rows * width, depth)
        term = jnp.dot(window, weight_ref[2 - tap if flip else tap], preferred_element_type=F32)
        total = term if total is None else total + term
    return total


def side_by_side(values):
    half = values.shape[0] // 2
    return jnp.concatenate([values[:half], values[half:]], axis=1)


def stacked_again(values):
    half = values.shape[1] // 2
    return jnp.concatenate([values[:, :half], values[:, half:]], axis=0)


def clear_edges(taps):
    rows = taps.shape[0]
    taps[0:1] = jnp.zeros((1,) + taps.shape[1:], taps.dtype)
    taps[rows - 1 : rows] = jnp.zeros((1,) + taps.shape[1:], taps.dtype)


def split_kernel(blocks, at_ref, *refs):
    arrays, outs = refs[:-blocks], refs[-blocks:]
    width = outs[0].shape[-1] // len(arrays)
    for away in range(blocks):
        for block in range(blocks):

            @pl.when(jnp.bitwise_xor(at_ref[0], away) == block)
            def _(away=away, block=block):
                for at, x_ref in enumerate(arrays):
                    lanes = slice(at * width, (at + 1) * width)
                    outs[away][:, :, lanes] = x_ref[:, :, block * width : (block + 1) * width]


def split_blocks(arrays, blocks, chip):
    height, width, channels = arrays[0].shape
    shape = jax.ShapeDtypeStruct((height, width, len(arrays) * channels // blocks), BF16)
    made, _ = run(
        functools.partial(split_kernel, blocks), "split_blocks", [shape] * blocks, [chip], arrays,
        held=50, fetch=True,
    )
    return made


def pack_kernel(at, *refs):
    slots, out = refs[:-1], refs[-1]
    width = slots[0].shape[-1] // 2
    for slot, ref in enumerate(slots):
        lanes = slice(slot % 2 * width, (slot % 2 + 1) * width)
        out[slot // 2, :, :, lanes] = ref[:, :, at * width : (at + 1) * width]


def pack_slots(slots, at, after=()):
    out = jax.ShapeDtypeStruct((len(slots) // 2, *slots[0].shape), BF16)
    (packed,), token = run(
        functools.partial(pack_kernel, at), "pack_slots", [out], [], slots, after
    )
    return packed, token


def assemble(whole, parts, places, pair, at_ref):
    for part, (away, who) in zip(parts, places):

        @pl.when(jnp.logical_or(who < 0, at_ref[1] == who))
        def _(part=part, away=away):
            band = part.shape[1]
            whole[pl.ds(jnp.bitwise_xor(at_ref[0], away) * band, band)] = part[pair]


def first_kernel(slots, places, count, at_ref, *refs):
    parts = refs[: len(places)]
    weight_ref, group_ref, basis_ref = refs[len(places) : len(places) + 3]
    whole, taps = refs[-2:]
    outs = refs[-2 - 2 * len(slots) : -2]
    rows, width, depth = outs[0].shape
    rank = basis_ref.shape[1] // 2
    cells = rows * width
    clear_edges(taps)
    held = None
    for at, slot in enumerate(slots):
        act_ref, sums_ref = outs[2 * at : 2 * at + 2]
        if slot // 2 != held:
            held = slot // 2
            assemble(whole, parts, places, held, at_ref)
        half = slot % 2
        values = whole[:, :, half * depth : (half + 1) * depth].astype(F32)
        unit, _ = normalized(values.reshape(cells, depth), group_ref[...], count)
        active = silu(unit).astype(BF16)
        act_ref[...] = active.reshape(act_ref.shape)
        taps[1 : rows + 1] = columns(active.astype(F32).reshape(act_ref.shape), False)
        total = conv_rows(taps, weight_ref, rows, False)
        along = jnp.dot(active, basis_ref[...], preferred_element_type=F32)
        along = along[:, :rank] + along[:, rank:]
        sums_ref[...] = jnp.concatenate([total, along], axis=1).astype(BF16)


def first_conv(parts, places, slots, weight, same_group, basis, row, rows, count, after=()):
    _, band, width, double = parts[0].shape
    depth = double // 2
    rank = basis.shape[1] // 2
    wide = weight.shape[2]
    cells = rows * width
    outs = [
        jax.ShapeDtypeStruct((rows, width, depth), BF16),
        jax.ShapeDtypeStruct((cells, wide + rank), BF16),
    ]
    made, token = run(
        functools.partial(first_kernel, slots, places, count),
        "first_conv",
        outs * len(slots),
        [row],
        [*parts, weight, same_group, basis],
        after,
        [
            pltpu.VMEM((rows, width, double), BF16),
            pltpu.VMEM((rows + 2, width, 3 * depth), BF16),
        ],
        14,
        18 * len(slots) * cells * depth * wide,
    )
    return [(made[2 * at], made[2 * at + 1]) for at in range(len(slots))], token


def back_kernel(slots, bands, at_ref, *refs):
    parts = refs[:bands]
    weight_ref, along_ref, other_ref = refs[bands : bands + 3]
    later_ref, whole, taps = refs[-3:]
    outs = refs[-3 - 2 * slots : -3]
    add_into(later_ref, along_ref, other_ref)
    rows, width, depth = outs[0].shape
    places = [(away, -1) for away in range(bands)]
    clear_edges(taps)
    for slot in reversed(range(slots)):
        cot_ref, sums_ref = outs[2 * slot : 2 * slot + 2]
        if slot % 2:
            assemble(whole, parts, places, slot // 2, at_ref)
        half = slot % 2
        values = whole[:, :, half * depth : (half + 1) * depth]
        cot_ref[...] = values
        taps[1 : rows + 1] = columns(values.astype(F32), True)
        sums_ref[...] = side_by_side(conv_rows(taps, weight_ref, rows, True)).astype(BF16)


def back_conv(parts, weight, alongs, row, rows, after=()):
    pairs, _, width, double = parts[0].shape
    depth = double // 2
    wide = weight.shape[2]
    cells = rows * width
    slots = 2 * pairs
    outs = [
        jax.ShapeDtypeStruct((rows, width, depth), BF16),
        jax.ShapeDtypeStruct((cells // 2, 2 * wide), BF16),
    ]
    made, token = run(
        functools.partial(back_kernel, slots, len(parts)),
        "back_conv",
        outs * slots + alongs[:1],
        [row],
        [*parts, weight, *alongs],
        after,
        [
            pltpu.VMEM((rows, width, double), BF16),
            pltpu.VMEM((rows + 2, width, 3 * depth), BF16),
        ],
        14,
        18 * slots * cells * depth * wide,
    )
    return [(made[2 * at], made[2 * at + 1]) for at in range(slots)], made[-1], token


def hidden_kernel(terms, count, *refs):
    group_ref, basis_ref = refs[terms : terms + 2]
    pay_ref, unit_ref, scale_ref, along_ref = refs[-4:]
    wide = unit_ref.shape[1]
    rank = basis_ref.shape[1] // 2
    total = refs[0][...].astype(F32)
    for term in refs[1:terms]:
        total = total + term[...].astype(F32)
    unit, scale = normalized(total[:, :wide], group_ref[...], count)
    unit_ref[...] = unit
    scale_ref[...] = scale
    hidden = silu(unit).astype(BF16)
    pay_ref[...] = jnp.concatenate([hidden.astype(F32), total[:, wide:]], axis=1).astype(BF16)
    along = jnp.dot(hidden, basis_ref[...], preferred_element_type=F32)
    along_ref[...] = side_by_side(along[:, :rank] + along[:, rank:]).astype(BF16)


def hidden_step(terms, same_group, basis, count, after=()):
    cells, both = terms[0].shape
    wide = same_group.shape[0]
    return run(
        functools.partial(hidden_kernel, len(terms), count),
        "hidden_step",
        [
            jax.ShapeDtypeStruct((cells, both), BF16),
            jax.ShapeDtypeStruct((cells, wide), F32),
            jax.ShapeDtypeStruct((1, wide), F32),
            jax.ShapeDtypeStruct((cells // 2, basis.shape[1]), BF16),
        ],
        [],
        [*terms, same_group, basis],
        after,
        held=12,
        flops=40 * cells * wide,
    )


def second_kernel(slots, bands, at_ref, *refs):
    pays = refs[:slots]
    weight_ref, along_ref, other_ref = refs[slots : slots + 3]
    later_ref, whole, taps = refs[-3:]
    outs = refs[-3 - bands : -3]
    add_into(later_ref, along_ref, other_ref)
    band, width, double = outs[0].shape[1:]
    rows = whole.shape[0]
    depth = taps.shape[2] // 3
    wide = double // 2
    clear_edges(taps)
    for slot in range(slots):
        hidden = pays[slot][:, :depth].astype(F32).reshape(rows, width, depth)
        taps[1 : rows + 1] = columns(hidden, False)
        whole[...] = conv_rows(taps, weight_ref, rows, False).reshape(rows, width, wide)
        lanes = slice(slot % 2 * wide, (slot % 2 + 1) * wide)
        for away in range(bands):
            start = jnp.bitwise_xor(at_ref[0], away) * band
            outs[away][slot // 2, :, :, lanes] = whole[pl.ds(start, band)].astype(BF16)


def second_conv(pays, weight, alongs, row, rows, bands, after=()):
    slots = len(pays)
    cells, _ = pays[0].shape
    width = cells // rows
    depth = weight.shape[1] // 3
    wide = weight.shape[2]
    out = jax.ShapeDtypeStruct((slots // 2, rows // bands, width, 2 * wide), BF16)
    return run(
        functools.partial(second_kernel, slots, bands),
        "second_conv",
        [out] * bands + alongs[:1],
        [row],
        [*pays, weight, *alongs],
        after,
        [
            pltpu.VMEM((rows, width, wide), F32),
            pltpu.VMEM((rows + 2, width, 3 * depth), BF16),
        ],
        14,
        18 * slots * cells * depth * wide,
    )


def band_kernel(terms, slots, *refs):
    outs = refs[-slots:]
    wide = outs[0].shape[-1]
    total = refs[0][...].astype(F32)
    for term in refs[1:terms]:
        total = total + term[...].astype(F32)
    for slot, out in enumerate(outs):
        lanes = slice(slot % 2 * wide, (slot % 2 + 1) * wide)
        out[...] = total[slot // 2, :, :, lanes].astype(BF16)


def band_step(terms, after=()):
    pairs, band, width, double = terms[0].shape
    out = jax.ShapeDtypeStruct((band, width, double // 2), BF16)
    return run(
        functools.partial(band_kernel, len(terms), 2 * pairs),
        "band_step",
        [out] * (2 * pairs),
        [],
        terms,
        after,
    )


def join_kernel(blocks, at_ref, x_ref, *refs):
    out = refs[-1]
    width = x_ref.shape[-1] // blocks
    for away in range(blocks):
        for block in range(blocks):

            @pl.when(jnp.bitwise_xor(at_ref[0], away) == block)
            def _(away=away, block=block):
                lanes = slice(block * width, (block + 1) * width)
                added = x_ref[:, :, lanes].astype(F32) + refs[away][...].astype(F32)
                out[:, :, lanes] = added.astype(BF16)


def join_blocks(x, parts, chip, after=()):
    return run(
        functools.partial(join_kernel, len(parts)),
        "join_blocks",
        [x],
        [chip],
        [x, *parts],
        after,
    )


def pre_kernel(terms, count, *refs):
    unit_ref, scale_ref, group_ref, along_ref, other_ref = refs[terms : terms + 5]
    out_ref, later_ref = refs[-2:]
    later_ref[0] = along_ref[...]
    later_ref[1] = other_ref[...]
    total = refs[0][...].astype(F32)
    for term in refs[1:terms]:
        total = total + term[...].astype(F32)
    unit = unit_ref[...]
    gate = 0.5 + 0.5 * jnp.tanh(0.5 * unit)
    grad = stacked_again(total) * (gate * (1.0 + unit * (1.0 - gate)))
    mean = group_sums(jnp.sum(grad, axis=0, keepdims=True), group_ref[...]) / count
    along = group_sums(jnp.sum(grad * unit, axis=0, keepdims=True), group_ref[...]) / count
    out_ref[...] = side_by_side(scale_ref[...] * (grad - mean - unit * along)).astype(BF16)


def pre_step(terms, unit, scale, same_group, alongs, count, after=()):
    cells, wide = unit.shape
    stacked = jax.ShapeDtypeStruct((2, *alongs[0].shape), BF16)
    return run(
        functools.partial(pre_kernel, len(terms), count),
        "pre_step",
        [jax.ShapeDtypeStruct((cells // 2, 2 * wide), BF16), stacked],
        [],
        [*terms, unit, scale, same_group, *alongs],
        after,
        held=12,
        flops=40 * cells * wide,
    )


def project(values, along, basis):
    both = jnp.concatenate([along, along], axis=1)
    return values - jnp.dot(both, basis, preferred_element_type=F32)


def grad_body(core_ref, left, left_t, taps, keep_ref, send_ref, width, flip):
    half = left.shape[1] // 2
    span = left.shape[0]
    wide = taps.shape[1] // 3
    turned = left[...].T

    @pl.when(core_ref[0] == 0)
    def _():
        left_t[...] = turned

    @pl.when(core_ref[0] != 0)
    def _():
        left_t[:half] = turned[half:]
        left_t[half:] = turned[:half]

    for tap in range(3):
        window = taps[tap * width : tap * width + span]
        result = jnp.dot(left_t[...], window, preferred_element_type=F32)
        first = 3 * (2 - tap if flip else tap)
        for q in range(3):
            lanes = slice(q * wide, (q + 1) * wide)
            keep_ref[first + q] = result[:half, lanes]
            send_ref[first + q] = result[half:, lanes].astype(BF16)


def fill_taps(taps, slot, rows, width, value):
    start = (slot * (rows + 1) + 1) * width
    taps[start : start + rows * width] = value.reshape(rows * width, value.shape[2])


def clear_gaps(left, taps, slots, rows, width):
    gap = rows + 1
    for slot in range(slots + 1):
        begin = slot * gap * width
        end = taps.shape[0] if slot == slots else begin + width
        taps[begin:end] = jnp.zeros((end - begin, taps.shape[1]), taps.dtype)
    for slot in range(slots):
        begin = (slot * gap + rows) * width
        end = left.shape[0] if slot == slots - 1 else begin + width
        left[begin:end] = jnp.zeros((end - begin, left.shape[1]), left.dtype)


def first_grad_kernel(slots, core_ref, *refs):
    acts, pays, grads = (refs[at * slots : (at + 1) * slots] for at in range(3))
    basis_ref = refs[3 * slots]
    keep_ref, send_ref, left, left_t, taps = refs[-5:]
    rows, width, depth = acts[0].shape
    cells = rows * width
    rank = basis_ref.shape[0] // 2
    wide = taps.shape[1] // 3
    clear_gaps(left, taps, slots, rows, width)
    for slot in range(slots):
        values = acts[slot][...].reshape(cells, depth).astype(F32)
        along = pays[slot][:, wide : wide + rank]
        begin = slot * (rows + 1) * width
        left[begin : begin + cells] = project(values, along, basis_ref[...]).astype(BF16)
        right = stacked_again(grads[slot][...].astype(F32)).reshape(rows, width, wide)
        fill_taps(taps, slot, rows, width, columns(right, True))
    grad_body(core_ref, left, left_t, taps, keep_ref, send_ref, width, True)


def second_grad_kernel(slots, core_ref, *refs):
    cots, pays = (refs[at * slots : (at + 1) * slots] for at in range(2))
    alongs = refs[2 * slots : 2 * slots + slots // 2]
    basis_ref = refs[2 * slots + slots // 2]
    keep_ref, send_ref, left, left_t, taps = refs[-5:]
    rows, width, depth = cots[0].shape
    cells = rows * width
    rank = basis_ref.shape[0] // 2
    wide = taps.shape[1] // 3
    clear_gaps(left, taps, slots, rows, width)
    for slot in range(slots):
        begin = slot * (rows + 1) * width
        left[begin : begin + cells] = cots[slot][...].reshape(cells, depth)
        packed = alongs[slot // 2][slot % 2]
        along = jnp.concatenate([packed[:, :rank], packed[:, rank:]], axis=0)
        values = pays[slot][:, :wide].astype(F32)
        right = project(values, along, basis_ref[...]).astype(BF16).astype(F32)
        fill_taps(taps, slot, rows, width, columns(right.reshape(rows, width, wide), False))
    grad_body(core_ref, left, left_t, taps, keep_ref, send_ref, width, False)


def weight_grad(kernel, name, core, lefts, firsts, seconds, basis, wide, after=()):
    slots = len(firsts)
    rows, width, depth = lefts[0].shape
    used = slots * (rows + 1) * width
    span = -(-used // 128) * 128
    half = depth // 2
    tap_rows = 2 * width + span
    return run(
        functools.partial(kernel, slots),
        name,
        [
            jax.ShapeDtypeStruct((9, half, wide), F32),
            jax.ShapeDtypeStruct((9, half, wide), BF16),
        ],
        [core],
        [*lefts, *firsts, *seconds, basis],
        after,
        [
            pltpu.VMEM((span, depth), BF16),
            pltpu.VMEM((depth, span), BF16),
            pltpu.VMEM((tap_rows, 3 * wide), BF16),
        ],
        28,
        18 * slots * rows * width * depth * wide,
    )


def halves_kernel(turn, core_ref, own_ref, other_ref, *refs):
    outs = refs[-2:] if turn else refs[-1:]
    half = own_ref.shape[1]

    @pl.when(core_ref[0] == 0)
    def _():
        outs[0][:, :half] = own_ref[...]
        outs[0][:, half:] = other_ref[...]

    @pl.when(core_ref[0] != 0)
    def _():
        outs[0][:, :half] = other_ref[...]
        outs[0][:, half:] = own_ref[...]

    if turn:
        for tap in range(9):
            outs[1][tap] = outs[0][tap].T


def join_halves(core, own, other, turn, after=()):
    _, half, wide = own.shape
    outs = [jax.ShapeDtypeStruct((9, 2 * half, wide), BF16)]
    if turn:
        outs.append(jax.ShapeDtypeStruct((9, wide, 2 * half), BF16))
    return run(
        functools.partial(halves_kernel, turn), "join_halves", outs, [core], [own, other], after,
        held=12,
    )


def basis_kernel(blocks, at_ref, basis_ref, *refs):
    rows_ref, columns_ref = refs[-2:]
    rank, channels = basis_ref.shape
    width = channels // blocks
    for block in range(blocks):

        @pl.when(at_ref[0] == block)
        def _(block=block):
            values = basis_ref[:, block * width : (block + 1) * width]
            high = values.astype(BF16).astype(F32)
            both = jnp.concatenate([high, values - high], axis=0)
            rows_ref[...] = both.astype(BF16)
            columns_ref[...] = both.T.astype(BF16)


def basis_parts(at, basis, blocks, after=()):
    rank, channels = basis.shape
    width = channels // blocks
    return run(
        functools.partial(basis_kernel, blocks),
        "basis_parts",
        [
            jax.ShapeDtypeStruct((2 * rank, width), BF16),
            jax.ShapeDtypeStruct((width, 2 * rank), BF16),
        ],
        [at],
        [basis],
        after,
    )


def flat_kernel(scale, keep_ref, got_ref, *refs):
    held = refs[-2 * (keep_ref.shape[2] // 128) - 2 :]
    out_ref = refs[-len(held) - 1]
    taps, half, wide = keep_ref.shape
    whole = wide // 128
    step = 2 * whole + 1
    count = half // 2
    zeros = jnp.zeros((half, 64), F32)
    for tap in range(taps):
        total = (keep_ref[tap] + got_ref[tap].astype(F32)) * scale
        for at in range(whole):
            held[at][...] = total[:, 128 * at : 128 * (at + 1)]
            held[whole + 2 + at][...] = total[:, 128 * at + 64 : 128 * (at + 1) + 64]
        held[whole][...] = jnp.concatenate([total[:, 128 * whole :], zeros], axis=1)
        held[whole + 1][...] = jnp.concatenate([zeros, total[:, :64]], axis=1)
        even, odd = pl.ds(0, count, stride=2), pl.ds(1, count, stride=2)
        rows = [held[at][even, :] for at in range(whole)]
        rows.append(held[whole][even, :] + held[whole + 1][odd, :])
        rows += [held[whole + 2 + at][odd, :] for at in range(whole)]
        for at, row in enumerate(rows):
            out_ref[pl.ds(tap * count * step + at, count, stride=step), :] = row


def flat_grad(keep, got, scale, after=()):
    taps, half, wide = keep.shape
    if wide % 128 != 64 or half % 2:
        made = (keep + got.astype(F32)) * scale
        return made, made
    (made,), token = run(
        functools.partial(flat_kernel, scale),
        "flat_grad",
        [jax.ShapeDtypeStruct((taps * half * wide // 128, 128), F32)],
        [],
        [keep, got],
        after,
        scratch=[pltpu.VMEM((half, 128), F32)] * (2 * (wide // 128) + 2),
        held=12,
    )
    return made, token


def same_groups(width, size):
    at = np.arange(width) // size
    return jnp.asarray((at[:, None] == at[None, :]).astype(np.float32), BF16)


def body(images, cotangent, first_weight, second_weight, first_basis, second_basis):
    n_dp = lax.axis_size("dp")
    n_rows = lax.axis_size("rows")
    chips = n_dp // 2
    _, band, width, channels = images.shape
    rows = band * n_rows
    dp_width = channels // n_dp
    chip_width = channels // chips
    row_width = channels // n_rows
    group = channels // GROUPS
    count = float(rows * width * group)
    grad_scale = 1.0 / math.sqrt(n_dp * images.shape[0] * rows * width)

    at_dp = lax.axis_index("dp")
    at_row = lax.axis_index("rows")
    chip = (at_dp // 2).astype(jnp.int32)
    core = (at_dp % 2).astype(jnp.int32)
    row = at_row.astype(jnp.int32)
    chip_at, core_at = chip[None], core[None]
    row_at = jnp.stack([row, (row + 1) // 2 % 2])

    def to_core(x):
        return lax.ppermute(x, "dp", [(i, i ^ 1) for i in range(n_dp)])

    def to_chip(x, away):
        return lax.ppermute(x, "dp", [(i, i ^ (2 * away)) for i in range(n_dp)])

    def to_row(x, away):
        return lax.ppermute(x, "rows", [(i, i ^ away) for i in range(n_rows)])

    def chips_gather(x):
        return [x] + [to_chip(x, away) for away in range(1, chips)]

    def rows_gather(x):
        if n_rows != 4:
            return [x] + [to_row(x, away) for away in range(1, n_rows)], [
                (away, -1) for away in range(n_rows)
            ]
        second = to_row(x, 2)
        first = to_row(x, 1)
        passed = lax.ppermute(second, "rows", [(2, 3), (1, 0)])
        later, _ = lax.optimization_barrier((x, second))
        middle = lax.ppermute(later, "rows", [(1, 2), (2, 1)])
        return [x, first, second, middle, passed], [(0, -1), (1, -1), (2, -1), (3, 1), (3, 0)]

    def chips_swap(parts):
        return [parts[0]] + [to_chip(parts[away], away) for away in range(1, chips)]

    def rows_swap(parts):
        far = [to_row(parts[away], away) for away in range(n_rows - 1, 0, -1)]
        return parts[:1] + far[::-1]

    chip_groups = same_groups(chip_width, group)
    row_groups = same_groups(row_width, group)

    slots = chips_swap(split_blocks([images[0], cotangent[0]], chips, chip_at))
    image_pack, _ = pack_slots(slots, 0)
    image_parts, places = rows_gather(image_pack)

    first_weight, second_weight, _ = lax.optimization_barrier(
        (first_weight, second_weight, slots[1])
    )
    own_first = first_weight.reshape(9, dp_width, row_width)
    own_second = second_weight.reshape(9, dp_width, row_width)
    early = tuple(image_parts[1:3])
    (second_full, second_turned), second_done = join_halves(
        core_at, own_second, to_core(own_second), True, early
    )
    (one_rows, one_columns), one_done = basis_parts(chip_at, first_basis, chips, early)
    (two_rows, two_columns), two_done = basis_parts(row_at, second_basis, n_rows, early)
    (first_full,), first_done = join_halves(core_at, own_first, to_core(own_first), False, early)
    cot_pack, cot_done = pack_slots(
        slots, 1, (*image_parts[3:], one_done, two_done, first_done, second_done)
    )
    cot_parts = [cot_pack] + [to_row(cot_pack, away) for away in range(1, n_rows)]
    weight_one = first_full.reshape(3, 3 * chip_width, row_width)
    weight_back = second_full.reshape(3, 3 * chip_width, row_width)
    weight_two = second_turned.reshape(3, 3 * row_width, chip_width)

    made, first_terms, done = {}, {}, (cot_done,)
    for slot in range(chips - 1, -1, -1):
        if slot == 0:
            done += (first_terms[chips - 1], *cot_parts[2:])
        ((active, sums),), token = first_conv(
            image_parts, places, [slot], weight_one, chip_groups, one_columns, row_at, rows, count,
            done,
        )
        made[slot] = active
        first_terms[slot] = to_chip(sums, slot) if slot else sums
        done = (token,)
    active = [made[slot] for slot in range(chips)]
    first_terms = [first_terms[slot] for slot in range(chips)]

    (pay, unit, scale, along), hidden_done = hidden_step(
        first_terms, row_groups, two_columns, count, tuple(cot_parts[1:2])
    )
    pays = chips_gather(pay)

    away = 4
    while away < n_rows:
        along = (along.astype(F32) + to_row(along, away).astype(F32)).astype(BF16)
        away *= 2
    back, along, back_done = back_conv(
        cot_parts, weight_back, [along, to_row(along, 1)], row_at, rows, (hidden_done,)
    )
    whole_cot = [pair[0] for pair in back]
    back_terms = chips_swap([pair[1] for pair in back])

    (*sums, along), sums_done = second_conv(
        pays, weight_two, [along, to_row(along, 2)], row_at, rows, n_rows, (back_done,)
    )
    band_terms = rows_swap(sums)

    (pre_grad, along), pre_done = pre_step(
        back_terms, unit, scale, row_groups, [along, to_chip(along, 1)], count,
        (sums_done, band_terms[-1]),
    )
    pre_grads = chips_gather(pre_grad)
    alongs = [along]
    away = 2
    while away < chips:
        alongs += [to_chip(part, away) for part in alongs]
        away *= 2

    second_halves, second_made = weight_grad(
        second_grad_kernel, "second_grad", core_at, whole_cot, pays, alongs, two_rows,
        row_width, (pre_done,),
    )
    blocks, blocks_done = band_step(band_terms, (second_made,))
    first_halves, _ = weight_grad(
        first_grad_kernel, "first_grad", core_at, active, pays, pre_grads, one_rows,
        row_width, (blocks_done,),
    )
    second_grad, flat_done = flat_grad(
        second_halves[0], to_core(second_halves[1]), grad_scale
    )
    (block_output,), output_done = join_blocks(
        images[0], chips_swap(blocks), chip_at, (flat_done,)
    )
    first_grad, _ = flat_grad(
        first_halves[0], to_core(first_halves[1]), grad_scale, (output_done,)
    )
    block_output = block_output[None]
    first_grad = first_grad.reshape(1, 1, 9, dp_width * row_width)
    second_grad = second_grad.reshape(1, 1, 9, dp_width * row_width)
    return (block_output, first_grad, second_grad)


def solution(mesh):
    split = P("dp", "rows", None, None)
    return jax.shard_map(
        body,
        mesh=mesh,
        in_specs=(split, split, split, split, P(), P()),
        out_specs=(split, split, split),
        check_vma=False,
    )
```

```python
import functools
import math

import jax
import jax.numpy as jnp
import numpy as np
from jax import lax
from jax.experimental import pallas as pl
from jax.experimental.pallas import tpu as pltpu
from jax.sharding import PartitionSpec as P

GROUPS = 32
EPS = 1e-5
MIB = 1024 * 1024
F32 = jnp.float32
BF16 = jnp.bfloat16


def smem():
    return pl.BlockSpec(memory_space=pltpu.SMEM)


def unread(after):
    return [pl.BlockSpec(memory_space=pltpu.VMEM)] * len(after)


def run(kernel, name, outs, scalars, arrays, after=(), scratch=(), held=8, flops=0, fetch=False):
    outs = [*outs, jax.ShapeDtypeStruct((8, 128), F32)]
    moved = sum(x.size * x.dtype.itemsize for x in list(arrays) + outs)
    held_there = pl.BlockSpec(memory_space=pltpu.VMEM)
    used = len(scalars) + len(arrays)
    token_at = used + len(after) + len(outs) - 1

    def whole(*refs):
        refs[token_at][...] = jnp.zeros((8, 128), F32)
        kernel(*refs[:used], *refs[used + len(after) : token_at], *refs[token_at + 1 :])

    *made, token = pl.pallas_call(
        whole,
        out_shape=outs,
        in_specs=[smem()] * len(scalars)
        + [pl.BlockSpec(memory_space=pl.ANY) if fetch else held_there for x in arrays]
        + unread(after),
        out_specs=[held_there] * len(outs),
        scratch_shapes=list(scratch),
        compiler_params=pltpu.CompilerParams(vmem_limit_bytes=held * MIB),
        cost_estimate=cost(flops, moved),
        name=name,
    )(*scalars, *arrays, *after)
    return made, token


def cost(flops, moved):
    return pl.CostEstimate(flops=int(flops), bytes_accessed=int(moved), transcendentals=0)


def group_sums(row, same_group):
    high = row.astype(BF16).astype(F32)
    rest = row - high
    middle = rest.astype(BF16).astype(F32)
    low = rest - middle
    at = lax.broadcasted_iota(jnp.int32, (16, row.shape[1]), 0)
    stacked = jnp.where(at == 0, high, jnp.where(at == 1, middle, jnp.where(at == 2, low, 0.0)))
    sums = jnp.dot(stacked.astype(BF16), same_group, preferred_element_type=F32)
    return jnp.sum(sums, axis=0, keepdims=True)


def normalized(values, same_group, count):
    center = group_sums(jnp.sum(values, axis=0, keepdims=True), same_group) / count
    moved = values - center
    spread = group_sums(jnp.sum(moved * moved, axis=0, keepdims=True), same_group) / count
    scale = 1.0 / jnp.sqrt(spread + EPS)
    return moved * scale, scale


def silu(unit):
    half = 0.5 * unit
    return half + half * jnp.tanh(half)


def add_into(out_ref, one_ref, other_ref):
    out_ref[...] = (one_ref[...].astype(F32) + other_ref[...].astype(F32)).astype(BF16)


def columns(values, flip):
    width = values.shape[1]
    at = lax.broadcasted_iota(jnp.int32, values.shape, 1)
    before = jnp.where(at == 0, 0.0, pltpu.roll(values, 1, axis=1))
    after = jnp.where(at == width - 1, 0.0, pltpu.roll(values, width - 1, axis=1))
    parts = [after, values, before] if flip else [before, values, after]
    return jnp.concatenate([part.astype(BF16) for part in parts], axis=2)


def conv_rows(taps, weight_ref, total, rows, flip):
    _, width, depth = taps.shape
    total[...] = jnp.zeros(total.shape, F32)

    @pl.loop(0, 3)
    def _(tap):
        window = taps[pl.ds(tap, rows)].reshape(rows * width, depth)
        weight = weight_ref[2 - tap if flip else tap]
        total[...] += jnp.dot(window, weight, preferred_element_type=F32)

    return total[...]


def side_by_side(values):
    half = values.shape[0] // 2
    return jnp.concatenate([values[:half], values[half:]], axis=1)


def stacked_again(values):
    half = values.shape[1] // 2
    return jnp.concatenate([values[:, :half], values[:, half:]], axis=0)


def clear_edges(taps):
    rows = taps.shape[0]
    taps[0:1] = jnp.zeros((1,) + taps.shape[1:], taps.dtype)
    taps[rows - 1 : rows] = jnp.zeros((1,) + taps.shape[1:], taps.dtype)


def split_kernel(blocks, arrays, at_ref, *refs):
    sources, outs = refs[:arrays], refs[arrays : arrays + blocks]
    held, arrived = refs[-2:]
    width = outs[0].shape[-1] // arrays
    copies = [
        pltpu.make_async_copy(source, held.at[at], arrived.at[at])
        for at, source in enumerate(sources)
    ]
    for copy in copies:
        copy.start()
    for at, copy in enumerate(copies):
        copy.wait()
        lanes = slice(at * width, (at + 1) * width)
        for away in range(blocks):
            for block in range(blocks):

                @pl.when(jnp.bitwise_xor(at_ref[0], away) == block)
                def _(away=away, block=block):
                    values = held[at, :, :, block * width : (block + 1) * width]
                    outs[away][:, :, lanes] = values


def split_blocks(arrays, blocks, chip):
    height, width, channels = arrays[0].shape
    shape = jax.ShapeDtypeStruct((height, width, len(arrays) * channels // blocks), BF16)
    made, _ = run(
        functools.partial(split_kernel, blocks, len(arrays)),
        "split_blocks",
        [shape] * blocks,
        [chip],
        arrays,
        scratch=[
            pltpu.VMEM((len(arrays), height, width, channels), BF16),
            pltpu.SemaphoreType.DMA((len(arrays),)),
        ],
        fetch=True,
    )
    return made


def pack_kernel(at, *refs):
    slots, out = refs[:-1], refs[-1]
    width = slots[0].shape[-1] // 2
    for slot, ref in enumerate(slots):
        lanes = slice(slot % 2 * width, (slot % 2 + 1) * width)
        out[slot // 2, :, :, lanes] = ref[:, :, at * width : (at + 1) * width]


def pack_slots(slots, at, after=()):
    out = jax.ShapeDtypeStruct((len(slots) // 2, *slots[0].shape), BF16)
    (packed,), token = run(
        functools.partial(pack_kernel, at), "pack_slots", [out], [], slots, after
    )
    return packed, token


def assemble(whole, parts, places, pair, at_ref):
    for part, (away, who) in zip(parts, places):

        @pl.when(jnp.logical_or(who < 0, at_ref[1] == who))
        def _(part=part, away=away):
            band = part.shape[1]
            whole[pl.ds(jnp.bitwise_xor(at_ref[0], away) * band, band)] = part[pair]


def first_kernel(slots, places, count, at_ref, *refs):
    parts = refs[: len(places)]
    weight_ref, group_ref, basis_ref = refs[len(places) : len(places) + 3]
    whole, taps, total_ref = refs[-3:]
    outs = refs[-3 - 2 * len(slots) : -3]
    rows, width, depth = outs[0].shape
    rank = basis_ref.shape[1] // 2
    cells = rows * width
    clear_edges(taps)
    held = None
    for at, slot in enumerate(slots):
        act_ref, sums_ref = outs[2 * at : 2 * at + 2]
        if slot // 2 != held:
            held = slot // 2
            assemble(whole, parts, places, held, at_ref)
        half = slot % 2
        values = whole[:, :, half * depth : (half + 1) * depth].astype(F32)
        unit, _ = normalized(values.reshape(cells, depth), group_ref[...], count)
        active = silu(unit).astype(BF16)
        act_ref[...] = active.reshape(act_ref.shape)
        taps[1 : rows + 1] = columns(active.astype(F32).reshape(act_ref.shape), False)
        total = conv_rows(taps, weight_ref, total_ref, rows, False)
        along = jnp.dot(active, basis_ref[...], preferred_element_type=F32)
        along = along[:, :rank] + along[:, rank:]
        sums_ref[...] = jnp.concatenate([total, along], axis=1).astype(BF16)


def first_conv(parts, places, slots, weight, same_group, basis, row, rows, count, after=()):
    _, band, width, double = parts[0].shape
    depth = double // 2
    rank = basis.shape[1] // 2
    wide = weight.shape[2]
    cells = rows * width
    outs = [
        jax.ShapeDtypeStruct((rows, width, depth), BF16),
        jax.ShapeDtypeStruct((cells, wide + rank), BF16),
    ]
    made, token = run(
        functools.partial(first_kernel, slots, places, count),
        "first_conv",
        outs * len(slots),
        [row],
        [*parts, weight, same_group, basis],
        after,
        [
            pltpu.VMEM((rows, width, double), BF16),
            pltpu.VMEM((rows + 2, width, 3 * depth), BF16),
            pltpu.VMEM((cells, wide), F32),
        ],
        14,
        18 * len(slots) * cells * depth * wide,
    )
    return [(made[2 * at], made[2 * at + 1]) for at in range(len(slots))], token


def back_kernel(slots, bands, at_ref, *refs):
    parts = refs[:bands]
    weight_ref, along_ref, other_ref = refs[bands : bands + 3]
    later_ref, whole, taps, total_ref = refs[-4:]
    outs = refs[-4 - 2 * slots : -4]
    add_into(later_ref, along_ref, other_ref)
    rows, width, depth = outs[0].shape
    places = [(away, -1) for away in range(bands)]
    clear_edges(taps)
    for slot in reversed(range(slots)):
        cot_ref, sums_ref = outs[2 * slot : 2 * slot + 2]
        if slot % 2:
            assemble(whole, parts, places, slot // 2, at_ref)
        half = slot % 2
        values = whole[:, :, half * depth : (half + 1) * depth]
        cot_ref[...] = values
        taps[1 : rows + 1] = columns(values.astype(F32), True)
        total = conv_rows(taps, weight_ref, total_ref, rows, True)
        sums_ref[...] = side_by_side(total).astype(BF16)


def back_conv(parts, weight, alongs, row, rows, after=()):
    pairs, _, width, double = parts[0].shape
    depth = double // 2
    wide = weight.shape[2]
    cells = rows * width
    slots = 2 * pairs
    outs = [
        jax.ShapeDtypeStruct((rows, width, depth), BF16),
        jax.ShapeDtypeStruct((cells // 2, 2 * wide), BF16),
    ]
    made, token = run(
        functools.partial(back_kernel, slots, len(parts)),
        "back_conv",
        outs * slots + alongs[:1],
        [row],
        [*parts, weight, *alongs],
        after,
        [
            pltpu.VMEM((rows, width, double), BF16),
            pltpu.VMEM((rows + 2, width, 3 * depth), BF16),
            pltpu.VMEM((cells, wide), F32),
        ],
        14,
        18 * slots * cells * depth * wide,
    )
    return [(made[2 * at], made[2 * at + 1]) for at in range(slots)], made[-1], token


def hidden_kernel(terms, count, *refs):
    group_ref, basis_ref = refs[terms : terms + 2]
    pay_ref, unit_ref, scale_ref, along_ref = refs[-4:]
    wide = unit_ref.shape[1]
    rank = basis_ref.shape[1] // 2
    total = refs[0][...].astype(F32)
    for term in refs[1:terms]:
        total = total + term[...].astype(F32)
    unit, scale = normalized(total[:, :wide], group_ref[...], count)
    unit_ref[...] = unit
    scale_ref[...] = scale
    hidden = silu(unit).astype(BF16)
    pay_ref[...] = jnp.concatenate([hidden.astype(F32), total[:, wide:]], axis=1).astype(BF16)
    along = jnp.dot(hidden, basis_ref[...], preferred_element_type=F32)
    along_ref[...] = side_by_side(along[:, :rank] + along[:, rank:]).astype(BF16)


def hidden_step(terms, same_group, basis, count, after=()):
    cells, both = terms[0].shape
    wide = same_group.shape[0]
    return run(
        functools.partial(hidden_kernel, len(terms), count),
        "hidden_step",
        [
            jax.ShapeDtypeStruct((cells, both), BF16),
            jax.ShapeDtypeStruct((cells, wide), F32),
            jax.ShapeDtypeStruct((1, wide), F32),
            jax.ShapeDtypeStruct((cells // 2, basis.shape[1]), BF16),
        ],
        [],
        [*terms, same_group, basis],
        after,
        held=12,
        flops=40 * cells * wide,
    )


def second_kernel(slots, bands, at_ref, *refs):
    pays = refs[:slots]
    weight_ref, along_ref, other_ref = refs[slots : slots + 3]
    later_ref, whole, taps, total_ref = refs[-4:]
    outs = refs[-4 - bands : -4]
    add_into(later_ref, along_ref, other_ref)
    band, width, double = outs[0].shape[1:]
    rows = whole.shape[0]
    depth = taps.shape[2] // 3
    wide = double // 2
    clear_edges(taps)
    for slot in range(slots):
        hidden = pays[slot][:, :depth].astype(F32).reshape(rows, width, depth)
        taps[1 : rows + 1] = columns(hidden, False)
        total = conv_rows(taps, weight_ref, total_ref, rows, False)
        whole[...] = total.reshape(rows, width, wide)
        lanes = slice(slot % 2 * wide, (slot % 2 + 1) * wide)
        for away in range(bands):
            start = jnp.bitwise_xor(at_ref[0], away) * band
            outs[away][slot // 2, :, :, lanes] = whole[pl.ds(start, band)].astype(BF16)


def second_conv(pays, weight, alongs, row, rows, bands, after=()):
    slots = len(pays)
    cells, _ = pays[0].shape
    width = cells // rows
    depth = weight.shape[1] // 3
    wide = weight.shape[2]
    out = jax.ShapeDtypeStruct((slots // 2, rows // bands, width, 2 * wide), BF16)
    return run(
        functools.partial(second_kernel, slots, bands),
        "second_conv",
        [out] * bands + alongs[:1],
        [row],
        [*pays, weight, *alongs],
        after,
        [
            pltpu.VMEM((rows, width, wide), F32),
            pltpu.VMEM((rows + 2, width, 3 * depth), BF16),
            pltpu.VMEM((cells, wide), F32),
        ],
        14,
        18 * slots * cells * depth * wide,
    )


def band_kernel(terms, slots, *refs):
    outs = refs[-slots:]
    wide = outs[0].shape[-1]
    total = refs[0][...].astype(F32)
    for term in refs[1:terms]:
        total = total + term[...].astype(F32)
    for slot, out in enumerate(outs):
        lanes = slice(slot % 2 * wide, (slot % 2 + 1) * wide)
        out[...] = total[slot // 2, :, :, lanes].astype(BF16)


def band_step(terms, after=()):
    pairs, band, width, double = terms[0].shape
    out = jax.ShapeDtypeStruct((band, width, double // 2), BF16)
    return run(
        functools.partial(band_kernel, len(terms), 2 * pairs),
        "band_step",
        [out] * (2 * pairs),
        [],
        terms,
        after,
    )


def join_kernel(blocks, at_ref, x_ref, *refs):
    out = refs[-1]
    width = x_ref.shape[-1] // blocks
    for away in range(blocks):
        for block in range(blocks):

            @pl.when(jnp.bitwise_xor(at_ref[0], away) == block)
            def _(away=away, block=block):
                lanes = slice(block * width, (block + 1) * width)
                added = x_ref[:, :, lanes].astype(F32) + refs[away][...].astype(F32)
                out[:, :, lanes] = added.astype(BF16)


def join_blocks(x, parts, chip, after=()):
    return run(
        functools.partial(join_kernel, len(parts)),
        "join_blocks",
        [x],
        [chip],
        [x, *parts],
        after,
    )


def pre_kernel(terms, count, *refs):
    unit_ref, scale_ref, group_ref, along_ref, other_ref = refs[terms : terms + 5]
    out_ref, later_ref = refs[-2:]
    later_ref[0] = along_ref[...]
    later_ref[1] = other_ref[...]
    total = refs[0][...].astype(F32)
    for term in refs[1:terms]:
        total = total + term[...].astype(F32)
    unit = unit_ref[...]
    gate = 0.5 + 0.5 * jnp.tanh(0.5 * unit)
    grad = stacked_again(total) * (gate * (1.0 + unit * (1.0 - gate)))
    mean = group_sums(jnp.sum(grad, axis=0, keepdims=True), group_ref[...]) / count
    along = group_sums(jnp.sum(grad * unit, axis=0, keepdims=True), group_ref[...]) / count
    out_ref[...] = side_by_side(scale_ref[...] * (grad - mean - unit * along)).astype(BF16)


def pre_step(terms, unit, scale, same_group, alongs, count, after=()):
    cells, wide = unit.shape
    stacked = jax.ShapeDtypeStruct((2, *alongs[0].shape), BF16)
    return run(
        functools.partial(pre_kernel, len(terms), count),
        "pre_step",
        [jax.ShapeDtypeStruct((cells // 2, 2 * wide), BF16), stacked],
        [],
        [*terms, unit, scale, same_group, *alongs],
        after,
        held=12,
        flops=40 * cells * wide,
    )


def project(values, along, basis):
    both = jnp.concatenate([along, along], axis=1)
    return values - jnp.dot(both, basis, preferred_element_type=F32)


def grad_body(core_ref, left, left_t, taps, keep_ref, send_ref, width, flip):
    half = left.shape[1] // 2
    span = left.shape[0]
    wide = taps.shape[1] // 3
    turned = left[...].T

    @pl.when(core_ref[0] == 0)
    def _():
        left_t[...] = turned

    @pl.when(core_ref[0] != 0)
    def _():
        left_t[:half] = turned[half:]
        left_t[half:] = turned[:half]

    @pl.loop(0, 3)
    def _(tap):
        window = taps[pl.ds(pl.multiple_of(tap * width, width), span)]
        result = jnp.dot(left_t[...], window, preferred_element_type=F32)
        first = 3 * (2 - tap if flip else tap)
        for q in range(3):
            lanes = slice(q * wide, (q + 1) * wide)
            keep_ref[first + q] = result[:half, lanes]
            send_ref[first + q] = result[half:, lanes].astype(BF16)


def fill_taps(taps, slot, rows, width, value):
    start = (slot * (rows + 1) + 1) * width
    taps[start : start + rows * width] = value.reshape(rows * width, value.shape[2])


def clear_gaps(left, taps, slots, rows, width):
    gap = rows + 1
    for slot in range(slots + 1):
        begin = slot * gap * width
        end = taps.shape[0] if slot == slots else begin + width
        taps[begin:end] = jnp.zeros((end - begin, taps.shape[1]), taps.dtype)
    for slot in range(slots):
        begin = (slot * gap + rows) * width
        end = left.shape[0] if slot == slots - 1 else begin + width
        left[begin:end] = jnp.zeros((end - begin, left.shape[1]), left.dtype)


def first_grad_kernel(slots, core_ref, *refs):
    acts, pays, grads = (refs[at * slots : (at + 1) * slots] for at in range(3))
    basis_ref = refs[3 * slots]
    keep_ref, send_ref, left, left_t, taps = refs[-5:]
    rows, width, depth = acts[0].shape
    cells = rows * width
    rank = basis_ref.shape[0] // 2
    wide = taps.shape[1] // 3
    clear_gaps(left, taps, slots, rows, width)
    for slot in range(slots):
        values = acts[slot][...].reshape(cells, depth).astype(F32)
        along = pays[slot][:, wide : wide + rank]
        begin = slot * (rows + 1) * width
        left[begin : begin + cells] = project(values, along, basis_ref[...]).astype(BF16)
        right = stacked_again(grads[slot][...].astype(F32)).reshape(rows, width, wide)
        fill_taps(taps, slot, rows, width, columns(right, True))
    grad_body(core_ref, left, left_t, taps, keep_ref, send_ref, width, True)


def second_grad_kernel(slots, core_ref, *refs):
    cots, pays = (refs[at * slots : (at + 1) * slots] for at in range(2))
    alongs = refs[2 * slots : 2 * slots + slots // 2]
    basis_ref = refs[2 * slots + slots // 2]
    keep_ref, send_ref, left, left_t, taps = refs[-5:]
    rows, width, depth = cots[0].shape
    cells = rows * width
    rank = basis_ref.shape[0] // 2
    wide = taps.shape[1] // 3
    clear_gaps(left, taps, slots, rows, width)
    for slot in range(slots):
        begin = slot * (rows + 1) * width
        left[begin : begin + cells] = cots[slot][...].reshape(cells, depth)
        packed = alongs[slot // 2][slot % 2]
        along = jnp.concatenate([packed[:, :rank], packed[:, rank:]], axis=0)
        values = pays[slot][:, :wide].astype(F32)
        right = project(values, along, basis_ref[...]).astype(BF16).astype(F32)
        fill_taps(taps, slot, rows, width, columns(right.reshape(rows, width, wide), False))
    grad_body(core_ref, left, left_t, taps, keep_ref, send_ref, width, False)


def weight_grad(kernel, name, core, lefts, firsts, seconds, basis, wide, after=()):
    slots = len(firsts)
    rows, width, depth = lefts[0].shape
    used = slots * (rows + 1) * width
    span = -(-used // 128) * 128
    half = depth // 2
    tap_rows = 2 * width + span
    return run(
        functools.partial(kernel, slots),
        name,
        [
            jax.ShapeDtypeStruct((9, half, wide), F32),
            jax.ShapeDtypeStruct((9, half, wide), BF16),
        ],
        [core],
        [*lefts, *firsts, *seconds, basis],
        after,
        [
            pltpu.VMEM((span, depth), BF16),
            pltpu.VMEM((depth, span), BF16),
            pltpu.VMEM((tap_rows, 3 * wide), BF16),
        ],
        28,
        18 * slots * rows * width * depth * wide,
    )


def halves_kernel(turn, core_ref, own_ref, other_ref, *refs):
    outs = refs[-2:] if turn else refs[-1:]
    half = own_ref.shape[1]

    @pl.when(core_ref[0] == 0)
    def _():
        outs[0][:, :half] = own_ref[...]
        outs[0][:, half:] = other_ref[...]

    @pl.when(core_ref[0] != 0)
    def _():
        outs[0][:, :half] = other_ref[...]
        outs[0][:, half:] = own_ref[...]

    if turn:
        for tap in range(9):
            outs[1][tap] = outs[0][tap].T


def join_halves(core, own, other, turn, after=()):
    _, half, wide = own.shape
    outs = [jax.ShapeDtypeStruct((9, 2 * half, wide), BF16)]
    if turn:
        outs.append(jax.ShapeDtypeStruct((9, wide, 2 * half), BF16))
    return run(
        functools.partial(halves_kernel, turn), "join_halves", outs, [core], [own, other], after,
        held=12,
    )


def basis_kernel(blocks, at_ref, basis_ref, *refs):
    rows_ref, columns_ref = refs[-2:]
    rank, channels = basis_ref.shape
    width = channels // blocks
    for block in range(blocks):

        @pl.when(at_ref[0] == block)
        def _(block=block):
            values = basis_ref[:, block * width : (block + 1) * width]
            high = values.astype(BF16).astype(F32)
            both = jnp.concatenate([high, values - high], axis=0)
            rows_ref[...] = both.astype(BF16)
            columns_ref[...] = both.T.astype(BF16)


def basis_parts(at, basis, blocks, after=()):
    rank, channels = basis.shape
    width = channels // blocks
    return run(
        functools.partial(basis_kernel, blocks),
        "basis_parts",
        [
            jax.ShapeDtypeStruct((2 * rank, width), BF16),
            jax.ShapeDtypeStruct((width, 2 * rank), BF16),
        ],
        [at],
        [basis],
        after,
    )


def flat_kernel(scale, keep_ref, got_ref, *refs):
    held = refs[-2 * (keep_ref.shape[2] // 128) - 2 :]
    out_ref = refs[-len(held) - 1]
    taps, half, wide = keep_ref.shape
    whole = wide // 128
    step = 2 * whole + 1
    count = half // 2
    zeros = jnp.zeros((half, 64), F32)
    for tap in range(taps):
        total = (keep_ref[tap] + got_ref[tap].astype(F32)) * scale
        for at in range(whole):
            held[at][...] = total[:, 128 * at : 128 * (at + 1)]
            held[whole + 2 + at][...] = total[:, 128 * at + 64 : 128 * (at + 1) + 64]
        held[whole][...] = jnp.concatenate([total[:, 128 * whole :], zeros], axis=1)
        held[whole + 1][...] = jnp.concatenate([zeros, total[:, :64]], axis=1)
        even, odd = pl.ds(0, count, stride=2), pl.ds(1, count, stride=2)
        rows = [held[at][even, :] for at in range(whole)]
        rows.append(held[whole][even, :] + held[whole + 1][odd, :])
        rows += [held[whole + 2 + at][odd, :] for at in range(whole)]
        for at, row in enumerate(rows):
            out_ref[pl.ds(tap * count * step + at, count, stride=step), :] = row


def flat_grad(keep, got, scale, after=()):
    taps, half, wide = keep.shape
    if wide % 128 != 64 or half % 2:
        made = (keep + got.astype(F32)) * scale
        return made, made
    (made,), token = run(
        functools.partial(flat_kernel, scale),
        "flat_grad",
        [jax.ShapeDtypeStruct((taps * half * wide // 128, 128), F32)],
        [],
        [keep, got],
        after,
        scratch=[pltpu.VMEM((half, 128), F32)] * (2 * (wide // 128) + 2),
        held=12,
    )
    return made, token


def same_groups(width, size):
    at = np.arange(width) // size
    return jnp.asarray((at[:, None] == at[None, :]).astype(np.float32), BF16)


def body(images, cotangent, first_weight, second_weight, first_basis, second_basis):
    n_dp = lax.axis_size("dp")
    n_rows = lax.axis_size("rows")
    chips = n_dp // 2
    _, band, width, channels = images.shape
    rows = band * n_rows
    dp_width = channels // n_dp
    chip_width = channels // chips
    row_width = channels // n_rows
    group = channels // GROUPS
    count = float(rows * width * group)
    grad_scale = 1.0 / math.sqrt(n_dp * images.shape[0] * rows * width)

    at_dp = lax.axis_index("dp")
    at_row = lax.axis_index("rows")
    chip = (at_dp // 2).astype(jnp.int32)
    core = (at_dp % 2).astype(jnp.int32)
    row = at_row.astype(jnp.int32)
    chip_at, core_at = chip[None], core[None]
    row_at = jnp.stack([row, (row + 1) // 2 % 2])

    def to_core(x):
        return lax.ppermute(x, "dp", [(i, i ^ 1) for i in range(n_dp)])

    def to_chip(x, away):
        return lax.ppermute(x, "dp", [(i, i ^ (2 * away)) for i in range(n_dp)])

    def to_row(x, away):
        return lax.ppermute(x, "rows", [(i, i ^ away) for i in range(n_rows)])

    def chips_gather(x):
        return [x] + [to_chip(x, away) for away in range(1, chips)]

    def rows_gather(x):
        if n_rows != 4:
            return [x] + [to_row(x, away) for away in range(1, n_rows)], [
                (away, -1) for away in range(n_rows)
            ]
        second = to_row(x, 2)
        first = to_row(x, 1)
        passed = lax.ppermute(second, "rows", [(2, 3), (1, 0)])
        later, _ = lax.optimization_barrier((x, second))
        middle = lax.ppermute(later, "rows", [(1, 2), (2, 1)])
        return [x, first, second, middle, passed], [(0, -1), (1, -1), (2, -1), (3, 1), (3, 0)]

    def chips_swap(parts):
        return [parts[0]] + [to_chip(parts[away], away) for away in range(1, chips)]

    def rows_swap(parts):
        far = [to_row(parts[away], away) for away in range(n_rows - 1, 0, -1)]
        return parts[:1] + far[::-1]

    chip_groups = same_groups(chip_width, group)
    row_groups = same_groups(row_width, group)

    slots = chips_swap(split_blocks([images[0], cotangent[0]], chips, chip_at))
    image_pack, _ = pack_slots(slots, 0)
    image_parts, places = rows_gather(image_pack)

    first_weight, second_weight, _ = lax.optimization_barrier(
        (first_weight, second_weight, slots[1])
    )
    own_first = first_weight.reshape(9, dp_width, row_width)
    own_second = second_weight.reshape(9, dp_width, row_width)
    early = tuple(image_parts[1:3])
    (second_full, second_turned), second_done = join_halves(
        core_at, own_second, to_core(own_second), True, early
    )
    (one_rows, one_columns), one_done = basis_parts(chip_at, first_basis, chips, early)
    (two_rows, two_columns), two_done = basis_parts(row_at, second_basis, n_rows, early)
    (first_full,), first_done = join_halves(core_at, own_first, to_core(own_first), False, early)
    cot_pack, cot_done = pack_slots(
        slots, 1, (*image_parts[3:], one_done, two_done, first_done, second_done)
    )
    cot_parts = [cot_pack] + [to_row(cot_pack, away) for away in range(1, n_rows)]
    weight_one = first_full.reshape(3, 3 * chip_width, row_width)
    weight_back = second_full.reshape(3, 3 * chip_width, row_width)
    weight_two = second_turned.reshape(3, 3 * row_width, chip_width)

    made, first_terms, done = {}, {}, (cot_done,)
    for slot in range(chips - 1, -1, -1):
        if slot == 0:
            done += (first_terms[chips - 1], *cot_parts[2:])
        ((active, sums),), token = first_conv(
            image_parts, places, [slot], weight_one, chip_groups, one_columns, row_at, rows, count,
            done,
        )
        made[slot] = active
        first_terms[slot] = to_chip(sums, slot) if slot else sums
        done = (token,)
    active = [made[slot] for slot in range(chips)]
    first_terms = [first_terms[slot] for slot in range(chips)]

    (pay, unit, scale, along), hidden_done = hidden_step(
        first_terms, row_groups, two_columns, count, tuple(cot_parts[1:2])
    )
    pays = chips_gather(pay)

    away = 4
    while away < n_rows:
        along = (along.astype(F32) + to_row(along, away).astype(F32)).astype(BF16)
        away *= 2
    back, along, back_done = back_conv(
        cot_parts, weight_back, [along, to_row(along, 1)], row_at, rows, (hidden_done,)
    )
    whole_cot = [pair[0] for pair in back]
    back_terms = chips_swap([pair[1] for pair in back])

    (*sums, along), sums_done = second_conv(
        pays, weight_two, [along, to_row(along, 2)], row_at, rows, n_rows, (back_done,)
    )
    band_terms = rows_swap(sums)

    (pre_grad, along), pre_done = pre_step(
        back_terms, unit, scale, row_groups, [along, to_chip(along, 1)], count,
        (sums_done,),
    )
    pre_grads = chips_gather(pre_grad)
    alongs = [along]
    away = 2
    while away < chips:
        alongs += [to_chip(part, away) for part in alongs]
        away *= 2

    second_halves, second_made = weight_grad(
        second_grad_kernel, "second_grad", core_at, whole_cot, pays, alongs, two_rows,
        row_width, (pre_done, band_terms[-1]),
    )
    blocks, blocks_done = band_step(band_terms, (second_made,))
    first_halves, _ = weight_grad(
        first_grad_kernel, "first_grad", core_at, active, pays, pre_grads, one_rows,
        row_width, (blocks_done,),
    )
    second_grad, flat_done = flat_grad(
        second_halves[0], to_core(second_halves[1]), grad_scale
    )
    (block_output,), output_done = join_blocks(
        images[0], chips_swap(blocks), chip_at, (flat_done,)
    )
    first_grad, _ = flat_grad(
        first_halves[0], to_core(first_halves[1]), grad_scale, (output_done,)
    )
    block_output = block_output[None]
    first_grad = first_grad.reshape(1, 1, 9, dp_width * row_width)
    second_grad = second_grad.reshape(1, 1, 9, dp_width * row_width)
    return (block_output, first_grad, second_grad)


def solution(mesh):
    split = P("dp", "rows", None, None)
    return jax.shard_map(
        body,
        mesh=mesh,
        in_specs=(split, split, split, split, P(), P()),
        out_specs=(split, split, split),
        check_vma=False,
    )
```

```python
import functools
import math

import jax
import jax.numpy as jnp
import numpy as np
from jax import lax
from jax.experimental import pallas as pl
from jax.experimental.pallas import tpu as pltpu
from jax.sharding import PartitionSpec as P

GROUPS = 32
EPS = 1e-5
MIB = 1024 * 1024
F32 = jnp.float32
BF16 = jnp.bfloat16


def whole_block(x):
    zeros = (0,) * len(x.shape)
    return pl.BlockSpec(x.shape, lambda _: zeros, pipeline_mode=pl.Buffered(1))


def smem():
    return pl.BlockSpec(memory_space=pltpu.SMEM)


def unread(after):
    return [pl.BlockSpec(memory_space=pltpu.VMEM)] * len(after)


def run(kernel, name, outs, scalars, arrays, after=(), scratch=(), held=8, flops=0, fetch=False):
    outs = [*outs, jax.ShapeDtypeStruct((8, 128), F32)]
    moved = sum(x.size * x.dtype.itemsize for x in list(arrays) + outs)
    held_there = pl.BlockSpec(memory_space=pltpu.VMEM)
    used = len(scalars) + len(arrays)
    token_at = used + len(after) + len(outs) - 1

    def whole(*refs):
        refs[token_at][...] = jnp.zeros((8, 128), F32)
        kernel(*refs[:used], *refs[used + len(after) : token_at], *refs[token_at + 1 :])

    *made, token = pl.pallas_call(
        whole,
        grid=(1,) if fetch else (),
        out_shape=outs,
        in_specs=[smem()] * len(scalars)
        + [whole_block(x) if fetch else held_there for x in arrays]
        + unread(after),
        out_specs=[held_there] * len(outs),
        scratch_shapes=list(scratch),
        compiler_params=pltpu.CompilerParams(vmem_limit_bytes=held * MIB),
        cost_estimate=cost(flops, moved),
        name=name,
    )(*scalars, *arrays, *after)
    return made, token


def cost(flops, moved):
    return pl.CostEstimate(flops=int(flops), bytes_accessed=int(moved), transcendentals=0)


def group_sums(row, same_group):
    high = row.astype(BF16).astype(F32)
    rest = row - high
    middle = rest.astype(BF16).astype(F32)
    low = rest - middle
    at = lax.broadcasted_iota(jnp.int32, (16, row.shape[1]), 0)
    stacked = jnp.where(at == 0, high, jnp.where(at == 1, middle, jnp.where(at == 2, low, 0.0)))
    sums = jnp.dot(stacked.astype(BF16), same_group, preferred_element_type=F32)
    return jnp.sum(sums, axis=0, keepdims=True)


def normalized(values, same_group, count):
    center = group_sums(jnp.sum(values, axis=0, keepdims=True), same_group) / count
    moved = values - center
    spread = group_sums(jnp.sum(moved * moved, axis=0, keepdims=True), same_group) / count
    scale = 1.0 / jnp.sqrt(spread + EPS)
    return moved * scale, scale


def silu(unit):
    half = 0.5 * unit
    return half + half * jnp.tanh(half)


def add_into(out_ref, one_ref, other_ref):
    out_ref[...] = (one_ref[...].astype(F32) + other_ref[...].astype(F32)).astype(BF16)


def columns(values, flip):
    width = values.shape[1]
    at = lax.broadcasted_iota(jnp.int32, values.shape, 1)
    before = jnp.where(at == 0, 0.0, pltpu.roll(values, 1, axis=1))
    after = jnp.where(at == width - 1, 0.0, pltpu.roll(values, width - 1, axis=1))
    parts = [after, values, before] if flip else [before, values, after]
    return jnp.concatenate([part.astype(BF16) for part in parts], axis=2)


def conv_rows(taps, weight_ref, rows, flip):
    _, width, depth = taps.shape
    total = None
    for tap in range(3):
        window = taps[tap : tap + rows].reshape(rows * width, depth)
        term = jnp.dot(window, weight_ref[2 - tap if flip else tap], preferred_element_type=F32)
        total = term if total is None else total + term
    return total


def side_by_side(values):
    half = values.shape[0] // 2
    return jnp.concatenate([values[:half], values[half:]], axis=1)


def stacked_again(values):
    half = values.shape[1] // 2
    return jnp.concatenate([values[:, :half], values[:, half:]], axis=0)


def clear_edges(taps):
    rows = taps.shape[0]
    taps[0:1] = jnp.zeros((1,) + taps.shape[1:], taps.dtype)
    taps[rows - 1 : rows] = jnp.zeros((1,) + taps.shape[1:], taps.dtype)


def split_kernel(blocks, merge, at_ref, *refs):
    arrays, outs = refs[:-blocks], refs[-blocks:]
    width = arrays[0].shape[-1] // blocks
    for away in range(blocks):
        for block in range(blocks):

            @pl.when(jnp.bitwise_xor(at_ref[0], away) == block)
            def _(away=away, block=block):
                taken = [x_ref[:, :, block * width : (block + 1) * width] for x_ref in arrays]
                if merge:
                    taken = [sum(taken[1:], taken[0])]
                for at, values in enumerate(taken):
                    outs[away][:, :, at * width : (at + 1) * width] = values


def split_blocks(arrays, blocks, chip, merge=False, after=()):
    height, width, channels = arrays[0].shape
    count = 1 if merge else len(arrays)
    shape = jax.ShapeDtypeStruct((height, width, count * channels // blocks), BF16)
    return run(
        functools.partial(split_kernel, blocks, merge),
        "split_blocks",
        [shape] * blocks,
        [chip],
        arrays,
        after,
    )


def pack_kernel(at, *refs):
    slots, out = refs[:-1], refs[-1]
    width = out.shape[-1] // 2
    for slot, ref in enumerate(slots):
        lanes = slice(slot % 2 * width, (slot % 2 + 1) * width)
        out[slot // 2, :, :, lanes] = ref[:, :, at * width : (at + 1) * width]


def pack_slots(slots, at, depth, after=()):
    band, width, _ = slots[0].shape
    out = jax.ShapeDtypeStruct((len(slots) // 2, band, width, 2 * depth), BF16)
    (packed,), token = run(
        functools.partial(pack_kernel, at), "pack_slots", [out], [], slots, after
    )
    return packed, token


def assemble(whole, parts, places, at_ref):
    depth = whole.shape[2]
    for index, block, away in places:
        part = parts[index]
        band = part.shape[0]
        start = jnp.bitwise_xor(at_ref[0], away) * band
        whole[pl.ds(start, band)] = part[:, :, block * depth : (block + 1) * depth]


def first_kernel(places, count, at_ref, *refs):
    used = 1 + max(place[0] for place in places)
    parts = refs[:used]
    weight_ref, group_ref, basis_ref, act_ref, sums_ref, whole, taps = refs[used:]
    rows, width, depth = act_ref.shape
    rank = basis_ref.shape[1] // 2
    clear_edges(taps)
    assemble(whole, parts, places, at_ref)
    values = whole[...].astype(F32).reshape(rows * width, depth)
    unit, _ = normalized(values, group_ref[...], count)
    active = silu(unit).astype(BF16)
    act_ref[...] = active.reshape(act_ref.shape)
    taps[1 : rows + 1] = columns(active.astype(F32).reshape(act_ref.shape), False)
    total = conv_rows(taps, weight_ref, rows, False)
    along = jnp.dot(active, basis_ref[...], preferred_element_type=F32)
    along = along[:, :rank] + along[:, rank:]
    sums_ref[...] = jnp.concatenate([total, along], axis=1).astype(BF16)


def first_conv(parts, places, weight, same_group, basis, row, rows, count, after=()):
    _, width, _ = parts[0].shape
    depth = same_group.shape[0]
    rank = basis.shape[1] // 2
    wide = weight.shape[2]
    cells = rows * width
    return run(
        functools.partial(first_kernel, places, count),
        "first_conv",
        [
            jax.ShapeDtypeStruct((rows, width, depth), BF16),
            jax.ShapeDtypeStruct((cells, wide + rank), BF16),
        ],
        [row],
        [*parts, weight, same_group, basis],
        after,
        [
            pltpu.VMEM((rows, width, depth), BF16),
            pltpu.VMEM((rows + 2, width, 3 * depth), BF16),
        ],
        14,
        18 * cells * depth * wide,
    )


def back_kernel(slots, bands, at_ref, *refs):
    parts = refs[:bands]
    weight_ref, along_ref, other_ref = refs[bands : bands + 3]
    later_ref, whole, taps = refs[-3:]
    outs = refs[-3 - 2 * slots : -3]
    add_into(later_ref, along_ref, other_ref)
    rows, width, depth = outs[0].shape
    clear_edges(taps)
    for slot in reversed(range(slots)):
        cot_ref, sums_ref = outs[2 * slot : 2 * slot + 2]
        if slot % 2:
            for away, part in enumerate(parts):
                band = part.shape[1]
                start = jnp.bitwise_xor(at_ref[0], away) * band
                whole[pl.ds(start, band)] = part[slot // 2]
        half = slot % 2
        values = whole[:, :, half * depth : (half + 1) * depth]
        cot_ref[...] = values
        taps[1 : rows + 1] = columns(values.astype(F32), True)
        sums_ref[...] = side_by_side(conv_rows(taps, weight_ref, rows, True)).astype(BF16)


def back_conv(parts, weight, alongs, row, rows, after=()):
    pairs, _, width, double = parts[0].shape
    depth = double // 2
    wide = weight.shape[2]
    cells = rows * width
    slots = 2 * pairs
    outs = [
        jax.ShapeDtypeStruct((rows, width, depth), BF16),
        jax.ShapeDtypeStruct((cells // 2, 2 * wide), BF16),
    ]
    made, token = run(
        functools.partial(back_kernel, slots, len(parts)),
        "back_conv",
        outs * slots + alongs[:1],
        [row],
        [*parts, weight, *alongs],
        after,
        [
            pltpu.VMEM((rows, width, double), BF16),
            pltpu.VMEM((rows + 2, width, 3 * depth), BF16),
        ],
        14,
        18 * slots * cells * depth * wide,
    )
    return [(made[2 * at], made[2 * at + 1]) for at in range(slots)], made[-1], token


def hidden_kernel(terms, count, *refs):
    group_ref, basis_ref = refs[terms : terms + 2]
    pay_ref, unit_ref, scale_ref, along_ref = refs[-4:]
    wide = unit_ref.shape[1]
    rank = basis_ref.shape[1] // 2
    total = refs[0][...].astype(F32)
    for term in refs[1:terms]:
        total = total + term[...].astype(F32)
    unit, scale = normalized(total[:, :wide], group_ref[...], count)
    unit_ref[...] = unit
    scale_ref[...] = scale
    hidden = silu(unit).astype(BF16)
    pay_ref[...] = jnp.concatenate([hidden.astype(F32), total[:, wide:]], axis=1).astype(BF16)
    along = jnp.dot(hidden, basis_ref[...], preferred_element_type=F32)
    along_ref[...] = side_by_side(along[:, :rank] + along[:, rank:]).astype(BF16)


def hidden_step(terms, same_group, basis, count, after=()):
    cells, both = terms[0].shape
    wide = same_group.shape[0]
    return run(
        functools.partial(hidden_kernel, len(terms), count),
        "hidden_step",
        [
            jax.ShapeDtypeStruct((cells, both), BF16),
            jax.ShapeDtypeStruct((cells, wide), F32),
            jax.ShapeDtypeStruct((1, wide), F32),
            jax.ShapeDtypeStruct((cells // 2, basis.shape[1]), BF16),
        ],
        [],
        [*terms, same_group, basis],
        after,
        held=12,
        flops=40 * cells * wide,
    )


def second_kernel(slots, bands, at_ref, *refs):
    pays = refs[:slots]
    weight_ref, along_ref, other_ref = refs[slots : slots + 3]
    later_ref, whole, taps = refs[-3:]
    outs = refs[-3 - bands : -3]
    add_into(later_ref, along_ref, other_ref)
    band, width, double = outs[0].shape[1:]
    rows = whole.shape[0]
    depth = taps.shape[2] // 3
    wide = double // 2
    clear_edges(taps)
    for slot in range(slots):
        hidden = pays[slot][:, :depth].astype(F32).reshape(rows, width, depth)
        taps[1 : rows + 1] = columns(hidden, False)
        whole[...] = conv_rows(taps, weight_ref, rows, False).reshape(rows, width, wide)
        lanes = slice(slot % 2 * wide, (slot % 2 + 1) * wide)
        for away in range(bands):
            start = jnp.bitwise_xor(at_ref[0], away) * band
            outs[away][slot // 2, :, :, lanes] = whole[pl.ds(start, band)].astype(BF16)


def second_conv(pays, weight, alongs, row, rows, bands, after=()):
    slots = len(pays)
    cells, _ = pays[0].shape
    width = cells // rows
    depth = weight.shape[1] // 3
    wide = weight.shape[2]
    out = jax.ShapeDtypeStruct((slots // 2, rows // bands, width, 2 * wide), BF16)
    return run(
        functools.partial(second_kernel, slots, bands),
        "second_conv",
        [out] * bands + alongs[:1],
        [row],
        [*pays, weight, *alongs],
        after,
        [
            pltpu.VMEM((rows, width, wide), F32),
            pltpu.VMEM((rows + 2, width, 3 * depth), BF16),
        ],
        14,
        18 * slots * cells * depth * wide,
    )


def band_kernel(terms, slots, *refs):
    outs = refs[-slots:]
    wide = outs[0].shape[-1]
    total = refs[0][...].astype(F32)
    for term in refs[1:terms]:
        total = total + term[...].astype(F32)
    for slot, out in enumerate(outs):
        lanes = slice(slot % 2 * wide, (slot % 2 + 1) * wide)
        out[...] = total[slot // 2, :, :, lanes].astype(BF16)


def band_step(terms, after=()):
    pairs, band, width, double = terms[0].shape
    out = jax.ShapeDtypeStruct((band, width, double // 2), BF16)
    return run(
        functools.partial(band_kernel, len(terms), 2 * pairs),
        "band_step",
        [out] * (2 * pairs),
        [],
        terms,
        after,
    )


def join_kernel(blocks, at_ref, x_ref, *refs):
    out = refs[-1]
    width = x_ref.shape[-1] // blocks
    for away in range(blocks):
        for block in range(blocks):

            @pl.when(jnp.bitwise_xor(at_ref[0], away) == block)
            def _(away=away, block=block):
                lanes = slice(block * width, (block + 1) * width)
                added = x_ref[:, :, lanes].astype(F32) + refs[away][...].astype(F32)
                out[:, :, lanes] = added.astype(BF16)


def join_blocks(x, parts, chip, after=()):
    return run(
        functools.partial(join_kernel, len(parts)),
        "join_blocks",
        [x],
        [chip],
        [x, *parts],
        after,
    )


def pre_kernel(terms, count, *refs):
    unit_ref, scale_ref, group_ref, along_ref, other_ref = refs[terms : terms + 5]
    out_ref, later_ref = refs[-2:]
    later_ref[0] = along_ref[...]
    later_ref[1] = other_ref[...]
    total = refs[0][...].astype(F32)
    for term in refs[1:terms]:
        total = total + term[...].astype(F32)
    unit = unit_ref[...]
    gate = 0.5 + 0.5 * jnp.tanh(0.5 * unit)
    grad = stacked_again(total) * (gate * (1.0 + unit * (1.0 - gate)))
    mean = group_sums(jnp.sum(grad, axis=0, keepdims=True), group_ref[...]) / count
    along = group_sums(jnp.sum(grad * unit, axis=0, keepdims=True), group_ref[...]) / count
    out_ref[...] = side_by_side(scale_ref[...] * (grad - mean - unit * along)).astype(BF16)


def pre_step(terms, unit, scale, same_group, alongs, count, after=()):
    cells, wide = unit.shape
    stacked = jax.ShapeDtypeStruct((2, *alongs[0].shape), BF16)
    return run(
        functools.partial(pre_kernel, len(terms), count),
        "pre_step",
        [jax.ShapeDtypeStruct((cells // 2, 2 * wide), BF16), stacked],
        [],
        [*terms, unit, scale, same_group, *alongs],
        after,
        held=12,
        flops=40 * cells * wide,
    )


def project(values, along, basis):
    both = jnp.concatenate([along, along], axis=1)
    return values - jnp.dot(both, basis, preferred_element_type=F32)


def grad_body(core_ref, left, left_t, taps, keep_ref, send_ref, width, flip):
    half = left.shape[1] // 2
    span = left.shape[0]
    wide = taps.shape[1] // 3
    turned = left[...].T

    @pl.when(core_ref[0] == 0)
    def _():
        left_t[...] = turned

    @pl.when(core_ref[0] != 0)
    def _():
        left_t[:half] = turned[half:]
        left_t[half:] = turned[:half]

    for tap in range(3):
        window = taps[tap * width : tap * width + span]
        result = jnp.dot(left_t[...], window, preferred_element_type=F32)
        first = 3 * (2 - tap if flip else tap)
        for q in range(3):
            lanes = slice(q * wide, (q + 1) * wide)
            keep_ref[first + q] = result[:half, lanes]
            send_ref[first + q] = result[half:, lanes].astype(BF16)


def fill_taps(taps, slot, rows, width, value):
    start = (slot * (rows + 1) + 1) * width
    taps[start : start + rows * width] = value.reshape(rows * width, value.shape[2])


def clear_gaps(left, taps, slots, rows, width):
    gap = rows + 1
    for slot in range(slots + 1):
        begin = slot * gap * width
        end = taps.shape[0] if slot == slots else begin + width
        taps[begin:end] = jnp.zeros((end - begin, taps.shape[1]), taps.dtype)
    for slot in range(slots):
        begin = (slot * gap + rows) * width
        end = left.shape[0] if slot == slots - 1 else begin + width
        left[begin:end] = jnp.zeros((end - begin, left.shape[1]), left.dtype)


def first_grad_kernel(slots, core_ref, *refs):
    acts, pays, grads = (refs[at * slots : (at + 1) * slots] for at in range(3))
    basis_ref = refs[3 * slots]
    keep_ref, send_ref, left, left_t, taps = refs[-5:]
    rows, width, depth = acts[0].shape
    cells = rows * width
    rank = basis_ref.shape[0] // 2
    wide = taps.shape[1] // 3
    clear_gaps(left, taps, slots, rows, width)
    for slot in range(slots):
        values = acts[slot][...].reshape(cells, depth).astype(F32)
        along = pays[slot][:, wide : wide + rank]
        begin = slot * (rows + 1) * width
        left[begin : begin + cells] = project(values, along, basis_ref[...]).astype(BF16)
        right = stacked_again(grads[slot][...].astype(F32)).reshape(rows, width, wide)
        fill_taps(taps, slot, rows, width, columns(right, True))
    grad_body(core_ref, left, left_t, taps, keep_ref, send_ref, width, True)


def second_grad_kernel(slots, core_ref, *refs):
    cots, pays = (refs[at * slots : (at + 1) * slots] for at in range(2))
    alongs = refs[2 * slots : 2 * slots + slots // 2]
    basis_ref = refs[2 * slots + slots // 2]
    keep_ref, send_ref, left, left_t, taps = refs[-5:]
    rows, width, depth = cots[0].shape
    cells = rows * width
    rank = basis_ref.shape[0] // 2
    wide = taps.shape[1] // 3
    clear_gaps(left, taps, slots, rows, width)
    for slot in range(slots):
        begin = slot * (rows + 1) * width
        left[begin : begin + cells] = cots[slot][...].reshape(cells, depth)
        packed = alongs[slot // 2][slot % 2]
        along = jnp.concatenate([packed[:, :rank], packed[:, rank:]], axis=0)
        values = pays[slot][:, :wide].astype(F32)
        right = project(values, along, basis_ref[...]).astype(BF16).astype(F32)
        fill_taps(taps, slot, rows, width, columns(right.reshape(rows, width, wide), False))
    grad_body(core_ref, left, left_t, taps, keep_ref, send_ref, width, False)


def weight_grad(kernel, name, core, lefts, firsts, seconds, basis, wide, after=()):
    slots = len(firsts)
    rows, width, depth = lefts[0].shape
    used = slots * (rows + 1) * width
    span = -(-used // 128) * 128
    half = depth // 2
    tap_rows = 2 * width + span
    return run(
        functools.partial(kernel, slots),
        name,
        [
            jax.ShapeDtypeStruct((9, half, wide), F32),
            jax.ShapeDtypeStruct((9, half, wide), BF16),
        ],
        [core],
        [*lefts, *firsts, *seconds, basis],
        after,
        [
            pltpu.VMEM((span, depth), BF16),
            pltpu.VMEM((depth, span), BF16),
            pltpu.VMEM((tap_rows, 3 * wide), BF16),
        ],
        28,
        18 * slots * rows * width * depth * wide,
    )


def halves_kernel(turn, core_ref, own_ref, other_ref, *refs):
    outs = refs[-2:] if turn else refs[-1:]
    half = own_ref.shape[1]

    @pl.when(core_ref[0] == 0)
    def _():
        outs[0][:, :half] = own_ref[...]
        outs[0][:, half:] = other_ref[...]

    @pl.when(core_ref[0] != 0)
    def _():
        outs[0][:, :half] = other_ref[...]
        outs[0][:, half:] = own_ref[...]

    if turn:
        for tap in range(9):
            outs[1][tap] = outs[0][tap].T


def join_halves(core, own, other, turn, after=()):
    _, half, wide = own.shape
    outs = [jax.ShapeDtypeStruct((9, 2 * half, wide), BF16)]
    if turn:
        outs.append(jax.ShapeDtypeStruct((9, wide, 2 * half), BF16))
    return run(
        functools.partial(halves_kernel, turn), "join_halves", outs, [core], [own, other], after,
        held=12,
    )


def basis_kernel(blocks, at_ref, basis_ref, *refs):
    rows_ref, columns_ref = refs[-2:]
    rank, channels = basis_ref.shape
    width = channels // blocks
    for block in range(blocks):

        @pl.when(at_ref[0] == block)
        def _(block=block):
            values = basis_ref[:, block * width : (block + 1) * width]
            high = values.astype(BF16).astype(F32)
            both = jnp.concatenate([high, values - high], axis=0)
            rows_ref[...] = both.astype(BF16)
            columns_ref[...] = both.T.astype(BF16)


def basis_parts(at, basis, blocks, after=()):
    rank, channels = basis.shape
    width = channels // blocks
    return run(
        functools.partial(basis_kernel, blocks),
        "basis_parts",
        [
            jax.ShapeDtypeStruct((2 * rank, width), BF16),
            jax.ShapeDtypeStruct((width, 2 * rank), BF16),
        ],
        [at],
        [basis],
        after,
    )


def flat_kernel(scale, keep_ref, got_ref, *refs):
    held = refs[-2 * (keep_ref.shape[2] // 128) - 2 :]
    out_ref = refs[-len(held) - 1]
    taps, half, wide = keep_ref.shape
    whole = wide // 128
    step = 2 * whole + 1
    count = half // 2
    zeros = jnp.zeros((half, 64), F32)
    for tap in range(taps):
        total = (keep_ref[tap] + got_ref[tap].astype(F32)) * scale
        for at in range(whole):
            held[at][...] = total[:, 128 * at : 128 * (at + 1)]
            held[whole + 2 + at][...] = total[:, 128 * at + 64 : 128 * (at + 1) + 64]
        held[whole][...] = jnp.concatenate([total[:, 128 * whole :], zeros], axis=1)
        held[whole + 1][...] = jnp.concatenate([zeros, total[:, :64]], axis=1)
        even, odd = pl.ds(0, count, stride=2), pl.ds(1, count, stride=2)
        rows = [held[at][even, :] for at in range(whole)]
        rows.append(held[whole][even, :] + held[whole + 1][odd, :])
        rows += [held[whole + 2 + at][odd, :] for at in range(whole)]
        for at, row in enumerate(rows):
            out_ref[pl.ds(tap * count * step + at, count, stride=step), :] = row


def flat_grad(keep, got, scale, after=()):
    taps, half, wide = keep.shape
    if wide % 128 != 64 or half % 2:
        made = (keep + got.astype(F32)) * scale
        return made, made
    (made,), token = run(
        functools.partial(flat_kernel, scale),
        "flat_grad",
        [jax.ShapeDtypeStruct((taps * half * wide // 128, 128), F32)],
        [],
        [keep, got],
        after,
        scratch=[pltpu.VMEM((half, 128), F32)] * (2 * (wide // 128) + 2),
        held=12,
    )
    return made, token


def same_groups(width, size):
    at = np.arange(width) // size
    return jnp.asarray((at[:, None] == at[None, :]).astype(np.float32), BF16)


def body(images, cotangent, first_weight, second_weight, first_basis, second_basis):
    n_dp = lax.axis_size("dp")
    n_rows = lax.axis_size("rows")
    chips = n_dp // 2
    _, band, width, channels = images.shape
    rows = band * n_rows
    dp_width = channels // n_dp
    chip_width = channels // chips
    row_width = channels // n_rows
    group = channels // GROUPS
    count = float(rows * width * group)
    grad_scale = 1.0 / math.sqrt(n_dp * images.shape[0] * rows * width)

    at_dp = lax.axis_index("dp")
    at_row = lax.axis_index("rows")
    chip = (at_dp // 2).astype(jnp.int32)
    core = (at_dp % 2).astype(jnp.int32)
    row = at_row.astype(jnp.int32)
    chip_at, core_at, row_at = chip[None], core[None], row[None]

    def to_core(x):
        return lax.ppermute(x, "dp", [(i, i ^ 1) for i in range(n_dp)])

    def to_chip(x, away):
        return lax.ppermute(x, "dp", [(i, i ^ (2 * away)) for i in range(n_dp)])

    def to_row(x, away):
        return lax.ppermute(x, "rows", [(i, i ^ away) for i in range(n_rows)])

    def chips_gather(x):
        return [x] + [to_chip(x, away) for away in range(1, chips)]

    def line_bands(x):
        if n_rows != 4:
            return [[to_row(x, away) for away in range(1, n_rows)]]
        second = to_row(x, 2)
        first = to_row(x, 1)
        passed = lax.ppermute(second, "rows", [(2, 3), (1, 0)])
        later, _ = lax.optimization_barrier((x, second))
        middle = lax.ppermute(later, "rows", [(1, 2), (2, 1)])
        return [[first, second], [passed, middle]]

    def chips_swap(parts):
        return [parts[0]] + [to_chip(parts[away], away) for away in range(1, chips)]

    def rows_swap(parts):
        far = [to_row(parts[away], away) for away in range(n_rows - 1, 0, -1)]
        return parts[:1] + far[::-1]

    chip_groups = same_groups(chip_width, group)
    row_groups = same_groups(row_width, group)

    near_bands, *far_bands = line_bands(images[0])
    own_first = first_weight.reshape(9, dp_width, row_width)
    own_second = second_weight.reshape(9, dp_width, row_width)
    other_second = to_core(own_second)
    (second_full, second_turned), second_done = join_halves(
        core_at, own_second, other_second, True
    )
    (one_rows, one_columns), one_done = basis_parts(chip_at, first_basis, chips)
    (two_rows, two_columns), two_done = basis_parts(row_at, second_basis, n_rows)
    (first_full,), first_done = join_halves(core_at, own_first, to_core(own_first), False)
    prepared = (first_done, other_second)

    near_blocks, arrived = split_blocks(
        [images[0], cotangent[0], *near_bands], chips, chip_at, after=prepared
    )
    slots = chips_swap(near_blocks)
    groups = [slots]
    places = [(0, 0, 0)] + [(0, at + 2, at + 1) for at in range(len(near_bands))]
    for bands in far_bands:
        far_blocks, arrived = split_blocks(bands, chips, chip_at, True)
        groups.append(chips_swap(far_blocks))
        places.append((1, 0, n_rows - 1))

    cot_pack, cot_done = pack_slots(
        slots, 1, chip_width, (arrived, second_done, one_done, two_done)
    )
    cot_parts = [cot_pack] + [to_row(cot_pack, away) for away in range(1, n_rows)]
    weight_one = first_full.reshape(3, 3 * chip_width, row_width)
    weight_back = second_full.reshape(3, 3 * chip_width, row_width)
    weight_two = second_turned.reshape(3, 3 * row_width, chip_width)

    made, first_terms, done = {}, {}, (cot_done,)
    for slot in range(chips - 1, -1, -1):
        if slot == 0:
            done += (first_terms[chips - 1], *cot_parts[2:])
        (active, sums), token = first_conv(
            [group[slot] for group in groups], places, weight_one, chip_groups, one_columns,
            row_at, rows, count, done,
        )
        made[slot] = active
        first_terms[slot] = to_chip(sums, slot) if slot else sums
        done = (token,)
    active = [made[slot] for slot in range(chips)]
    first_terms = [first_terms[slot] for slot in range(chips)]

    (pay, unit, scale, along), hidden_done = hidden_step(
        first_terms, row_groups, two_columns, count, tuple(cot_parts[1:2])
    )
    pays = chips_gather(pay)

    away = 4
    while away < n_rows:
        along = (along.astype(F32) + to_row(along, away).astype(F32)).astype(BF16)
        away *= 2
    back, along, back_done = back_conv(
        cot_parts, weight_back, [along, to_row(along, 1)], row_at, rows, (hidden_done,)
    )
    whole_cot = [pair[0] for pair in back]
    back_terms = chips_swap([pair[1] for pair in back])

    (*sums, along), sums_done = second_conv(
        pays, weight_two, [along, to_row(along, 2)], row_at, rows, n_rows, (back_done,)
    )
    band_terms = rows_swap(sums)

    (pre_grad, along), pre_done = pre_step(
        back_terms, unit, scale, row_groups, [along, to_chip(along, 1)], count,
        (sums_done,),
    )
    pre_grads = chips_gather(pre_grad)
    alongs = [along]
    away = 2
    while away < chips:
        alongs += [to_chip(part, away) for part in alongs]
        away *= 2

    second_halves, second_made = weight_grad(
        second_grad_kernel, "second_grad", core_at, whole_cot, pays, alongs, two_rows,
        row_width, (pre_done, band_terms[-1]),
    )
    blocks, blocks_done = band_step(band_terms, (second_made,))
    first_halves, _ = weight_grad(
        first_grad_kernel, "first_grad", core_at, active, pays, pre_grads, one_rows,
        row_width, (blocks_done,),
    )
    second_grad, flat_done = flat_grad(
        second_halves[0], to_core(second_halves[1]), grad_scale
    )
    (block_output,), output_done = join_blocks(
        images[0], chips_swap(blocks), chip_at, (flat_done,)
    )
    first_grad, _ = flat_grad(
        first_halves[0], to_core(first_halves[1]), grad_scale, (output_done,)
    )
    block_output = block_output[None]
    first_grad = first_grad.reshape(1, 1, 9, dp_width * row_width)
    second_grad = second_grad.reshape(1, 1, 9, dp_width * row_width)
    return (block_output, first_grad, second_grad)


def solution(mesh):
    split = P("dp", "rows", None, None)
    return jax.shard_map(
        body,
        mesh=mesh,
        in_specs=(split, split, split, split, P(), P()),
        out_specs=(split, split, split),
        check_vma=False,
    )
```

```python
import functools
import math

import jax
import jax.numpy as jnp
import numpy as np
from jax import lax
from jax.experimental import pallas as pl
from jax.experimental.pallas import tpu as pltpu
from jax.sharding import PartitionSpec as P

GROUPS = 32
EPS = 1e-5
MIB = 1024 * 1024
F32 = jnp.float32
BF16 = jnp.bfloat16


def whole_block(x):
    zeros = (0,) * len(x.shape)
    return pl.BlockSpec(x.shape, lambda _: zeros, pipeline_mode=pl.Buffered(1))


def smem():
    return pl.BlockSpec(memory_space=pltpu.SMEM)


def unread(after):
    return [pl.BlockSpec(memory_space=pltpu.VMEM)] * len(after)


def run(kernel, name, outs, scalars, arrays, after=(), scratch=(), held=8, flops=0, fetch=False):
    outs = [*outs, jax.ShapeDtypeStruct((8, 128), F32)]
    moved = sum(x.size * x.dtype.itemsize for x in list(arrays) + outs)
    held_there = pl.BlockSpec(memory_space=pltpu.VMEM)
    used = len(scalars) + len(arrays)
    token_at = used + len(after) + len(outs) - 1

    def whole(*refs):
        refs[token_at][...] = jnp.zeros((8, 128), F32)
        kernel(*refs[:used], *refs[used + len(after) : token_at], *refs[token_at + 1 :])

    *made, token = pl.pallas_call(
        whole,
        grid=(1,) if fetch else (),
        out_shape=outs,
        in_specs=[smem()] * len(scalars)
        + [whole_block(x) if fetch else held_there for x in arrays]
        + unread(after),
        out_specs=[held_there] * len(outs),
        scratch_shapes=list(scratch),
        compiler_params=pltpu.CompilerParams(vmem_limit_bytes=held * MIB),
        cost_estimate=cost(flops, moved),
        name=name,
    )(*scalars, *arrays, *after)
    return made, token


def cost(flops, moved):
    return pl.CostEstimate(flops=int(flops), bytes_accessed=int(moved), transcendentals=0)


def group_sums(row, same_group):
    high = row.astype(BF16).astype(F32)
    rest = row - high
    middle = rest.astype(BF16).astype(F32)
    low = rest - middle
    at = lax.broadcasted_iota(jnp.int32, (16, row.shape[1]), 0)
    stacked = jnp.where(at == 0, high, jnp.where(at == 1, middle, jnp.where(at == 2, low, 0.0)))
    sums = jnp.dot(stacked.astype(BF16), same_group, preferred_element_type=F32)
    return jnp.sum(sums, axis=0, keepdims=True)


def normalized(values, same_group, count):
    center = group_sums(jnp.sum(values, axis=0, keepdims=True), same_group) / count
    moved = values - center
    spread = group_sums(jnp.sum(moved * moved, axis=0, keepdims=True), same_group) / count
    scale = 1.0 / jnp.sqrt(spread + EPS)
    return moved * scale, scale


def silu(unit):
    half = 0.5 * unit
    return half + half * jnp.tanh(half)


def add_into(out_ref, one_ref, other_ref):
    out_ref[...] = (one_ref[...].astype(F32) + other_ref[...].astype(F32)).astype(BF16)


def columns(values, flip):
    width = values.shape[1]
    at = lax.broadcasted_iota(jnp.int32, values.shape, 1)
    before = jnp.where(at == 0, 0.0, pltpu.roll(values, 1, axis=1))
    after = jnp.where(at == width - 1, 0.0, pltpu.roll(values, width - 1, axis=1))
    parts = [after, values, before] if flip else [before, values, after]
    return jnp.concatenate([part.astype(BF16) for part in parts], axis=2)


def conv_rows(taps, weight_ref, rows, flip):
    _, width, depth = taps.shape
    total = None
    for tap in range(3):
        window = taps[tap : tap + rows].reshape(rows * width, depth)
        term = jnp.dot(window, weight_ref[2 - tap if flip else tap], preferred_element_type=F32)
        total = term if total is None else total + term
    return total


def side_by_side(values):
    half = values.shape[0] // 2
    return jnp.concatenate([values[:half], values[half:]], axis=1)


def stacked_again(values):
    half = values.shape[1] // 2
    return jnp.concatenate([values[:, :half], values[:, half:]], axis=0)


def clear_edges(taps):
    rows = taps.shape[0]
    taps[0:1] = jnp.zeros((1,) + taps.shape[1:], taps.dtype)
    taps[rows - 1 : rows] = jnp.zeros((1,) + taps.shape[1:], taps.dtype)


def split_kernel(blocks, at_ref, *refs):
    arrays, outs = refs[:-blocks], refs[-blocks:]
    width = outs[0].shape[-1] // len(arrays)
    for away in range(blocks):
        for block in range(blocks):

            @pl.when(jnp.bitwise_xor(at_ref[0], away) == block)
            def _(away=away, block=block):
                for at, x_ref in enumerate(arrays):
                    lanes = slice(at * width, (at + 1) * width)
                    outs[away][:, :, lanes] = x_ref[:, :, block * width : (block + 1) * width]


def split_blocks(arrays, blocks, chip):
    height, width, channels = arrays[0].shape
    shape = jax.ShapeDtypeStruct((height, width, len(arrays) * channels // blocks), BF16)
    made, _ = run(
        functools.partial(split_kernel, blocks), "split_blocks", [shape] * blocks, [chip], arrays,
    )
    return made


def pack_kernel(at, *refs):
    slots, out = refs[:-1], refs[-1]
    width = slots[0].shape[-1] // 2
    for slot, ref in enumerate(slots):
        lanes = slice(slot % 2 * width, (slot % 2 + 1) * width)
        out[slot // 2, :, :, lanes] = ref[:, :, at * width : (at + 1) * width]


def pack_slots(slots, at, after=()):
    out = jax.ShapeDtypeStruct((len(slots) // 2, *slots[0].shape), BF16)
    (packed,), token = run(
        functools.partial(pack_kernel, at), "pack_slots", [out], [], slots, after
    )
    return packed, token


def assemble(whole, parts, places, pair, at_ref):
    for part, (away, who) in zip(parts, places):

        @pl.when(jnp.logical_or(who < 0, at_ref[1] == who))
        def _(part=part, away=away):
            band = part.shape[1]
            whole[pl.ds(jnp.bitwise_xor(at_ref[0], away) * band, band)] = part[pair]


def first_kernel(slots, places, count, at_ref, *refs):
    parts = refs[: len(places)]
    weight_ref, group_ref, basis_ref = refs[len(places) : len(places) + 3]
    whole, taps = refs[-2:]
    outs = refs[-2 - 2 * len(slots) : -2]
    rows, width, depth = outs[0].shape
    rank = basis_ref.shape[1] // 2
    cells = rows * width
    clear_edges(taps)
    held = None
    for at, slot in enumerate(slots):
        act_ref, sums_ref = outs[2 * at : 2 * at + 2]
        if slot // 2 != held:
            held = slot // 2
            assemble(whole, parts, places, held, at_ref)
        half = slot % 2
        values = whole[:, :, half * depth : (half + 1) * depth].astype(F32)
        unit, _ = normalized(values.reshape(cells, depth), group_ref[...], count)
        active = silu(unit).astype(BF16)
        act_ref[...] = active.reshape(act_ref.shape)
        taps[1 : rows + 1] = columns(active.astype(F32).reshape(act_ref.shape), False)
        total = conv_rows(taps, weight_ref, rows, False)
        along = jnp.dot(active, basis_ref[...], preferred_element_type=F32)
        along = along[:, :rank] + along[:, rank:]
        sums_ref[...] = jnp.concatenate([total, along], axis=1).astype(BF16)


def first_conv(parts, places, slots, weight, same_group, basis, row, rows, count, after=()):
    _, band, width, double = parts[0].shape
    depth = double // 2
    rank = basis.shape[1] // 2
    wide = weight.shape[2]
    cells = rows * width
    outs = [
        jax.ShapeDtypeStruct((rows, width, depth), BF16),
        jax.ShapeDtypeStruct((cells, wide + rank), BF16),
    ]
    made, token = run(
        functools.partial(first_kernel, slots, places, count),
        "first_conv",
        outs * len(slots),
        [row],
        [*parts, weight, same_group, basis],
        after,
        [
            pltpu.VMEM((rows, width, double), BF16),
            pltpu.VMEM((rows + 2, width, 3 * depth), BF16),
        ],
        14,
        18 * len(slots) * cells * depth * wide,
    )
    return [(made[2 * at], made[2 * at + 1]) for at in range(len(slots))], token


def back_kernel(slots, places, at_ref, *refs):
    bands = len(places)
    parts = refs[:bands]
    weight_ref, along_ref, other_ref = refs[bands : bands + 3]
    later_ref, whole, taps = refs[-3:]
    outs = refs[-3 - 2 * slots : -3]
    add_into(later_ref, along_ref, other_ref)
    rows, width, depth = outs[0].shape
    clear_edges(taps)
    for slot in reversed(range(slots)):
        cot_ref, sums_ref = outs[2 * slot : 2 * slot + 2]
        if slot % 2:
            assemble(whole, parts, places, slot // 2, at_ref)
        half = slot % 2
        values = whole[:, :, half * depth : (half + 1) * depth]
        cot_ref[...] = values
        taps[1 : rows + 1] = columns(values.astype(F32), True)
        sums_ref[...] = side_by_side(conv_rows(taps, weight_ref, rows, True)).astype(BF16)


def back_conv(parts, places, weight, alongs, row, rows, after=()):
    pairs, _, width, double = parts[0].shape
    depth = double // 2
    wide = weight.shape[2]
    cells = rows * width
    slots = 2 * pairs
    outs = [
        jax.ShapeDtypeStruct((rows, width, depth), BF16),
        jax.ShapeDtypeStruct((cells // 2, 2 * wide), BF16),
    ]
    made, token = run(
        functools.partial(back_kernel, slots, places),
        "back_conv",
        outs * slots + alongs[:1],
        [row],
        [*parts, weight, *alongs],
        after,
        [
            pltpu.VMEM((rows, width, double), BF16),
            pltpu.VMEM((rows + 2, width, 3 * depth), BF16),
        ],
        14,
        18 * slots * cells * depth * wide,
    )
    return [(made[2 * at], made[2 * at + 1]) for at in range(slots)], made[-1], token


def hidden_kernel(terms, count, *refs):
    group_ref, basis_ref = refs[terms : terms + 2]
    pay_ref, unit_ref, scale_ref, along_ref = refs[-4:]
    wide = unit_ref.shape[1]
    rank = basis_ref.shape[1] // 2
    total = refs[0][...].astype(F32)
    for term in refs[1:terms]:
        total = total + term[...].astype(F32)
    unit, scale = normalized(total[:, :wide], group_ref[...], count)
    unit_ref[...] = unit
    scale_ref[...] = scale
    hidden = silu(unit).astype(BF16)
    pay_ref[...] = jnp.concatenate([hidden.astype(F32), total[:, wide:]], axis=1).astype(BF16)
    along = jnp.dot(hidden, basis_ref[...], preferred_element_type=F32)
    along_ref[...] = side_by_side(along[:, :rank] + along[:, rank:]).astype(BF16)


def hidden_step(terms, same_group, basis, count, after=()):
    cells, both = terms[0].shape
    wide = same_group.shape[0]
    return run(
        functools.partial(hidden_kernel, len(terms), count),
        "hidden_step",
        [
            jax.ShapeDtypeStruct((cells, both), BF16),
            jax.ShapeDtypeStruct((cells, wide), F32),
            jax.ShapeDtypeStruct((1, wide), F32),
            jax.ShapeDtypeStruct((cells // 2, basis.shape[1]), BF16),
        ],
        [],
        [*terms, same_group, basis],
        after,
        held=12,
        flops=40 * cells * wide,
    )


def second_kernel(slots, bands, at_ref, *refs):
    pays = refs[:slots]
    weight_ref, along_ref, other_ref = refs[slots : slots + 3]
    later_ref, whole, taps = refs[-3:]
    outs = refs[-3 - bands : -3]
    add_into(later_ref, along_ref, other_ref)
    band, width, double = outs[0].shape[1:]
    rows = whole.shape[0]
    depth = taps.shape[2] // 3
    wide = double // 2
    clear_edges(taps)
    for slot in range(slots):
        hidden = pays[slot][:, :depth].astype(F32).reshape(rows, width, depth)
        taps[1 : rows + 1] = columns(hidden, False)
        whole[...] = conv_rows(taps, weight_ref, rows, False).reshape(rows, width, wide)
        lanes = slice(slot % 2 * wide, (slot % 2 + 1) * wide)
        for away in range(bands):
            start = jnp.bitwise_xor(at_ref[0], away) * band
            outs[away][slot // 2, :, :, lanes] = whole[pl.ds(start, band)].astype(BF16)


def second_conv(pays, weight, alongs, row, rows, bands, after=()):
    slots = len(pays)
    cells, _ = pays[0].shape
    width = cells // rows
    depth = weight.shape[1] // 3
    wide = weight.shape[2]
    out = jax.ShapeDtypeStruct((slots // 2, rows // bands, width, 2 * wide), BF16)
    return run(
        functools.partial(second_kernel, slots, bands),
        "second_conv",
        [out] * bands + alongs[:1],
        [row],
        [*pays, weight, *alongs],
        after,
        [
            pltpu.VMEM((rows, width, wide), F32),
            pltpu.VMEM((rows + 2, width, 3 * depth), BF16),
        ],
        14,
        18 * slots * cells * depth * wide,
    )


def band_kernel(terms, slots, *refs):
    outs = refs[-slots:]
    wide = outs[0].shape[-1]
    total = refs[0][...].astype(F32)
    for term in refs[1:terms]:
        total = total + term[...].astype(F32)
    for slot, out in enumerate(outs):
        lanes = slice(slot % 2 * wide, (slot % 2 + 1) * wide)
        out[...] = total[slot // 2, :, :, lanes].astype(BF16)


def band_step(terms, after=()):
    pairs, band, width, double = terms[0].shape
    out = jax.ShapeDtypeStruct((band, width, double // 2), BF16)
    return run(
        functools.partial(band_kernel, len(terms), 2 * pairs),
        "band_step",
        [out] * (2 * pairs),
        [],
        terms,
        after,
    )


def join_kernel(blocks, at_ref, x_ref, *refs):
    out = refs[-1]
    width = x_ref.shape[-1] // blocks
    for away in range(blocks):
        for block in range(blocks):

            @pl.when(jnp.bitwise_xor(at_ref[0], away) == block)
            def _(away=away, block=block):
                lanes = slice(block * width, (block + 1) * width)
                added = x_ref[:, :, lanes].astype(F32) + refs[away][...].astype(F32)
                out[:, :, lanes] = added.astype(BF16)


def join_blocks(x, parts, chip, after=()):
    return run(
        functools.partial(join_kernel, len(parts)),
        "join_blocks",
        [x],
        [chip],
        [x, *parts],
        after,
    )


def pre_kernel(terms, count, *refs):
    unit_ref, scale_ref, group_ref, along_ref, other_ref = refs[terms : terms + 5]
    out_ref, later_ref = refs[-2:]
    later_ref[0] = along_ref[...]
    later_ref[1] = other_ref[...]
    total = refs[0][...].astype(F32)
    for term in refs[1:terms]:
        total = total + term[...].astype(F32)
    unit = unit_ref[...]
    gate = 0.5 + 0.5 * jnp.tanh(0.5 * unit)
    grad = stacked_again(total) * (gate * (1.0 + unit * (1.0 - gate)))
    mean = group_sums(jnp.sum(grad, axis=0, keepdims=True), group_ref[...]) / count
    along = group_sums(jnp.sum(grad * unit, axis=0, keepdims=True), group_ref[...]) / count
    out_ref[...] = side_by_side(scale_ref[...] * (grad - mean - unit * along)).astype(BF16)


def pre_step(terms, unit, scale, same_group, alongs, count, after=()):
    cells, wide = unit.shape
    stacked = jax.ShapeDtypeStruct((2, *alongs[0].shape), BF16)
    return run(
        functools.partial(pre_kernel, len(terms), count),
        "pre_step",
        [jax.ShapeDtypeStruct((cells // 2, 2 * wide), BF16), stacked],
        [],
        [*terms, unit, scale, same_group, *alongs],
        after,
        held=12,
        flops=40 * cells * wide,
    )


def project(values, along, basis):
    both = jnp.concatenate([along, along], axis=1)
    return values - jnp.dot(both, basis, preferred_element_type=F32)


def grad_body(core_ref, left, left_t, taps, keep_ref, send_ref, width, flip):
    half = left.shape[1] // 2
    span = left.shape[0]
    wide = taps.shape[1] // 3
    turned = left[...].T

    @pl.when(core_ref[0] == 0)
    def _():
        left_t[...] = turned

    @pl.when(core_ref[0] != 0)
    def _():
        left_t[:half] = turned[half:]
        left_t[half:] = turned[:half]

    for tap in range(3):
        window = taps[tap * width : tap * width + span]
        result = jnp.dot(left_t[...], window, preferred_element_type=F32)
        first = 3 * (2 - tap if flip else tap)
        for q in range(3):
            lanes = slice(q * wide, (q + 1) * wide)
            keep_ref[first + q] = result[:half, lanes]
            send_ref[first + q] = result[half:, lanes].astype(BF16)


def fill_taps(taps, slot, rows, width, value):
    start = (slot * (rows + 1) + 1) * width
    taps[start : start + rows * width] = value.reshape(rows * width, value.shape[2])


def clear_gaps(left, taps, slots, rows, width):
    gap = rows + 1
    for slot in range(slots + 1):
        begin = slot * gap * width
        end = taps.shape[0] if slot == slots else begin + width
        taps[begin:end] = jnp.zeros((end - begin, taps.shape[1]), taps.dtype)
    for slot in range(slots):
        begin = (slot * gap + rows) * width
        end = left.shape[0] if slot == slots - 1 else begin + width
        left[begin:end] = jnp.zeros((end - begin, left.shape[1]), left.dtype)


def first_grad_kernel(slots, core_ref, *refs):
    acts, pays, grads = (refs[at * slots : (at + 1) * slots] for at in range(3))
    basis_ref = refs[3 * slots]
    keep_ref, send_ref, left, left_t, taps = refs[-5:]
    rows, width, depth = acts[0].shape
    cells = rows * width
    rank = basis_ref.shape[0] // 2
    wide = taps.shape[1] // 3
    clear_gaps(left, taps, slots, rows, width)
    for slot in range(slots):
        values = acts[slot][...].reshape(cells, depth).astype(F32)
        along = pays[slot][:, wide : wide + rank]
        begin = slot * (rows + 1) * width
        left[begin : begin + cells] = project(values, along, basis_ref[...]).astype(BF16)
        right = stacked_again(grads[slot][...].astype(F32)).reshape(rows, width, wide)
        fill_taps(taps, slot, rows, width, columns(right, True))
    grad_body(core_ref, left, left_t, taps, keep_ref, send_ref, width, True)


def second_grad_kernel(slots, core_ref, *refs):
    cots, pays = (refs[at * slots : (at + 1) * slots] for at in range(2))
    alongs = refs[2 * slots : 2 * slots + slots // 2]
    basis_ref = refs[2 * slots + slots // 2]
    keep_ref, send_ref, left, left_t, taps = refs[-5:]
    rows, width, depth = cots[0].shape
    cells = rows * width
    rank = basis_ref.shape[0] // 2
    wide = taps.shape[1] // 3
    clear_gaps(left, taps, slots, rows, width)
    for slot in range(slots):
        begin = slot * (rows + 1) * width
        left[begin : begin + cells] = cots[slot][...].reshape(cells, depth)
        packed = alongs[slot // 2][slot % 2]
        along = jnp.concatenate([packed[:, :rank], packed[:, rank:]], axis=0)
        values = pays[slot][:, :wide].astype(F32)
        right = project(values, along, basis_ref[...]).astype(BF16).astype(F32)
        fill_taps(taps, slot, rows, width, columns(right.reshape(rows, width, wide), False))
    grad_body(core_ref, left, left_t, taps, keep_ref, send_ref, width, False)


def weight_grad(kernel, name, core, lefts, firsts, seconds, basis, wide, after=()):
    slots = len(firsts)
    rows, width, depth = lefts[0].shape
    used = slots * (rows + 1) * width
    span = -(-used // 128) * 128
    half = depth // 2
    tap_rows = 2 * width + span
    return run(
        functools.partial(kernel, slots),
        name,
        [
            jax.ShapeDtypeStruct((9, half, wide), F32),
            jax.ShapeDtypeStruct((9, half, wide), BF16),
        ],
        [core],
        [*lefts, *firsts, *seconds, basis],
        after,
        [
            pltpu.VMEM((span, depth), BF16),
            pltpu.VMEM((depth, span), BF16),
            pltpu.VMEM((tap_rows, 3 * wide), BF16),
        ],
        28,
        18 * slots * rows * width * depth * wide,
    )


def halves_kernel(turn, core_ref, own_ref, other_ref, *refs):
    outs = refs[-2:] if turn else refs[-1:]
    half = own_ref.shape[1]

    @pl.when(core_ref[0] == 0)
    def _():
        outs[0][:, :half] = own_ref[...]
        outs[0][:, half:] = other_ref[...]

    @pl.when(core_ref[0] != 0)
    def _():
        outs[0][:, :half] = other_ref[...]
        outs[0][:, half:] = own_ref[...]

    if turn:
        for tap in range(9):
            outs[1][tap] = outs[0][tap].T


def join_halves(core, own, other, turn, after=()):
    _, half, wide = own.shape
    outs = [jax.ShapeDtypeStruct((9, 2 * half, wide), BF16)]
    if turn:
        outs.append(jax.ShapeDtypeStruct((9, wide, 2 * half), BF16))
    return run(
        functools.partial(halves_kernel, turn), "join_halves", outs, [core], [own, other], after,
        held=12,
    )


def basis_kernel(blocks, at_ref, basis_ref, *refs):
    rows_ref, columns_ref = refs[-2:]
    rank, channels = basis_ref.shape
    width = channels // blocks
    for block in range(blocks):

        @pl.when(at_ref[0] == block)
        def _(block=block):
            values = basis_ref[:, block * width : (block + 1) * width]
            high = values.astype(BF16).astype(F32)
            both = jnp.concatenate([high, values - high], axis=0)
            rows_ref[...] = both.astype(BF16)
            columns_ref[...] = both.T.astype(BF16)


def basis_parts(at, basis, blocks, after=()):
    rank, channels = basis.shape
    width = channels // blocks
    return run(
        functools.partial(basis_kernel, blocks),
        "basis_parts",
        [
            jax.ShapeDtypeStruct((2 * rank, width), BF16),
            jax.ShapeDtypeStruct((width, 2 * rank), BF16),
        ],
        [at],
        [basis],
        after,
    )


def flat_kernel(scale, keep_ref, got_ref, *refs):
    held = refs[-2 * (keep_ref.shape[2] // 128) - 2 :]
    out_ref = refs[-len(held) - 1]
    taps, half, wide = keep_ref.shape
    whole = wide // 128
    step = 2 * whole + 1
    count = half // 2
    zeros = jnp.zeros((half, 64), F32)
    for tap in range(taps):
        total = (keep_ref[tap] + got_ref[tap].astype(F32)) * scale
        for at in range(whole):
            held[at][...] = total[:, 128 * at : 128 * (at + 1)]
            held[whole + 2 + at][...] = total[:, 128 * at + 64 : 128 * (at + 1) + 64]
        held[whole][...] = jnp.concatenate([total[:, 128 * whole :], zeros], axis=1)
        held[whole + 1][...] = jnp.concatenate([zeros, total[:, :64]], axis=1)
        even, odd = pl.ds(0, count, stride=2), pl.ds(1, count, stride=2)
        rows = [held[at][even, :] for at in range(whole)]
        rows.append(held[whole][even, :] + held[whole + 1][odd, :])
        rows += [held[whole + 2 + at][odd, :] for at in range(whole)]
        for at, row in enumerate(rows):
            out_ref[pl.ds(tap * count * step + at, count, stride=step), :] = row


def flat_grad(keep, got, scale, after=()):
    taps, half, wide = keep.shape
    if wide % 128 != 64 or half % 2:
        made = (keep + got.astype(F32)) * scale
        return made, made
    (made,), token = run(
        functools.partial(flat_kernel, scale),
        "flat_grad",
        [jax.ShapeDtypeStruct((taps * half * wide // 128, 128), F32)],
        [],
        [keep, got],
        after,
        scratch=[pltpu.VMEM((half, 128), F32)] * (2 * (wide // 128) + 2),
        held=12,
    )
    return made, token


def same_groups(width, size):
    at = np.arange(width) // size
    return jnp.asarray((at[:, None] == at[None, :]).astype(np.float32), BF16)


def body(images, cotangent, first_weight, second_weight, first_basis, second_basis):
    n_dp = lax.axis_size("dp")
    n_rows = lax.axis_size("rows")
    chips = n_dp // 2
    _, band, width, channels = images.shape
    rows = band * n_rows
    dp_width = channels // n_dp
    chip_width = channels // chips
    row_width = channels // n_rows
    group = channels // GROUPS
    count = float(rows * width * group)
    grad_scale = 1.0 / math.sqrt(n_dp * images.shape[0] * rows * width)

    at_dp = lax.axis_index("dp")
    at_row = lax.axis_index("rows")
    chip = (at_dp // 2).astype(jnp.int32)
    core = (at_dp % 2).astype(jnp.int32)
    row = at_row.astype(jnp.int32)
    chip_at, core_at = chip[None], core[None]
    row_at = jnp.stack([row, (row + 1) // 2 % 2])

    def to_core(x):
        return lax.ppermute(x, "dp", [(i, i ^ 1) for i in range(n_dp)])

    def to_chip(x, away):
        return lax.ppermute(x, "dp", [(i, i ^ (2 * away)) for i in range(n_dp)])

    def to_row(x, away):
        return lax.ppermute(x, "rows", [(i, i ^ away) for i in range(n_rows)])

    def chips_gather(x):
        return [x] + [to_chip(x, away) for away in range(1, chips)]

    def rows_gather(x):
        if n_rows != 4:
            return [x] + [to_row(x, away) for away in range(1, n_rows)], [
                (away, -1) for away in range(n_rows)
            ]
        second = to_row(x, 2)
        first = to_row(x, 1)
        passed = lax.ppermute(second, "rows", [(2, 3), (1, 0)])
        later, _ = lax.optimization_barrier((x, second))
        middle = lax.ppermute(later, "rows", [(1, 2), (2, 1)])
        return [x, first, second, middle, passed], [(0, -1), (1, -1), (2, -1), (3, 1), (3, 0)]

    def chips_swap(parts):
        return [parts[0]] + [to_chip(parts[away], away) for away in range(1, chips)]

    def rows_swap(parts):
        far = [to_row(parts[away], away) for away in range(n_rows - 1, 0, -1)]
        return parts[:1] + far[::-1]

    chip_groups = same_groups(chip_width, group)
    row_groups = same_groups(row_width, group)

    slots = chips_swap(split_blocks([images[0], cotangent[0]], chips, chip_at))
    image_pack, _ = pack_slots(slots, 0)
    image_parts, places = rows_gather(image_pack)

    first_weight, _ = lax.optimization_barrier((first_weight, slots[1]))
    second_weight, _ = lax.optimization_barrier((second_weight, image_parts[1:3]))
    own_first = first_weight.reshape(9, dp_width, row_width)
    own_second = second_weight.reshape(9, dp_width, row_width)
    early = tuple(image_parts[1:3])
    (second_full, second_turned), second_done = join_halves(
        core_at, own_second, to_core(own_second), True, early
    )
    (one_rows, one_columns), one_done = basis_parts(chip_at, first_basis, chips, early)
    (two_rows, two_columns), two_done = basis_parts(row_at, second_basis, n_rows, early)
    (first_full,), first_done = join_halves(core_at, own_first, to_core(own_first), False, early)
    cot_pack, cot_done = pack_slots(
        slots, 1, (*image_parts[3:], one_done, two_done, first_done, second_done)
    )
    cot_parts, _ = rows_gather(cot_pack)
    weight_one = first_full.reshape(3, 3 * chip_width, row_width)
    weight_back = second_full.reshape(3, 3 * chip_width, row_width)
    weight_two = second_turned.reshape(3, 3 * row_width, chip_width)

    made, first_terms, done = {}, {}, (cot_done,)
    for slot in range(chips - 1, -1, -1):
        if slot == 0:
            done += (first_terms[chips - 1], *cot_parts[3:])
        ((active, sums),), token = first_conv(
            image_parts, places, [slot], weight_one, chip_groups, one_columns, row_at, rows, count,
            done,
        )
        made[slot] = active
        first_terms[slot] = to_chip(sums, slot) if slot else sums
        done = (token,)
    active = [made[slot] for slot in range(chips)]
    first_terms = [first_terms[slot] for slot in range(chips)]

    (pay, unit, scale, along), hidden_done = hidden_step(
        first_terms, row_groups, two_columns, count, tuple(cot_parts[1:3])
    )
    pays = chips_gather(pay)

    away = 4
    while away < n_rows:
        along = (along.astype(F32) + to_row(along, away).astype(F32)).astype(BF16)
        away *= 2
    back, along, back_done = back_conv(
        cot_parts, places, weight_back, [along, to_row(along, 1)], row_at, rows, (hidden_done,)
    )
    whole_cot = [pair[0] for pair in back]
    back_terms = chips_swap([pair[1] for pair in back])

    (*sums, along), sums_done = second_conv(
        pays, weight_two, [along, to_row(along, 2)], row_at, rows, n_rows, (back_done,)
    )
    band_terms = rows_swap(sums)

    (pre_grad, along), pre_done = pre_step(
        back_terms, unit, scale, row_groups, [along, to_chip(along, 1)], count,
        (sums_done,),
    )
    pre_grads = chips_gather(pre_grad)
    alongs = [along]
    away = 2
    while away < chips:
        alongs += [to_chip(part, away) for part in alongs]
        away *= 2

    second_halves, second_made = weight_grad(
        second_grad_kernel, "second_grad", core_at, whole_cot, pays, alongs, two_rows,
        row_width, (pre_done, band_terms[-1]),
    )
    blocks, blocks_done = band_step(band_terms, (second_made,))
    first_halves, _ = weight_grad(
        first_grad_kernel, "first_grad", core_at, active, pays, pre_grads, one_rows,
        row_width, (blocks_done,),
    )
    second_grad, flat_done = flat_grad(
        second_halves[0], to_core(second_halves[1]), grad_scale
    )
    (block_output,), output_done = join_blocks(
        images[0], chips_swap(blocks), chip_at, (flat_done,)
    )
    first_grad, _ = flat_grad(
        first_halves[0], to_core(first_halves[1]), grad_scale, (output_done,)
    )
    block_output = block_output[None]
    first_grad = first_grad.reshape(1, 1, 9, dp_width * row_width)
    second_grad = second_grad.reshape(1, 1, 9, dp_width * row_width)
    return (block_output, first_grad, second_grad)


def solution(mesh):
    split = P("dp", "rows", None, None)
    return jax.shard_map(
        body,
        mesh=mesh,
        in_specs=(split, split, split, split, P(), P()),
        out_specs=(split, split, split),
        check_vma=False,
    )
```

```python
import functools
import math

import jax
import jax.numpy as jnp
import numpy as np
from jax import lax
from jax.experimental import pallas as pl
from jax.experimental.pallas import tpu as pltpu
from jax.sharding import PartitionSpec as P

GROUPS = 32
EPS = 1e-5
MIB = 1024 * 1024
F32 = jnp.float32
BF16 = jnp.bfloat16


def whole_block(x):
    zeros = (0,) * len(x.shape)
    return pl.BlockSpec(x.shape, lambda _: zeros, pipeline_mode=pl.Buffered(1))


def smem():
    return pl.BlockSpec(memory_space=pltpu.SMEM)


def unread(after):
    return [pl.BlockSpec(memory_space=pltpu.VMEM)] * len(after)


def run(kernel, name, outs, scalars, arrays, after=(), scratch=(), held=8, flops=0, fetch=False):
    outs = [*outs, jax.ShapeDtypeStruct((8, 128), F32)]
    moved = sum(x.size * x.dtype.itemsize for x in list(arrays) + outs)
    held_there = pl.BlockSpec(memory_space=pltpu.VMEM)
    used = len(scalars) + len(arrays)
    token_at = used + len(after) + len(outs) - 1

    def whole(*refs):
        refs[token_at][...] = jnp.zeros((8, 128), F32)
        kernel(*refs[:used], *refs[used + len(after) : token_at], *refs[token_at + 1 :])

    *made, token = pl.pallas_call(
        whole,
        grid=(1,) if fetch else (),
        out_shape=outs,
        in_specs=[smem()] * len(scalars)
        + [whole_block(x) if fetch else held_there for x in arrays]
        + unread(after),
        out_specs=[held_there] * len(outs),
        scratch_shapes=list(scratch),
        compiler_params=pltpu.CompilerParams(vmem_limit_bytes=held * MIB),
        cost_estimate=cost(flops, moved),
        name=name,
    )(*scalars, *arrays, *after)
    return made, token


def cost(flops, moved):
    return pl.CostEstimate(flops=int(flops), bytes_accessed=int(moved), transcendentals=0)


def group_sums(row, same_group):
    high = row.astype(BF16).astype(F32)
    rest = row - high
    middle = rest.astype(BF16).astype(F32)
    low = rest - middle
    at = lax.broadcasted_iota(jnp.int32, (16, row.shape[1]), 0)
    stacked = jnp.where(at == 0, high, jnp.where(at == 1, middle, jnp.where(at == 2, low, 0.0)))
    sums = jnp.dot(stacked.astype(BF16), same_group, preferred_element_type=F32)
    return jnp.sum(sums, axis=0, keepdims=True)


def normalized(values, same_group, count):
    center = group_sums(jnp.sum(values, axis=0, keepdims=True), same_group) / count
    moved = values - center
    spread = group_sums(jnp.sum(moved * moved, axis=0, keepdims=True), same_group) / count
    scale = 1.0 / jnp.sqrt(spread + EPS)
    return moved * scale, scale


def silu(unit):
    half = 0.5 * unit
    return half + half * jnp.tanh(half)


def add_into(out_ref, one_ref, other_ref):
    out_ref[...] = (one_ref[...].astype(F32) + other_ref[...].astype(F32)).astype(BF16)


def columns(values, flip):
    width = values.shape[1]
    at = lax.broadcasted_iota(jnp.int32, values.shape, 1)
    before = jnp.where(at == 0, 0.0, pltpu.roll(values, 1, axis=1))
    after = jnp.where(at == width - 1, 0.0, pltpu.roll(values, width - 1, axis=1))
    parts = [after, values, before] if flip else [before, values, after]
    return jnp.concatenate([part.astype(BF16) for part in parts], axis=2)


def conv_rows(taps, weight_ref, rows, flip):
    _, width, depth = taps.shape
    total = None
    for tap in range(3):
        window = taps[tap : tap + rows].reshape(rows * width, depth)
        term = jnp.dot(window, weight_ref[2 - tap if flip else tap], preferred_element_type=F32)
        total = term if total is None else total + term
    return total


def side_by_side(values):
    half = values.shape[0] // 2
    return jnp.concatenate([values[:half], values[half:]], axis=1)


def stacked_again(values):
    half = values.shape[1] // 2
    return jnp.concatenate([values[:, :half], values[:, half:]], axis=0)


def clear_edges(taps):
    rows = taps.shape[0]
    taps[0:1] = jnp.zeros((1,) + taps.shape[1:], taps.dtype)
    taps[rows - 1 : rows] = jnp.zeros((1,) + taps.shape[1:], taps.dtype)


def split_kernel(blocks, at_ref, *refs):
    arrays, outs = refs[:-blocks], refs[-blocks:]
    width = outs[0].shape[-1] // len(arrays)
    for away in range(blocks):
        for block in range(blocks):

            @pl.when(jnp.bitwise_xor(at_ref[0], away) == block)
            def _(away=away, block=block):
                for at, x_ref in enumerate(arrays):
                    lanes = slice(at * width, (at + 1) * width)
                    outs[away][:, :, lanes] = x_ref[:, :, block * width : (block + 1) * width]


def split_blocks(arrays, blocks, chip):
    height, width, channels = arrays[0].shape
    shape = jax.ShapeDtypeStruct((height, width, len(arrays) * channels // blocks), BF16)
    made, _ = run(
        functools.partial(split_kernel, blocks), "split_blocks", [shape] * blocks, [chip], arrays,
    )
    return made


def pack_kernel(at, *refs):
    slots, out = refs[:-1], refs[-1]
    width = slots[0].shape[-1] // 2
    for slot, ref in enumerate(slots):
        lanes = slice(slot % 2 * width, (slot % 2 + 1) * width)
        out[slot // 2, :, :, lanes] = ref[:, :, at * width : (at + 1) * width]


def pack_slots(slots, at, after=()):
    out = jax.ShapeDtypeStruct((len(slots) // 2, *slots[0].shape), BF16)
    (packed,), token = run(
        functools.partial(pack_kernel, at), "pack_slots", [out], [], slots, after
    )
    return packed, token


def assemble(whole, parts, places, pair, at_ref):
    for part, (away, who) in zip(parts, places):

        @pl.when(jnp.logical_or(who < 0, at_ref[1] == who))
        def _(part=part, away=away):
            band = part.shape[1]
            whole[pl.ds(jnp.bitwise_xor(at_ref[0], away) * band, band)] = part[pair]


def first_kernel(slots, places, count, at_ref, *refs):
    parts = refs[: len(places)]
    weight_ref, group_ref, basis_ref = refs[len(places) : len(places) + 3]
    whole, taps = refs[-2:]
    outs = refs[-2 - 2 * len(slots) : -2]
    rows, width, depth = outs[0].shape
    rank = basis_ref.shape[1] // 2
    cells = rows * width
    clear_edges(taps)
    held = None
    for at, slot in enumerate(slots):
        act_ref, sums_ref = outs[2 * at : 2 * at + 2]
        if slot // 2 != held:
            held = slot // 2
            assemble(whole, parts, places, held, at_ref)
        half = slot % 2
        values = whole[:, :, half * depth : (half + 1) * depth].astype(F32)
        unit, _ = normalized(values.reshape(cells, depth), group_ref[...], count)
        active = silu(unit).astype(BF16)
        act_ref[...] = active.reshape(act_ref.shape)
        taps[1 : rows + 1] = columns(active.astype(F32).reshape(act_ref.shape), False)
        total = conv_rows(taps, weight_ref, rows, False)
        along = jnp.dot(active, basis_ref[...], preferred_element_type=F32)
        along = along[:, :rank] + along[:, rank:]
        sums_ref[...] = jnp.concatenate([total, along], axis=1).astype(BF16)


def first_conv(parts, places, slots, weight, same_group, basis, row, rows, count, after=()):
    _, band, width, double = parts[0].shape
    depth = double // 2
    rank = basis.shape[1] // 2
    wide = weight.shape[2]
    cells = rows * width
    outs = [
        jax.ShapeDtypeStruct((rows, width, depth), BF16),
        jax.ShapeDtypeStruct((cells, wide + rank), BF16),
    ]
    made, token = run(
        functools.partial(first_kernel, slots, places, count),
        "first_conv",
        outs * len(slots),
        [row],
        [*parts, weight, same_group, basis],
        after,
        [
            pltpu.VMEM((rows, width, double), BF16),
            pltpu.VMEM((rows + 2, width, 3 * depth), BF16),
        ],
        14,
        18 * len(slots) * cells * depth * wide,
    )
    return [(made[2 * at], made[2 * at + 1]) for at in range(len(slots))], token


def back_kernel(slots, places, at_ref, *refs):
    bands = len(places)
    parts = refs[:bands]
    weight_ref, along_ref, other_ref = refs[bands : bands + 3]
    later_ref, whole, taps = refs[-3:]
    outs = refs[-3 - 2 * slots : -3]
    add_into(later_ref, along_ref, other_ref)
    rows, width, depth = outs[0].shape
    clear_edges(taps)
    for slot in reversed(range(slots)):
        cot_ref, sums_ref = outs[2 * slot : 2 * slot + 2]
        if slot % 2:
            assemble(whole, parts, places, slot // 2, at_ref)
        half = slot % 2
        values = whole[:, :, half * depth : (half + 1) * depth]
        cot_ref[...] = values
        taps[1 : rows + 1] = columns(values.astype(F32), True)
        sums_ref[...] = side_by_side(conv_rows(taps, weight_ref, rows, True)).astype(BF16)


def back_conv(parts, places, weight, alongs, row, rows, after=()):
    pairs, _, width, double = parts[0].shape
    depth = double // 2
    wide = weight.shape[2]
    cells = rows * width
    slots = 2 * pairs
    outs = [
        jax.ShapeDtypeStruct((rows, width, depth), BF16),
        jax.ShapeDtypeStruct((cells // 2, 2 * wide), BF16),
    ]
    made, token = run(
        functools.partial(back_kernel, slots, places),
        "back_conv",
        outs * slots + alongs[:1],
        [row],
        [*parts, weight, *alongs],
        after,
        [
            pltpu.VMEM((rows, width, double), BF16),
            pltpu.VMEM((rows + 2, width, 3 * depth), BF16),
        ],
        14,
        18 * slots * cells * depth * wide,
    )
    return [(made[2 * at], made[2 * at + 1]) for at in range(slots)], made[-1], token


def hidden_kernel(terms, count, *refs):
    group_ref, basis_ref = refs[terms : terms + 2]
    pay_ref, unit_ref, scale_ref, along_ref = refs[-4:]
    wide = unit_ref.shape[1]
    rank = basis_ref.shape[1] // 2
    total = refs[0][...].astype(F32)
    for term in refs[1:terms]:
        total = total + term[...].astype(F32)
    unit, scale = normalized(total[:, :wide], group_ref[...], count)
    unit_ref[...] = unit
    scale_ref[...] = scale
    hidden = silu(unit).astype(BF16)
    pay_ref[...] = jnp.concatenate([hidden.astype(F32), total[:, wide:]], axis=1).astype(BF16)
    along = jnp.dot(hidden, basis_ref[...], preferred_element_type=F32)
    along_ref[...] = side_by_side(along[:, :rank] + along[:, rank:]).astype(BF16)


def hidden_step(terms, same_group, basis, count, after=()):
    cells, both = terms[0].shape
    wide = same_group.shape[0]
    return run(
        functools.partial(hidden_kernel, len(terms), count),
        "hidden_step",
        [
            jax.ShapeDtypeStruct((cells, both), BF16),
            jax.ShapeDtypeStruct((cells, wide), F32),
            jax.ShapeDtypeStruct((1, wide), F32),
            jax.ShapeDtypeStruct((cells // 2, basis.shape[1]), BF16),
        ],
        [],
        [*terms, same_group, basis],
        after,
        held=12,
        flops=40 * cells * wide,
    )


def second_kernel(slots, bands, at_ref, *refs):
    pays = refs[:slots]
    weight_ref, along_ref, other_ref = refs[slots : slots + 3]
    later_ref, whole, taps = refs[-3:]
    outs = refs[-3 - bands : -3]
    add_into(later_ref, along_ref, other_ref)
    band, width, double = outs[0].shape[1:]
    rows = whole.shape[0]
    depth = taps.shape[2] // 3
    wide = double // 2
    clear_edges(taps)
    for slot in range(slots):
        hidden = pays[slot][:, :depth].astype(F32).reshape(rows, width, depth)
        taps[1 : rows + 1] = columns(hidden, False)
        whole[...] = conv_rows(taps, weight_ref, rows, False).reshape(rows, width, wide)
        lanes = slice(slot % 2 * wide, (slot % 2 + 1) * wide)
        for away in range(bands):
            start = jnp.bitwise_xor(at_ref[0], away) * band
            outs[away][slot // 2, :, :, lanes] = whole[pl.ds(start, band)].astype(BF16)


def second_conv(pays, weight, alongs, row, rows, bands, after=()):
    slots = len(pays)
    cells, _ = pays[0].shape
    width = cells // rows
    depth = weight.shape[1] // 3
    wide = weight.shape[2]
    out = jax.ShapeDtypeStruct((slots // 2, rows // bands, width, 2 * wide), BF16)
    return run(
        functools.partial(second_kernel, slots, bands),
        "second_conv",
        [out] * bands + alongs[:1],
        [row],
        [*pays, weight, *alongs],
        after,
        [
            pltpu.VMEM((rows, width, wide), F32),
            pltpu.VMEM((rows + 2, width, 3 * depth), BF16),
        ],
        14,
        18 * slots * cells * depth * wide,
    )


def band_kernel(terms, slots, *refs):
    outs = refs[-slots:]
    wide = outs[0].shape[-1]
    total = refs[0][...].astype(F32)
    for term in refs[1:terms]:
        total = total + term[...].astype(F32)
    for slot, out in enumerate(outs):
        lanes = slice(slot % 2 * wide, (slot % 2 + 1) * wide)
        out[...] = total[slot // 2, :, :, lanes].astype(BF16)


def band_step(terms, after=()):
    pairs, band, width, double = terms[0].shape
    out = jax.ShapeDtypeStruct((band, width, double // 2), BF16)
    return run(
        functools.partial(band_kernel, len(terms), 2 * pairs),
        "band_step",
        [out] * (2 * pairs),
        [],
        terms,
        after,
    )


def join_kernel(blocks, at_ref, x_ref, *refs):
    out = refs[-1]
    width = x_ref.shape[-1] // blocks
    for away in range(blocks):
        for block in range(blocks):

            @pl.when(jnp.bitwise_xor(at_ref[0], away) == block)
            def _(away=away, block=block):
                lanes = slice(block * width, (block + 1) * width)
                added = x_ref[:, :, lanes].astype(F32) + refs[away][...].astype(F32)
                out[:, :, lanes] = added.astype(BF16)


def join_blocks(x, parts, chip, after=()):
    return run(
        functools.partial(join_kernel, len(parts)),
        "join_blocks",
        [x],
        [chip],
        [x, *parts],
        after,
    )


def pre_kernel(terms, count, *refs):
    unit_ref, scale_ref, group_ref, along_ref, other_ref = refs[terms : terms + 5]
    out_ref, later_ref = refs[-2:]
    later_ref[0] = along_ref[...]
    later_ref[1] = other_ref[...]
    total = refs[0][...].astype(F32)
    for term in refs[1:terms]:
        total = total + term[...].astype(F32)
    unit = unit_ref[...]
    gate = 0.5 + 0.5 * jnp.tanh(0.5 * unit)
    grad = stacked_again(total) * (gate * (1.0 + unit * (1.0 - gate)))
    mean = group_sums(jnp.sum(grad, axis=0, keepdims=True), group_ref[...]) / count
    along = group_sums(jnp.sum(grad * unit, axis=0, keepdims=True), group_ref[...]) / count
    out_ref[...] = side_by_side(scale_ref[...] * (grad - mean - unit * along)).astype(BF16)


def pre_step(terms, unit, scale, same_group, alongs, count, after=()):
    cells, wide = unit.shape
    stacked = jax.ShapeDtypeStruct((2, *alongs[0].shape), BF16)
    return run(
        functools.partial(pre_kernel, len(terms), count),
        "pre_step",
        [jax.ShapeDtypeStruct((cells // 2, 2 * wide), BF16), stacked],
        [],
        [*terms, unit, scale, same_group, *alongs],
        after,
        held=12,
        flops=40 * cells * wide,
    )


def project(values, along, basis):
    both = jnp.concatenate([along, along], axis=1)
    return values - jnp.dot(both, basis, preferred_element_type=F32)


def grad_body(core_ref, left, left_t, taps, keep_ref, send_ref, width, flip):
    half = left.shape[1] // 2
    span = left.shape[0]
    wide = taps.shape[1] // 3
    turned = left[...].T

    @pl.when(core_ref[0] == 0)
    def _():
        left_t[...] = turned

    @pl.when(core_ref[0] != 0)
    def _():
        left_t[:half] = turned[half:]
        left_t[half:] = turned[:half]

    for tap in range(3):
        window = taps[tap * width : tap * width + span]
        result = jnp.dot(left_t[...], window, preferred_element_type=F32)
        first = 3 * (2 - tap if flip else tap)
        for q in range(3):
            lanes = slice(q * wide, (q + 1) * wide)
            keep_ref[first + q] = result[:half, lanes]
            send_ref[first + q] = result[half:, lanes].astype(BF16)


def fill_taps(taps, slot, rows, width, value):
    start = (slot * (rows + 1) + 1) * width
    taps[start : start + rows * width] = value.reshape(rows * width, value.shape[2])


def clear_gaps(left, taps, slots, rows, width):
    gap = rows + 1
    for slot in range(slots + 1):
        begin = slot * gap * width
        end = taps.shape[0] if slot == slots else begin + width
        taps[begin:end] = jnp.zeros((end - begin, taps.shape[1]), taps.dtype)
    for slot in range(slots):
        begin = (slot * gap + rows) * width
        end = left.shape[0] if slot == slots - 1 else begin + width
        left[begin:end] = jnp.zeros((end - begin, left.shape[1]), left.dtype)


def first_grad_kernel(slots, core_ref, *refs):
    acts, pays, grads = (refs[at * slots : (at + 1) * slots] for at in range(3))
    basis_ref = refs[3 * slots]
    keep_ref, send_ref, left, left_t, taps = refs[-5:]
    rows, width, depth = acts[0].shape
    cells = rows * width
    rank = basis_ref.shape[0] // 2
    wide = taps.shape[1] // 3
    clear_gaps(left, taps, slots, rows, width)
    for slot in range(slots):
        values = acts[slot][...].reshape(cells, depth).astype(F32)
        along = pays[slot][:, wide : wide + rank]
        begin = slot * (rows + 1) * width
        left[begin : begin + cells] = project(values, along, basis_ref[...]).astype(BF16)
        right = stacked_again(grads[slot][...].astype(F32)).reshape(rows, width, wide)
        fill_taps(taps, slot, rows, width, columns(right, True))
    grad_body(core_ref, left, left_t, taps, keep_ref, send_ref, width, True)


def second_grad_kernel(slots, core_ref, *refs):
    cots, pays = (refs[at * slots : (at + 1) * slots] for at in range(2))
    alongs = refs[2 * slots : 2 * slots + slots // 2]
    basis_ref = refs[2 * slots + slots // 2]
    keep_ref, send_ref, left, left_t, taps = refs[-5:]
    rows, width, depth = cots[0].shape
    cells = rows * width
    rank = basis_ref.shape[0] // 2
    wide = taps.shape[1] // 3
    clear_gaps(left, taps, slots, rows, width)
    for slot in range(slots):
        begin = slot * (rows + 1) * width
        left[begin : begin + cells] = cots[slot][...].reshape(cells, depth)
        packed = alongs[slot // 2][slot % 2]
        along = jnp.concatenate([packed[:, :rank], packed[:, rank:]], axis=0)
        values = pays[slot][:, :wide].astype(F32)
        right = project(values, along, basis_ref[...]).astype(BF16).astype(F32)
        fill_taps(taps, slot, rows, width, columns(right.reshape(rows, width, wide), False))
    grad_body(core_ref, left, left_t, taps, keep_ref, send_ref, width, False)


def weight_grad(kernel, name, core, lefts, firsts, seconds, basis, wide, after=()):
    slots = len(firsts)
    rows, width, depth = lefts[0].shape
    used = slots * (rows + 1) * width
    span = -(-used // 128) * 128
    half = depth // 2
    tap_rows = 2 * width + span
    return run(
        functools.partial(kernel, slots),
        name,
        [
            jax.ShapeDtypeStruct((9, half, wide), F32),
            jax.ShapeDtypeStruct((9, half, wide), BF16),
        ],
        [core],
        [*lefts, *firsts, *seconds, basis],
        after,
        [
            pltpu.VMEM((span, depth), BF16),
            pltpu.VMEM((depth, span), BF16),
            pltpu.VMEM((tap_rows, 3 * wide), BF16),
        ],
        28,
        18 * slots * rows * width * depth * wide,
    )


def halves_kernel(turn, core_ref, own_ref, other_ref, *refs):
    outs = refs[-2:] if turn else refs[-1:]
    half = own_ref.shape[1]

    @pl.when(core_ref[0] == 0)
    def _():
        outs[0][:, :half] = own_ref[...]
        outs[0][:, half:] = other_ref[...]

    @pl.when(core_ref[0] != 0)
    def _():
        outs[0][:, :half] = other_ref[...]
        outs[0][:, half:] = own_ref[...]

    if turn:
        for tap in range(9):
            outs[1][tap] = outs[0][tap].T


def join_halves(core, own, other, turn, after=()):
    _, half, wide = own.shape
    outs = [jax.ShapeDtypeStruct((9, 2 * half, wide), BF16)]
    if turn:
        outs.append(jax.ShapeDtypeStruct((9, wide, 2 * half), BF16))
    return run(
        functools.partial(halves_kernel, turn), "join_halves", outs, [core], [own, other], after,
        held=12,
    )


def basis_kernel(blocks, at_ref, basis_ref, *refs):
    rows_ref, columns_ref = refs[-2:]
    rank, channels = basis_ref.shape
    width = channels // blocks
    for block in range(blocks):

        @pl.when(at_ref[0] == block)
        def _(block=block):
            values = basis_ref[:, block * width : (block + 1) * width]
            high = values.astype(BF16).astype(F32)
            both = jnp.concatenate([high, values - high], axis=0)
            rows_ref[...] = both.astype(BF16)
            columns_ref[...] = both.T.astype(BF16)


def basis_parts(at, basis, blocks, after=()):
    rank, channels = basis.shape
    width = channels // blocks
    return run(
        functools.partial(basis_kernel, blocks),
        "basis_parts",
        [
            jax.ShapeDtypeStruct((2 * rank, width), BF16),
            jax.ShapeDtypeStruct((width, 2 * rank), BF16),
        ],
        [at],
        [basis],
        after,
    )


def flat_kernel(scale, keep_ref, got_ref, *refs):
    held = refs[-2 * (keep_ref.shape[2] // 128) - 2 :]
    out_ref = refs[-len(held) - 1]
    taps, half, wide = keep_ref.shape
    whole = wide // 128
    step = 2 * whole + 1
    count = half // 2
    zeros = jnp.zeros((half, 64), F32)
    for tap in range(taps):
        total = (keep_ref[tap] + got_ref[tap].astype(F32)) * scale
        for at in range(whole):
            held[at][...] = total[:, 128 * at : 128 * (at + 1)]
            held[whole + 2 + at][...] = total[:, 128 * at + 64 : 128 * (at + 1) + 64]
        held[whole][...] = jnp.concatenate([total[:, 128 * whole :], zeros], axis=1)
        held[whole + 1][...] = jnp.concatenate([zeros, total[:, :64]], axis=1)
        even, odd = pl.ds(0, count, stride=2), pl.ds(1, count, stride=2)
        rows = [held[at][even, :] for at in range(whole)]
        rows.append(held[whole][even, :] + held[whole + 1][odd, :])
        rows += [held[whole + 2 + at][odd, :] for at in range(whole)]
        for at, row in enumerate(rows):
            out_ref[pl.ds(tap * count * step + at, count, stride=step), :] = row


def flat_grad(keep, got, scale, after=()):
    taps, half, wide = keep.shape
    if wide % 128 != 64 or half % 2:
        made = (keep + got.astype(F32)) * scale
        return made, made
    (made,), token = run(
        functools.partial(flat_kernel, scale),
        "flat_grad",
        [jax.ShapeDtypeStruct((taps * half * wide // 128, 128), F32)],
        [],
        [keep, got],
        after,
        scratch=[pltpu.VMEM((half, 128), F32)] * (2 * (wide // 128) + 2),
        held=12,
    )
    return made, token


def same_groups(width, size):
    at = np.arange(width) // size
    return jnp.asarray((at[:, None] == at[None, :]).astype(np.float32), BF16)


def body(images, cotangent, first_weight, second_weight, first_basis, second_basis):
    n_dp = lax.axis_size("dp")
    n_rows = lax.axis_size("rows")
    chips = n_dp // 2
    _, band, width, channels = images.shape
    rows = band * n_rows
    dp_width = channels // n_dp
    chip_width = channels // chips
    row_width = channels // n_rows
    group = channels // GROUPS
    count = float(rows * width * group)
    grad_scale = 1.0 / math.sqrt(n_dp * images.shape[0] * rows * width)

    at_dp = lax.axis_index("dp")
    at_row = lax.axis_index("rows")
    chip = (at_dp // 2).astype(jnp.int32)
    core = (at_dp % 2).astype(jnp.int32)
    row = at_row.astype(jnp.int32)
    chip_at, core_at = chip[None], core[None]
    row_at = jnp.stack([row, (row + 1) // 2 % 2])

    def to_core(x):
        return lax.ppermute(x, "dp", [(i, i ^ 1) for i in range(n_dp)])

    def to_chip(x, away):
        return lax.ppermute(x, "dp", [(i, i ^ (2 * away)) for i in range(n_dp)])

    def to_row(x, away):
        return lax.ppermute(x, "rows", [(i, i ^ away) for i in range(n_rows)])

    def chips_gather(x):
        return [x] + [to_chip(x, away) for away in range(1, chips)]

    def rows_gather(x):
        if n_rows != 4:
            return [x] + [to_row(x, away) for away in range(1, n_rows)], [
                (away, -1) for away in range(n_rows)
            ]
        second = to_row(x, 2)
        first = to_row(x, 1)
        passed = lax.ppermute(second, "rows", [(2, 3), (1, 0)])
        later, _ = lax.optimization_barrier((x, second))
        middle = lax.ppermute(later, "rows", [(1, 2), (2, 1)])
        return [x, first, second, middle, passed], [(0, -1), (1, -1), (2, -1), (3, 1), (3, 0)]

    def chips_swap(parts):
        return [parts[0]] + [to_chip(parts[away], away) for away in range(1, chips)]

    def rows_swap(parts):
        far = [to_row(parts[away], away) for away in range(n_rows - 1, 0, -1)]
        return parts[:1] + far[::-1]

    chip_groups = same_groups(chip_width, group)
    row_groups = same_groups(row_width, group)

    slots = chips_swap(split_blocks([images[0], cotangent[0]], chips, chip_at))
    image_pack, _ = pack_slots(slots, 0)
    image_parts, places = rows_gather(image_pack)

    first_weight, _ = lax.optimization_barrier((first_weight, slots[1]))
    second_weight, _ = lax.optimization_barrier((second_weight, image_parts[1:3]))
    own_first = first_weight.reshape(9, dp_width, row_width)
    own_second = second_weight.reshape(9, dp_width, row_width)
    early = tuple(image_parts[1:3])
    (second_full, second_turned), second_done = join_halves(
        core_at, own_second, to_core(own_second), True, early
    )
    (one_rows, one_columns), one_done = basis_parts(chip_at, first_basis, chips, early)
    (two_rows, two_columns), two_done = basis_parts(row_at, second_basis, n_rows, early)
    (first_full,), first_done = join_halves(core_at, own_first, to_core(own_first), False, early)
    cot_pack, cot_done = pack_slots(
        slots, 1, (*image_parts[3:], one_done, two_done, first_done, second_done)
    )
    cot_parts = [cot_pack] + [to_row(cot_pack, away) for away in range(1, n_rows)]
    cot_places = [(away, -1) for away in range(n_rows)]
    weight_one = first_full.reshape(3, 3 * chip_width, row_width)
    weight_back = second_full.reshape(3, 3 * chip_width, row_width)
    weight_two = second_turned.reshape(3, 3 * row_width, chip_width)

    made, first_terms, done = {}, {}, (cot_done,)
    for slot in range(chips - 1, -1, -1):
        if slot == 0:
            done += (first_terms[chips - 1], cot_parts[2])
        ((active, sums),), token = first_conv(
            image_parts, places, [slot], weight_one, chip_groups, one_columns, row_at, rows, count,
            done,
        )
        made[slot] = active
        first_terms[slot] = to_chip(sums, slot) if slot else sums
        done = (token,)
    active = [made[slot] for slot in range(chips)]
    first_terms = [first_terms[slot] for slot in range(chips)]

    (pay, unit, scale, along), hidden_done = hidden_step(
        first_terms, row_groups, two_columns, count
    )
    pays = chips_gather(pay)

    away = 4
    while away < n_rows:
        along = (along.astype(F32) + to_row(along, away).astype(F32)).astype(BF16)
        away *= 2
    back, along, back_done = back_conv(
        cot_parts, cot_places, weight_back, [along, to_row(along, 1)], row_at, rows, (hidden_done,)
    )
    whole_cot = [pair[0] for pair in back]
    back_terms = chips_swap([pair[1] for pair in back])

    (*sums, along), sums_done = second_conv(
        pays, weight_two, [along, to_row(along, 2)], row_at, rows, n_rows, (back_done,)
    )
    band_terms = rows_swap(sums)

    (pre_grad, along), pre_done = pre_step(
        back_terms, unit, scale, row_groups, [along, to_chip(along, 1)], count,
        (sums_done,),
    )
    pre_grads = chips_gather(pre_grad)
    alongs = [along]
    away = 2
    while away < chips:
        alongs += [to_chip(part, away) for part in alongs]
        away *= 2

    second_halves, second_made = weight_grad(
        second_grad_kernel, "second_grad", core_at, whole_cot, pays, alongs, two_rows,
        row_width, (pre_done, band_terms[-1]),
    )
    blocks, blocks_done = band_step(band_terms, (second_made,))
    first_halves, _ = weight_grad(
        first_grad_kernel, "first_grad", core_at, active, pays, pre_grads, one_rows,
        row_width, (blocks_done,),
    )
    second_grad, flat_done = flat_grad(
        second_halves[0], to_core(second_halves[1]), grad_scale
    )
    (block_output,), output_done = join_blocks(
        images[0], chips_swap(blocks), chip_at, (flat_done,)
    )
    first_grad, _ = flat_grad(
        first_halves[0], to_core(first_halves[1]), grad_scale, (output_done,)
    )
    block_output = block_output[None]
    first_grad = first_grad.reshape(1, 1, 9, dp_width * row_width)
    second_grad = second_grad.reshape(1, 1, 9, dp_width * row_width)
    return (block_output, first_grad, second_grad)


def solution(mesh):
    split = P("dp", "rows", None, None)
    return jax.shard_map(
        body,
        mesh=mesh,
        in_specs=(split, split, split, split, P(), P()),
        out_specs=(split, split, split),
        check_vma=False,
    )
```

```python
import functools
import math

import jax
import jax.numpy as jnp
import numpy as np
from jax import lax
from jax.experimental import pallas as pl
from jax.experimental.pallas import tpu as pltpu
from jax.sharding import PartitionSpec as P

GROUPS = 32
EPS = 1e-5
MIB = 1024 * 1024
F32 = jnp.float32
BF16 = jnp.bfloat16


def whole_block(x):
    zeros = (0,) * len(x.shape)
    return pl.BlockSpec(x.shape, lambda _: zeros, pipeline_mode=pl.Buffered(1))


def smem():
    return pl.BlockSpec(memory_space=pltpu.SMEM)


def unread(after):
    return [pl.BlockSpec(memory_space=pltpu.VMEM)] * len(after)


def run(kernel, name, outs, scalars, arrays, after=(), scratch=(), held=8, flops=0, fetch=False):
    outs = [*outs, jax.ShapeDtypeStruct((8, 128), F32)]
    moved = sum(x.size * x.dtype.itemsize for x in list(arrays) + outs)
    held_there = pl.BlockSpec(memory_space=pltpu.VMEM)
    used = len(scalars) + len(arrays)
    token_at = used + len(after) + len(outs) - 1

    def whole(*refs):
        refs[token_at][...] = jnp.zeros((8, 128), F32)
        kernel(*refs[:used], *refs[used + len(after) : token_at], *refs[token_at + 1 :])

    *made, token = pl.pallas_call(
        whole,
        grid=(1,) if fetch else (),
        out_shape=outs,
        in_specs=[smem()] * len(scalars)
        + [whole_block(x) if fetch else held_there for x in arrays]
        + unread(after),
        out_specs=[held_there] * len(outs),
        scratch_shapes=list(scratch),
        compiler_params=pltpu.CompilerParams(vmem_limit_bytes=held * MIB),
        cost_estimate=cost(flops, moved),
        name=name,
    )(*scalars, *arrays, *after)
    return made, token


def cost(flops, moved):
    return pl.CostEstimate(flops=int(flops), bytes_accessed=int(moved), transcendentals=0)


def group_sums(row, same_group):
    high = row.astype(BF16).astype(F32)
    rest = row - high
    middle = rest.astype(BF16).astype(F32)
    low = rest - middle
    at = lax.broadcasted_iota(jnp.int32, (16, row.shape[1]), 0)
    stacked = jnp.where(at == 0, high, jnp.where(at == 1, middle, jnp.where(at == 2, low, 0.0)))
    sums = jnp.dot(stacked.astype(BF16), same_group, preferred_element_type=F32)
    return jnp.sum(sums, axis=0, keepdims=True)


def normalized(values, same_group, count):
    center = group_sums(jnp.sum(values, axis=0, keepdims=True), same_group) / count
    moved = values - center
    spread = group_sums(jnp.sum(moved * moved, axis=0, keepdims=True), same_group) / count
    scale = 1.0 / jnp.sqrt(spread + EPS)
    return moved * scale, scale


def silu(unit):
    half = 0.5 * unit
    return half + half * jnp.tanh(half)


def add_into(out_ref, one_ref, other_ref):
    out_ref[...] = (one_ref[...].astype(F32) + other_ref[...].astype(F32)).astype(BF16)


def columns(values, flip):
    width = values.shape[1]
    at = lax.broadcasted_iota(jnp.int32, values.shape, 1)
    before = jnp.where(at == 0, 0.0, pltpu.roll(values, 1, axis=1))
    after = jnp.where(at == width - 1, 0.0, pltpu.roll(values, width - 1, axis=1))
    parts = [after, values, before] if flip else [before, values, after]
    return jnp.concatenate([part.astype(BF16) for part in parts], axis=2)


def conv_rows(taps, weight_ref, rows, flip):
    _, width, depth = taps.shape
    total = None
    for tap in range(3):
        window = taps[tap : tap + rows].reshape(rows * width, depth)
        term = jnp.dot(window, weight_ref[2 - tap if flip else tap], preferred_element_type=F32)
        total = term if total is None else total + term
    return total


def side_by_side(values):
    half = values.shape[0] // 2
    return jnp.concatenate([values[:half], values[half:]], axis=1)


def stacked_again(values):
    half = values.shape[1] // 2
    return jnp.concatenate([values[:, :half], values[:, half:]], axis=0)


def clear_edges(taps):
    rows = taps.shape[0]
    taps[0:1] = jnp.zeros((1,) + taps.shape[1:], taps.dtype)
    taps[rows - 1 : rows] = jnp.zeros((1,) + taps.shape[1:], taps.dtype)


def split_kernel(blocks, at_ref, *refs):
    arrays, outs = refs[:-blocks], refs[-blocks:]
    width = outs[0].shape[-1] // len(arrays)
    for away in range(blocks):
        for block in range(blocks):

            @pl.when(jnp.bitwise_xor(at_ref[0], away) == block)
            def _(away=away, block=block):
                for at, x_ref in enumerate(arrays):
                    lanes = slice(at * width, (at + 1) * width)
                    outs[away][:, :, lanes] = x_ref[:, :, block * width : (block + 1) * width]


def split_blocks(arrays, blocks, chip):
    height, width, channels = arrays[0].shape
    shape = jax.ShapeDtypeStruct((height, width, len(arrays) * channels // blocks), BF16)
    made, _ = run(
        functools.partial(split_kernel, blocks), "split_blocks", [shape] * blocks, [chip], arrays,
    )
    return made


def pack_kernel(at, *refs):
    slots, out = refs[:-1], refs[-1]
    width = slots[0].shape[-1] // 2
    for slot, ref in enumerate(slots):
        lanes = slice(slot % 2 * width, (slot % 2 + 1) * width)
        out[slot // 2, :, :, lanes] = ref[:, :, at * width : (at + 1) * width]


def pack_slots(slots, at, after=()):
    out = jax.ShapeDtypeStruct((len(slots) // 2, *slots[0].shape), BF16)
    (packed,), token = run(
        functools.partial(pack_kernel, at), "pack_slots", [out], [], slots, after
    )
    return packed, token


def assemble(whole, parts, places, pair, at_ref):
    for part, (away, who) in zip(parts, places):

        @pl.when(jnp.logical_or(who < 0, at_ref[1] == who))
        def _(part=part, away=away):
            band = part.shape[1]
            whole[pl.ds(jnp.bitwise_xor(at_ref[0], away) * band, band)] = part[pair]


def first_kernel(slots, places, count, at_ref, *refs):
    parts = refs[: len(places)]
    weight_ref, group_ref, basis_ref = refs[len(places) : len(places) + 3]
    whole, taps = refs[-2:]
    outs = refs[-2 - 2 * len(slots) : -2]
    rows, width, depth = outs[0].shape
    rank = basis_ref.shape[1] // 2
    cells = rows * width
    clear_edges(taps)
    held = None
    for at, slot in enumerate(slots):
        act_ref, sums_ref = outs[2 * at : 2 * at + 2]
        if slot // 2 != held:
            held = slot // 2
            assemble(whole, parts, places, held, at_ref)
        half = slot % 2
        values = whole[:, :, half * depth : (half + 1) * depth].astype(F32)
        unit, _ = normalized(values.reshape(cells, depth), group_ref[...], count)
        active = silu(unit).astype(BF16)
        act_ref[...] = active.reshape(act_ref.shape)
        taps[1 : rows + 1] = columns(active.astype(F32).reshape(act_ref.shape), False)
        total = conv_rows(taps, weight_ref, rows, False)
        along = jnp.dot(active, basis_ref[...], preferred_element_type=F32)
        along = along[:, :rank] + along[:, rank:]
        sums_ref[...] = jnp.concatenate([total, along], axis=1).astype(BF16)


def first_conv(parts, places, slots, weight, same_group, basis, row, rows, count, after=()):
    _, band, width, double = parts[0].shape
    depth = double // 2
    rank = basis.shape[1] // 2
    wide = weight.shape[2]
    cells = rows * width
    outs = [
        jax.ShapeDtypeStruct((rows, width, depth), BF16),
        jax.ShapeDtypeStruct((cells, wide + rank), BF16),
    ]
    made, token = run(
        functools.partial(first_kernel, slots, places, count),
        "first_conv",
        outs * len(slots),
        [row],
        [*parts, weight, same_group, basis],
        after,
        [
            pltpu.VMEM((rows, width, double), BF16),
            pltpu.VMEM((rows + 2, width, 3 * depth), BF16),
        ],
        14,
        18 * len(slots) * cells * depth * wide,
    )
    return [(made[2 * at], made[2 * at + 1]) for at in range(len(slots))], token


def back_kernel(slots, places, at_ref, *refs):
    bands = len(places)
    parts = refs[:bands]
    weight_ref, along_ref, other_ref = refs[bands : bands + 3]
    later_ref, whole, taps = refs[-3:]
    outs = refs[-3 - 2 * slots : -3]
    add_into(later_ref, along_ref, other_ref)
    rows, width, depth = outs[0].shape
    clear_edges(taps)
    for slot in reversed(range(slots)):
        cot_ref, sums_ref = outs[2 * slot : 2 * slot + 2]
        if slot % 2:
            assemble(whole, parts, places, slot // 2, at_ref)
        half = slot % 2
        values = whole[:, :, half * depth : (half + 1) * depth]
        cot_ref[...] = values
        taps[1 : rows + 1] = columns(values.astype(F32), True)
        sums_ref[...] = side_by_side(conv_rows(taps, weight_ref, rows, True)).astype(BF16)


def back_conv(parts, places, weight, alongs, row, rows, after=()):
    pairs, _, width, double = parts[0].shape
    depth = double // 2
    wide = weight.shape[2]
    cells = rows * width
    slots = 2 * pairs
    outs = [
        jax.ShapeDtypeStruct((rows, width, depth), BF16),
        jax.ShapeDtypeStruct((cells // 2, 2 * wide), BF16),
    ]
    made, token = run(
        functools.partial(back_kernel, slots, places),
        "back_conv",
        outs * slots + alongs[:1],
        [row],
        [*parts, weight, *alongs],
        after,
        [
            pltpu.VMEM((rows, width, double), BF16),
            pltpu.VMEM((rows + 2, width, 3 * depth), BF16),
        ],
        14,
        18 * slots * cells * depth * wide,
    )
    return [(made[2 * at], made[2 * at + 1]) for at in range(slots)], made[-1], token


def hidden_kernel(terms, count, *refs):
    group_ref, basis_ref = refs[terms : terms + 2]
    pay_ref, unit_ref, scale_ref, along_ref = refs[-4:]
    wide = unit_ref.shape[1]
    rank = basis_ref.shape[1] // 2
    total = refs[0][...].astype(F32)
    for term in refs[1:terms]:
        total = total + term[...].astype(F32)
    unit, scale = normalized(total[:, :wide], group_ref[...], count)
    unit_ref[...] = unit
    scale_ref[...] = scale
    hidden = silu(unit).astype(BF16)
    pay_ref[...] = jnp.concatenate([hidden.astype(F32), total[:, wide:]], axis=1).astype(BF16)
    along = jnp.dot(hidden, basis_ref[...], preferred_element_type=F32)
    along_ref[...] = side_by_side(along[:, :rank] + along[:, rank:]).astype(BF16)


def hidden_step(terms, same_group, basis, count, after=()):
    cells, both = terms[0].shape
    wide = same_group.shape[0]
    return run(
        functools.partial(hidden_kernel, len(terms), count),
        "hidden_step",
        [
            jax.ShapeDtypeStruct((cells, both), BF16),
            jax.ShapeDtypeStruct((cells, wide), F32),
            jax.ShapeDtypeStruct((1, wide), F32),
            jax.ShapeDtypeStruct((cells // 2, basis.shape[1]), BF16),
        ],
        [],
        [*terms, same_group, basis],
        after,
        held=12,
        flops=40 * cells * wide,
    )


def second_kernel(slots, bands, at_ref, *refs):
    pays = refs[:slots]
    weight_ref, along_ref, other_ref = refs[slots : slots + 3]
    later_ref, whole, taps = refs[-3:]
    outs = refs[-3 - bands : -3]
    add_into(later_ref, along_ref, other_ref)
    band, width, double = outs[0].shape[1:]
    rows = whole.shape[0]
    depth = taps.shape[2] // 3
    wide = double // 2
    clear_edges(taps)
    for slot in range(slots):
        hidden = pays[slot][:, :depth].astype(F32).reshape(rows, width, depth)
        taps[1 : rows + 1] = columns(hidden, False)
        whole[...] = conv_rows(taps, weight_ref, rows, False).reshape(rows, width, wide)
        lanes = slice(slot % 2 * wide, (slot % 2 + 1) * wide)
        for away in range(bands):
            start = jnp.bitwise_xor(at_ref[0], away) * band
            outs[away][slot // 2, :, :, lanes] = whole[pl.ds(start, band)].astype(BF16)


def second_conv(pays, weight, alongs, row, rows, bands, after=()):
    slots = len(pays)
    cells, _ = pays[0].shape
    width = cells // rows
    depth = weight.shape[1] // 3
    wide = weight.shape[2]
    out = jax.ShapeDtypeStruct((slots // 2, rows // bands, width, 2 * wide), BF16)
    return run(
        functools.partial(second_kernel, slots, bands),
        "second_conv",
        [out] * bands + alongs[:1],
        [row],
        [*pays, weight, *alongs],
        after,
        [
            pltpu.VMEM((rows, width, wide), F32),
            pltpu.VMEM((rows + 2, width, 3 * depth), BF16),
        ],
        14,
        18 * slots * cells * depth * wide,
    )


def band_kernel(terms, slots, *refs):
    outs = refs[-slots:]
    wide = outs[0].shape[-1]
    total = refs[0][...].astype(F32)
    for term in refs[1:terms]:
        total = total + term[...].astype(F32)
    for slot, out in enumerate(outs):
        lanes = slice(slot % 2 * wide, (slot % 2 + 1) * wide)
        out[...] = total[slot // 2, :, :, lanes].astype(BF16)


def band_step(terms, after=()):
    pairs, band, width, double = terms[0].shape
    out = jax.ShapeDtypeStruct((band, width, double // 2), BF16)
    return run(
        functools.partial(band_kernel, len(terms), 2 * pairs),
        "band_step",
        [out] * (2 * pairs),
        [],
        terms,
        after,
    )


def join_kernel(blocks, at_ref, x_ref, *refs):
    out = refs[-1]
    width = x_ref.shape[-1] // blocks
    for away in range(blocks):
        for block in range(blocks):

            @pl.when(jnp.bitwise_xor(at_ref[0], away) == block)
            def _(away=away, block=block):
                lanes = slice(block * width, (block + 1) * width)
                added = x_ref[:, :, lanes].astype(F32) + refs[away][...].astype(F32)
                out[:, :, lanes] = added.astype(BF16)


def join_blocks(x, parts, chip, after=()):
    return run(
        functools.partial(join_kernel, len(parts)),
        "join_blocks",
        [x],
        [chip],
        [x, *parts],
        after,
    )


def pre_kernel(terms, count, *refs):
    unit_ref, scale_ref, group_ref, along_ref, other_ref = refs[terms : terms + 5]
    out_ref, later_ref = refs[-2:]
    later_ref[0] = along_ref[...]
    later_ref[1] = other_ref[...]
    total = refs[0][...].astype(F32)
    for term in refs[1:terms]:
        total = total + term[...].astype(F32)
    unit = unit_ref[...]
    gate = 0.5 + 0.5 * jnp.tanh(0.5 * unit)
    grad = stacked_again(total) * (gate * (1.0 + unit * (1.0 - gate)))
    mean = group_sums(jnp.sum(grad, axis=0, keepdims=True), group_ref[...]) / count
    along = group_sums(jnp.sum(grad * unit, axis=0, keepdims=True), group_ref[...]) / count
    out_ref[...] = side_by_side(scale_ref[...] * (grad - mean - unit * along)).astype(BF16)


def pre_step(terms, unit, scale, same_group, alongs, count, after=()):
    cells, wide = unit.shape
    stacked = jax.ShapeDtypeStruct((2, *alongs[0].shape), BF16)
    return run(
        functools.partial(pre_kernel, len(terms), count),
        "pre_step",
        [jax.ShapeDtypeStruct((cells // 2, 2 * wide), BF16), stacked],
        [],
        [*terms, unit, scale, same_group, *alongs],
        after,
        held=12,
        flops=40 * cells * wide,
    )


def project(values, along, basis):
    both = jnp.concatenate([along, along], axis=1)
    return values - jnp.dot(both, basis, preferred_element_type=F32)


def grad_body(core_ref, left, left_t, taps, keep_ref, send_ref, width, flip):
    half = left.shape[1] // 2
    span = left.shape[0]
    wide = taps.shape[1] // 3
    turned = left[...].T

    @pl.when(core_ref[0] == 0)
    def _():
        left_t[...] = turned

    @pl.when(core_ref[0] != 0)
    def _():
        left_t[:half] = turned[half:]
        left_t[half:] = turned[:half]

    for tap in range(3):
        window = taps[tap * width : tap * width + span]
        result = jnp.dot(left_t[...], window, preferred_element_type=F32)
        first = 3 * (2 - tap if flip else tap)
        for q in range(3):
            lanes = slice(q * wide, (q + 1) * wide)
            keep_ref[first + q] = result[:half, lanes]
            send_ref[first + q] = result[half:, lanes].astype(BF16)


def fill_taps(taps, slot, rows, width, value):
    start = (slot * (rows + 1) + 1) * width
    taps[start : start + rows * width] = value.reshape(rows * width, value.shape[2])


def clear_gaps(left, taps, slots, rows, width):
    gap = rows + 1
    for slot in range(slots + 1):
        begin = slot * gap * width
        end = taps.shape[0] if slot == slots else begin + width
        taps[begin:end] = jnp.zeros((end - begin, taps.shape[1]), taps.dtype)
    for slot in range(slots):
        begin = (slot * gap + rows) * width
        end = left.shape[0] if slot == slots - 1 else begin + width
        left[begin:end] = jnp.zeros((end - begin, left.shape[1]), left.dtype)


def first_grad_kernel(slots, core_ref, *refs):
    acts, pays, grads = (refs[at * slots : (at + 1) * slots] for at in range(3))
    basis_ref = refs[3 * slots]
    keep_ref, send_ref, left, left_t, taps = refs[-5:]
    rows, width, depth = acts[0].shape
    cells = rows * width
    rank = basis_ref.shape[0] // 2
    wide = taps.shape[1] // 3
    clear_gaps(left, taps, slots, rows, width)
    for slot in range(slots):
        values = acts[slot][...].reshape(cells, depth).astype(F32)
        along = pays[slot][:, wide : wide + rank]
        begin = slot * (rows + 1) * width
        left[begin : begin + cells] = project(values, along, basis_ref[...]).astype(BF16)
        right = stacked_again(grads[slot][...].astype(F32)).reshape(rows, width, wide)
        fill_taps(taps, slot, rows, width, columns(right, True))
    grad_body(core_ref, left, left_t, taps, keep_ref, send_ref, width, True)


def second_grad_kernel(slots, core_ref, *refs):
    cots, pays = (refs[at * slots : (at + 1) * slots] for at in range(2))
    alongs = refs[2 * slots : 2 * slots + slots // 2]
    basis_ref = refs[2 * slots + slots // 2]
    keep_ref, send_ref, left, left_t, taps = refs[-5:]
    rows, width, depth = cots[0].shape
    cells = rows * width
    rank = basis_ref.shape[0] // 2
    wide = taps.shape[1] // 3
    clear_gaps(left, taps, slots, rows, width)
    for slot in range(slots):
        begin = slot * (rows + 1) * width
        left[begin : begin + cells] = cots[slot][...].reshape(cells, depth)
        packed = alongs[slot // 2][slot % 2]
        along = jnp.concatenate([packed[:, :rank], packed[:, rank:]], axis=0)
        values = pays[slot][:, :wide].astype(F32)
        right = project(values, along, basis_ref[...]).astype(BF16).astype(F32)
        fill_taps(taps, slot, rows, width, columns(right.reshape(rows, width, wide), False))
    grad_body(core_ref, left, left_t, taps, keep_ref, send_ref, width, False)


def weight_grad(kernel, name, core, lefts, firsts, seconds, basis, wide, after=()):
    slots = len(firsts)
    rows, width, depth = lefts[0].shape
    used = slots * (rows + 1) * width
    span = -(-used // 128) * 128
    half = depth // 2
    tap_rows = 2 * width + span
    return run(
        functools.partial(kernel, slots),
        name,
        [
            jax.ShapeDtypeStruct((9, half, wide), F32),
            jax.ShapeDtypeStruct((9, half, wide), BF16),
        ],
        [core],
        [*lefts, *firsts, *seconds, basis],
        after,
        [
            pltpu.VMEM((span, depth), BF16),
            pltpu.VMEM((depth, span), BF16),
            pltpu.VMEM((tap_rows, 3 * wide), BF16),
        ],
        28,
        18 * slots * rows * width * depth * wide,
    )


def halves_kernel(turn, core_ref, own_ref, other_ref, *refs):
    outs = refs[-2:] if turn else refs[-1:]
    half = own_ref.shape[1]

    @pl.when(core_ref[0] == 0)
    def _():
        outs[0][:, :half] = own_ref[...]
        outs[0][:, half:] = other_ref[...]

    @pl.when(core_ref[0] != 0)
    def _():
        outs[0][:, :half] = other_ref[...]
        outs[0][:, half:] = own_ref[...]

    if turn:
        for tap in range(9):
            outs[1][tap] = outs[0][tap].T


def join_halves(core, own, other, turn, after=()):
    _, half, wide = own.shape
    outs = [jax.ShapeDtypeStruct((9, 2 * half, wide), BF16)]
    if turn:
        outs.append(jax.ShapeDtypeStruct((9, wide, 2 * half), BF16))
    return run(
        functools.partial(halves_kernel, turn), "join_halves", outs, [core], [own, other], after,
        held=12,
    )


def basis_kernel(blocks, at_ref, basis_ref, *refs):
    rows_ref, columns_ref = refs[-2:]
    rank, channels = basis_ref.shape
    width = channels // blocks
    for block in range(blocks):

        @pl.when(at_ref[0] == block)
        def _(block=block):
            values = basis_ref[:, block * width : (block + 1) * width]
            high = values.astype(BF16).astype(F32)
            both = jnp.concatenate([high, values - high], axis=0)
            rows_ref[...] = both.astype(BF16)
            columns_ref[...] = both.T.astype(BF16)


def basis_parts(at, basis, blocks, after=()):
    rank, channels = basis.shape
    width = channels // blocks
    return run(
        functools.partial(basis_kernel, blocks),
        "basis_parts",
        [
            jax.ShapeDtypeStruct((2 * rank, width), BF16),
            jax.ShapeDtypeStruct((width, 2 * rank), BF16),
        ],
        [at],
        [basis],
        after,
    )


def flat_kernel(scale, keep_ref, got_ref, *refs):
    held = refs[-2 * (keep_ref.shape[2] // 128) - 2 :]
    out_ref = refs[-len(held) - 1]
    taps, half, wide = keep_ref.shape
    whole = wide // 128
    step = 2 * whole + 1
    count = half // 2
    zeros = jnp.zeros((half, 64), F32)
    for tap in range(taps):
        total = (keep_ref[tap] + got_ref[tap].astype(F32)) * scale
        for at in range(whole):
            held[at][...] = total[:, 128 * at : 128 * (at + 1)]
            held[whole + 2 + at][...] = total[:, 128 * at + 64 : 128 * (at + 1) + 64]
        held[whole][...] = jnp.concatenate([total[:, 128 * whole :], zeros], axis=1)
        held[whole + 1][...] = jnp.concatenate([zeros, total[:, :64]], axis=1)
        even, odd = pl.ds(0, count, stride=2), pl.ds(1, count, stride=2)
        rows = [held[at][even, :] for at in range(whole)]
        rows.append(held[whole][even, :] + held[whole + 1][odd, :])
        rows += [held[whole + 2 + at][odd, :] for at in range(whole)]
        for at, row in enumerate(rows):
            out_ref[pl.ds(tap * count * step + at, count, stride=step), :] = row


def flat_grad(keep, got, scale, after=()):
    taps, half, wide = keep.shape
    if wide % 128 != 64 or half % 2:
        made = (keep + got.astype(F32)) * scale
        return made, made
    (made,), token = run(
        functools.partial(flat_kernel, scale),
        "flat_grad",
        [jax.ShapeDtypeStruct((taps * half * wide // 128, 128), F32)],
        [],
        [keep, got],
        after,
        scratch=[pltpu.VMEM((half, 128), F32)] * (2 * (wide // 128) + 2),
        held=12,
    )
    return made, token


def same_groups(width, size):
    at = np.arange(width) // size
    return jnp.asarray((at[:, None] == at[None, :]).astype(np.float32), BF16)


def body(images, cotangent, first_weight, second_weight, first_basis, second_basis):
    n_dp = lax.axis_size("dp")
    n_rows = lax.axis_size("rows")
    chips = n_dp // 2
    _, band, width, channels = images.shape
    rows = band * n_rows
    dp_width = channels // n_dp
    chip_width = channels // chips
    row_width = channels // n_rows
    group = channels // GROUPS
    count = float(rows * width * group)
    grad_scale = 1.0 / math.sqrt(n_dp * images.shape[0] * rows * width)

    at_dp = lax.axis_index("dp")
    at_row = lax.axis_index("rows")
    chip = (at_dp // 2).astype(jnp.int32)
    core = (at_dp % 2).astype(jnp.int32)
    row = at_row.astype(jnp.int32)
    chip_at, core_at = chip[None], core[None]
    row_at = jnp.stack([row, (row + 1) // 2 % 2])

    def to_core(x):
        return lax.ppermute(x, "dp", [(i, i ^ 1) for i in range(n_dp)])

    def to_chip(x, away):
        return lax.ppermute(x, "dp", [(i, i ^ (2 * away)) for i in range(n_dp)])

    def to_row(x, away):
        return lax.ppermute(x, "rows", [(i, i ^ away) for i in range(n_rows)])

    def chips_gather(x):
        return [x] + [to_chip(x, away) for away in range(1, chips)]

    def rows_gather(x):
        if n_rows != 4:
            return [x] + [to_row(x, away) for away in range(1, n_rows)], [
                (away, -1) for away in range(n_rows)
            ]
        second = to_row(x, 2)
        first = to_row(x, 1)
        passed = lax.ppermute(second, "rows", [(2, 3), (1, 0)])
        later, _ = lax.optimization_barrier((x, second))
        middle = lax.ppermute(later, "rows", [(1, 2), (2, 1)])
        return [x, first, second, middle, passed], [(0, -1), (1, -1), (2, -1), (3, 1), (3, 0)]

    def chips_swap(parts):
        return [parts[0]] + [to_chip(parts[away], away) for away in range(1, chips)]

    def rows_swap(parts):
        far = [to_row(parts[away], away) for away in range(n_rows - 1, 0, -1)]
        return parts[:1] + far[::-1]

    chip_groups = same_groups(chip_width, group)
    row_groups = same_groups(row_width, group)

    slots = chips_swap(split_blocks([images[0], cotangent[0]], chips, chip_at))
    image_pack, _ = pack_slots(slots, 0)
    image_parts, places = rows_gather(image_pack)

    first_weight, _ = lax.optimization_barrier((first_weight, slots[1]))
    second_weight, _ = lax.optimization_barrier((second_weight, image_parts[1:3]))
    own_first = first_weight.reshape(9, dp_width, row_width)
    own_second = second_weight.reshape(9, dp_width, row_width)
    early = tuple(image_parts[1:3])
    (second_full, second_turned), second_done = join_halves(
        core_at, own_second, to_core(own_second), True, early
    )
    (one_rows, one_columns), one_done = basis_parts(chip_at, first_basis, chips, early)
    (two_rows, two_columns), two_done = basis_parts(row_at, second_basis, n_rows, early)
    (first_full,), first_done = join_halves(core_at, own_first, to_core(own_first), False, early)
    cot_pack, cot_done = pack_slots(
        slots, 1, (*image_parts[3:], one_done, two_done, first_done, second_done)
    )
    cot_parts, _ = rows_gather(cot_pack)
    weight_one = first_full.reshape(3, 3 * chip_width, row_width)
    weight_back = second_full.reshape(3, 3 * chip_width, row_width)
    weight_two = second_turned.reshape(3, 3 * row_width, chip_width)

    made, first_terms, done = {}, {}, (cot_done,)
    for slot in range(chips - 1, -1, -1):
        if slot == 0:
            done += (first_terms[chips - 1], first_terms[2], *cot_parts[3:])
        ((active, sums),), token = first_conv(
            image_parts, places, [slot], weight_one, chip_groups, one_columns, row_at, rows, count,
            done,
        )
        made[slot] = active
        first_terms[slot] = to_chip(sums, slot) if slot else sums
        done = (token,)
    active = [made[slot] for slot in range(chips)]
    first_terms = [first_terms[slot] for slot in range(chips)]

    (pay, unit, scale, along), hidden_done = hidden_step(
        first_terms, row_groups, two_columns, count, tuple(cot_parts[1:3])
    )
    pays = chips_gather(pay)

    away = 4
    while away < n_rows:
        along = (along.astype(F32) + to_row(along, away).astype(F32)).astype(BF16)
        away *= 2
    back, along, back_done = back_conv(
        cot_parts, places, weight_back, [along, to_row(along, 1)], row_at, rows, (hidden_done,)
    )
    whole_cot = [pair[0] for pair in back]
    back_terms = chips_swap([pair[1] for pair in back])

    (*sums, along), sums_done = second_conv(
        pays, weight_two, [along, to_row(along, 2)], row_at, rows, n_rows, (back_done,)
    )
    band_terms = rows_swap(sums)

    (pre_grad, along), pre_done = pre_step(
        back_terms, unit, scale, row_groups, [along, to_chip(along, 1)], count,
        (sums_done,),
    )
    pre_grads = chips_gather(pre_grad)
    alongs = [along]
    away = 2
    while away < chips:
        alongs += [to_chip(part, away) for part in alongs]
        away *= 2

    second_halves, second_made = weight_grad(
        second_grad_kernel, "second_grad", core_at, whole_cot, pays, alongs, two_rows,
        row_width, (pre_done, band_terms[-1]),
    )
    blocks, blocks_done = band_step(band_terms, (second_made,))
    first_halves, _ = weight_grad(
        first_grad_kernel, "first_grad", core_at, active, pays, pre_grads, one_rows,
        row_width, (blocks_done,),
    )
    second_grad, second_flat = flat_grad(
        second_halves[0], to_core(second_halves[1]), grad_scale
    )
    first_grad, first_flat = flat_grad(
        first_halves[0], to_core(first_halves[1]), grad_scale, (second_flat,)
    )
    (block_output,), _ = join_blocks(
        images[0], chips_swap(blocks), chip_at, (first_flat,)
    )
    block_output = block_output[None]
    first_grad = first_grad.reshape(1, 1, 9, dp_width * row_width)
    second_grad = second_grad.reshape(1, 1, 9, dp_width * row_width)
    return (block_output, first_grad, second_grad)


def solution(mesh):
    split = P("dp", "rows", None, None)
    return jax.shard_map(
        body,
        mesh=mesh,
        in_specs=(split, split, split, split, P(), P()),
        out_specs=(split, split, split),
        check_vma=False,
    )
```

```python
import functools
import math

import jax
import jax.numpy as jnp
import numpy as np
from jax import lax
from jax.experimental import pallas as pl
from jax.experimental.pallas import tpu as pltpu
from jax.sharding import PartitionSpec as P

GROUPS = 32
EPS = 1e-5
MIB = 1024 * 1024
F32 = jnp.float32
BF16 = jnp.bfloat16


def whole_block(x):
    zeros = (0,) * len(x.shape)
    return pl.BlockSpec(x.shape, lambda _: zeros, pipeline_mode=pl.Buffered(1))


def smem():
    return pl.BlockSpec(memory_space=pltpu.SMEM)


def unread(after):
    return [pl.BlockSpec(memory_space=pltpu.VMEM)] * len(after)


def run(kernel, name, outs, scalars, arrays, after=(), scratch=(), held=8, flops=0, fetch=False):
    outs = [*outs, jax.ShapeDtypeStruct((8, 128), F32)]
    moved = sum(x.size * x.dtype.itemsize for x in list(arrays) + outs)
    held_there = pl.BlockSpec(memory_space=pltpu.VMEM)
    used = len(scalars) + len(arrays)
    token_at = used + len(after) + len(outs) - 1

    def whole(*refs):
        refs[token_at][...] = jnp.zeros((8, 128), F32)
        kernel(*refs[:used], *refs[used + len(after) : token_at], *refs[token_at + 1 :])

    *made, token = pl.pallas_call(
        whole,
        grid=(1,) if fetch else (),
        out_shape=outs,
        in_specs=[smem()] * len(scalars)
        + [whole_block(x) if fetch else held_there for x in arrays]
        + unread(after),
        out_specs=[held_there] * len(outs),
        scratch_shapes=list(scratch),
        compiler_params=pltpu.CompilerParams(vmem_limit_bytes=held * MIB),
        cost_estimate=cost(flops, moved),
        name=name,
    )(*scalars, *arrays, *after)
    return made, token


def cost(flops, moved):
    return pl.CostEstimate(flops=int(flops), bytes_accessed=int(moved), transcendentals=0)


def group_sums(row, same_group):
    high = row.astype(BF16).astype(F32)
    rest = row - high
    middle = rest.astype(BF16).astype(F32)
    low = rest - middle
    at = lax.broadcasted_iota(jnp.int32, (16, row.shape[1]), 0)
    stacked = jnp.where(at == 0, high, jnp.where(at == 1, middle, jnp.where(at == 2, low, 0.0)))
    sums = jnp.dot(stacked.astype(BF16), same_group, preferred_element_type=F32)
    return jnp.sum(sums, axis=0, keepdims=True)


def normalized(values, same_group, count):
    center = group_sums(jnp.sum(values, axis=0, keepdims=True), same_group) / count
    moved = values - center
    spread = group_sums(jnp.sum(moved * moved, axis=0, keepdims=True), same_group) / count
    scale = 1.0 / jnp.sqrt(spread + EPS)
    return moved * scale, scale


def silu(unit):
    half = 0.5 * unit
    return half + half * jnp.tanh(half)


def add_into(out_ref, one_ref, other_ref):
    out_ref[...] = (one_ref[...].astype(F32) + other_ref[...].astype(F32)).astype(BF16)


def columns(values, flip):
    width = values.shape[1]
    at = lax.broadcasted_iota(jnp.int32, values.shape, 1)
    before = jnp.where(at == 0, 0.0, pltpu.roll(values, 1, axis=1))
    after = jnp.where(at == width - 1, 0.0, pltpu.roll(values, width - 1, axis=1))
    parts = [after, values, before] if flip else [before, values, after]
    return jnp.concatenate([part.astype(BF16) for part in parts], axis=2)


def conv_rows(taps, weight_ref, rows, flip):
    _, width, depth = taps.shape
    total = None
    for tap in range(3):
        window = taps[tap : tap + rows].reshape(rows * width, depth)
        term = jnp.dot(window, weight_ref[2 - tap if flip else tap], preferred_element_type=F32)
        total = term if total is None else total + term
    return total


def side_by_side(values):
    half = values.shape[0] // 2
    return jnp.concatenate([values[:half], values[half:]], axis=1)


def stacked_again(values):
    half = values.shape[1] // 2
    return jnp.concatenate([values[:, :half], values[:, half:]], axis=0)


def clear_edges(taps):
    rows = taps.shape[0]
    taps[0:1] = jnp.zeros((1,) + taps.shape[1:], taps.dtype)
    taps[rows - 1 : rows] = jnp.zeros((1,) + taps.shape[1:], taps.dtype)


def split_kernel(blocks, at_ref, *refs):
    arrays, outs = refs[:-blocks], refs[-blocks:]
    width = outs[0].shape[-1] // len(arrays)
    for away in range(blocks):
        for block in range(blocks):

            @pl.when(jnp.bitwise_xor(at_ref[0], away) == block)
            def _(away=away, block=block):
                for at, x_ref in enumerate(arrays):
                    lanes = slice(at * width, (at + 1) * width)
                    outs[away][:, :, lanes] = x_ref[:, :, block * width : (block + 1) * width]


def split_blocks(arrays, blocks, chip):
    height, width, channels = arrays[0].shape
    shape = jax.ShapeDtypeStruct((height, width, len(arrays) * channels // blocks), BF16)
    made, _ = run(
        functools.partial(split_kernel, blocks), "split_blocks", [shape] * blocks, [chip], arrays,
    )
    return made


def pack_kernel(at, *refs):
    slots, out = refs[:-1], refs[-1]
    width = slots[0].shape[-1] // 2
    for slot, ref in enumerate(slots):
        lanes = slice(slot % 2 * width, (slot % 2 + 1) * width)
        out[slot // 2, :, :, lanes] = ref[:, :, at * width : (at + 1) * width]


def pack_slots(slots, at, after=()):
    out = jax.ShapeDtypeStruct((len(slots) // 2, *slots[0].shape), BF16)
    (packed,), token = run(
        functools.partial(pack_kernel, at), "pack_slots", [out], [], slots, after
    )
    return packed, token


def assemble(whole, parts, places, pair, at_ref):
    for part, (away, who) in zip(parts, places):

        @pl.when(jnp.logical_or(who < 0, at_ref[1] == who))
        def _(part=part, away=away):
            band = part.shape[1]
            whole[pl.ds(jnp.bitwise_xor(at_ref[0], away) * band, band)] = part[pair]


def first_kernel(slots, places, count, at_ref, *refs):
    parts = refs[: len(places)]
    weight_ref, group_ref, basis_ref = refs[len(places) : len(places) + 3]
    whole, taps = refs[-2:]
    outs = refs[-2 - 2 * len(slots) : -2]
    rows, width, depth = outs[0].shape
    rank = basis_ref.shape[1] // 2
    cells = rows * width
    clear_edges(taps)
    held = None
    for at, slot in enumerate(slots):
        act_ref, sums_ref = outs[2 * at : 2 * at + 2]
        if slot // 2 != held:
            held = slot // 2
            assemble(whole, parts, places, held, at_ref)
        half = slot % 2
        values = whole[:, :, half * depth : (half + 1) * depth].astype(F32)
        unit, _ = normalized(values.reshape(cells, depth), group_ref[...], count)
        active = silu(unit).astype(BF16)
        act_ref[...] = active.reshape(act_ref.shape)
        taps[1 : rows + 1] = columns(active.astype(F32).reshape(act_ref.shape), False)
        total = conv_rows(taps, weight_ref, rows, False)
        along = jnp.dot(active, basis_ref[...], preferred_element_type=F32)
        along = along[:, :rank] + along[:, rank:]
        sums_ref[...] = jnp.concatenate([total, along], axis=1).astype(BF16)


def first_conv(parts, places, slots, weight, same_group, basis, row, rows, count, after=()):
    _, band, width, double = parts[0].shape
    depth = double // 2
    rank = basis.shape[1] // 2
    wide = weight.shape[2]
    cells = rows * width
    outs = [
        jax.ShapeDtypeStruct((rows, width, depth), BF16),
        jax.ShapeDtypeStruct((cells, wide + rank), BF16),
    ]
    made, token = run(
        functools.partial(first_kernel, slots, places, count),
        "first_conv",
        outs * len(slots),
        [row],
        [*parts, weight, same_group, basis],
        after,
        [
            pltpu.VMEM((rows, width, double), BF16),
            pltpu.VMEM((rows + 2, width, 3 * depth), BF16),
        ],
        14,
        18 * len(slots) * cells * depth * wide,
    )
    return [(made[2 * at], made[2 * at + 1]) for at in range(len(slots))], token


def back_kernel(slots, places, at_ref, *refs):
    bands = len(places)
    parts = refs[:bands]
    weight_ref, along_ref, other_ref = refs[bands : bands + 3]
    later_ref, whole, taps = refs[-3:]
    outs = refs[-3 - 2 * slots : -3]
    add_into(later_ref, along_ref, other_ref)
    rows, width, depth = outs[0].shape
    clear_edges(taps)
    for slot in reversed(range(slots)):
        cot_ref, sums_ref = outs[2 * slot : 2 * slot + 2]
        if slot % 2:
            assemble(whole, parts, places, slot // 2, at_ref)
        half = slot % 2
        values = whole[:, :, half * depth : (half + 1) * depth]
        cot_ref[...] = values
        taps[1 : rows + 1] = columns(values.astype(F32), True)
        sums_ref[...] = side_by_side(conv_rows(taps, weight_ref, rows, True)).astype(BF16)


def back_conv(parts, places, weight, alongs, row, rows, after=()):
    pairs, _, width, double = parts[0].shape
    depth = double // 2
    wide = weight.shape[2]
    cells = rows * width
    slots = 2 * pairs
    outs = [
        jax.ShapeDtypeStruct((rows, width, depth), BF16),
        jax.ShapeDtypeStruct((cells // 2, 2 * wide), BF16),
    ]
    made, token = run(
        functools.partial(back_kernel, slots, places),
        "back_conv",
        outs * slots + alongs[:1],
        [row],
        [*parts, weight, *alongs],
        after,
        [
            pltpu.VMEM((rows, width, double), BF16),
            pltpu.VMEM((rows + 2, width, 3 * depth), BF16),
        ],
        14,
        18 * slots * cells * depth * wide,
    )
    return [(made[2 * at], made[2 * at + 1]) for at in range(slots)], made[-1], token


def hidden_kernel(terms, count, *refs):
    group_ref, basis_ref = refs[terms : terms + 2]
    pay_ref, unit_ref, scale_ref, along_ref = refs[-4:]
    wide = unit_ref.shape[1]
    rank = basis_ref.shape[1] // 2
    total = refs[0][...].astype(F32)
    for term in refs[1:terms]:
        total = total + term[...].astype(F32)
    unit, scale = normalized(total[:, :wide], group_ref[...], count)
    unit_ref[...] = unit
    scale_ref[...] = scale
    hidden = silu(unit).astype(BF16)
    pay_ref[...] = jnp.concatenate([hidden.astype(F32), total[:, wide:]], axis=1).astype(BF16)
    along = jnp.dot(hidden, basis_ref[...], preferred_element_type=F32)
    along_ref[...] = side_by_side(along[:, :rank] + along[:, rank:]).astype(BF16)


def hidden_step(terms, same_group, basis, count, after=()):
    cells, both = terms[0].shape
    wide = same_group.shape[0]
    return run(
        functools.partial(hidden_kernel, len(terms), count),
        "hidden_step",
        [
            jax.ShapeDtypeStruct((cells, both), BF16),
            jax.ShapeDtypeStruct((cells, wide), F32),
            jax.ShapeDtypeStruct((1, wide), F32),
            jax.ShapeDtypeStruct((cells // 2, basis.shape[1]), BF16),
        ],
        [],
        [*terms, same_group, basis],
        after,
        held=12,
        flops=40 * cells * wide,
    )


def second_kernel(slots, bands, at_ref, *refs):
    pays = refs[:slots]
    weight_ref, along_ref, other_ref = refs[slots : slots + 3]
    later_ref, whole, taps = refs[-3:]
    outs = refs[-3 - bands : -3]
    add_into(later_ref, along_ref, other_ref)
    band, width, double = outs[0].shape[1:]
    rows = whole.shape[0]
    depth = taps.shape[2] // 3
    wide = double // 2
    clear_edges(taps)
    for slot in range(slots):
        hidden = pays[slot][:, :depth].astype(F32).reshape(rows, width, depth)
        taps[1 : rows + 1] = columns(hidden, False)
        whole[...] = conv_rows(taps, weight_ref, rows, False).reshape(rows, width, wide)
        lanes = slice(slot % 2 * wide, (slot % 2 + 1) * wide)
        for away in range(bands):
            start = jnp.bitwise_xor(at_ref[0], away) * band
            outs[away][slot // 2, :, :, lanes] = whole[pl.ds(start, band)].astype(BF16)


def second_conv(pays, weight, alongs, row, rows, bands, after=()):
    slots = len(pays)
    cells, _ = pays[0].shape
    width = cells // rows
    depth = weight.shape[1] // 3
    wide = weight.shape[2]
    out = jax.ShapeDtypeStruct((slots // 2, rows // bands, width, 2 * wide), BF16)
    return run(
        functools.partial(second_kernel, slots, bands),
        "second_conv",
        [out] * bands + alongs[:1],
        [row],
        [*pays, weight, *alongs],
        after,
        [
            pltpu.VMEM((rows, width, wide), F32),
            pltpu.VMEM((rows + 2, width, 3 * depth), BF16),
        ],
        14,
        18 * slots * cells * depth * wide,
    )


def band_kernel(terms, slots, *refs):
    outs = refs[-slots:]
    wide = outs[0].shape[-1]
    total = refs[0][...].astype(F32)
    for term in refs[1:terms]:
        total = total + term[...].astype(F32)
    for slot, out in enumerate(outs):
        lanes = slice(slot % 2 * wide, (slot % 2 + 1) * wide)
        out[...] = total[slot // 2, :, :, lanes].astype(BF16)


def band_step(terms, after=()):
    pairs, band, width, double = terms[0].shape
    out = jax.ShapeDtypeStruct((band, width, double // 2), BF16)
    return run(
        functools.partial(band_kernel, len(terms), 2 * pairs),
        "band_step",
        [out] * (2 * pairs),
        [],
        terms,
        after,
    )


def join_kernel(blocks, at_ref, x_ref, *refs):
    out = refs[-1]
    width = x_ref.shape[-1] // blocks
    for away in range(blocks):
        for block in range(blocks):

            @pl.when(jnp.bitwise_xor(at_ref[0], away) == block)
            def _(away=away, block=block):
                lanes = slice(block * width, (block + 1) * width)
                added = x_ref[:, :, lanes].astype(F32) + refs[away][...].astype(F32)
                out[:, :, lanes] = added.astype(BF16)


def join_blocks(x, parts, chip, after=()):
    return run(
        functools.partial(join_kernel, len(parts)),
        "join_blocks",
        [x],
        [chip],
        [x, *parts],
        after,
    )


def pre_kernel(terms, count, *refs):
    unit_ref, scale_ref, group_ref, along_ref, other_ref = refs[terms : terms + 5]
    out_ref, later_ref = refs[-2:]
    later_ref[0] = along_ref[...]
    later_ref[1] = other_ref[...]
    total = refs[0][...].astype(F32)
    for term in refs[1:terms]:
        total = total + term[...].astype(F32)
    unit = unit_ref[...]
    gate = 0.5 + 0.5 * jnp.tanh(0.5 * unit)
    grad = stacked_again(total) * (gate * (1.0 + unit * (1.0 - gate)))
    mean = group_sums(jnp.sum(grad, axis=0, keepdims=True), group_ref[...]) / count
    along = group_sums(jnp.sum(grad * unit, axis=0, keepdims=True), group_ref[...]) / count
    out_ref[...] = side_by_side(scale_ref[...] * (grad - mean - unit * along)).astype(BF16)


def pre_step(terms, unit, scale, same_group, alongs, count, after=()):
    cells, wide = unit.shape
    stacked = jax.ShapeDtypeStruct((2, *alongs[0].shape), BF16)
    return run(
        functools.partial(pre_kernel, len(terms), count),
        "pre_step",
        [jax.ShapeDtypeStruct((cells // 2, 2 * wide), BF16), stacked],
        [],
        [*terms, unit, scale, same_group, *alongs],
        after,
        held=12,
        flops=40 * cells * wide,
    )


def project(values, along, basis):
    both = jnp.concatenate([along, along], axis=1)
    return values - jnp.dot(both, basis, preferred_element_type=F32)


def grad_body(core_ref, left, left_t, taps, keep_ref, send_ref, width, flip):
    half = left.shape[1] // 2
    span = left.shape[0]
    wide = taps.shape[1] // 3
    turned = left[...].T

    @pl.when(core_ref[0] == 0)
    def _():
        left_t[...] = turned

    @pl.when(core_ref[0] != 0)
    def _():
        left_t[:half] = turned[half:]
        left_t[half:] = turned[:half]

    for tap in range(3):
        window = taps[tap * width : tap * width + span]
        result = jnp.dot(left_t[...], window, preferred_element_type=F32)
        first = 3 * (2 - tap if flip else tap)
        for q in range(3):
            lanes = slice(q * wide, (q + 1) * wide)
            keep_ref[first + q] = result[:half, lanes]
            send_ref[first + q] = result[half:, lanes].astype(BF16)


def fill_taps(taps, slot, rows, width, value):
    start = (slot * (rows + 1) + 1) * width
    taps[start : start + rows * width] = value.reshape(rows * width, value.shape[2])


def clear_gaps(left, taps, slots, rows, width):
    gap = rows + 1
    for slot in range(slots + 1):
        begin = slot * gap * width
        end = taps.shape[0] if slot == slots else begin + width
        taps[begin:end] = jnp.zeros((end - begin, taps.shape[1]), taps.dtype)
    for slot in range(slots):
        begin = (slot * gap + rows) * width
        end = left.shape[0] if slot == slots - 1 else begin + width
        left[begin:end] = jnp.zeros((end - begin, left.shape[1]), left.dtype)


def first_grad_kernel(slots, core_ref, *refs):
    acts, pays, grads = (refs[at * slots : (at + 1) * slots] for at in range(3))
    basis_ref = refs[3 * slots]
    keep_ref, send_ref, left, left_t, taps = refs[-5:]
    rows, width, depth = acts[0].shape
    cells = rows * width
    rank = basis_ref.shape[0] // 2
    wide = taps.shape[1] // 3
    clear_gaps(left, taps, slots, rows, width)
    for slot in range(slots):
        values = acts[slot][...].reshape(cells, depth).astype(F32)
        along = pays[slot][:, wide : wide + rank]
        begin = slot * (rows + 1) * width
        left[begin : begin + cells] = project(values, along, basis_ref[...]).astype(BF16)
        right = stacked_again(grads[slot][...].astype(F32)).reshape(rows, width, wide)
        fill_taps(taps, slot, rows, width, columns(right, True))
    grad_body(core_ref, left, left_t, taps, keep_ref, send_ref, width, True)


def second_grad_kernel(slots, core_ref, *refs):
    cots, pays = (refs[at * slots : (at + 1) * slots] for at in range(2))
    alongs = refs[2 * slots : 2 * slots + slots // 2]
    basis_ref = refs[2 * slots + slots // 2]
    keep_ref, send_ref, left, left_t, taps = refs[-5:]
    rows, width, depth = cots[0].shape
    cells = rows * width
    rank = basis_ref.shape[0] // 2
    wide = taps.shape[1] // 3
    clear_gaps(left, taps, slots, rows, width)
    for slot in range(slots):
        begin = slot * (rows + 1) * width
        left[begin : begin + cells] = cots[slot][...].reshape(cells, depth)
        packed = alongs[slot // 2][slot % 2]
        along = jnp.concatenate([packed[:, :rank], packed[:, rank:]], axis=0)
        values = pays[slot][:, :wide].astype(F32)
        right = project(values, along, basis_ref[...]).astype(BF16).astype(F32)
        fill_taps(taps, slot, rows, width, columns(right.reshape(rows, width, wide), False))
    grad_body(core_ref, left, left_t, taps, keep_ref, send_ref, width, False)


def weight_grad(kernel, name, core, lefts, firsts, seconds, basis, wide, after=()):
    slots = len(firsts)
    rows, width, depth = lefts[0].shape
    used = slots * (rows + 1) * width
    span = -(-used // 128) * 128
    half = depth // 2
    tap_rows = 2 * width + span
    return run(
        functools.partial(kernel, slots),
        name,
        [
            jax.ShapeDtypeStruct((9, half, wide), F32),
            jax.ShapeDtypeStruct((9, half, wide), BF16),
        ],
        [core],
        [*lefts, *firsts, *seconds, basis],
        after,
        [
            pltpu.VMEM((span, depth), BF16),
            pltpu.VMEM((depth, span), BF16),
            pltpu.VMEM((tap_rows, 3 * wide), BF16),
        ],
        28,
        18 * slots * rows * width * depth * wide,
    )


def halves_kernel(turn, core_ref, own_ref, other_ref, *refs):
    outs = refs[-2:] if turn else refs[-1:]
    half = own_ref.shape[1]

    @pl.when(core_ref[0] == 0)
    def _():
        outs[0][:, :half] = own_ref[...]
        outs[0][:, half:] = other_ref[...]

    @pl.when(core_ref[0] != 0)
    def _():
        outs[0][:, :half] = other_ref[...]
        outs[0][:, half:] = own_ref[...]

    if turn:
        for tap in range(9):
            outs[1][tap] = outs[0][tap].T


def join_halves(core, own, other, turn, after=()):
    _, half, wide = own.shape
    outs = [jax.ShapeDtypeStruct((9, 2 * half, wide), BF16)]
    if turn:
        outs.append(jax.ShapeDtypeStruct((9, wide, 2 * half), BF16))
    return run(
        functools.partial(halves_kernel, turn), "join_halves", outs, [core], [own, other], after,
        held=12,
    )


def basis_kernel(blocks, at_ref, basis_ref, *refs):
    rows_ref, columns_ref = refs[-2:]
    rank, channels = basis_ref.shape
    width = channels // blocks
    for block in range(blocks):

        @pl.when(at_ref[0] == block)
        def _(block=block):
            values = basis_ref[:, block * width : (block + 1) * width]
            high = values.astype(BF16).astype(F32)
            both = jnp.concatenate([high, values - high], axis=0)
            rows_ref[...] = both.astype(BF16)
            columns_ref[...] = both.T.astype(BF16)


def basis_parts(at, basis, blocks, after=()):
    rank, channels = basis.shape
    width = channels // blocks
    return run(
        functools.partial(basis_kernel, blocks),
        "basis_parts",
        [
            jax.ShapeDtypeStruct((2 * rank, width), BF16),
            jax.ShapeDtypeStruct((width, 2 * rank), BF16),
        ],
        [at],
        [basis],
        after,
    )


def flat_kernel(scale, keep_ref, got_ref, *refs):
    held = refs[-2 * (keep_ref.shape[2] // 128) - 2 :]
    out_ref = refs[-len(held) - 1]
    taps, half, wide = keep_ref.shape
    whole = wide // 128
    step = 2 * whole + 1
    count = half // 2
    zeros = jnp.zeros((half, 64), F32)
    for tap in range(taps):
        total = (keep_ref[tap] + got_ref[tap].astype(F32)) * scale
        for at in range(whole):
            held[at][...] = total[:, 128 * at : 128 * (at + 1)]
            held[whole + 2 + at][...] = total[:, 128 * at + 64 : 128 * (at + 1) + 64]
        held[whole][...] = jnp.concatenate([total[:, 128 * whole :], zeros], axis=1)
        held[whole + 1][...] = jnp.concatenate([zeros, total[:, :64]], axis=1)
        even, odd = pl.ds(0, count, stride=2), pl.ds(1, count, stride=2)
        rows = [held[at][even, :] for at in range(whole)]
        rows.append(held[whole][even, :] + held[whole + 1][odd, :])
        rows += [held[whole + 2 + at][odd, :] for at in range(whole)]
        for at, row in enumerate(rows):
            out_ref[pl.ds(tap * count * step + at, count, stride=step), :] = row


def flat_grad(keep, got, scale, after=()):
    taps, half, wide = keep.shape
    if wide % 128 != 64 or half % 2:
        made = (keep + got.astype(F32)) * scale
        return made, made
    (made,), token = run(
        functools.partial(flat_kernel, scale),
        "flat_grad",
        [jax.ShapeDtypeStruct((taps * half * wide // 128, 128), F32)],
        [],
        [keep, got],
        after,
        scratch=[pltpu.VMEM((half, 128), F32)] * (2 * (wide // 128) + 2),
        held=12,
    )
    return made, token


def same_groups(width, size):
    at = np.arange(width) // size
    return jnp.asarray((at[:, None] == at[None, :]).astype(np.float32), BF16)


def body(images, cotangent, first_weight, second_weight, first_basis, second_basis):
    n_dp = lax.axis_size("dp")
    n_rows = lax.axis_size("rows")
    chips = n_dp // 2
    _, band, width, channels = images.shape
    rows = band * n_rows
    dp_width = channels // n_dp
    chip_width = channels // chips
    row_width = channels // n_rows
    group = channels // GROUPS
    count = float(rows * width * group)
    grad_scale = 1.0 / math.sqrt(n_dp * images.shape[0] * rows * width)

    at_dp = lax.axis_index("dp")
    at_row = lax.axis_index("rows")
    chip = (at_dp // 2).astype(jnp.int32)
    core = (at_dp % 2).astype(jnp.int32)
    row = at_row.astype(jnp.int32)
    chip_at, core_at = chip[None], core[None]
    row_at = jnp.stack([row, (row + 1) // 2 % 2])

    def to_core(x):
        return lax.ppermute(x, "dp", [(i, i ^ 1) for i in range(n_dp)])

    def to_chip(x, away):
        return lax.ppermute(x, "dp", [(i, i ^ (2 * away)) for i in range(n_dp)])

    def to_row(x, away):
        return lax.ppermute(x, "rows", [(i, i ^ away) for i in range(n_rows)])

    def chips_gather(x):
        return [x] + [to_chip(x, away) for away in range(1, chips)]

    def rows_gather(x):
        if n_rows != 4:
            return [x] + [to_row(x, away) for away in range(1, n_rows)], [
                (away, -1) for away in range(n_rows)
            ]
        second = to_row(x, 2)
        first = to_row(x, 1)
        passed = lax.ppermute(second, "rows", [(2, 3), (1, 0)])
        later, _ = lax.optimization_barrier((x, second))
        middle = lax.ppermute(later, "rows", [(1, 2), (2, 1)])
        return [x, first, second, middle, passed], [(0, -1), (1, -1), (2, -1), (3, 1), (3, 0)]

    def chips_swap(parts):
        return [parts[0]] + [to_chip(parts[away], away) for away in range(1, chips)]

    def rows_swap(parts):
        far = [to_row(parts[away], away) for away in range(n_rows - 1, 0, -1)]
        return parts[:1] + far[::-1]

    chip_groups = same_groups(chip_width, group)
    row_groups = same_groups(row_width, group)

    slots = chips_swap(split_blocks([images[0], cotangent[0]], chips, chip_at))
    image_pack, _ = pack_slots(slots, 0)
    image_parts, places = rows_gather(image_pack)

    first_weight, _ = lax.optimization_barrier((first_weight, slots[1]))
    second_weight, _ = lax.optimization_barrier((second_weight, image_parts[1:3]))
    own_first = first_weight.reshape(9, dp_width, row_width)
    own_second = second_weight.reshape(9, dp_width, row_width)
    early = tuple(image_parts[1:3])
    (second_full, second_turned), second_done = join_halves(
        core_at, own_second, to_core(own_second), True, early
    )
    (one_rows, one_columns), one_done = basis_parts(chip_at, first_basis, chips, early)
    (two_rows, two_columns), two_done = basis_parts(row_at, second_basis, n_rows, early)
    (first_full,), first_done = join_halves(core_at, own_first, to_core(own_first), False, early)
    cot_pack, cot_done = pack_slots(
        slots, 1, (*image_parts[3:], one_done, two_done, first_done, second_done)
    )
    cot_parts, _ = rows_gather(cot_pack)
    weight_one = first_full.reshape(3, 3 * chip_width, row_width)
    weight_back = second_full.reshape(3, 3 * chip_width, row_width)
    weight_two = second_turned.reshape(3, 3 * row_width, chip_width)

    made, first_terms, done = {}, {}, (cot_done,)
    for slot in range(chips - 1, -1, -1):
        if slot == 0:
            done += (first_terms[chips - 1], first_terms[2], *cot_parts[3:])
        ((active, sums),), token = first_conv(
            image_parts, places, [slot], weight_one, chip_groups, one_columns, row_at, rows, count,
            done,
        )
        made[slot] = active
        first_terms[slot] = to_chip(sums, slot) if slot else sums
        done = (token,)
    active = [made[slot] for slot in range(chips)]
    first_terms = [first_terms[slot] for slot in range(chips)]

    (pay, unit, scale, along), hidden_done = hidden_step(
        first_terms, row_groups, two_columns, count
    )
    pays = chips_gather(pay)

    away = 4
    while away < n_rows:
        along = (along.astype(F32) + to_row(along, away).astype(F32)).astype(BF16)
        away *= 2
    back, along, back_done = back_conv(
        cot_parts, places, weight_back, [along, to_row(along, 1)], row_at, rows, (hidden_done,)
    )
    whole_cot = [pair[0] for pair in back]
    back_terms = chips_swap([pair[1] for pair in back])

    (*sums, along), sums_done = second_conv(
        pays, weight_two, [along, to_row(along, 2)], row_at, rows, n_rows, (back_done,)
    )
    band_terms = rows_swap(sums)

    (pre_grad, along), pre_done = pre_step(
        back_terms, unit, scale, row_groups, [along, to_chip(along, 1)], count,
        (sums_done,),
    )
    pre_grads = chips_gather(pre_grad)
    alongs = [along]
    away = 2
    while away < chips:
        alongs += [to_chip(part, away) for part in alongs]
        away *= 2

    second_halves, second_made = weight_grad(
        second_grad_kernel, "second_grad", core_at, whole_cot, pays, alongs, two_rows,
        row_width, (pre_done, band_terms[-1]),
    )
    blocks, blocks_done = band_step(band_terms, (second_made,))
    first_halves, _ = weight_grad(
        first_grad_kernel, "first_grad", core_at, active, pays, pre_grads, one_rows,
        row_width, (blocks_done,),
    )
    second_grad, second_flat = flat_grad(
        second_halves[0], to_core(second_halves[1]), grad_scale
    )
    first_grad, first_flat = flat_grad(
        first_halves[0], to_core(first_halves[1]), grad_scale, (second_flat,)
    )
    (block_output,), _ = join_blocks(
        images[0], chips_swap(blocks), chip_at, (first_flat,)
    )
    block_output = block_output[None]
    first_grad = first_grad.reshape(1, 1, 9, dp_width * row_width)
    second_grad = second_grad.reshape(1, 1, 9, dp_width * row_width)
    return (block_output, first_grad, second_grad)


def solution(mesh):
    split = P("dp", "rows", None, None)
    return jax.shard_map(
        body,
        mesh=mesh,
        in_specs=(split, split, split, split, P(), P()),
        out_specs=(split, split, split),
        check_vma=False,
    )
```
